32 devices in a mesh: dp: 4 (over y, x), seq: 8 (over z, core).
Axes of the slice: x: 2, y: 2, z: 4, core: 2. Of those that a mesh axis runs over, the one named last changes fastest.
Arguments:
- history: bfloat16 [9, 4, 3072, 1024], P(None, 'dp', 'seq'), may hold values from -6 to 6
- documents: int32 [4, 3072], P('dp'), may hold values from 0 to 4, as said below
- cotangent: bfloat16 [4, 3072, 1024], P('dp', 'seq'), may hold values from -6 to 6
- mixer_gain: bfloat16 [1024], replicated, may hold values from 0.25 to 1.75
- mixer_inner: bfloat16 [1024, 36], replicated, may hold values from -0.1875 to 0.1875
- mixer_outer: bfloat16 [36, 36], replicated, may hold values from -0.5 to 0.5
- mixer_bias: bfloat16 [36], replicated, may hold values from -1.5 to 1.5
- stream_gain: bfloat16 [4, 1024], replicated, may hold values from 0.25 to 1.75
- stream_bias: bfloat16 [4, 1024], replicated, may hold values from -1.5 to 1.5
- inbound_weight: bfloat16 [1024, 3072], P(('dp', 'seq')), may hold values from -0.1875 to 0.1875
- inbound_bias: bfloat16 [3072], replicated, may hold values from -1.5 to 1.5
- outbound_weight: bfloat16 [1024, 1024], P(('dp', 'seq')), may hold values from -1.5 to 1.5
- outbound_bias: bfloat16 [1024], replicated, may hold values from -1.5 to 1.5
- expand: bfloat16 [1024, 4096], P(('dp', 'seq')), may hold values from -0.1875 to 0.1875
- expand_bias: bfloat16 [4096], replicated, may hold values from -1.5 to 1.5
- contract: bfloat16 [1024, 4096], P(('dp', 'seq')), may hold values from -0.09375 to 0.09375
- contract_bias: bfloat16 [1024], replicated, may hold values from -1.5 to 1.5
Outputs:
- layer_out: bfloat16 [4, 3072, 1024], P('dp', 'seq')
- history_grad: float32 [9, 4, 3072, 1024], P(None, 'dp', 'seq')
- mixer_gain_grad: float32 [1024], replicated
- mixer_inner_grad: float32 [1024, 36], replicated
- mixer_outer_grad: float32 [36, 36], replicated
- mixer_bias_grad: float32 [36], replicated
- stream_gain_grad: float32 [4, 1024], replicated
- stream_bias_grad: float32 [4, 1024], replicated
- inbound_weight_grad: float32 [1024, 3072], P(('dp', 'seq'))
- inbound_bias_grad: float32 [3072], replicated
- outbound_weight_grad: float32 [1024, 1024], P(('dp', 'seq'))
- outbound_bias_grad: float32 [1024], replicated
- expand_grad: float32 [1024, 4096], P(('dp', 'seq'))
- expand_bias_grad: float32 [4096], replicated
- contract_grad: float32 [1024, 4096], P(('dp', 'seq'))
- contract_bias_grad: float32 [1024], replicated
The draws below stay inside these ranges and needn't reach their ends.
Inputs may be any that keep to these rules, and one draw needn't show every extreme that they name: Along each sequence the ids never fall and rise by one at each of four document starts, so there are five documents; document 2 begins within the first 384 positions and ends within the last 384 positions.
All inputs are finite; a program needn't handle non-finite values.
Results may differ from the reference program's by a relative error of at most 0.012.
The reference program's roundings to bfloat16 on the way count: a program that leaves them out, or rounds other values in their place, can miss the bound.
Values may be sent and summed in bfloat16 or wider, within the bound.
A program may use at most 256 MiB of HBM per device.

```python
import jax
import jax.numpy as jnp
from jax import lax

D = 1024
FF = 4096
HEADS = 16
HEAD_DIM = 64
ROT_DIMS = 16
HIST = 9
MIX = 36
TOK_DEV = 384
LENGTH = 3072
BATCH = 4


def draw_documents(key, part):
    key = jax.random.fold_in(key, 7)
    first, second, third, fourth = jax.random.split(key, 4)
    start = jax.random.randint(first, (BATCH, 1), 2, TOK_DEV)
    finish = jax.random.randint(second, (BATCH, 1), LENGTH - TOK_DEV + 1, LENGTH - 1)
    before = jax.random.randint(third, (BATCH, 1), 1, start)
    after = jax.random.randint(fourth, (BATCH, 1), finish + 1, LENGTH)
    places = jnp.arange(LENGTH, dtype=jnp.int32)[None, :]
    return (places >= before).astype(jnp.int32) + (places >= start).astype(jnp.int32) + (places >= finish).astype(jnp.int32) + (places >= after).astype(jnp.int32)


def shard_levels(stream_key, shape, cuts, least, largest):
    loudness, own = 1.0, jax.random.fold_in(stream_key, 6)
    for dim, parts in cuts:
        steps = jnp.exp(jax.random.uniform(jax.random.fold_in(own, dim), (parts,), jnp.float32, least / len(cuts), largest / len(cuts)))
        loudness = loudness * jnp.repeat(steps, shape[dim] // parts).reshape([-1 if axis == dim else 1 for axis in range(len(shape))])
    return loudness


def noise(own_key, shape, width, limit, pieces=(), held_as=jnp.bfloat16):
    level = shard_levels(own_key, shape, pieces, -0.22, 0.18) if pieces else 1.0
    drawn = jax.random.normal(own_key, shape, jnp.float32) * width * level
    return jnp.minimum(jnp.maximum(drawn, -limit), limit).astype(held_as)


def setup_inputs(seed: int = 0) -> dict:
    splits = jax.random.split(jax.random.key(seed), 18)
    history = noise(splits[0], (HIST, BATCH, LENGTH, D), 1.0, 6.0, ((1, 4), (2, 8)))
    documents = draw_documents(jax.random.fold_in(splits[17], 71), 0)
    cotangent = noise(splits[2], (BATCH, LENGTH, D), 1.0, 6.0, ((0, 4), (1, 8)))
    mixer_gain = jnp.clip(1.0 + 0.15 * jax.random.normal(splits[3], (D,), jnp.float32), 0.25, 1.75).astype(jnp.bfloat16)
    mixer_inner = noise(splits[4], (D, MIX), D ** -0.5, 0.1875)
    mixer_outer = noise(splits[5], (MIX, MIX), (4 * MIX) ** -0.5, 0.5)
    mixer_bias = noise(splits[6], (MIX,), 0.3, 1.5)
    stream_gain = jnp.clip(1.0 + 0.15 * jax.random.normal(splits[7], (4, D), jnp.float32), 0.25, 1.75).astype(jnp.bfloat16)
    stream_bias = noise(splits[8], (4, D), 0.3, 1.5)
    inbound_weight = noise(splits[9], (D, 3 * D), D ** -0.5, 0.1875, ((0, 32),))
    inbound_bias = noise(splits[10], (3 * D,), 0.3, 1.5)
    outbound_weight = noise(splits[11], (D, D), (D // 64) ** -0.5, 1.5, ((0, 32),))
    outbound_bias = noise(splits[12], (D,), 0.3, 1.5)
    expand = noise(splits[13], (D, FF), D ** -0.5, 0.1875, ((0, 32),))
    expand_bias = noise(splits[14], (FF,), 0.3, 1.5)
    contract = noise(splits[15], (D, FF), FF ** -0.5, 0.09375, ((0, 32),))
    contract_bias = noise(splits[16], (D,), 0.3, 1.5)
    return {"history": history, "documents": documents, "cotangent": cotangent, "mixer_gain": mixer_gain, "mixer_inner": mixer_inner, "mixer_outer": mixer_outer, "mixer_bias": mixer_bias, "stream_gain": stream_gain, "stream_bias": stream_bias, "inbound_weight": inbound_weight, "inbound_bias": inbound_bias, "outbound_weight": outbound_weight, "outbound_bias": outbound_bias, "expand": expand, "expand_bias": expand_bias, "contract": contract, "contract_bias": contract_bias}


EPS = 1e-05
HIGHEST = lax.Precision.HIGHEST
NEG = -1e+30

@jax.custom_vjp
def low(v):
    return lax.optimization_barrier(v.astype(jnp.bfloat16)).astype(jnp.float32)

@jax.custom_vjp
def low_back(v):
    return v

def low_keep(v):
    return (low(v), None)

def low_pass(kept, grad):
    return (grad,)

def back_keep(v):
    return (v, None)

def back_low(kept, grad):
    return (low(grad),)
low.defvjp(low_keep, low_pass)
low_back.defvjp(back_keep, back_low)

def matmul(left, right):
    return jnp.dot(left, right, precision=HIGHEST)

def exact_gelu(value):
    return jax.nn.gelu(value, approximate=False)

def rms_scale(last, gain):
    return last * lax.rsqrt(lax.optimization_barrier(jnp.mean(last * last, axis=-1, keepdims=True)) + EPS) * gain

def layer_norm(streams, gains, biases):
    center = lax.optimization_barrier(jnp.mean(streams, axis=-1, keepdims=True))
    centered = streams - center
    spread = lax.optimization_barrier(jnp.mean(centered * centered, axis=-1, keepdims=True))
    return centered * lax.rsqrt(spread + EPS) * gains[:, None, :] + biases[:, None, :]

def rotary_tables(positions):
    half = ROT_DIMS // 2
    freq = 10000.0 ** (-jnp.arange(half).astype(jnp.float32) * 2.0 / ROT_DIMS)
    angles = positions.astype(jnp.float32)[:, None] * freq[None, :]
    angles = jnp.concatenate([angles, angles], axis=-1)
    return (jnp.cos(angles)[:, None, :], jnp.sin(angles)[:, None, :])

def rotate(value, cosine, sine):
    half = ROT_DIMS // 2
    part = value[..., :ROT_DIMS]
    turned = jnp.concatenate([-part[..., half:], part[..., :half]], axis=-1)
    return jnp.concatenate([part * cosine + turned * sine, value[..., ROT_DIMS:]], axis=-1)

def one_sequence(params, history, docs):
    mixer_gain, mixer_inner, mixer_outer, mixer_bias, stream_gain, stream_bias, inbound_weight, inbound_bias, outbound_weight, outbound_bias, expand, expand_bias, contract, contract_bias = params
    scaled = rms_scale(history[HIST - 1], mixer_gain)
    mix_pre = low_back(matmul(low(scaled), mixer_inner))
    mix_hidden = low(exact_gelu(mix_pre))
    coeffs = (low_back(matmul(mix_hidden, mixer_outer)) + mixer_bias).reshape(LENGTH, 4, HIST)
    streams = jnp.einsum('tcj,jtd->ctd', coeffs, history, precision=HIGHEST)
    lowered = low(layer_norm(streams, stream_gain, stream_bias))
    queries = low_back(matmul(lowered[0], inbound_weight[:, :D])) + inbound_bias[:D]
    keys = low_back(matmul(lowered[1], inbound_weight[:, D:2 * D])) + inbound_bias[D:2 * D]
    values = low(low_back(matmul(lowered[2], inbound_weight[:, 2 * D:])) + inbound_bias[2 * D:])
    positions = jnp.arange(LENGTH).astype(jnp.int32)
    cosine, sine = rotary_tables(positions)
    queries = low(rotate(queries.reshape(LENGTH, HEADS, HEAD_DIM), cosine, sine))
    keys = low(rotate(keys.reshape(LENGTH, HEADS, HEAD_DIM), cosine, sine))
    values = values.reshape(LENGTH, HEADS, HEAD_DIM)
    block = min(512, LENGTH)
    scale = 1.0 / HEAD_DIM ** 0.5

    def attend(args):
        query_block, doc_block, place_block = args
        scores = low_back(jnp.einsum('qhd,khd->hqk', query_block, keys, precision=HIGHEST) * scale)
        allowed = (doc_block[:, None] == docs[None, :]) & (positions[None, :] <= place_block[:, None])
        scores = jnp.where(allowed[None], scores, NEG)
        top = lax.optimization_barrier(jnp.max(scores, axis=-1, keepdims=True))
        weights = jnp.exp(scores - top)
        probs = weights / lax.optimization_barrier(jnp.sum(weights, axis=-1, keepdims=True))
        return jnp.einsum('hqk,khd->qhd', low(probs), values, precision=HIGHEST)
    blocks = LENGTH // block
    attended = lax.map(jax.checkpoint(attend), (queries.reshape(blocks, block, HEADS, HEAD_DIM), docs.reshape(blocks, block), positions.reshape(blocks, block)))
    attended = low(low_back(attended.reshape(LENGTH, D)))
    attention = low_back(matmul(attended, outbound_weight.T)) + outbound_bias
    expanded = low_back(matmul(lowered[3], expand)) + expand_bias
    hidden = low(exact_gelu(expanded))
    feed = low_back(matmul(hidden, contract.T)) + contract_bias
    return streams[3] + attention + feed

def reference(history, documents, cotangent, mixer_gain, mixer_inner, mixer_outer, mixer_bias, stream_gain, stream_bias, inbound_weight, inbound_bias, outbound_weight, outbound_bias, expand, expand_bias, contract, contract_bias):
    params = tuple((w.astype(jnp.float32) for w in (mixer_gain, mixer_inner, mixer_outer, mixer_bias, stream_gain, stream_bias, inbound_weight, inbound_bias, outbound_weight, outbound_bias, expand, expand_bias, contract, contract_bias)))
    history_full = history.astype(jnp.float32)

    def forward(history_all, weights):

        def per_sequence(args):
            seq_history, seq_docs = args
            return one_sequence(weights, seq_history, seq_docs)
        return lax.map(jax.checkpoint(per_sequence), (jnp.moveaxis(history_all, 1, 0), documents))
    output, pull = jax.vjp(forward, history_full, params)
    history_grad, grads = pull(cotangent.astype(jnp.float32))
    return (output.astype(jnp.bfloat16), history_grad, grads[0], grads[1], grads[2], grads[3], grads[4], grads[5], grads[6], grads[7], grads[8], grads[9], grads[10], grads[11], grads[12], grads[13])
```

```python
import functools
import math

import jax
import jax.numpy as jnp
from jax import lax
from jax.experimental import pallas as pl
from jax.experimental.pallas import tpu as pltpu
from jax.sharding import PartitionSpec as P

HEADS = 16
HEAD_DIM = 64
ROT_DIMS = 16
EPS = 1e-05
HIGHEST = lax.Precision.HIGHEST
NEG = -1e30
MESH = pl.DeviceIdType.MESH
F32 = jnp.float32
BF16 = jnp.bfloat16
VMEM_LIMIT = 56 * 1024 * 1024


def inner(left, right):
    return lax.dot_general(left, right, (((0,), (0,)), ((), ())), preferred_element_type=F32)


def against(left, right):
    return lax.dot_general(left, right, (((1,), (1,)), ((), ())), preferred_element_type=F32)


def product(left, right):
    return jnp.dot(left, right, preferred_element_type=F32)


def exact_gelu(value):
    return jax.nn.gelu(value, approximate=False)


def rms_scale(last, gain):
    return last * lax.rsqrt(jnp.mean(last * last, axis=-1, keepdims=True) + EPS) * gain


def layer_norm(streams, gains, biases):
    center = jnp.mean(streams, axis=-1, keepdims=True)
    centered = streams - center
    spread = jnp.mean(centered * centered, axis=-1, keepdims=True)
    return centered * lax.rsqrt(spread + EPS) * gains[:, None, :] + biases[:, None, :]


def rotary_tables(positions, width):
    half = ROT_DIMS // 2
    place = jnp.arange(width) % HEAD_DIM
    freq = 10000.0 ** (-(place % half).astype(F32) * 2.0 / ROT_DIMS)
    angles = positions.astype(F32)[:, None] * freq[None, :]
    turned = (place < ROT_DIMS)[None, :]
    cosine = jnp.where(turned, jnp.cos(angles), 1.0)
    sine = jnp.where(turned, jnp.sin(angles), 0.0)
    above = jnp.where((place < half)[None, :], -sine, 0.0)
    below = jnp.where((place < half)[None, :], 0.0, sine)
    return cosine, above, below


def rotate(value, tables, sign):
    half = ROT_DIMS // 2
    cosine, above, below = tables
    up = jnp.roll(value, -half, axis=-1)
    down = jnp.roll(value, half, axis=-1)
    return value * cosine + sign * (up * above + down * below)


class Grid:
    def __init__(self, n_dp, n_seq):
        self.n_dp, self.n_seq = n_dp, n_seq
        self.na, self.nb, self.nz = 2, n_dp // 2, n_seq // 2

    def here(self):
        dp, seq = lax.axis_index("dp"), lax.axis_index("seq")
        return dp // self.nb, lax.rem(dp, self.nb), seq // 2, lax.rem(seq, 2)

    def device(self, a, b, z, c):
        return (a * self.nb + b, z * 2 + c)

    def peers(self, a, b, z, c):
        found = [self.device(a, b, z, 1 - c), self.device(1 - a, b, z, c)]
        found += [self.device(a, lax.rem(b + k, self.nb), z, c) for k in range(1, self.nb)]
        found += [self.device(a, b, lax.rem(z + k, self.nz), c) for k in range(1, self.nz)]
        return found

    def greet(self, a, b, z, c):
        barrier = pltpu.get_barrier_semaphore()
        found = self.peers(a, b, z, c)
        for peer in found:
            pl.semaphore_signal(barrier, inc=1, device_id=peer, device_id_type=MESH)
        pl.semaphore_wait(barrier, len(found))


def remote(src, dst, send, recv, device):
    return pltpu.make_async_remote_copy(
        src_ref=src, dst_ref=dst, send_sem=send, recv_sem=recv, device_id=device, device_id_type=MESH
    )


def gather_kernel(grid, rows, chunks, n_in, n_out, *refs):
    ins, outs = refs[:n_in], refs[n_in : n_in + n_out]
    local_sem, send_sem, recv_sem = refs[n_in + n_out :]
    a, b, z, c = grid.here()
    nz, nb = grid.nz, grid.nb
    grid.greet(a, b, z, c)
    slots = {"pair": 0, "z": 1, "b": nz, "a": nz + nb - 1}

    def begin(t, stage):
        src_i, base, dst_i, col, n, order = chunks[t]
        out = outs[dst_i]
        cols = pl.ds(col, n)
        copies = []
        if stage == 0:
            mine = ins[src_i].at[:, pl.ds(pl.multiple_of(base(c), 128), n)]
            theirs = ins[src_i].at[:, pl.ds(pl.multiple_of(base(1 - c), 128), n)]
            spot = out.at[a, b, z, pl.ds(pl.multiple_of(c * rows, rows), rows), cols]
            copies.append(pltpu.make_async_copy(mine, spot, local_sem.at[t]))
            copies.append(remote(theirs, spot, send_sem.at[t, 0], recv_sem.at[t, 0], grid.device(a, b, z, 1 - c)))
        elif stage == 1:
            block = out.at[a, b, z, :, cols]
            for k in range(1, nz):
                s = slots["z"] + k - 1
                copies.append(remote(block, block, send_sem.at[t, s], recv_sem.at[t, s], grid.device(a, b, lax.rem(z + k, nz), c)))
        else:
            axis = order[stage - 2]
            if axis == "b":
                block = out.at[a, b, :, :, cols] if stage == 2 else out.at[:, b, :, :, cols]
                for k in range(1, nb):
                    s = slots["b"] + k - 1
                    copies.append(remote(block, block, send_sem.at[t, s], recv_sem.at[t, s], grid.device(a, lax.rem(b + k, nb), z, c)))
            else:
                block = out.at[a, b, :, :, cols] if stage == 2 else out.at[a, :, :, :, cols]
                s = slots["a"]
                copies.append(remote(block, block, send_sem.at[t, s], recv_sem.at[t, s], grid.device(1 - a, b, z, c)))
        for copy in copies:
            copy.start()
        return copies

    started = {}
    count = len(chunks)
    for turn in range(count + 4):
        for stage in (4, 3, 2, 1, 0):
            t = turn - stage
            if 0 <= t < count:
                if stage > 0:
                    for copy in started[t, stage - 1]:
                        copy.wait()
                if stage < 4:
                    started[t, stage] = begin(t, stage)


def gather(grid, arrays, chunks, widths, collective_id, name):
    rows = arrays[0].shape[0]
    slots = grid.nz + grid.nb
    outs = [jax.ShapeDtypeStruct((grid.na, grid.nb, grid.nz, 2 * rows, w), BF16) for w in widths]
    moved = sum(w for w in widths) * 2 * rows * grid.na * grid.nb * grid.nz * 2
    results = pl.pallas_call(
        functools.partial(gather_kernel, grid, rows, chunks, len(arrays), len(outs)),
        out_shape=outs,
        in_specs=[pl.BlockSpec(memory_space=pl.ANY)] * len(arrays),
        out_specs=[pl.BlockSpec(memory_space=pl.ANY)] * len(outs),
        scratch_shapes=[
            pltpu.SemaphoreType.DMA((len(chunks),)),
            pltpu.SemaphoreType.DMA((len(chunks), slots)),
            pltpu.SemaphoreType.DMA((len(chunks), slots)),
        ],
        compiler_params=pltpu.CompilerParams(collective_id=collective_id, has_side_effects=True),
        cost_estimate=pl.CostEstimate(flops=0, bytes_accessed=moved * 20, transcendentals=0),
        name=name,
    )(*arrays)
    return [r.reshape(-1, r.shape[-1]) for r in results]


def scatter_kernel(grid, orders, *refs):
    count = len(orders)
    parts, outs = refs[:count], refs[count : 2 * count]
    scratch = refs[2 * count :]
    first, second, third, final, theirs = (scratch[i * count : (i + 1) * count] for i in range(5))
    send_sem, recv_sem = scratch[5 * count :]
    a, b, z, c = grid.here()
    na, nb, nz = grid.na, grid.nb, grid.nz
    rows = parts[0].shape[3] // 2
    grid.greet(a, b, z, c)
    slots = {"pair": 0, "z": 1, "b": nz, "a": nz + nb - 1}

    def launch(copies):
        for copy in copies:
            copy.start()
        return copies

    def to_b(t, src, dst):
        return [
            remote(src(lax.rem(b + k, nb)), dst(k - 1), send_sem.at[t, slots["b"] + k - 1], recv_sem.at[t, slots["b"] + k - 1],
                   grid.device(a, lax.rem(b + k, nb), z, c))
            for k in range(1, nb)
        ]

    def to_a(t, src, dst):
        return [remote(src(1 - a), dst(0), send_sem.at[t, slots["a"]], recv_sem.at[t, slots["a"]], grid.device(1 - a, b, z, c))]

    def begin(t, stage):
        part, order = parts[t], orders[t]
        n = part.shape[-1]
        if stage == 0:
            if order == "ab":
                return launch(to_a(t, lambda o: part.at[o], lambda k: first[t].at[k]))
            return launch(to_b(t, lambda o: part.at[:, o], lambda k: first[t].at[k]))
        if stage == 1:
            peers, length = first[t].shape[0], first[t].shape[1]

            def add(i, carry):
                o, j = i // nz, lax.rem(i, nz)
                own = part[a, o, j] if order == "ab" else part[o, b, j]
                total = own.astype(F32)
                for k in range(peers):
                    total = total + first[t][k, o, j].astype(F32)
                first[t][0, o, j] = total.astype(BF16)
                return carry

            lax.fori_loop(0, length * nz, add, 0)
            if order == "ab":
                return launch(to_b(t, lambda o: first[t].at[0, o], lambda k: second[t].at[k]))
            return launch(to_a(t, lambda o: first[t].at[0, o], lambda k: second[t].at[k]))
        if stage == 2:
            peers = second[t].shape[0]
            mine = b if order == "ab" else a

            def add(j, carry):
                total = first[t][0, mine, j].astype(F32)
                for k in range(peers):
                    total = total + second[t][k, j].astype(F32)
                second[t][0, j] = total.astype(BF16)
                return carry

            lax.fori_loop(0, nz, add, 0)
            return launch([
                remote(second[t].at[0, lax.rem(z + k, nz)], third[t].at[k - 1], send_sem.at[t, k], recv_sem.at[t, k],
                       grid.device(a, b, lax.rem(z + k, nz), c))
                for k in range(1, nz)
            ])
        total = second[t][0, z].astype(F32)
        for k in range(nz - 1):
            total = total + third[t][k].astype(F32)
        final[t][...] = total.reshape(2, rows, n)
        return launch([remote(final[t].at[1 - c], theirs[t], send_sem.at[t, 0], recv_sem.at[t, 0], grid.device(a, b, z, 1 - c))])

    started = {}
    for turn in range(count + 4):
        for stage in (4, 3, 2, 1, 0):
            t = turn - stage
            if 0 <= t < count:
                if stage > 0:
                    for copy in started[t, stage - 1]:
                        copy.wait()
                if stage < 4:
                    started[t, stage] = begin(t, stage)
                else:
                    n = parts[t].shape[-1]
                    outs[t][c] = final[t][c]
                    outs[t][1 - c] = theirs[t][...]


def scatter(grid, parts, orders, collective_id, name):
    rows = parts[0].shape[0] // (grid.na * grid.nb * grid.nz)
    na, nb, nz = grid.na, grid.nb, grid.nz
    shaped = [p.reshape(na, nb, nz, rows, p.shape[1]) for p in parts]
    widths = [p.shape[1] for p in parts]
    first = [pltpu.VMEM((1, nb, nz, rows, w) if o == "ab" else (nb - 1, na, nz, rows, w), BF16) for o, w in zip(orders, widths)]
    second = [pltpu.VMEM((nb - 1, nz, rows, w) if o == "ab" else (1, nz, rows, w), BF16) for o, w in zip(orders, widths)]
    third = [pltpu.VMEM((nz - 1, rows, w), BF16) for w in widths]
    final = [pltpu.VMEM((2, rows // 2, w), F32) for w in widths]
    theirs = [pltpu.VMEM((rows // 2, w), F32) for w in widths]
    moved = sum(widths) * rows * na * nb * nz * 2
    return pl.pallas_call(
        functools.partial(scatter_kernel, grid, orders),
        out_shape=[jax.ShapeDtypeStruct((2, rows // 2, w), F32) for w in widths],
        in_specs=[pl.BlockSpec(memory_space=pltpu.VMEM)] * len(parts),
        out_specs=[pl.BlockSpec(memory_space=pltpu.VMEM)] * len(parts),
        scratch_shapes=first + second + third + final + theirs + [
            pltpu.SemaphoreType.DMA((len(parts), nz + nb)),
            pltpu.SemaphoreType.DMA((len(parts), nz + nb)),
        ],
        compiler_params=pltpu.CompilerParams(collective_id=collective_id, has_side_effects=True, vmem_limit_bytes=VMEM_LIMIT),
        cost_estimate=pl.CostEstimate(flops=0, bytes_accessed=moved * 20, transcendentals=0),
        name=name,
    )(*shaped)


def small_kernel(n_dp, n_seq, x_ref, out_ref, held, total, send_sem, recv_sem):
    count = n_dp * n_seq
    me = lax.axis_index("dp") * n_seq + lax.axis_index("seq")

    def device(k):
        other = lax.rem(me + k, count)
        return other, (other // n_seq, lax.rem(other, n_seq))

    barrier = pltpu.get_barrier_semaphore()

    def greet(k, carry):
        pl.semaphore_signal(barrier, inc=1, device_id=device(k)[1], device_id_type=MESH)
        return carry

    lax.fori_loop(1, count, greet, 0)
    pl.semaphore_wait(barrier, count - 1)

    def deal(k, carry):
        other, place = device(k)
        remote(x_ref.at[other], held.at[me], send_sem.at[0], recv_sem.at[0], place).start()
        return carry

    lax.fori_loop(1, count, deal, 0)
    held[me] = x_ref[me]
    most = pl.ds(0, count - 1)
    everyone = device(1)[1]
    remote(x_ref.at[most], held.at[most], send_sem.at[0], recv_sem.at[0], everyone).wait()
    total[...] = lax.fori_loop(1, count, lambda k, s: s + held[k], held[0])

    def tell(k, carry):
        place = device(k)[1]
        remote(total, out_ref.at[me], send_sem.at[1], recv_sem.at[1], place).start()
        return carry

    lax.fori_loop(1, count, tell, 0)
    out_ref[me] = total[...]
    remote(x_ref.at[most], out_ref.at[most], send_sem.at[1], recv_sem.at[1], everyone).wait()


def small_sum(n_dp, n_seq, arrays, collective_id):
    count = n_dp * n_seq
    flat = jnp.concatenate([x.reshape(-1) for x in arrays])
    rows = -(-flat.shape[0] // (count * 128 * 8)) * 8
    padded = jnp.pad(flat, (0, count * rows * 128 - flat.shape[0])).reshape(count, rows, 128)
    summed = pl.pallas_call(
        functools.partial(small_kernel, n_dp, n_seq),
        out_shape=jax.ShapeDtypeStruct(padded.shape, F32),
        in_specs=[pl.BlockSpec(memory_space=pltpu.VMEM)],
        out_specs=pl.BlockSpec(memory_space=pltpu.VMEM),
        scratch_shapes=[
            pltpu.VMEM(padded.shape, F32),
            pltpu.VMEM((rows, 128), F32),
            pltpu.SemaphoreType.DMA((2,)),
            pltpu.SemaphoreType.DMA((2,)),
        ],
        compiler_params=pltpu.CompilerParams(collective_id=collective_id, has_side_effects=True),
        name="small_sum",
    )(padded).reshape(-1)
    results, at = [], 0
    for x in arrays:
        results.append(summed[at : at + x.size].reshape(x.shape))
        at += x.size
    return results


def pair_kernel(n_in, *refs):
    ins, outs = refs[:n_in], refs[n_in : 2 * n_in]
    local_sem, send_sem, recv_sem = refs[2 * n_in :]
    dp, seq = lax.axis_index("dp"), lax.axis_index("seq")
    c = lax.rem(seq, 2)
    other = (dp, seq + 1 - 2 * c)
    barrier = pltpu.get_barrier_semaphore()
    pl.semaphore_signal(barrier, inc=1, device_id=other, device_id_type=MESH)
    pl.semaphore_wait(barrier, 1)
    copies = []
    for i in range(n_in):
        copies.append(remote(ins[i], outs[i].at[:, c], send_sem.at[i], recv_sem.at[i], other))
        copies.append(pltpu.make_async_copy(ins[i], outs[i].at[:, c], local_sem.at[i]))
    for copy in copies:
        copy.start()
    for copy in copies:
        copy.wait()


def pair_gather(arrays, collective_id):
    n = len(arrays)
    return pl.pallas_call(
        functools.partial(pair_kernel, n),
        out_shape=[jax.ShapeDtypeStruct((x.shape[0], 2, *x.shape[1:]), x.dtype) for x in arrays],
        in_specs=[pl.BlockSpec(memory_space=pl.ANY)] * n,
        out_specs=[pl.BlockSpec(memory_space=pl.ANY)] * n,
        scratch_shapes=[pltpu.SemaphoreType.DMA((n,))] * 3,
        compiler_params=pltpu.CompilerParams(collective_id=collective_id, has_side_effects=True),
        name="pair_gather",
    )(*arrays)


def attention_kernel(width, heads, tile, edge, length, x_ref, kdoc_ref, qdoc_ref, o_ref, dq_ref, dk_ref, dv_ref,
                     s_ref, kt_ref, vt_ref, ot_ref, dqt_ref):
    i = pl.program_id(0)
    tiles = length // tile
    scale = 1.0 / math.sqrt(HEAD_DIM)

    @pl.when(i == 0)
    def _():
        dk_ref[...] = jnp.zeros_like(dk_ref)
        dv_ref[...] = jnp.zeros_like(dv_ref)

        def turn(j, carry):
            at = pl.ds(pl.multiple_of(j * tile, tile), tile)
            kt_ref[:, at] = x_ref[at, width : 2 * width].T
            vt_ref[:, at] = x_ref[at, 2 * width : 3 * width].T
            return carry

        lax.fori_loop(0, tiles, turn, 0)

    rows = pl.ds(pl.multiple_of(i * tile, tile), tile)
    lanes = lax.broadcasted_iota(jnp.int32, (tile, width), 1) // HEAD_DIM
    query = x_ref[rows, 0:width] * jnp.asarray(scale, BF16)
    grad = x_ref[rows, 3 * width : 4 * width]
    queries = [jnp.where(lanes == h, query, jnp.zeros_like(query)) for h in range(heads)]
    grads = [jnp.where(lanes == h, grad, jnp.zeros_like(grad)) for h in range(heads)]
    all_queries = jnp.concatenate(queries, axis=0)
    all_grads = jnp.concatenate(grads, axis=0)
    qdoc = qdoc_ref[:, rows]
    qpos = i * tile + lax.broadcasted_iota(jnp.int32, (tile, tile), 1)
    head_edge = -(-edge // tile)
    tail_edge = (length - edge) // tile

    def scores(j, tops):
        at = pl.ds(pl.multiple_of(j * tile, tile), tile)
        keys = x_ref[at, width : 2 * width]
        found = [against(keys, queries[h]) for h in range(heads)]
        checked = (j == i) | (j < head_edge) | (i >= tail_edge)

        def masked():
            kdoc = jnp.concatenate([kdoc_ref[at, :]] * (tile // 128), axis=1)
            kpos = j * tile + lax.broadcasted_iota(jnp.int32, (tile, tile), 0)
            allowed = (kdoc == qdoc) & (kpos <= qpos)
            return [jnp.where(allowed, s, NEG) for s in found]

        found = lax.cond(checked, masked, lambda: found)
        for h in range(heads):
            s_ref[h, at, :] = found[h]
        return [jnp.maximum(t, jnp.max(s.reshape(tile // 8, 8, tile), axis=0)) for t, s in zip(tops, found)]

    tops = lax.fori_loop(0, i + 1, scores, [jnp.full((8, tile), NEG, F32)] * heads)
    tops = [jnp.max(t, axis=0, keepdims=True) for t in tops]
    ot_ref[...] = jnp.zeros_like(ot_ref)
    dqt_ref[...] = jnp.zeros_like(dqt_ref)

    def weigh(j, totals):
        at = pl.ds(pl.multiple_of(j * tile, tile), tile)
        new = []
        for h in range(heads):
            own = slice(h * HEAD_DIM, (h + 1) * HEAD_DIM)
            weights = jnp.exp(s_ref[h, at, :] - tops[h])
            s_ref[h, at, :] = weights
            new.append(totals[h] + jnp.sum(weights.reshape(tile // 8, 8, tile), axis=0))
            ot_ref[own, :] += product(vt_ref[own, at], weights.astype(BF16))
        return new

    totals = lax.fori_loop(0, i + 1, weigh, [jnp.zeros((8, tile), F32)] * heads)
    inverse = [1.0 / jnp.sum(t, axis=0, keepdims=True) for t in totals]
    grad_t = grad.astype(F32).T
    deltas = []
    for h in range(heads):
        own = slice(h * HEAD_DIM, (h + 1) * HEAD_DIM)
        value = ot_ref[own, :] * inverse[h]
        ot_ref[own, :] = value
        deltas.append(jnp.sum(value * grad_t[own], axis=0, keepdims=True))
    o_ref[...] = ot_ref[...].T.astype(BF16)

    def back(j, carry):
        at = pl.ds(pl.multiple_of(j * tile, tile), tile)
        values = x_ref[at, 2 * width : 3 * width]
        probs_low, grads_low = [], []
        for h in range(heads):
            own = slice(h * HEAD_DIM, (h + 1) * HEAD_DIM)
            probs = s_ref[h, at, :] * inverse[h]
            probs_grad = against(values, grads[h])
            scores_grad = (probs * (probs_grad - deltas[h])).astype(BF16)
            probs_low.append(probs.astype(BF16))
            grads_low.append(scores_grad)
            dqt_ref[own, :] += product(kt_ref[own, at], scores_grad)
        dv_ref[at, :] += product(jnp.concatenate(probs_low, axis=1), all_grads)
        dk_ref[at, :] += product(jnp.concatenate(grads_low, axis=1), all_queries)
        return carry

    lax.fori_loop(0, i + 1, back, 0)
    dq_ref[...] = dqt_ref[...].T * scale


def attention(dealt, documents, heads, edge):
    length = dealt.shape[0]
    width = heads * HEAD_DIM
    tile = 256
    kdoc = jnp.broadcast_to(documents[:, None], (length, 128))
    qdoc = documents[None, :]
    whole = lambda i: (0, 0)
    part = lambda i: (i, 0)
    pairs = length * length // 2 * heads
    return pl.pallas_call(
        functools.partial(attention_kernel, width, heads, tile, edge, length),
        grid=(length // tile,),
        out_shape=[jax.ShapeDtypeStruct((length, width), BF16)] + [jax.ShapeDtypeStruct((length, width), F32)] * 3,
        in_specs=[
            pl.BlockSpec((length, 4 * width), whole),
            pl.BlockSpec((length, 128), whole),
            pl.BlockSpec((1, length), whole),
        ],
        out_specs=[
            pl.BlockSpec((tile, width), part),
            pl.BlockSpec((tile, width), part),
            pl.BlockSpec((length, width), whole),
            pl.BlockSpec((length, width), whole),
        ],
        scratch_shapes=[
            pltpu.VMEM((heads, length, tile), F32),
            pltpu.VMEM((width, length), BF16),
            pltpu.VMEM((width, length), BF16),
            pltpu.VMEM((width, tile), F32),
            pltpu.VMEM((width, tile), F32),
        ],
        compiler_params=pltpu.CompilerParams(vmem_limit_bytes=VMEM_LIMIT),
        cost_estimate=pl.CostEstimate(flops=pairs * 64 * 2 * 6 * 4, bytes_accessed=length * width * 20, transcendentals=pairs),
        name="attention",
    )(dealt, kdoc, qdoc)


def on_device(
    grid,
    history,
    documents,
    cotangent,
    mixer_gain,
    mixer_inner,
    mixer_outer,
    mixer_bias,
    stream_gain,
    stream_bias,
    inbound_weight,
    inbound_bias,
    outbound_weight,
    outbound_bias,
    expand,
    expand_bias,
    contract,
    contract_bias,
):
    n_dp, n_seq, nz = grid.n_dp, grid.n_seq, grid.nz
    tokens, width = history.shape[2], history.shape[3]
    hidden_width = expand.shape[1]
    half, hidden_half = width // 2, hidden_width // 2
    both = 2 * tokens
    length = documents.shape[1]
    heads = HEADS // n_seq
    own_width = heads * HEAD_DIM
    seq = lax.axis_index("seq")
    z, c = seq // 2, lax.rem(seq, 2)

    def take(array, start, size, axis=0):
        return lax.dynamic_slice_in_dim(array, start, size, axis)

    pick = lambda base: (lambda core: base + core * half)
    weight_k, weight_v, weight_q, weight_o = gather(
        grid,
        [inbound_weight, outbound_weight],
        [
            (0, pick(width), 0, 0, half, "ba"),
            (0, pick(2 * width), 1, 0, half, "ab"),
            (0, pick(0), 2, 0, half, "ba"),
            (1, pick(0), 3, 0, half, "ab"),
        ],
        [half] * 4,
        1,
        "gather_attention",
    )

    history_full = history[:, 0].astype(F32)
    last = history_full[-1]
    scaled, rms_pull = jax.vjp(rms_scale, last, mixer_gain.astype(F32))
    scaled_low = scaled.astype(BF16)
    mix_pre = product(scaled_low, mixer_inner)
    mix_value, mix_pull = jax.vjp(exact_gelu, mix_pre)
    mix_hidden = mix_value.astype(BF16)
    coeffs = (product(mix_hidden, mixer_outer) + mixer_bias.astype(F32)).reshape(tokens, 4, -1)
    streams = jnp.einsum("tcj,jtd->ctd", coeffs, history_full, precision=HIGHEST)
    normed, norm_pull = jax.vjp(layer_norm, streams, stream_gain.astype(F32), stream_bias.astype(F32))
    lowered_own = normed.astype(BF16)
    grad_own = cotangent[0]

    lowered, grad_low = pair_gather([lowered_own, cotangent], 2)
    lowered = lowered.reshape(4, both, width)
    grad_low = grad_low.reshape(both, width)

    bias_in = inbound_bias.astype(F32)
    positions = z * both + jnp.arange(both, dtype=jnp.int32)
    tables = rotary_tables(positions, half)
    query = product(lowered[0], weight_q) + take(bias_in, c * half, half)
    key = product(lowered[1], weight_k) + take(bias_in, width + c * half, half)
    value = product(lowered[2], weight_v) + take(bias_in, 2 * width + c * half, half)
    attended_grad = product(grad_low, weight_o)
    sent = [rotate(query, tables, 1.0), rotate(key, tables, 1.0), value, attended_grad]
    sent = jnp.concatenate([x.astype(BF16).reshape(both, nz, own_width) for x in sent], axis=-1)
    sent = jnp.transpose(sent, (1, 0, 2))
    groups = [[2 * k + core for k in range(nz)] for core in range(2)]
    dealt = lax.all_to_all(sent, "seq", 0, 0, axis_index_groups=groups, tiled=True)

    expand_in, contract_in, sent_seen = lax.optimization_barrier((expand, contract, sent[0, 0]))
    quarter = hidden_half // 2
    chunks = []
    for part in range(2):
        chunks.append((0, (lambda core, part=part: core * hidden_half + part * quarter), 0, part * quarter, quarter, "ba"))
        chunks.append((1, (lambda core, part=part: core * hidden_half + part * quarter), 1, part * quarter, quarter, "ab"))
    weight_e, weight_c = gather(grid, [expand_in, contract_in], chunks, [hidden_half] * 2, 3, "gather_feed")

    expanded = product(lowered[3], weight_e) + take(expand_bias.astype(F32), c * hidden_half, hidden_half)
    hidden_value, hidden_pull = jax.vjp(exact_gelu, expanded)
    hidden_low = hidden_value.astype(BF16)
    feed = against(hidden_low, weight_c)

    attended, dq, dk, dv = attention(dealt.reshape(length, 4 * own_width), documents[0], heads, tokens)
    back_tables = rotary_tables(jnp.arange(length, dtype=jnp.int32), own_width)
    dq = rotate(dq, back_tables, -1.0)
    dk = rotate(dk, back_tables, -1.0)
    head_bias_grads = [jnp.sum(x, axis=0) for x in (dq, dk, dv)]
    returned = jnp.concatenate([attended, dq.astype(BF16), dk.astype(BF16), dv.astype(BF16)], axis=-1)
    returned = returned.reshape(nz, both, 4 * own_width)
    collected = lax.all_to_all(returned, "seq", 0, 0, axis_index_groups=groups, tiled=True)

    expanded_grad = hidden_pull(product(grad_low, weight_c))[0]
    expanded_grad_low = expanded_grad.astype(BF16)
    expand_part = inner(lowered[3], expanded_grad_low).astype(BF16)
    contract_part = inner(grad_low, hidden_low).astype(BF16)
    expand_own, contract_own = scatter(grid, [expand_part, contract_part], ["ab", "ba"], 4, "scatter_feed")

    pieces = [
        jnp.transpose(collected[:, :, k * own_width : (k + 1) * own_width], (1, 0, 2)).reshape(both, half) for k in range(4)
    ]
    attended_low, dq_low, dk_low, dv_low = pieces

    out_part = against(attended_low, weight_o) + feed
    swap = [(s, s + 1 - 2 * (s % 2)) for s in range(n_seq)]
    out_theirs = lax.ppermute(take(out_part, (1 - c) * tokens, tokens), "seq", swap)
    out_own = take(out_part, c * tokens, tokens) + out_theirs
    layer_out = (streams[3] + (out_own + outbound_bias.astype(F32) + contract_bias.astype(F32))).astype(BF16)

    normed_part = jnp.stack(
        [
            against(dq_low, weight_q),
            against(dk_low, weight_k),
            against(dv_low, weight_v),
            against(expanded_grad_low, weight_e),
        ]
    )
    normed_theirs = lax.ppermute(take(normed_part, (1 - c) * tokens, tokens, 1).astype(BF16), "seq", swap)
    normed_grad = take(normed_part, c * tokens, tokens, 1) + normed_theirs.astype(F32)

    owned_q, owned_k, owned_v, owned_o = scatter(
        grid,
        [
            inner(lowered[0], dq_low).astype(BF16),
            inner(lowered[1], dk_low).astype(BF16),
            inner(lowered[2], dv_low).astype(BF16),
            inner(grad_low, attended_low).astype(BF16),
        ],
        ["ab", "ba", "ab", "ba"],
        5,
        "scatter_attention",
    )

    grad_full = grad_own.astype(F32)
    streams_grad, stream_gain_grad, stream_bias_grad = norm_pull(normed_grad)
    streams_grad = jnp.concatenate([streams_grad[:3], streams_grad[3:] + grad_full[None]], axis=0)
    history_grad = jnp.einsum("tcj,ctd->jtd", coeffs, streams_grad, precision=HIGHEST)
    coeffs_grad = jnp.einsum("ctd,jtd->tcj", streams_grad, history_full, precision=HIGHEST).reshape(tokens, -1)
    mixer_bias_grad = jnp.sum(coeffs_grad, axis=0)
    coeffs_grad_low = coeffs_grad.astype(BF16)
    mixer_outer_grad = inner(mix_hidden, coeffs_grad_low)
    mix_pre_grad_low = mix_pull(against(coeffs_grad_low, mixer_outer))[0].astype(BF16)
    mixer_inner_grad = inner(scaled_low, mix_pre_grad_low)
    last_grad, mixer_gain_grad = rms_pull(against(mix_pre_grad_low, mixer_inner))
    history_grad = jnp.concatenate([history_grad[:-1], history_grad[-1:] + last_grad[None]], axis=0)

    first = c * half + z * own_width
    inbound_bias_grad = jnp.zeros((3 * width,), F32)
    for k in range(3):
        inbound_bias_grad = lax.dynamic_update_slice_in_dim(inbound_bias_grad, head_bias_grads[k], k * width + first, 0)
    expand_bias_grad = lax.dynamic_update_slice_in_dim(
        jnp.zeros((hidden_width,), F32), jnp.sum(expanded_grad, axis=0), c * hidden_half, 0
    )
    small = small_sum(
        n_dp,
        n_seq,
        [
            mixer_gain_grad,
            mixer_inner_grad,
            mixer_outer_grad,
            mixer_bias_grad,
            stream_gain_grad,
            stream_bias_grad,
            inbound_bias_grad,
            jnp.sum(grad_full, axis=0),
            expand_bias_grad,
        ],
        6,
    )

    def side(x):
        return jnp.concatenate([x[0], x[1]], axis=-1)

    return (
        layer_out[None],
        history_grad[:, None],
        small[0],
        small[1],
        small[2],
        small[3],
        small[4],
        small[5],
        jnp.concatenate([owned_q[0], owned_q[1], owned_k[0], owned_k[1], owned_v[0], owned_v[1]], axis=-1),
        small[6],
        side(owned_o),
        small[7],
        side(expand_own),
        small[8],
        side(contract_own),
        small[7],
    )


def solution(mesh):
    rows = P(("dp", "seq"), None)
    placed = (
        P(None, "dp", "seq", None),
        P("dp", None),
        P("dp", "seq", None),
        P(),
        P(),
        P(),
        P(),
        P(),
        P(),
        rows,
        P(),
        rows,
        P(),
        rows,
        P(),
        rows,
        P(),
    )
    grid = Grid(mesh.shape["dp"], mesh.shape["seq"])
    return jax.shard_map(
        functools.partial(on_device, grid),
        mesh=mesh,
        in_specs=placed,
        out_specs=(
            P("dp", "seq", None),
            P(None, "dp", "seq", None),
            P(),
            P(),
            P(),
            P(),
            P(),
            P(),
            rows,
            P(),
            rows,
            P(),
            rows,
            P(),
            rows,
            P(),
        ),
        check_vma=False,
    )
```

```python
import functools
import math

import jax
import jax.numpy as jnp
from jax import lax
from jax.experimental import pallas as pl
from jax.experimental.pallas import tpu as pltpu
from jax.sharding import PartitionSpec as P

HEADS = 16
HEAD_DIM = 64
ROT_DIMS = 16
EPS = 1e-05
HIGHEST = lax.Precision.HIGHEST
NEG = -1e30
MESH = pl.DeviceIdType.MESH
F32 = jnp.float32
BF16 = jnp.bfloat16
VMEM_LIMIT = 56 * 1024 * 1024


def inner(left, right):
    return lax.dot_general(left, right, (((0,), (0,)), ((), ())), preferred_element_type=F32)


def against(left, right):
    return lax.dot_general(left, right, (((1,), (1,)), ((), ())), preferred_element_type=F32)


def product(left, right):
    return jnp.dot(left, right, preferred_element_type=F32)


def exact_gelu(value):
    return jax.nn.gelu(value, approximate=False)


def phi(value):
    return 0.5 * (1.0 + lax.erf(value * (1.0 / math.sqrt(2.0))))


def gelu_slope(value):
    return phi(value) + value * jnp.exp(-0.5 * value * value) * (1.0 / math.sqrt(2.0 * math.pi))


def rotary_tables(positions, width):
    half = ROT_DIMS // 2
    place = jnp.arange(width) % HEAD_DIM
    freq = 10000.0 ** (-jnp.arange(half).astype(F32) * 2.0 / ROT_DIMS)
    angles = positions.astype(F32)[:, None] * freq[None, :]
    spread = lambda x: jnp.tile(x, (1, width // half))
    turned = (place < ROT_DIMS)[None, :]
    cosine = jnp.where(turned, spread(jnp.cos(angles)), 1.0)
    sine = jnp.where(turned, spread(jnp.sin(angles)), 0.0)
    above = jnp.where((place < half)[None, :], -sine, 0.0)
    below = jnp.where((place < half)[None, :], 0.0, sine)
    return cosine, above, below


def rotate(value, tables, sign):
    half = ROT_DIMS // 2
    cosine, above, below = tables
    width = value.shape[-1]
    up = pltpu.roll(value, width - half, 1)
    down = pltpu.roll(value, half, 1)
    return value * cosine + sign * (up * above + down * below)


class Grid:
    def __init__(self, n_dp, n_seq):
        self.n_dp, self.n_seq = n_dp, n_seq
        self.na, self.nb, self.nz = 2, n_dp // 2, n_seq // 2

    def here(self):
        dp, seq = lax.axis_index("dp"), lax.axis_index("seq")
        return dp // self.nb, lax.rem(dp, self.nb), seq // 2, lax.rem(seq, 2)

    def device(self, a, b, z, c):
        return (a * self.nb + b, z * 2 + c)

    def peers(self, a, b, z, c):
        found = [self.device(a, b, z, 1 - c), self.device(1 - a, b, z, c)]
        found += [self.device(a, lax.rem(b + k, self.nb), z, c) for k in range(1, self.nb)]
        found += [self.device(a, b, lax.rem(z + k, self.nz), c) for k in range(1, self.nz)]
        return found

    def greet(self, a, b, z, c):
        barrier = pltpu.get_barrier_semaphore()
        found = self.peers(a, b, z, c)
        for peer in found:
            pl.semaphore_signal(barrier, inc=1, device_id=peer, device_id_type=MESH)
        pl.semaphore_wait(barrier, len(found))


def remote(src, dst, send, recv, device):
    return pltpu.make_async_remote_copy(
        src_ref=src, dst_ref=dst, send_sem=send, recv_sem=recv, device_id=device, device_id_type=MESH
    )


def remote(src, dst, send, recv, device):
    return pltpu.make_async_remote_copy(
        src_ref=src, dst_ref=dst, send_sem=send, recv_sem=recv, device_id=device, device_id_type=MESH
    )


def start(copies):
    for copy in copies:
        copy.start()


def finish(copies):
    for copy in copies:
        copy.wait()


class Gathering:
    def __init__(self, grid, place, rows, chunks, ins, outs, local_sem, send_sem, recv_sem):
        self.grid, self.place, self.rows, self.chunks = grid, place, rows, chunks
        self.ins, self.outs = ins, outs
        self.local_sem, self.send_sem, self.recv_sem = local_sem, send_sem, recv_sem

    def copies(self, t, stage):
        a, b, z, c = self.place
        grid, rows = self.grid, self.rows
        nz, nb = grid.nz, grid.nb
        source, base, result, col, n, order = self.chunks[t]
        out, cols = self.outs[result], pl.ds(col, n)

        def send(src, dst, slot, device):
            return remote(src, dst, self.send_sem.at[t, slot], self.recv_sem.at[t, slot], device)

        if stage == 0:
            mine = self.ins[source].at[:, pl.ds(pl.multiple_of(base(c), 128), n)]
            theirs = self.ins[source].at[:, pl.ds(pl.multiple_of(base(1 - c), 128), n)]
            spot = out.at[a, b, z, pl.ds(pl.multiple_of(c * rows, rows), rows), cols]
            return [pltpu.make_async_copy(mine, spot, self.local_sem.at[t]), send(theirs, spot, 0, grid.device(a, b, z, 1 - c))]
        if stage == 1:
            block = out.at[a, b, z, :, cols]
            return [send(block, block, k, grid.device(a, b, lax.rem(z + k, nz), c)) for k in range(1, nz)]
        if order[stage - 2] == "b":
            block = out.at[a, b, :, :, cols] if stage == 2 else out.at[:, b, :, :, cols]
            return [send(block, block, nz + k - 1, grid.device(a, lax.rem(b + k, nb), z, c)) for k in range(1, nb)]
        block = out.at[a, b, :, :, cols] if stage == 2 else out.at[a, :, :, :, cols]
        return [send(block, block, nz + nb - 1, grid.device(1 - a, b, z, c))]

    def events(self, groups):
        def begin(u, stage):
            for t in groups[u]:
                start(self.copies(t, stage))

        def end(u, stage):
            for t in groups[u]:
                finish(self.copies(t, stage))

        def first():
            for u in range(len(groups)):
                begin(u, 0)

        def second():
            end(0, 0)
            begin(0, 1)

        found = [first, second]

        def turn(u):
            if u < len(groups):
                end(u, 1)
                begin(u, 2)
                if u + 1 < len(groups):
                    end(u + 1, 0)
                    begin(u + 1, 1)
            if 0 <= u - 1 < len(groups):
                end(u - 1, 2)
                begin(u - 1, 3)
            if 0 <= u - 2 < len(groups):
                end(u - 2, 3)

        return found + [functools.partial(turn, u) for u in range(len(groups) + 2)]


def gather_kernel(grid, rows, chunks, groups, n_in, n_out, *refs):
    ins, outs = refs[:n_in], refs[n_in : n_in + n_out]
    place = grid.here()
    grid.greet(*place)
    for event in Gathering(grid, place, rows, chunks, ins, outs, *refs[n_in + n_out :]).events(groups):
        event()


def gather_sems(grid, chunks):
    slots = grid.nz + grid.nb
    return [
        pltpu.SemaphoreType.DMA((len(chunks),)),
        pltpu.SemaphoreType.DMA((len(chunks), slots)),
        pltpu.SemaphoreType.DMA((len(chunks), slots)),
    ]


def gather(grid, arrays, chunks, groups, widths, collective_id, name):
    rows = arrays[0].shape[0]
    outs = [jax.ShapeDtypeStruct((grid.na, grid.nb, grid.nz, 2 * rows, w), BF16) for w in widths]
    moved = sum(w for w in widths) * 2 * rows * grid.na * grid.nb * grid.nz * 2
    results = pl.pallas_call(
        functools.partial(gather_kernel, grid, rows, chunks, groups, len(arrays), len(outs)),
        out_shape=outs,
        in_specs=[pl.BlockSpec(memory_space=pltpu.VMEM)] * len(arrays),
        out_specs=[pl.BlockSpec(memory_space=pl.ANY)] * len(outs),
        scratch_shapes=gather_sems(grid, chunks),
        compiler_params=pltpu.CompilerParams(collective_id=collective_id, has_side_effects=True),
        cost_estimate=pl.CostEstimate(flops=0, bytes_accessed=moved * 20, transcendentals=0),
        name=name,
    )(*arrays)
    return [r.reshape(-1, r.shape[-1]) for r in results]


class Scattering:
    def __init__(self, grid, place, chunks, parts, outs, scratch):
        self.grid, self.place, self.chunks, self.parts, self.outs = grid, place, chunks, parts, outs
        count = len(chunks)
        self.first, self.second, self.third, self.final = (scratch[i * count : (i + 1) * count] for i in range(4))
        self.local_sem, self.send_sem, self.recv_sem = scratch[4 * count :]

    def copies(self, t, stage):
        a, b, z, c = self.place
        grid = self.grid
        nz, nb = grid.nz, grid.nb
        source, col, n, order, result, base = self.chunks[t]
        part, cols = self.parts[source], pl.ds(col, n)
        first, second, third, final = self.first[t], self.second[t], self.third[t], self.final[t]

        def send(src, dst, slot, device):
            return remote(src, dst, self.send_sem.at[t, slot], self.recv_sem.at[t, slot], device)

        def over_a(src, dst):
            return [send(src(1 - a), dst(0), nz + nb - 1, grid.device(1 - a, b, z, c))]

        def over_b(src, dst):
            return [send(src(lax.rem(b + k, nb)), dst(k - 1), nz + k - 1, grid.device(a, lax.rem(b + k, nb), z, c)) for k in range(1, nb)]

        if stage == 0:
            if order == "ab":
                return over_a(lambda o: part.at[o, :, :, :, cols], lambda k: first.at[k])
            return over_b(lambda o: part.at[:, o, :, :, cols], lambda k: first.at[k])
        if stage == 1:
            return (over_b if order == "ab" else over_a)(lambda o: first.at[0, o], lambda k: second.at[k])
        if stage == 2:
            return [
                send(second.at[0, lax.rem(z + k, nz)], third.at[k - 1], k, grid.device(a, b, lax.rem(z + k, nz), c))
                for k in range(1, nz)
            ]
        spot = self.outs[result].at[:, pl.ds(pl.multiple_of(base(c), 128), n)]
        return [
            send(final.at[1 - c], spot, 0, grid.device(a, b, z, 1 - c)),
            pltpu.make_async_copy(final.at[c], spot, self.local_sem.at[t]),
        ]

    def add(self, t, stage):
        a, b, z, c = self.place
        nz = self.grid.nz
        source, col, n, order, result, base = self.chunks[t]
        part, cols = self.parts[source], pl.ds(col, n)
        first, second, third, final = self.first[t], self.second[t], self.third[t], self.final[t]
        if stage == 0:

            def step(i, carry):
                o, j = i // nz, lax.rem(i, nz)
                own = part[a, o, j, :, cols] if order == "ab" else part[o, b, j, :, cols]
                total = own.astype(F32)
                for k in range(first.shape[0]):
                    total = total + first[k, o, j].astype(F32)
                first[0, o, j] = total.astype(BF16)
                return carry

            lax.fori_loop(0, first.shape[1] * nz, step, 0)
        elif stage == 1:
            mine = b if order == "ab" else a

            def step(j, carry):
                total = first[0, mine, j].astype(F32)
                for k in range(second.shape[0]):
                    total = total + second[k, j].astype(F32)
                second[0, j] = total.astype(BF16)
                return carry

            lax.fori_loop(0, nz, step, 0)
        else:
            total = second[0, z].astype(F32)
            for k in range(nz - 1):
                total = total + third[k].astype(F32)
            final[...] = total.reshape(final.shape)

    def events(self, groups):
        def begin(u, stage):
            for t in groups[u]:
                start(self.copies(t, stage))

        def end(u, stage):
            for t in groups[u]:
                finish(self.copies(t, stage))
                if stage < 3:
                    self.add(t, stage)
                    start(self.copies(t, stage + 1))

        def first():
            for u in range(min(2, len(groups))):
                begin(u, 0)

        def turn(u):
            if u < len(groups):
                end(u, 0)
                if u + 2 < len(groups):
                    begin(u + 2, 0)
            for stage in (1, 2, 3):
                if 0 <= u - stage < len(groups):
                    end(u - stage, stage)

        return [first] + [functools.partial(turn, u) for u in range(len(groups) + 3)]


def scatter_kernel(grid, chunks, groups, n_in, n_out, *refs):
    place = grid.here()
    grid.greet(*place)
    work = Scattering(grid, place, chunks, refs[:n_in], refs[n_in : n_in + n_out], refs[n_in + n_out :])
    for event in work.events(groups):
        event()


def scatter_scratch(grid, chunks, rows):
    na, nb, nz = grid.na, grid.nb, grid.nz
    first = [pltpu.VMEM((1, nb, nz, rows, n) if o == "ab" else (nb - 1, na, nz, rows, n), BF16) for _, _, n, o, _, _ in chunks]
    second = [pltpu.VMEM((nb - 1, nz, rows, n) if o == "ab" else (1, nz, rows, n), BF16) for _, _, n, o, _, _ in chunks]
    third = [pltpu.VMEM((nz - 1, rows, n), BF16) for _, _, n, _, _, _ in chunks]
    final = [pltpu.VMEM((2, rows // 2, n), F32) for _, _, n, _, _, _ in chunks]
    return first + second + third + final + gather_sems(grid, chunks)


def scatter(grid, parts, chunks, groups, widths, collective_id, name):
    na, nb, nz = grid.na, grid.nb, grid.nz
    rows = parts[0].shape[0] // (na * nb * nz)
    shaped = [p.reshape(na, nb, nz, rows, p.shape[1]) for p in parts]
    moved = sum(p.size for p in parts) * 2
    return pl.pallas_call(
        functools.partial(scatter_kernel, grid, chunks, groups, len(parts), len(widths)),
        out_shape=[jax.ShapeDtypeStruct((rows // 2, w), F32) for w in widths],
        in_specs=[pl.BlockSpec(memory_space=pltpu.VMEM)] * len(parts),
        out_specs=[pl.BlockSpec(memory_space=pl.ANY)] * len(widths),
        scratch_shapes=scatter_scratch(grid, chunks, rows),
        compiler_params=pltpu.CompilerParams(collective_id=collective_id, has_side_effects=True, vmem_limit_bytes=VMEM_LIMIT),
        cost_estimate=pl.CostEstimate(flops=0, bytes_accessed=moved * 20, transcendentals=0),
        name=name,
    )(*shaped)


def small_kernel(n_dp, n_seq, x_ref, out_ref, held, total, send_sem, recv_sem):
    count = n_dp * n_seq
    me = lax.axis_index("dp") * n_seq + lax.axis_index("seq")

    def device(k):
        other = lax.rem(me + k, count)
        return other, (other // n_seq, lax.rem(other, n_seq))

    barrier = pltpu.get_barrier_semaphore()

    def greet(k, carry):
        pl.semaphore_signal(barrier, inc=1, device_id=device(k)[1], device_id_type=MESH)
        return carry

    lax.fori_loop(1, count, greet, 0)
    pl.semaphore_wait(barrier, count - 1)

    def deal(k, carry):
        other, place = device(k)
        remote(x_ref.at[other], held.at[me], send_sem.at[0], recv_sem.at[0], place).start()
        return carry

    lax.fori_loop(1, count, deal, 0)
    held[me] = x_ref[me]
    most = pl.ds(0, count - 1)
    everyone = device(1)[1]
    remote(x_ref.at[most], held.at[most], send_sem.at[0], recv_sem.at[0], everyone).wait()
    total[...] = lax.fori_loop(1, count, lambda k, s: s + held[k], held[0])

    def tell(k, carry):
        place = device(k)[1]
        remote(total, out_ref.at[me], send_sem.at[1], recv_sem.at[1], place).start()
        return carry

    lax.fori_loop(1, count, tell, 0)
    out_ref[me] = total[...]
    remote(x_ref.at[most], out_ref.at[most], send_sem.at[1], recv_sem.at[1], everyone).wait()


def small_sum(n_dp, n_seq, arrays, collective_id):
    count = n_dp * n_seq
    flat = jnp.concatenate([x.reshape(-1) for x in arrays])
    rows = -(-flat.shape[0] // (count * 128 * 8)) * 8
    padded = jnp.pad(flat, (0, count * rows * 128 - flat.shape[0])).reshape(count, rows, 128)
    summed = pl.pallas_call(
        functools.partial(small_kernel, n_dp, n_seq),
        out_shape=jax.ShapeDtypeStruct(padded.shape, F32),
        in_specs=[pl.BlockSpec(memory_space=pltpu.VMEM)],
        out_specs=pl.BlockSpec(memory_space=pltpu.VMEM),
        scratch_shapes=[
            pltpu.VMEM(padded.shape, F32),
            pltpu.VMEM((rows, 128), F32),
            pltpu.SemaphoreType.DMA((2,)),
            pltpu.SemaphoreType.DMA((2,)),
        ],
        compiler_params=pltpu.CompilerParams(collective_id=collective_id, has_side_effects=True),
        name="small_sum",
    )(padded).reshape(-1)
    results, at = [], 0
    for x in arrays:
        results.append(summed[at : at + x.size].reshape(x.shape))
        at += x.size
    return results


def blend(h_ref, coeffs, streams_ref):
    hist, block, width = h_ref.shape[0], h_ref.shape[2], h_ref.shape[3]
    spread = [jnp.broadcast_to(coeffs[:, k : k + 1], (block, 128)) for k in range(4 * hist)]
    for at in range(0, width, 128):
        lanes = slice(at, at + 128)
        inputs = [h_ref[j, 0, :, lanes].astype(F32) for j in range(hist)]
        for c in range(4):
            total = spread[c * hist] * inputs[0]
            for j in range(1, hist):
                total = total + spread[c * hist + j] * inputs[j]
            streams_ref[c, :, lanes] = total
    return spread


def mix_kernel(grid, rows, chunks, groups, h_ref, g_ref, gain_ref, inner_ref, outer_ref, bias_ref, sgain_ref, sbias_ref, in_ref, out_ref,
               lowered_ref, gpair_ref, last_ref, pre_ref, coeffs_ref, wk_ref, wv_ref, wq_ref, wo_ref,
               streams_ref, held_ref, local_sem, send_sem, recv_sem, pair_local, pair_send, pair_recv):
    i, steps = pl.program_id(0), pl.num_programs(0)
    a, b, z, c = place = grid.here()
    block = h_ref.shape[2]
    work = Gathering(grid, place, rows, chunks, [in_ref, out_ref], [wk_ref, wv_ref, wq_ref, wo_ref], local_sem, send_sem, recv_sem)
    events = work.events(groups)
    other = grid.device(a, b, z, 1 - c)

    def pair(k, src, dst):
        return [
            pltpu.make_async_copy(src, dst, pair_local.at[k]),
            remote(src, dst, pair_send.at[k], pair_recv.at[k], other),
        ]

    grads = lambda: pair(0, g_ref.at[0], gpair_ref.at[c])
    lowereds = lambda: pair(1, held_ref, lowered_ref.at[:, c])

    @pl.when(i == 0)
    def _():
        grid.greet(*place)
        events[0]()
        start(grads())

    @pl.when(i == 1)
    def _():
        events[1]()

    last = h_ref[h_ref.shape[0] - 1, 0].astype(F32)
    r = lax.rsqrt(jnp.mean(last * last, axis=1, keepdims=True) + EPS)
    scaled_low = (last * r * gain_ref[...]).astype(BF16)
    pre = product(scaled_low, inner_ref[...])
    pre_ref[...] = pre
    coeffs = product((pre * phi(pre)).astype(BF16), outer_ref[...]) + bias_ref[...]
    coeffs_ref[...] = coeffs
    blend(h_ref, coeffs, streams_ref)
    at = pl.ds(pl.multiple_of(i * block, block), block)
    for k in range(4):
        stream = streams_ref[k]
        centered = stream - jnp.mean(stream, axis=1, keepdims=True)
        rs = lax.rsqrt(jnp.mean(centered * centered, axis=1, keepdims=True) + EPS)
        held_ref[k, at, :] = (centered * rs * sgain_ref[k : k + 1, :] + sbias_ref[k : k + 1, :]).astype(BF16)
    last_ref[...] = streams_ref[3]

    @pl.when(i == steps - 1)
    def _():
        start(lowereds())
        for event in events[2:]:
            event()
        finish(grads())
        finish(lowereds())


def mix_forward(grid, history, cotangent, params, weights, chunks, groups, widths, collective_id):
    hist, _, tokens, width = history.shape
    mix = params[1].shape[1]
    block = 32
    rows = weights[0].shape[0]
    whole = pl.BlockSpec(memory_space=pltpu.VMEM)
    anywhere = pl.BlockSpec(memory_space=pl.ANY)
    part = lambda n: pl.BlockSpec((block, n), lambda i: (i, 0))
    results = pl.pallas_call(
        functools.partial(mix_kernel, grid, rows, chunks, groups),
        grid=(tokens // block,),
        out_shape=[
            jax.ShapeDtypeStruct((4, 2, tokens, width), BF16),
            jax.ShapeDtypeStruct((2, tokens, width), BF16),
            jax.ShapeDtypeStruct((tokens, width), F32),
            jax.ShapeDtypeStruct((tokens, mix), F32),
            jax.ShapeDtypeStruct((tokens, mix), F32),
        ]
        + [jax.ShapeDtypeStruct((grid.na, grid.nb, grid.nz, 2 * rows, w), BF16) for w in widths],
        in_specs=[pl.BlockSpec((hist, 1, block, width), lambda i: (0, 0, i, 0))] + [whole] * 9,
        out_specs=[anywhere, anywhere, part(width), part(mix), part(mix)] + [anywhere] * len(widths),
        scratch_shapes=[
            pltpu.VMEM((4, block, width), F32),
            pltpu.VMEM((4, tokens, width), BF16),
            *gather_sems(grid, chunks),
            pltpu.SemaphoreType.DMA((2,)),
            pltpu.SemaphoreType.DMA((2,)),
            pltpu.SemaphoreType.DMA((2,)),
        ],
        compiler_params=pltpu.CompilerParams(collective_id=collective_id, has_side_effects=True, vmem_limit_bytes=VMEM_LIMIT),
        cost_estimate=pl.CostEstimate(flops=tokens * width * 80, bytes_accessed=history.size * 40, transcendentals=0),
        name="mix_forward",
    )(history, cotangent, *params, *weights)
    lowered, gpair, last, pre, coeffs = results[:5]
    return (
        lowered.reshape(4, 2 * tokens, width),
        gpair.reshape(2 * tokens, width),
        last,
        pre,
        coeffs,
        [w.reshape(-1, w.shape[-1]) for w in results[5:]],
    )


def unmix_kernel(h_ref, own_ref, theirs_ref, g_ref, pre_ref, coeffs_ref, gain_ref, inner_ref, outer_ref, sgain_ref,
                 hist_ref, sgg_ref, sbg_ref, gg_ref, ig_ref, og_ref, bg_ref, ob_ref,
                 streams_ref, sg_ref, scaled_ref, mpg_ref, hidden_ref, cgl_ref):
    i, steps = pl.program_id(0), pl.num_programs(0)
    hist, block, width = h_ref.shape[0], h_ref.shape[2], h_ref.shape[3]
    mix = 4 * hist

    @pl.when(i == 0)
    def _():
        for ref in (sgg_ref, sbg_ref, gg_ref, bg_ref, ob_ref):
            ref[...] = jnp.zeros_like(ref)

    def down(x):
        return jnp.sum(x, axis=0, keepdims=True)

    coeffs = coeffs_ref[...]
    spread = blend(h_ref, coeffs, streams_ref)
    grad = g_ref[0].astype(F32)
    ob_ref[...] += down(grad)
    for c in range(4):
        stream = streams_ref[c]
        centered = stream - jnp.mean(stream, axis=1, keepdims=True)
        rs = lax.rsqrt(jnp.mean(centered * centered, axis=1, keepdims=True) + EPS)
        n = centered * rs
        ng = own_ref[c] + theirs_ref[c].astype(F32)
        sgg_ref[c : c + 1, :] += down(ng * n)
        sbg_ref[c : c + 1, :] += down(ng)
        w = ng * sgain_ref[c : c + 1, :]
        pulled = rs * (w - jnp.mean(w, axis=1, keepdims=True) - n * jnp.mean(w * n, axis=1, keepdims=True))
        sg_ref[c] = pulled + grad if c == 3 else pulled

    lane = lax.broadcasted_iota(jnp.int32, (block, mix), 1)
    cg = jnp.zeros((block, mix), F32)
    for j in range(hist):
        value = h_ref[j, 0].astype(F32)
        for c in range(4):
            cg = jnp.where(lane == c * hist + j, jnp.sum(value * sg_ref[c], axis=1, keepdims=True), cg)
    bg_ref[...] += down(cg)
    cg_low = cg.astype(BF16)
    pre = pre_ref[...]
    at = pl.ds(pl.multiple_of(i * block, block), block)
    mpg = (against(cg_low, outer_ref[...]) * gelu_slope(pre)).astype(BF16)
    last = h_ref[hist - 1, 0].astype(F32)
    r = lax.rsqrt(jnp.mean(last * last, axis=1, keepdims=True) + EPS)
    scaled_ref[at, :] = (last * r * gain_ref[...]).astype(BF16)
    mpg_ref[at, :] = mpg
    hidden_ref[at, :] = (pre * phi(pre)).astype(BF16)
    cgl_ref[at, :] = cg_low
    scaled_grad = against(mpg, inner_ref[...])
    gg_ref[...] += down(scaled_grad * last * r)
    w = scaled_grad * gain_ref[...]
    last_grad = r * (w - last * (r * r) * jnp.mean(w * last, axis=1, keepdims=True))
    for from_ in range(0, width, 128):
        lanes = slice(from_, from_ + 128)
        pulls = [sg_ref[c, :, lanes] for c in range(4)]
        for j in range(hist):
            total = spread[j] * pulls[0]
            for c in range(1, 4):
                total = total + spread[c * hist + j] * pulls[c]
            hist_ref[j, 0, :, lanes] = total + last_grad[:, lanes] if j == hist - 1 else total

    @pl.when(i == steps - 1)
    def _():
        ig_ref[...] = inner(mpg_ref[...], scaled_ref[...])
        og_ref[...] = inner(hidden_ref[...], cgl_ref[...])


def mix_backward(history, own, theirs, cotangent, pre, coeffs, params):
    hist, _, tokens, width = history.shape
    mix = pre.shape[1]
    block = 32
    whole = pl.BlockSpec(memory_space=pltpu.VMEM)
    part = lambda n: pl.BlockSpec((block, n), lambda i: (i, 0))
    four = pl.BlockSpec((4, block, width), lambda i: (0, i, 0))
    story = pl.BlockSpec((hist, 1, block, width), lambda i: (0, 0, i, 0))
    fixed = lambda *shape: pl.BlockSpec(shape, lambda i: (0,) * len(shape))
    return pl.pallas_call(
        unmix_kernel,
        grid=(tokens // block,),
        out_shape=[
            jax.ShapeDtypeStruct(history.shape, F32),
            jax.ShapeDtypeStruct((4, width), F32),
            jax.ShapeDtypeStruct((4, width), F32),
            jax.ShapeDtypeStruct((1, width), F32),
            jax.ShapeDtypeStruct((mix, width), F32),
            jax.ShapeDtypeStruct((mix, mix), F32),
            jax.ShapeDtypeStruct((1, mix), F32),
            jax.ShapeDtypeStruct((1, width), F32),
        ],
        in_specs=[story, four, four, pl.BlockSpec((1, block, width), lambda i: (0, i, 0)), part(mix), part(mix)] + [whole] * 4,
        out_specs=[story, fixed(4, width), fixed(4, width), fixed(1, width), fixed(mix, width), fixed(mix, mix), fixed(1, mix), fixed(1, width)],
        scratch_shapes=[
            pltpu.VMEM((4, block, width), F32),
            pltpu.VMEM((4, block, width), F32),
            pltpu.VMEM((tokens, width), BF16),
            pltpu.VMEM((tokens, mix), BF16),
            pltpu.VMEM((tokens, mix), BF16),
            pltpu.VMEM((tokens, mix), BF16),
        ],
        compiler_params=pltpu.CompilerParams(vmem_limit_bytes=VMEM_LIMIT),
        cost_estimate=pl.CostEstimate(flops=tokens * width * 300, bytes_accessed=history.size * 8, transcendentals=0),
        name="mix_backward",
    )(history, own, theirs, cotangent, pre, coeffs, *params)


def project_kernel(width, low_ref, g_ref, wq_ref, wk_ref, wv_ref, wo_ref, bias_ref, cos_ref, above_ref, below_ref, sent_ref):
    wide = wq_ref.shape[1]
    reps = wide // cos_ref.shape[1] if wide >= cos_ref.shape[1] else 1
    tables = [jnp.concatenate([t[:, :wide]] * reps, axis=1) for t in (cos_ref, above_ref, below_ref)]
    q = rotate(product(low_ref[0], wq_ref[...]) + bias_ref[0:1, :], tables, 1.0)
    k = rotate(product(low_ref[1], wk_ref[...]) + bias_ref[1:2, :], tables, 1.0)
    v = product(low_ref[2], wv_ref[...]) + bias_ref[2:3, :]
    g = product(g_ref[...], wo_ref[...])
    for n, x in enumerate((q, k, v, g)):
        x = x.astype(BF16)
        for m in range(wide // width):
            sent_ref[m, :, n * width : (n + 1) * width] = x[:, m * width : (m + 1) * width]


def project(grid, lowered, grad_low, weights, biases, tables, own_width):
    both = lowered.shape[1]
    nz = grid.nz
    wide = 2 * own_width
    whole = pl.BlockSpec(memory_space=pltpu.VMEM)
    cols = lambda n: pl.BlockSpec((n, wide), lambda i: (0, i))
    return pl.pallas_call(
        functools.partial(project_kernel, own_width),
        grid=(nz // 2,),
        out_shape=jax.ShapeDtypeStruct((nz, both, 4 * own_width), BF16),
        in_specs=[whole, whole] + [cols(weights[0].shape[0])] * 4 + [cols(3)] + [whole] * 3,
        out_specs=pl.BlockSpec((2, both, 4 * own_width), lambda i: (i, 0, 0)),
        compiler_params=pltpu.CompilerParams(vmem_limit_bytes=VMEM_LIMIT),
        cost_estimate=pl.CostEstimate(flops=8 * both * weights[0].size, bytes_accessed=lowered.size * 4, transcendentals=0),
        name="project",
    )(lowered, grad_low, *weights, biases, *tables)


def attention_kernel(width, heads, tile, step, edge, length, x_ref, kdoc_ref, qdoc_ref, o_ref, dq_ref, dk_ref, dv_ref,
                     s_ref, kt_ref, vt_ref, ot_ref, dqt_ref, dka_ref, dva_ref, top_ref):
    i = pl.program_id(0)
    tiles = length // tile
    scale = 1.0 / math.sqrt(HEAD_DIM)
    @pl.when(i == 0)
    def _():
        dka_ref[...] = jnp.zeros_like(dka_ref)
        dva_ref[...] = jnp.zeros_like(dva_ref)
        def turn(j, carry):
            at = pl.ds(pl.multiple_of(j * tile, tile), tile)
            kt_ref[:, at] = x_ref[at, width : 2 * width].T
            vt_ref[:, at] = x_ref[at, 2 * width : 3 * width].T
            return carry
        lax.fori_loop(0, tiles, turn, 0)
    rows = pl.ds(pl.multiple_of(i * tile, tile), tile)
    query = x_ref[rows, 0:width] * jnp.asarray(scale, BF16)
    grad = x_ref[rows, 3 * width : 4 * width]
    query_t, grad_t = query.T, grad.T
    lanes = lax.broadcasted_iota(jnp.int32, (tile, width), 1) // HEAD_DIM
    subs = lax.broadcasted_iota(jnp.int32, (width, tile), 0) // HEAD_DIM
    zero = jnp.zeros((), BF16)
    queries_t = [jnp.where(subs == h, query_t, zero) for h in range(heads)]
    grads_t = [jnp.where(subs == h, grad_t, zero) for h in range(heads)]
    all_queries = jnp.concatenate([jnp.where(lanes == h, query, zero) for h in range(heads)], axis=0)
    all_grads = jnp.concatenate([jnp.where(lanes == h, grad, zero) for h in range(heads)], axis=0)
    qdoc = qdoc_ref[:, rows]
    qpos = i * tile + lax.broadcasted_iota(jnp.int32, (step, tile), 1)
    head_edge = -(-edge // step)
    tail_edge = (length - edge) // tile
    per = tile // step
    count = (i + 1) * per
    ot_ref[...] = jnp.zeros_like(ot_ref)
    dqt_ref[...] = jnp.zeros_like(dqt_ref)
    top_ref[...] = jnp.full_like(top_ref, NEG)

    def fold(x, f):
        return f(x.reshape(step // 8, 8, tile), axis=0)

    def scores(j, carry):
        at = pl.ds(pl.multiple_of(j * step, step), step)
        checked = (j >= i * per) | (j < head_edge) | (i >= tail_edge)
        def run(mask):
            keys = x_ref[at, width : 2 * width]
            if mask:
                kdoc = jnp.concatenate([kdoc_ref[at, :]] * (tile // 128), axis=1)
                kpos = j * step + lax.broadcasted_iota(jnp.int32, (step, tile), 0)
                allowed = (kdoc == qdoc) & (kpos <= qpos)
            for h in range(heads):
                s = product(keys, queries_t[h])
                if mask:
                    s = jnp.where(allowed, s, NEG)
                s_ref[h, at, :] = s
                top_ref[h] = jnp.maximum(top_ref[h], fold(s, jnp.max))
        pl.when(checked)(lambda: run(True))
        pl.when(jnp.logical_not(checked))(lambda: run(False))
        return carry
    lax.fori_loop(0, count, scores, 0)
    tops = [jnp.max(top_ref[h], axis=0, keepdims=True) for h in range(heads)]

    def weigh(j, totals):
        at = pl.ds(pl.multiple_of(j * step, step), step)
        new = []
        for h in range(heads):
            own = slice(h * HEAD_DIM, (h + 1) * HEAD_DIM)
            weights = jnp.exp(s_ref[h, at, :] - tops[h])
            s_ref[h, at, :] = weights
            new.append(totals[h] + fold(weights, jnp.sum))
            ot_ref[own, :] += product(vt_ref[own, at], weights.astype(BF16))
        return new
    totals = lax.fori_loop(0, count, weigh, [jnp.zeros((8, tile), F32)] * heads)
    inverse = [1.0 / jnp.sum(t, axis=0, keepdims=True) for t in totals]
    grad_f = grad_t.astype(F32)
    deltas = []
    for h in range(heads):
        own = slice(h * HEAD_DIM, (h + 1) * HEAD_DIM)
        value = ot_ref[own, :] * inverse[h]
        ot_ref[own, :] = value
        deltas.append(jnp.sum(value * grad_f[own], axis=0, keepdims=True))
    o_ref[...] = ot_ref[...].T.astype(BF16)

    def back(j, carry):
        at = pl.ds(pl.multiple_of(j * step, step), step)
        values = x_ref[at, 2 * width : 3 * width]
        probs_low, grads_low = [], []
        for h in range(heads):
            own = slice(h * HEAD_DIM, (h + 1) * HEAD_DIM)
            probs_grad = product(values, grads_t[h])
            probs = s_ref[h, at, :] * inverse[h]
            scores_grad = (probs * (probs_grad - deltas[h])).astype(BF16)
            probs_low.append(probs.astype(BF16))
            grads_low.append(scores_grad)
            dqt_ref[own, :] += product(kt_ref[own, at], scores_grad)
        dva_ref[at, :] += product(jnp.concatenate(probs_low, axis=1), all_grads)
        dka_ref[at, :] += product(jnp.concatenate(grads_low, axis=1), all_queries)
        return carry
    lax.fori_loop(0, count, back, 0)
    dq_ref[...] = (dqt_ref[...].T * scale).astype(BF16)
    @pl.when(i == tiles - 1)
    def _():
        dk_ref[...] = dka_ref[...].astype(BF16)
        dv_ref[...] = dva_ref[...].astype(BF16)

def attention(dealt, documents, heads, edge):
    length = dealt.shape[0]
    width = heads * HEAD_DIM
    tile = step = 2 * edge
    pairs = length * length // 2 * heads
    kdoc = jnp.broadcast_to(documents[:, None], (length, 128)); qdoc = documents[None, :]
    whole = lambda i: (0, 0)
    part = lambda i: (i, 0)
    return pl.pallas_call(
        functools.partial(attention_kernel, width, heads, tile, step, edge, length),
        grid=(length // tile,),
        out_shape=[jax.ShapeDtypeStruct((length, width), BF16)]*4,
        in_specs=[pl.BlockSpec((length, 4 * width), whole), pl.BlockSpec((length, 128), whole), pl.BlockSpec((1, length), whole)],
        out_specs=[pl.BlockSpec((tile, width), part), pl.BlockSpec((tile, width), part), pl.BlockSpec((length, width), whole), pl.BlockSpec((length, width), whole)],
        scratch_shapes=[
            pltpu.VMEM((heads, length, tile), F32), pltpu.VMEM((width, length), BF16), pltpu.VMEM((width, length), BF16),
            pltpu.VMEM((width, tile), F32), pltpu.VMEM((width, tile), F32), pltpu.VMEM((length, width), F32), pltpu.VMEM((length, width), F32),
            pltpu.VMEM((heads, 8, tile), F32)],
        compiler_params=pltpu.CompilerParams(vmem_limit_bytes=VMEM_LIMIT),
        cost_estimate=pl.CostEstimate(flops=pairs * 64 * 2 * 6 * 4, bytes_accessed=length * width * 20, transcendentals=pairs),
        name="attention",
    )(dealt, kdoc, qdoc)


def on_device(
    grid,
    history,
    documents,
    cotangent,
    mixer_gain,
    mixer_inner,
    mixer_outer,
    mixer_bias,
    stream_gain,
    stream_bias,
    inbound_weight,
    inbound_bias,
    outbound_weight,
    outbound_bias,
    expand,
    expand_bias,
    contract,
    contract_bias,
):
    n_dp, n_seq, nz = grid.n_dp, grid.n_seq, grid.nz
    tokens, width = history.shape[2], history.shape[3]
    hidden_width = expand.shape[1]
    half, hidden_half = width // 2, hidden_width // 2
    both = 2 * tokens
    length = documents.shape[1]
    heads = HEADS // n_seq
    own_width = heads * HEAD_DIM
    seq = lax.axis_index("seq")
    z, c = seq // 2, lax.rem(seq, 2)

    def take(array, start, size, axis=0):
        return lax.dynamic_slice_in_dim(array, start, size, axis)

    gain = mixer_gain.astype(F32)[None]
    stream_gain_full = stream_gain.astype(F32)
    pick = lambda base, n: (lambda core: base + core * n)
    lowered, grad_low, last_stream, mix_pre, coeffs, (weight_k, weight_v, weight_q, weight_o) = mix_forward(
        grid,
        history,
        cotangent,
        [gain, mixer_inner, mixer_outer, mixer_bias.astype(F32)[None], stream_gain_full, stream_bias.astype(F32)],
        [inbound_weight, outbound_weight],
        [
            (0, pick(width, half), 0, 0, half, "ba"),
            (0, pick(2 * width, half), 1, 0, half, "ab"),
            (0, pick(0, half), 2, 0, half, "ba"),
            (1, pick(0, half), 3, 0, half, "ab"),
        ],
        [[0, 1], [2, 3]],
        [half] * 4,
        1,
    )

    bias_in = inbound_bias.astype(F32).reshape(3, width)
    positions = z * both + jnp.arange(both, dtype=jnp.int32)
    tables = rotary_tables(positions, 128)
    sent = project(
        grid, lowered, grad_low, [weight_q, weight_k, weight_v, weight_o], take(bias_in, c * half, half, 1), tables, own_width
    )
    groups = [[2 * k + core for k in range(nz)] for core in range(2)]
    dealt = lax.all_to_all(sent, "seq", 0, 0, axis_index_groups=groups, tiled=True)

    expand_in, contract_in, _ = lax.optimization_barrier((expand, contract, sent[0, 0]))
    parts = 4
    piece = hidden_half // parts
    chunks = []
    for part in range(parts):
        base = lambda core, part=part: core * hidden_half + part * piece
        chunks.append((0, base, 0, part * piece, piece, "ba"))
        chunks.append((1, base, 1, part * piece, piece, "ab"))
    pairs = [[2 * part, 2 * part + 1] for part in range(parts)]
    weight_e, weight_c = gather(grid, [expand_in, contract_in], chunks, pairs, [hidden_half] * 2, 3, "gather_feed")

    expanded = product(lowered[3], weight_e) + take(expand_bias.astype(F32), c * hidden_half, hidden_half)
    hidden_value, hidden_pull = jax.vjp(exact_gelu, expanded)
    hidden_low = hidden_value.astype(BF16)
    feed = against(hidden_low, weight_c)

    results = attention(dealt.reshape(length, 4 * own_width), documents[0], heads, tokens)
    returned = jnp.concatenate(results, axis=-1).reshape(nz, both, 4 * own_width)
    collected = lax.all_to_all(returned, "seq", 0, 0, axis_index_groups=groups, tiled=True)

    expanded_grad = hidden_pull(product(grad_low, weight_c))[0]
    expanded_grad_low = expanded_grad.astype(BF16)
    expand_part = inner(lowered[3], expanded_grad_low).astype(BF16)
    contract_part = inner(grad_low, hidden_low).astype(BF16)
    chunks = []
    for part in range(parts):
        base = lambda core, part=part: core * hidden_half + part * piece
        chunks.append((0, part * piece, piece, "ab", 0, base))
        chunks.append((1, part * piece, piece, "ba", 1, base))
    expand_grad, contract_grad = scatter(grid, [expand_part, contract_part], chunks, pairs, [hidden_width] * 2, 4, "scatter_feed")

    pieces = [
        jnp.concatenate([collected[m, :, k * own_width : (k + 1) * own_width] for m in range(nz)], axis=-1) for k in range(4)
    ]
    attended_low, value_low = pieces[0], pieces[3]
    spread = [jnp.tile(t, (1, half // 128)) for t in tables]

    def unturn(grad):
        grad = grad.astype(F32)
        up = jnp.roll(grad, -(ROT_DIMS // 2), axis=-1)
        down = jnp.roll(grad, ROT_DIMS // 2, axis=-1)
        return grad * spread[0] - (up * spread[1] + down * spread[2])

    dq, dk = unturn(pieces[1]), unturn(pieces[2])
    dq_low, dk_low, dv_low = dq.astype(BF16), dk.astype(BF16), value_low
    head_bias_grads = jnp.stack([jnp.sum(x.astype(F32), axis=0) for x in (dq, dk, value_low)])

    out_part = against(attended_low, weight_o) + feed
    swap = [(s, s + 1 - 2 * (s % 2)) for s in range(n_seq)]
    out_theirs = lax.ppermute(take(out_part, (1 - c) * tokens, tokens), "seq", swap)
    out_own = take(out_part, c * tokens, tokens) + out_theirs
    layer_out = (last_stream + (out_own + outbound_bias.astype(F32) + contract_bias.astype(F32))).astype(BF16)

    normed_part = jnp.stack(
        [
            against(dq_low, weight_q),
            against(dk_low, weight_k),
            against(dv_low, weight_v),
            against(expanded_grad_low, weight_e),
        ]
    )
    normed_theirs = lax.ppermute(take(normed_part, (1 - c) * tokens, tokens, 1).astype(BF16), "seq", swap)
    normed_own = take(normed_part, c * tokens, tokens, 1)

    inbound_grad, outbound_grad = scatter(
        grid,
        [
            inner(lowered[0], dq_low).astype(BF16),
            inner(lowered[1], dk_low).astype(BF16),
            inner(lowered[2], dv_low).astype(BF16),
            inner(grad_low, attended_low).astype(BF16),
        ],
        [
            (0, 0, half, "ab", 0, pick(0, half)),
            (1, 0, half, "ba", 0, pick(width, half)),
            (2, 0, half, "ab", 0, pick(2 * width, half)),
            (3, 0, half, "ba", 1, pick(0, half)),
        ],
        [[0, 1], [2, 3]],
        [3 * width, width],
        5,
        "scatter_attention",
    )

    history_grad, sgg, sbg, gg, ig, og, bg, ob = mix_backward(
        history,
        normed_own,
        normed_theirs,
        cotangent,
        mix_pre,
        coeffs,
        [gain, mixer_inner, mixer_outer, stream_gain_full],
    )
    inbound_bias_grad = lax.dynamic_update_slice_in_dim(jnp.zeros((3, width), F32), head_bias_grads, c * half, 1)
    expand_bias_grad = lax.dynamic_update_slice_in_dim(
        jnp.zeros((hidden_width,), F32), jnp.sum(expanded_grad, axis=0), c * hidden_half, 0
    )
    small = small_sum(n_dp, n_seq, [gg, ig, og, bg, sgg, sbg, inbound_bias_grad, ob, expand_bias_grad], 6)
    return (
        layer_out[None],
        history_grad,
        small[0].reshape(width),
        small[1].T,
        small[2],
        small[3].reshape(-1),
        small[4],
        small[5],
        inbound_grad,
        small[6].reshape(3 * width),
        outbound_grad,
        small[7].reshape(width),
        expand_grad,
        small[8],
        contract_grad,
        small[7].reshape(width),
    )


def solution(mesh):
    rows = P(("dp", "seq"), None)
    placed = (
        P(None, "dp", "seq", None),
        P("dp", None),
        P("dp", "seq", None),
        P(),
        P(),
        P(),
        P(),
        P(),
        P(),
        rows,
        P(),
        rows,
        P(),
        rows,
        P(),
        rows,
        P(),
    )
    grid = Grid(mesh.shape["dp"], mesh.shape["seq"])
    return jax.shard_map(
        functools.partial(on_device, grid),
        mesh=mesh,
        in_specs=placed,
        out_specs=(
            P("dp", "seq", None),
            P(None, "dp", "seq", None),
            P(),
            P(),
            P(),
            P(),
            P(),
            P(),
            rows,
            P(),
            rows,
            P(),
            rows,
            P(),
            rows,
            P(),
        ),
        check_vma=False,
    )
```

```python
import functools
import math

import jax
import jax.numpy as jnp
from jax import lax
from jax.experimental import pallas as pl
from jax.experimental.pallas import tpu as pltpu
from jax.sharding import PartitionSpec as P

HEADS = 16
HEAD_DIM = 64
ROT_DIMS = 16
EPS = 1e-05
HIGHEST = lax.Precision.HIGHEST
NEG = -1e30
MESH = pl.DeviceIdType.MESH
F32 = jnp.float32
BF16 = jnp.bfloat16
VMEM_LIMIT = 56 * 1024 * 1024


def inner(left, right):
    return lax.dot_general(left, right, (((0,), (0,)), ((), ())), preferred_element_type=F32)


def against(left, right):
    return lax.dot_general(left, right, (((1,), (1,)), ((), ())), preferred_element_type=F32)


def product(left, right):
    return jnp.dot(left, right, preferred_element_type=F32)


def exact_gelu(value):
    return jax.nn.gelu(value, approximate=False)


def phi(value):
    return 0.5 * (1.0 + lax.erf(value * (1.0 / math.sqrt(2.0))))


def gelu_slope(value):
    return phi(value) + value * jnp.exp(-0.5 * value * value) * (1.0 / math.sqrt(2.0 * math.pi))


def rotary_tables(positions, width):
    half = ROT_DIMS // 2
    place = jnp.arange(width) % HEAD_DIM
    freq = 10000.0 ** (-jnp.arange(half).astype(F32) * 2.0 / ROT_DIMS)
    angles = positions.astype(F32)[:, None] * freq[None, :]
    spread = lambda x: jnp.tile(x, (1, width // half))
    turned = (place < ROT_DIMS)[None, :]
    cosine = jnp.where(turned, spread(jnp.cos(angles)), 1.0)
    sine = jnp.where(turned, spread(jnp.sin(angles)), 0.0)
    above = jnp.where((place < half)[None, :], -sine, 0.0)
    below = jnp.where((place < half)[None, :], 0.0, sine)
    return cosine, above, below


def rotate(value, tables, sign):
    half = ROT_DIMS // 2
    cosine, above, below = tables
    width = value.shape[-1]
    up = pltpu.roll(value, width - half, 1)
    down = pltpu.roll(value, half, 1)
    return value * cosine + sign * (up * above + down * below)


class Grid:
    def __init__(self, n_dp, n_seq):
        self.n_dp, self.n_seq = n_dp, n_seq
        self.na, self.nb, self.nz = 2, n_dp // 2, n_seq // 2

    def here(self):
        dp, seq = lax.axis_index("dp"), lax.axis_index("seq")
        return dp // self.nb, lax.rem(dp, self.nb), seq // 2, lax.rem(seq, 2)

    def device(self, a, b, z, c):
        return (a * self.nb + b, z * 2 + c)

    def peers(self, a, b, z, c):
        found = [self.device(a, b, z, 1 - c), self.device(1 - a, b, z, c)]
        found += [self.device(a, lax.rem(b + k, self.nb), z, c) for k in range(1, self.nb)]
        found += [self.device(a, b, lax.rem(z + k, self.nz), c) for k in range(1, self.nz)]
        return found

    def greet(self, a, b, z, c):
        barrier = pltpu.get_barrier_semaphore()
        found = self.peers(a, b, z, c)
        for peer in found:
            pl.semaphore_signal(barrier, inc=1, device_id=peer, device_id_type=MESH)
        pl.semaphore_wait(barrier, len(found))


def remote(src, dst, send, recv, device):
    return pltpu.make_async_remote_copy(
        src_ref=src, dst_ref=dst, send_sem=send, recv_sem=recv, device_id=device, device_id_type=MESH
    )


def remote(src, dst, send, recv, device):
    return pltpu.make_async_remote_copy(
        src_ref=src, dst_ref=dst, send_sem=send, recv_sem=recv, device_id=device, device_id_type=MESH
    )


def start(copies):
    for copy in copies:
        copy.start()


def finish(copies):
    for copy in copies:
        copy.wait()


class Gathering:
    def __init__(self, grid, place, rows, chunks, ins, outs, local_sem, send_sem, recv_sem):
        self.grid, self.place, self.rows, self.chunks = grid, place, rows, chunks
        self.ins, self.outs = ins, outs
        self.local_sem, self.send_sem, self.recv_sem = local_sem, send_sem, recv_sem

    def copies(self, t, stage):
        a, b, z, c = self.place
        grid, rows = self.grid, self.rows
        nz, nb = grid.nz, grid.nb
        source, base, result, col, n, order = self.chunks[t]
        out, cols = self.outs[result], pl.ds(col, n)

        def send(src, dst, slot, device):
            return remote(src, dst, self.send_sem.at[t, slot], self.recv_sem.at[t, slot], device)

        if stage == 0:
            mine = self.ins[source].at[:, pl.ds(pl.multiple_of(base(c), 128), n)]
            theirs = self.ins[source].at[:, pl.ds(pl.multiple_of(base(1 - c), 128), n)]
            spot = out.at[a, b, z, pl.ds(pl.multiple_of(c * rows, rows), rows), cols]
            return [pltpu.make_async_copy(mine, spot, self.local_sem.at[t]), send(theirs, spot, 0, grid.device(a, b, z, 1 - c))]
        if stage == 1:
            block = out.at[a, b, z, :, cols]
            return [send(block, block, k, grid.device(a, b, lax.rem(z + k, nz), c)) for k in range(1, nz)]
        if order[stage - 2] == "b":
            block = out.at[a, b, :, :, cols] if stage == 2 else out.at[:, b, :, :, cols]
            return [send(block, block, nz + k - 1, grid.device(a, lax.rem(b + k, nb), z, c)) for k in range(1, nb)]
        block = out.at[a, b, :, :, cols] if stage == 2 else out.at[a, :, :, :, cols]
        return [send(block, block, nz + nb - 1, grid.device(1 - a, b, z, c))]

    def begin(self, group, stage):
        for t in group:
            start(self.copies(t, stage))

    def end(self, group, stage):
        for t in group:
            finish(self.copies(t, stage))

    def events(self, whole, partial):
        groups = whole + partial

        def first():
            for group in groups:
                self.begin(group, 0)

        def second():
            self.end(groups[0], 0)
            self.begin(groups[0], 1)

        def turn(u):
            if u < len(groups):
                self.end(groups[u], 1)
                if u + 1 < len(groups):
                    self.end(groups[u + 1], 0)
                    self.begin(groups[u + 1], 1)
                if u < len(whole):
                    self.begin(groups[u], 2)
            if 0 <= u - 1 < len(whole):
                self.end(groups[u - 1], 2)
                self.begin(groups[u - 1], 3)
            if 0 <= u - 2 < len(whole):
                self.end(groups[u - 2], 3)

        turns = max(len(whole) + 2, len(groups))
        return [first, second] + [functools.partial(turn, u) for u in range(turns)]

    def late_events(self, groups):
        def turn(u):
            if u < len(groups):
                self.begin(groups[u], 2)
            if 0 <= u - 1 < len(groups):
                self.end(groups[u - 1], 2)
                self.begin(groups[u - 1], 3)
            if 0 <= u - 2 < len(groups):
                self.end(groups[u - 2], 3)

        return [functools.partial(turn, u) for u in range(len(groups) + 2)]


def gather_kernel(grid, chunks, groups, n, *refs):
    outs = refs[n : 2 * n]
    place = grid.here()
    grid.greet(*place)
    for event in Gathering(grid, place, None, chunks, None, outs, *refs[2 * n :]).late_events(groups):
        event()


def gather_sems(grid, chunks):
    slots = grid.nz + grid.nb
    return [
        pltpu.SemaphoreType.DMA((len(chunks),)),
        pltpu.SemaphoreType.DMA((len(chunks), slots)),
        pltpu.SemaphoreType.DMA((len(chunks), slots)),
    ]


def gather(grid, arrays, chunks, groups, collective_id, name):
    n = len(arrays)
    moved = sum(x.size for x in arrays) * 2
    results = pl.pallas_call(
        functools.partial(gather_kernel, grid, chunks, groups, n),
        out_shape=[jax.ShapeDtypeStruct(x.shape, x.dtype) for x in arrays],
        in_specs=[pl.BlockSpec(memory_space=pl.ANY)] * n,
        out_specs=[pl.BlockSpec(memory_space=pl.ANY)] * n,
        input_output_aliases={k: k for k in range(n)},
        scratch_shapes=gather_sems(grid, chunks),
        compiler_params=pltpu.CompilerParams(collective_id=collective_id, has_side_effects=True),
        cost_estimate=pl.CostEstimate(flops=0, bytes_accessed=moved * 20, transcendentals=0),
        name=name,
    )(*arrays)
    return [r.reshape(-1, r.shape[-1]) for r in results]


class Scattering:
    def __init__(self, grid, place, chunks, parts, outs, scratch):
        self.grid, self.place, self.chunks, self.parts, self.outs = grid, place, chunks, parts, outs
        count = len(chunks)
        folds = sum(1 for chunk in chunks if chunk[2])
        self.own, scratch = scratch[:count], scratch[count:]
        self.first, self.second, scratch = scratch[:folds], scratch[folds : 2 * folds], scratch[2 * folds :]
        self.third, self.final = scratch[:count], scratch[count : 2 * count]
        self.local_sem, self.send_sem, self.recv_sem = scratch[2 * count :]

    def copies(self, t, stage):
        a, b, z, c = self.place
        grid = self.grid
        nz = grid.nz
        source, n, order, result, base = self.chunks[t]
        part, third, final = self.parts[source], self.third[t], self.final[t]
        sems = (self.send_sem.at[t], self.recv_sem.at[t])

        def send(src, dst, slot, device):
            return remote(src, dst, sems[0].at[slot], sems[1].at[slot], device)

        if stage < 2:
            found = fold_copies(grid, self.place, order, stage, part, self.first[t], self.second[t], sems)
            if stage == 0:
                kept = part.at[a] if order == "ab" else part.at[:, b]
                found.append(pltpu.make_async_copy(kept, self.own[t], self.local_sem.at[t]))
            return found
        if stage == 2:
            source = self.second[t].at[0] if order else part
            found = [send(source.at[lax.rem(z + k, nz)], third.at[k - 1], k, grid.device(a, b, lax.rem(z + k, nz), c)) for k in range(1, nz)]
            if not order:
                found.append(pltpu.make_async_copy(part.at[z], self.own[t], self.local_sem.at[t]))
            return found
        spot = self.outs[result].at[:, pl.ds(pl.multiple_of(base(c), 128), n)]
        return [
            send(final.at[1 - c], spot, 0, grid.device(a, b, z, 1 - c)),
            pltpu.make_async_copy(final.at[c], spot, self.local_sem.at[t]),
        ]

    def add(self, t, stage):
        z = self.place[2]
        order = self.chunks[t][2]
        third, final = self.third[t], self.final[t]
        if stage < 2:
            fold_add(self.grid, self.place, order, stage, self.own[t], self.first[t], self.second[t])
            return
        total = (self.second[t][0, z] if order else self.own[t][...]).astype(F32)
        for k in range(self.grid.nz - 1):
            total = total + third[k].astype(F32)
        final[...] = total.reshape(final.shape)

    def end(self, group, stage):
        for t in group:
            finish(self.copies(t, stage))
            if stage < 3:
                self.add(t, stage)
                start(self.copies(t, stage + 1))

    def events(self, groups):
        late = [t for t, chunk in enumerate(self.chunks) if not chunk[2]]

        def first():
            for group in groups:
                for t in group:
                    start(self.copies(t, 0))
            for t in late:
                start(self.copies(t, 2))

        def turn(u):
            for stage in range(4):
                if 0 <= u - stage < len(groups):
                    self.end(groups[u - stage], stage)

        def last():
            self.end(late, 2)
            self.end(late, 3)

        return [first] + [functools.partial(turn, u) for u in range(len(groups) + 3)] + [last]


def fold_copies(grid, place, order, stage, part, first, second, sems):
    a, b, z, c = place
    nz, nb = grid.nz, grid.nb

    def send(src, dst, slot, device):
        return remote(src, dst, sems[0].at[slot], sems[1].at[slot], device)

    if (order == "ab") == (stage == 0):
        src = part.at[1 - a] if stage == 0 else first.at[0, 1 - a]
        dst = first.at[0] if stage == 0 else second.at[0]
        return [send(src, dst, nz + nb - 1, grid.device(1 - a, b, z, c))]
    found = []
    for k in range(1, nb):
        to = lax.rem(b + k, nb)
        src = part.at[:, to] if stage == 0 else first.at[0, to]
        dst = first.at[k - 1] if stage == 0 else second.at[k - 1]
        found.append(send(src, dst, nz + k - 1, grid.device(a, to, z, c)))
    return found


def fold_add(grid, place, order, stage, own, first, second):
    a, b, z, c = place
    nz = grid.nz
    if stage == 0:

        def step(i, carry):
            o, j = i // nz, lax.rem(i, nz)
            total = own[o, j].astype(F32)
            for k in range(first.shape[0]):
                total = total + first[k, o, j].astype(F32)
            first[0, o, j] = total.astype(BF16)
            return carry

        lax.fori_loop(0, first.shape[1] * nz, step, 0)
        return
    mine = b if order == "ab" else a

    def step(j, carry):
        total = first[0, mine, j].astype(F32)
        for k in range(second.shape[0]):
            total = total + second[k, j].astype(F32)
        second[0, j] = total.astype(BF16)
        return carry

    lax.fori_loop(0, nz, step, 0)


def fold_scratch(grid, order, rows, n):
    na, nb, nz = grid.na, grid.nb, grid.nz
    own = pltpu.VMEM((nb if order == "ab" else na, nz, rows, n), BF16)
    first = pltpu.VMEM((1, nb, nz, rows, n) if order == "ab" else (nb - 1, na, nz, rows, n), BF16)
    second = pltpu.VMEM((nb - 1, nz, rows, n) if order == "ab" else (1, nz, rows, n), BF16)
    return own, first, second


def scatter_scratch(grid, chunks, rows):
    folds = [fold_scratch(grid, order, rows, n) for _, n, order, _, _ in chunks if order]
    own = [fold_scratch(grid, order, rows, n)[0] if order else pltpu.VMEM((rows, n), BF16) for _, n, order, _, _ in chunks]
    third = [pltpu.VMEM((grid.nz - 1, rows, n), BF16) for _, n, _, _, _ in chunks]
    final = [pltpu.VMEM((2, rows // 2, n), F32) for _, n, _, _, _ in chunks]
    return own + [f for _, f, _ in folds] + [s for _, _, s in folds] + third + final + gather_sems(grid, chunks)


class Summing:
    def __init__(self, grid, mine, held, total, done, send_sem, recv_sem):
        self.n_seq, self.count = grid.n_seq, grid.n_dp * grid.n_seq
        self.mine, self.held, self.total, self.done = mine, held, total, done
        self.send_sem, self.recv_sem = send_sem, recv_sem
        self.rows = total.shape[0]
        self.me = lax.axis_index("dp") * grid.n_seq + lax.axis_index("seq")

    def device(self, k):
        other = lax.rem(self.me + k, self.count)
        return other, (other // self.n_seq, lax.rem(other, self.n_seq))

    def part(self, ref, k):
        return ref.at[pl.ds(pl.multiple_of(k * self.rows, self.rows), self.rows)]

    def greet(self):
        barrier = pltpu.get_barrier_semaphore()

        def step(k, carry):
            pl.semaphore_signal(barrier, inc=1, device_id=self.device(k)[1], device_id_type=MESH)
            return carry

        lax.fori_loop(1, self.count, step, 0)
        pl.semaphore_wait(barrier, self.count - 1)

    def settle(self, dst, slot):
        most = pl.ds(0, (self.count - 1) * self.rows)
        remote(self.mine.at[most], dst.at[most], self.send_sem.at[slot], self.recv_sem.at[slot], self.device(1)[1]).wait()

    def deal(self):
        def step(k, carry):
            other, place = self.device(k)
            remote(self.part(self.mine, other), self.part(self.held, self.me), self.send_sem.at[0], self.recv_sem.at[0], place).start()
            return carry

        lax.fori_loop(1, self.count, step, 0)
        at = pl.ds(pl.multiple_of(self.me * self.rows, self.rows), self.rows)
        self.held[at, :] = self.mine[at, :]

    def tell(self):
        self.settle(self.held, 0)

        def add(k, carry):
            return carry + self.held[pl.ds(pl.multiple_of(k * self.rows, self.rows), self.rows), :]

        self.total[...] = lax.fori_loop(0, self.count, add, jnp.zeros(self.total.shape, F32))

        def step(k, carry):
            place = self.device(k)[1]
            remote(self.total, self.part(self.done, self.me), self.send_sem.at[1], self.recv_sem.at[1], place).start()
            return carry

        lax.fori_loop(1, self.count, step, 0)
        self.done[pl.ds(pl.multiple_of(self.me * self.rows, self.rows), self.rows), :] = self.total[...]

    def close(self):
        self.settle(self.done, 1)


def blend(h_ref, coeffs, streams_ref):
    hist, block, width = h_ref.shape[0], h_ref.shape[2], h_ref.shape[3]
    spread = [jnp.broadcast_to(coeffs[:, k : k + 1], (block, 128)) for k in range(4 * hist)]
    for at in range(0, width, 128):
        lanes = slice(at, at + 128)
        inputs = [h_ref[j, 0, :, lanes].astype(F32) for j in range(hist)]
        for c in range(4):
            total = spread[c * hist] * inputs[0]
            for j in range(1, hist):
                total = total + spread[c * hist + j] * inputs[j]
            streams_ref[c, :, lanes] = total
    return spread


def mix_kernel(grid, rows, chunks, whole, partial, h_ref, g_ref, gain_ref, inner_ref, outer_ref, bias_ref, sgain_ref, sbias_ref, *refs):
    ins, (lowered_ref, gpair_ref, last_ref, pre_ref, coeffs_ref), outs = refs[:4], refs[4:9], refs[9:15]
    streams_ref, held_ref, local_sem, send_sem, recv_sem, pair_local, pair_send, pair_recv = refs[15:]
    i, steps = pl.program_id(0), pl.num_programs(0)
    a, b, z, c = place = grid.here()
    block = h_ref.shape[2]
    events = Gathering(grid, place, rows, chunks, ins, outs, local_sem, send_sem, recv_sem).events(whole, partial)
    other = grid.device(a, b, z, 1 - c)

    def pair(k, src, dst):
        return [
            pltpu.make_async_copy(src, dst, pair_local.at[k]),
            remote(src, dst, pair_send.at[k], pair_recv.at[k], other),
        ]

    grads = lambda: pair(0, g_ref.at[0], gpair_ref.at[c])
    lowereds = lambda: pair(1, held_ref, lowered_ref.at[:, c])

    @pl.when(i == 0)
    def _():
        grid.greet(*place)
        events[0]()
        start(grads())

    @pl.when(i == 1)
    def _():
        events[1]()

    last = h_ref[h_ref.shape[0] - 1, 0].astype(F32)
    r = lax.rsqrt(jnp.mean(last * last, axis=1, keepdims=True) + EPS)
    scaled_low = (last * r * gain_ref[...]).astype(BF16)
    pre = product(scaled_low, inner_ref[...])
    pre_ref[...] = pre
    coeffs = product((pre * phi(pre)).astype(BF16), outer_ref[...]) + bias_ref[...]
    coeffs_ref[...] = coeffs
    blend(h_ref, coeffs, streams_ref)
    at = pl.ds(pl.multiple_of(i * block, block), block)
    for k in range(4):
        stream = streams_ref[k]
        centered = stream - jnp.mean(stream, axis=1, keepdims=True)
        rs = lax.rsqrt(jnp.mean(centered * centered, axis=1, keepdims=True) + EPS)
        held_ref[k, at, :] = (centered * rs * sgain_ref[k : k + 1, :] + sbias_ref[k : k + 1, :]).astype(BF16)
    last_ref[...] = streams_ref[3]

    @pl.when(i == steps - 1)
    def _():
        start(lowereds())
        for event in events[2:]:
            event()
        finish(grads())
        finish(lowereds())


def mix_forward(grid, history, cotangent, params, weights, chunks, groups, partial, widths, collective_id):
    hist, _, tokens, width = history.shape
    mix = params[1].shape[1]
    block = 32
    rows = weights[0].shape[0]
    whole = pl.BlockSpec(memory_space=pltpu.VMEM)
    anywhere = pl.BlockSpec(memory_space=pl.ANY)
    part = lambda n: pl.BlockSpec((block, n), lambda i: (i, 0))
    results = pl.pallas_call(
        functools.partial(mix_kernel, grid, rows, chunks, groups, partial),
        grid=(tokens // block,),
        out_shape=[
            jax.ShapeDtypeStruct((4, 2, tokens, width), BF16),
            jax.ShapeDtypeStruct((2, tokens, width), BF16),
            jax.ShapeDtypeStruct((tokens, width), F32),
            jax.ShapeDtypeStruct((tokens, mix), F32),
            jax.ShapeDtypeStruct((tokens, mix), F32),
        ]
        + [jax.ShapeDtypeStruct((grid.na, grid.nb, grid.nz, 2 * rows, w), BF16) for w in widths],
        in_specs=[pl.BlockSpec((hist, 1, block, width), lambda i: (0, 0, i, 0))] + [whole] * 11,
        out_specs=[anywhere, anywhere, part(width), part(mix), part(mix)] + [anywhere] * len(widths),
        scratch_shapes=[
            pltpu.VMEM((4, block, width), F32),
            pltpu.VMEM((4, tokens, width), BF16),
            *gather_sems(grid, chunks),
            pltpu.SemaphoreType.DMA((2,)),
            pltpu.SemaphoreType.DMA((2,)),
            pltpu.SemaphoreType.DMA((2,)),
        ],
        compiler_params=pltpu.CompilerParams(collective_id=collective_id, has_side_effects=True, vmem_limit_bytes=VMEM_LIMIT),
        cost_estimate=pl.CostEstimate(flops=tokens * width * 80, bytes_accessed=history.size * 40, transcendentals=0),
        name="mix_forward",
    )(history, cotangent, *params, *weights)
    lowered, gpair, last, pre, coeffs = results[:5]
    return (
        lowered.reshape(4, 2 * tokens, width),
        gpair.reshape(2 * tokens, width),
        last,
        pre,
        coeffs,
        [w.reshape(-1, w.shape[-1]) for w in results[5:9]],
        results[9:],
    )


def small_rows(width, mix, hidden_width):
    wl, padded = width // 128, -(-mix // 8) * 8
    sizes = [wl, wl * padded, padded, 8, 4 * wl, 4 * wl, 3 * wl, wl, hidden_width // 128]
    firsts = [sum(sizes[:k]) for k in range(len(sizes))]
    return firsts, sum(sizes)


def unmix_kernel(grid, chunks, groups, n_parts, n_outs, h_ref, own_ref, theirs_ref, g_ref, pre_ref, coeffs_ref, gain_ref, inner_ref, outer_ref,
                 sgain_ref, hb_ref, eb_ref, *refs):
    parts, refs = refs[:n_parts], refs[n_parts:]
    hist_ref, small, outs, refs = refs[0], refs[1:10], refs[10 : 10 + n_outs], refs[10 + n_outs :]
    streams_ref, sg_ref, scaled_ref, mpg_ref, hidden_ref, cgl_ref, sgg_ref, sbg_ref, gg_ref, bg_ref, ob_ref = refs[:11]
    i, steps = pl.program_id(0), pl.num_programs(0)
    hist, block, width = h_ref.shape[0], h_ref.shape[2], h_ref.shape[3]
    mix = 4 * hist
    place = grid.here()
    c = place[3]
    sums = Summing(grid, *refs[11:17])
    events = Scattering(grid, place, chunks, parts, outs, refs[17:]).events(groups)

    @pl.when(i == 0)
    def _():
        sums.greet()
        events[0]()
        for ref in (sgg_ref, sbg_ref, gg_ref, bg_ref, ob_ref):
            ref[...] = jnp.zeros_like(ref)

    @pl.when(i == 6)
    def _():
        events[1]()

    def down(x):
        return jnp.sum(x, axis=0, keepdims=True)

    coeffs = coeffs_ref[...]
    spread = blend(h_ref, coeffs, streams_ref)
    grad = g_ref[0].astype(F32)
    ob_ref[...] += down(grad)
    for k in range(4):
        stream = streams_ref[k]
        centered = stream - jnp.mean(stream, axis=1, keepdims=True)
        rs = lax.rsqrt(jnp.mean(centered * centered, axis=1, keepdims=True) + EPS)
        n = centered * rs
        ng = own_ref[k] + theirs_ref[k].astype(F32)
        sgg_ref[k : k + 1, :] += down(ng * n)
        sbg_ref[k : k + 1, :] += down(ng)
        w = ng * sgain_ref[k : k + 1, :]
        pulled = rs * (w - jnp.mean(w, axis=1, keepdims=True) - n * jnp.mean(w * n, axis=1, keepdims=True))
        sg_ref[k] = pulled + grad if k == 3 else pulled

    lane = lax.broadcasted_iota(jnp.int32, (block, mix), 1)
    cg = jnp.zeros((block, mix), F32)
    for j in range(hist):
        value = h_ref[j, 0].astype(F32)
        for k in range(4):
            cg = jnp.where(lane == k * hist + j, jnp.sum(value * sg_ref[k], axis=1, keepdims=True), cg)
    bg_ref[...] += down(cg)
    cg_low = cg.astype(BF16)
    pre = pre_ref[...]
    at = pl.ds(pl.multiple_of(i * block, block), block)
    mpg = (against(cg_low, outer_ref[...]) * gelu_slope(pre)).astype(BF16)
    last = h_ref[hist - 1, 0].astype(F32)
    r = lax.rsqrt(jnp.mean(last * last, axis=1, keepdims=True) + EPS)
    scaled_ref[at, :] = (last * r * gain_ref[...]).astype(BF16)
    mpg_ref[at, :] = mpg
    hidden_ref[at, :] = (pre * phi(pre)).astype(BF16)
    cgl_ref[at, :] = cg_low
    scaled_grad = against(mpg, inner_ref[...])
    gg_ref[...] += down(scaled_grad * last * r)
    w = scaled_grad * gain_ref[...]
    last_grad = r * (w - last * (r * r) * jnp.mean(w * last, axis=1, keepdims=True))
    for from_ in range(0, width, 128):
        lanes = slice(from_, from_ + 128)
        pulls = [sg_ref[k, :, lanes] for k in range(4)]
        for j in range(hist):
            total = spread[j] * pulls[0]
            for k in range(1, 4):
                total = total + spread[k * hist + j] * pulls[k]
            hist_ref[j, 0, :, lanes] = total + last_grad[:, lanes] if j == hist - 1 else total

    @pl.when(i == steps - 1)
    def _():
        mine, done = sums.mine, sums.done
        wl = width // 128
        padded = -(-mix // 8) * 8
        hidden_rows = eb_ref.shape[1] // 128
        firsts, _ = small_rows(width, mix, 2 * eb_ref.shape[1])
        mine[...] = jnp.zeros_like(mine)
        inner_grad = inner(mpg_ref[...], scaled_ref[...])
        for l in range(wl):
            lanes = slice(l * 128, (l + 1) * 128)
            mine[firsts[0] + l : firsts[0] + l + 1, :] = gg_ref[:, lanes]
            mine[firsts[1] + l * padded : firsts[1] + l * padded + mix, :] = inner_grad[:, lanes]
            mine[firsts[4] + 4 * l : firsts[4] + 4 * l + 4, :] = sgg_ref[:, lanes]
            mine[firsts[5] + 4 * l : firsts[5] + 4 * l + 4, :] = sbg_ref[:, lanes]
            mine[firsts[7] + l : firsts[7] + l + 1, :] = ob_ref[:, lanes]
        mine[firsts[2] : firsts[2] + mix, 0:mix] = inner(hidden_ref[...], cgl_ref[...])
        mine[firsts[3] : firsts[3] + 1, 0:mix] = bg_ref[...]
        for k in range(3):
            for l in range(wl // 2):
                mine[pl.ds(firsts[6] + k * wl + c * (wl // 2) + l, 1), :] = hb_ref[k : k + 1, l * 128 : (l + 1) * 128]
        for l in range(hidden_rows):
            mine[pl.ds(firsts[8] + c * hidden_rows + l, 1), :] = eb_ref[:, l * 128 : (l + 1) * 128]
        sums.deal()
        for n, event in enumerate(events[2:]):
            event()
            if n == 0:
                sums.tell()
            if n == 1:
                sums.close()
        for l in range(wl):
            lanes = slice(l * 128, (l + 1) * 128)
            small[0][:, lanes] = done[firsts[0] + l : firsts[0] + l + 1, :]
            small[1][:, lanes] = done[firsts[1] + l * padded : firsts[1] + l * padded + mix, :]
            small[4][:, lanes] = done[firsts[4] + 4 * l : firsts[4] + 4 * l + 4, :]
            small[5][:, lanes] = done[firsts[5] + 4 * l : firsts[5] + 4 * l + 4, :]
            small[7][:, lanes] = done[firsts[7] + l : firsts[7] + l + 1, :]
        small[2][...] = done[firsts[2] : firsts[2] + mix, 0:mix]
        small[3][...] = done[firsts[3] : firsts[3] + 1, 0:mix]
        for l in range(3 * wl):
            small[6][:, l * 128 : (l + 1) * 128] = done[firsts[6] + l : firsts[6] + l + 1, :]
        for l in range(2 * hidden_rows):
            small[8][:, l * 128 : (l + 1) * 128] = done[firsts[8] + l : firsts[8] + l + 1, :]


def mix_backward(grid, history, own, theirs, cotangent, pre, coeffs, params, biases, parts, folded, chunks, groups, widths, collective_id):
    hist, _, tokens, width = history.shape
    mix = pre.shape[1]
    hidden_width = 2 * biases[1].shape[1]
    na, nb, nz = grid.na, grid.nb, grid.nz
    rows = parts[0].shape[0] // (na * nb * nz)
    parts = [p.reshape(na, nb, nz, rows, p.shape[1]) for p in parts] + list(folded)
    devices = grid.n_dp * grid.n_seq
    small_each = -(-small_rows(width, mix, hidden_width)[1] // (devices * 8)) * 8
    block = 32
    whole = pl.BlockSpec(memory_space=pltpu.VMEM)
    anywhere = pl.BlockSpec(memory_space=pl.ANY)
    part = lambda n: pl.BlockSpec((block, n), lambda i: (i, 0))
    four = pl.BlockSpec((4, block, width), lambda i: (0, i, 0))
    story = pl.BlockSpec((hist, 1, block, width), lambda i: (0, 0, i, 0))
    small = [(1, width), (mix, width), (mix, mix), (1, mix), (4, width), (4, width), (1, 3 * width), (1, width), (1, hidden_width)]
    fixed = [pl.BlockSpec(shape, lambda i: (0, 0)) for shape in small]
    moved = sum(p.size for p in parts) * 2
    results = pl.pallas_call(
        functools.partial(unmix_kernel, grid, chunks, groups, len(parts), len(widths)),
        grid=(tokens // block,),
        out_shape=[jax.ShapeDtypeStruct(history.shape, F32)]
        + [jax.ShapeDtypeStruct(shape, F32) for shape in small]
        + [jax.ShapeDtypeStruct((rows // 2, w), F32) for w in widths],
        in_specs=[story, four, four, pl.BlockSpec((1, block, width), lambda i: (0, i, 0)), part(mix), part(mix)]
        + [whole] * 6
        + [anywhere] * len(parts),
        out_specs=[story] + fixed + [anywhere] * len(widths),
        scratch_shapes=[
            pltpu.VMEM((4, block, width), F32),
            pltpu.VMEM((4, block, width), F32),
            pltpu.VMEM((tokens, width), BF16),
            pltpu.VMEM((tokens, mix), BF16),
            pltpu.VMEM((tokens, mix), BF16),
            pltpu.VMEM((tokens, mix), BF16),
            pltpu.VMEM((4, width), F32),
            pltpu.VMEM((4, width), F32),
            pltpu.VMEM((1, width), F32),
            pltpu.VMEM((1, mix), F32),
            pltpu.VMEM((1, width), F32),
            pltpu.VMEM((devices * small_each, 128), F32),
            pltpu.VMEM((devices * small_each, 128), F32),
            pltpu.VMEM((small_each, 128), F32),
            pltpu.VMEM((devices * small_each, 128), F32),
            pltpu.SemaphoreType.DMA((2,)),
            pltpu.SemaphoreType.DMA((2,)),
            *scatter_scratch(grid, chunks, rows),
        ],
        compiler_params=pltpu.CompilerParams(collective_id=collective_id, has_side_effects=True, vmem_limit_bytes=VMEM_LIMIT),
        cost_estimate=pl.CostEstimate(flops=tokens * width * 300, bytes_accessed=moved * 20, transcendentals=0),
        name="mix_backward",
    )(history, own, theirs, cotangent, pre, coeffs, *params, *biases, *parts)
    return results[0], results[10:], results[1:10]


def project_kernel(width, low_ref, g_ref, wq_ref, wk_ref, wv_ref, wo_ref, bias_ref, cos_ref, above_ref, below_ref, sent_ref):
    wide = wq_ref.shape[1]
    reps = wide // cos_ref.shape[1] if wide >= cos_ref.shape[1] else 1
    tables = [jnp.concatenate([t[:, :wide]] * reps, axis=1) for t in (cos_ref, above_ref, below_ref)]
    q = rotate(product(low_ref[0], wq_ref[...]) + bias_ref[0:1, :], tables, 1.0)
    k = rotate(product(low_ref[1], wk_ref[...]) + bias_ref[1:2, :], tables, 1.0)
    v = product(low_ref[2], wv_ref[...]) + bias_ref[2:3, :]
    g = product(g_ref[...], wo_ref[...])
    for n, x in enumerate((q, k, v, g)):
        x = x.astype(BF16)
        for m in range(wide // width):
            sent_ref[m, :, n * width : (n + 1) * width] = x[:, m * width : (m + 1) * width]


def project(grid, lowered, grad_low, weights, biases, tables, own_width):
    both = lowered.shape[1]
    nz = grid.nz
    wide = 2 * own_width
    whole = pl.BlockSpec(memory_space=pltpu.VMEM)
    cols = lambda n: pl.BlockSpec((n, wide), lambda i: (0, i))
    return pl.pallas_call(
        functools.partial(project_kernel, own_width),
        grid=(nz // 2,),
        out_shape=jax.ShapeDtypeStruct((nz, both, 4 * own_width), BF16),
        in_specs=[whole, whole] + [cols(weights[0].shape[0])] * 4 + [cols(3)] + [whole] * 3,
        out_specs=pl.BlockSpec((2, both, 4 * own_width), lambda i: (i, 0, 0)),
        compiler_params=pltpu.CompilerParams(vmem_limit_bytes=VMEM_LIMIT),
        cost_estimate=pl.CostEstimate(flops=8 * both * weights[0].size, bytes_accessed=lowered.size * 4, transcendentals=0),
        name="project",
    )(lowered, grad_low, *weights, biases, *tables)


def feed_kernel(grid, steps, low_ref, g_ref, we_ref, wc_ref, bias_ref, feed_ref, normed_ref, eb_ref, e2_ref, c2_ref, *refs):
    parts, refs = refs[: 2 * steps], refs[2 * steps :]
    first, second, refs = refs[: 2 * steps], refs[2 * steps : 4 * steps], refs[4 * steps :]
    send_sem, recv_sem, out_sem = refs
    i = pl.program_id(0)
    a, b, z, c = place = grid.here()
    orders = ["ab", "ba"] * steps
    outs = (e2_ref, c2_ref)

    def copies(t, stage):
        if stage < 2:
            return fold_copies(grid, place, orders[t], stage, parts[t], first[t], second[t], (send_sem.at[t], recv_sem.at[t]))
        n = parts[t].shape[-1]
        return [pltpu.make_async_copy(second[t].at[0], outs[t % 2].at[:, :, pl.ds((t // 2) * n, n)], out_sem.at[t])]

    def begin(u):
        for t in (2 * u, 2 * u + 1):
            start(copies(t, 0))

    def end(u, stage):
        for t in (2 * u, 2 * u + 1):
            finish(copies(t, stage))
            if stage < 2:
                own = parts[t].at[a] if orders[t] == "ab" else parts[t].at[:, b]
                fold_add(grid, place, orders[t], stage, own, first[t], second[t])
                start(copies(t, stage + 1))

    def turn(u):
        if u < steps:
            end(u, 0)
        if 0 <= u - 1 < steps:
            end(u - 1, 1)

    @pl.when(i == 0)
    def _():
        grid.greet(*place)
        feed_ref[...] = jnp.zeros_like(feed_ref)
        normed_ref[...] = jnp.zeros_like(normed_ref)

    low, grad, expand, contract = low_ref[0], g_ref[...], we_ref[...], wc_ref[...]
    expanded = product(low, expand) + bias_ref[...]
    share = phi(expanded)
    hidden = (expanded * share).astype(BF16)
    slope = share + expanded * jnp.exp(-0.5 * expanded * expanded) * (1.0 / math.sqrt(2.0 * math.pi))
    feed_ref[...] += against(hidden, contract)
    hidden_grad = inner(grad, hidden).astype(BF16)
    pulled = product(grad, contract) * slope
    eb_ref[...] = jnp.sum(pulled, axis=0, keepdims=True)
    pulled_low = pulled.astype(BF16)
    normed_ref[...] += against(pulled_low, expand)
    expand_grad = inner(low, pulled_low).astype(BF16)
    for u in range(steps):

        @pl.when(i == u)
        def _(u=u):
            parts[2 * u][...] = expand_grad.reshape(parts[2 * u].shape)
            parts[2 * u + 1][...] = hidden_grad.reshape(parts[2 * u + 1].shape)
            begin(u)
            if u >= 2:
                turn(u - 2)
            if u == steps - 1:
                for v in range(max(steps - 2, 0), steps + 1):
                    turn(v)
                for v in range(steps):
                    end(v, 2)


def feed_forward(grid, lowered, grad_low, weight_e, weight_c, bias, steps, collective_id):
    both, width = grad_low.shape
    n = weight_e.shape[1] // steps
    na, nb, nz = grid.na, grid.nb, grid.nz
    rows = width // (na * nb * nz)
    whole = lambda *shape: pl.BlockSpec(shape, lambda i: (0,) * len(shape))
    cols = lambda m: pl.BlockSpec((m, n), lambda i: (0, i))
    orders = ["ab", "ba"] * steps
    folds = [fold_scratch(grid, order, rows, n) for order in orders]
    sem = pltpu.SemaphoreType.DMA((2 * steps, nz + nb))
    return pl.pallas_call(
        functools.partial(feed_kernel, grid, steps),
        grid=(steps,),
        out_shape=[
            jax.ShapeDtypeStruct((both, width), F32),
            jax.ShapeDtypeStruct((both, width), F32),
            jax.ShapeDtypeStruct((1, n * steps), F32),
            jax.ShapeDtypeStruct((nz, rows, n * steps), BF16),
            jax.ShapeDtypeStruct((nz, rows, n * steps), BF16),
        ],
        in_specs=[
            pl.BlockSpec((1, both, width), lambda i: (3, 0, 0)),
            whole(both, width),
            cols(width),
            cols(width),
            cols(1),
        ],
        out_specs=[
            whole(both, width),
            whole(both, width),
            cols(1),
            pl.BlockSpec(memory_space=pl.ANY),
            pl.BlockSpec(memory_space=pl.ANY),
        ],
        scratch_shapes=[pltpu.VMEM((na, nb, nz, rows, n), BF16)] * (2 * steps)
        + [f for _, f, _ in folds]
        + [s for _, _, s in folds]
        + [sem, sem, pltpu.SemaphoreType.DMA((2 * steps,))],
        compiler_params=pltpu.CompilerParams(collective_id=collective_id, has_side_effects=True, vmem_limit_bytes=VMEM_LIMIT),
        cost_estimate=pl.CostEstimate(flops=12 * both * width * n * steps * 2, bytes_accessed=width * n * steps * 20, transcendentals=0),
        name="feed_forward",
    )(lowered, grad_low, weight_e, weight_c, bias)


def attention_kernel(width, heads, tile, step, edge, length, x_ref, kdoc_ref, qdoc_ref, out_ref,
                     s_ref, kt_ref, vt_ref, ot_ref, dqt_ref, dka_ref, dva_ref, top_ref):
    i = pl.program_id(0)
    tiles = length // tile
    scale = 1.0 / math.sqrt(HEAD_DIM)
    @pl.when(i == 0)
    def _():
        dka_ref[...] = jnp.zeros_like(dka_ref)
        dva_ref[...] = jnp.zeros_like(dva_ref)
        def turn(j, carry):
            at = pl.ds(pl.multiple_of(j * tile, tile), tile)
            kt_ref[:, at] = x_ref[at, width : 2 * width].T
            vt_ref[:, at] = x_ref[at, 2 * width : 3 * width].T
            return carry
        lax.fori_loop(0, tiles, turn, 0)
    rows = pl.ds(pl.multiple_of(i * tile, tile), tile)
    query = x_ref[rows, 0:width] * jnp.asarray(scale, BF16)
    grad = x_ref[rows, 3 * width : 4 * width]
    query_t, grad_t = query.T, grad.T
    lanes = lax.broadcasted_iota(jnp.int32, (tile, width), 1) // HEAD_DIM
    subs = lax.broadcasted_iota(jnp.int32, (width, tile), 0) // HEAD_DIM
    zero = jnp.zeros((), BF16)
    queries_t = [jnp.where(subs == h, query_t, zero) for h in range(heads)]
    grads_t = [jnp.where(subs == h, grad_t, zero) for h in range(heads)]
    all_queries = jnp.concatenate([jnp.where(lanes == h, query, zero) for h in range(heads)], axis=0)
    all_grads = jnp.concatenate([jnp.where(lanes == h, grad, zero) for h in range(heads)], axis=0)
    qdoc = qdoc_ref[:, rows]
    qpos = i * tile + lax.broadcasted_iota(jnp.int32, (step, tile), 1)
    head_edge = -(-edge // step)
    tail_edge = (length - edge) // tile
    per = tile // step
    count = (i + 1) * per
    ot_ref[...] = jnp.zeros_like(ot_ref)
    dqt_ref[...] = jnp.zeros_like(dqt_ref)
    top_ref[...] = jnp.full_like(top_ref, NEG)

    def fold(x, f):
        return f(x.reshape(step // 8, 8, tile), axis=0)

    def scores(j, carry):
        at = pl.ds(pl.multiple_of(j * step, step), step)
        checked = (j >= i * per) | (j < head_edge) | (i >= tail_edge)
        def run(mask):
            keys = x_ref[at, width : 2 * width]
            if mask:
                kdoc = jnp.concatenate([kdoc_ref[at, :]] * (tile // 128), axis=1)
                kpos = j * step + lax.broadcasted_iota(jnp.int32, (step, tile), 0)
                allowed = (kdoc == qdoc) & (kpos <= qpos)
            for h in range(heads):
                s = product(keys, queries_t[h])
                if mask:
                    s = jnp.where(allowed, s, NEG)
                s_ref[h, at, :] = s
                top_ref[h] = jnp.maximum(top_ref[h], fold(s, jnp.max))
        pl.when(checked)(lambda: run(True))
        pl.when(jnp.logical_not(checked))(lambda: run(False))
        return carry
    lax.fori_loop(0, count, scores, 0)
    tops = [jnp.max(top_ref[h], axis=0, keepdims=True) for h in range(heads)]

    def weigh(j, totals):
        at = pl.ds(pl.multiple_of(j * step, step), step)
        new = []
        for h in range(heads):
            own = slice(h * HEAD_DIM, (h + 1) * HEAD_DIM)
            weights = jnp.exp(s_ref[h, at, :] - tops[h])
            s_ref[h, at, :] = weights
            new.append(totals[h] + fold(weights, jnp.sum))
            ot_ref[own, :] += product(vt_ref[own, at], weights.astype(BF16))
        return new
    totals = lax.fori_loop(0, count, weigh, [jnp.zeros((8, tile), F32)] * heads)
    inverse = [1.0 / jnp.sum(t, axis=0, keepdims=True) for t in totals]
    grad_f = grad_t.astype(F32)
    deltas = []
    for h in range(heads):
        own = slice(h * HEAD_DIM, (h + 1) * HEAD_DIM)
        value = ot_ref[own, :] * inverse[h]
        ot_ref[own, :] = value
        deltas.append(jnp.sum(value * grad_f[own], axis=0, keepdims=True))
    out_ref[rows, 0:width] = ot_ref[...].T.astype(BF16)

    def back(j, carry):
        at = pl.ds(pl.multiple_of(j * step, step), step)
        values = x_ref[at, 2 * width : 3 * width]
        probs_low, grads_low = [], []
        for h in range(heads):
            own = slice(h * HEAD_DIM, (h + 1) * HEAD_DIM)
            probs_grad = product(values, grads_t[h])
            probs = s_ref[h, at, :] * inverse[h]
            scores_grad = (probs * (probs_grad - deltas[h])).astype(BF16)
            probs_low.append(probs.astype(BF16))
            grads_low.append(scores_grad)
            dqt_ref[own, :] += product(kt_ref[own, at], scores_grad)
        dva_ref[at, :] += product(jnp.concatenate(probs_low, axis=1), all_grads)
        dka_ref[at, :] += product(jnp.concatenate(grads_low, axis=1), all_queries)
        return carry
    lax.fori_loop(0, count, back, 0)
    out_ref[rows, width : 2 * width] = (dqt_ref[...].T * scale).astype(BF16)

    @pl.when(i == tiles - 1)
    def _():
        out_ref[:, 2 * width : 3 * width] = dka_ref[...].astype(BF16)
        out_ref[:, 3 * width : 4 * width] = dva_ref[...].astype(BF16)


def attention(dealt, documents, heads, edge):
    length = dealt.shape[0]
    width = heads * HEAD_DIM
    tile = step = 2 * edge
    pairs = length * length // 2 * heads
    kdoc = jnp.broadcast_to(documents[:, None], (length, 128)); qdoc = documents[None, :]
    whole = lambda i: (0, 0)
    return pl.pallas_call(
        functools.partial(attention_kernel, width, heads, tile, step, edge, length),
        grid=(length // tile,),
        out_shape=jax.ShapeDtypeStruct((length, 4 * width), BF16),
        in_specs=[pl.BlockSpec((length, 4 * width), whole), pl.BlockSpec((length, 128), whole), pl.BlockSpec((1, length), whole)],
        out_specs=pl.BlockSpec((length, 4 * width), whole),
        scratch_shapes=[
            pltpu.VMEM((heads, length, tile), F32), pltpu.VMEM((width, length), BF16), pltpu.VMEM((width, length), BF16),
            pltpu.VMEM((width, tile), F32), pltpu.VMEM((width, tile), F32), pltpu.VMEM((length, width), F32), pltpu.VMEM((length, width), F32),
            pltpu.VMEM((heads, 8, tile), F32)],
        compiler_params=pltpu.CompilerParams(vmem_limit_bytes=VMEM_LIMIT),
        cost_estimate=pl.CostEstimate(flops=pairs * 64 * 2 * 6 * 4, bytes_accessed=length * width * 20, transcendentals=pairs),
        name="attention",
    )(dealt, kdoc, qdoc)


def on_device(
    grid,
    history,
    documents,
    cotangent,
    mixer_gain,
    mixer_inner,
    mixer_outer,
    mixer_bias,
    stream_gain,
    stream_bias,
    inbound_weight,
    inbound_bias,
    outbound_weight,
    outbound_bias,
    expand,
    expand_bias,
    contract,
    contract_bias,
):
    n_seq, nz = grid.n_seq, grid.nz
    tokens, width = history.shape[2], history.shape[3]
    hidden_width = expand.shape[1]
    half, hidden_half = width // 2, hidden_width // 2
    both = 2 * tokens
    length = documents.shape[1]
    heads = HEADS // n_seq
    own_width = heads * HEAD_DIM
    seq = lax.axis_index("seq")
    z, c = seq // 2, lax.rem(seq, 2)

    def take(array, start, size, axis=0):
        return lax.dynamic_slice_in_dim(array, start, size, axis)

    gain = mixer_gain.astype(F32)[None]
    stream_gain_full = stream_gain.astype(F32)
    pick = lambda base, n: (lambda core: base + core * n)
    parts = 4
    piece = hidden_half // parts
    feed = []
    for part in range(parts):
        base = lambda core, part=part: core * hidden_half + part * piece
        feed.append((2, base, 4, part * piece, piece, "ba"))
        feed.append((3, base, 5, part * piece, piece, "ab"))
    lowered, grad_low, last_stream, mix_pre, coeffs, (weight_k, weight_v, weight_q, weight_o), started = mix_forward(
        grid,
        history,
        cotangent,
        [gain, mixer_inner, mixer_outer, mixer_bias.astype(F32)[None], stream_gain_full, stream_bias.astype(F32)],
        [inbound_weight, outbound_weight, expand, contract],
        [
            (0, pick(width, half), 0, 0, half, "ba"),
            (0, pick(2 * width, half), 1, 0, half, "ab"),
            (0, pick(0, half), 2, 0, half, "ba"),
            (1, pick(0, half), 3, 0, half, "ab"),
        ]
        + feed,
        [[0, 1], [2, 3]],
        [[4 + 2 * part, 5 + 2 * part] for part in range(parts)],
        [half] * 4 + [hidden_half] * 2,
        1,
    )

    bias_in = inbound_bias.astype(F32).reshape(3, width)
    positions = z * both + jnp.arange(both, dtype=jnp.int32)
    tables = rotary_tables(positions, 128)
    sent = project(
        grid, lowered, grad_low, [weight_q, weight_k, weight_v, weight_o], take(bias_in, c * half, half, 1), tables, own_width
    )
    groups = [[2 * k + core for k in range(nz)] for core in range(2)]
    dealt = lax.all_to_all(sent, "seq", 0, 0, axis_index_groups=groups, tiled=True)

    started_e, started_c, _ = lax.optimization_barrier((*started, sent[0, 0]))
    chunks = [(0, None, n - 4, col, size, order) for _, _, n, col, size, order in feed]
    pairs = [[2 * part, 2 * part + 1] for part in range(parts)]
    weight_e, weight_c = gather(grid, [started_e, started_c], chunks, pairs, 3, "gather_feed")
    dealt, weight_e, weight_c = lax.optimization_barrier((dealt, weight_e, weight_c))

    returned = attention(dealt.reshape(length, 4 * own_width), documents[0], heads, tokens).reshape(nz, both, 4 * own_width)
    collected = lax.all_to_all(returned, "seq", 0, 0, axis_index_groups=groups, tiled=True)

    bias_e = take(expand_bias.astype(F32), c * hidden_half, hidden_half)[None]
    lowered_seen, _ = lax.optimization_barrier((lowered, returned[0, 0]))
    feed_part, normed_feed, expand_bias_part, *folded = feed_forward(
        grid, lowered_seen, grad_low, weight_e, weight_c, bias_e, parts, 5
    )

    pieces = [
        jnp.concatenate([collected[m, :, k * own_width : (k + 1) * own_width] for m in range(nz)], axis=-1) for k in range(4)
    ]
    attended_low, value_low = pieces[0], pieces[3]
    spread = [jnp.tile(t, (1, half // 128)) for t in tables]

    def unturn(grad):
        grad = grad.astype(F32)
        up = jnp.roll(grad, -(ROT_DIMS // 2), axis=-1)
        down = jnp.roll(grad, ROT_DIMS // 2, axis=-1)
        return grad * spread[0] - (up * spread[1] + down * spread[2])

    dq, dk = unturn(pieces[1]), unturn(pieces[2])
    dq_low, dk_low, dv_low = dq.astype(BF16), dk.astype(BF16), value_low
    head_bias_grads = jnp.stack([jnp.sum(x.astype(F32), axis=0) for x in (dq, dk, value_low)])

    out_part = against(attended_low, weight_o) + feed_part
    swap = [(s, s + 1 - 2 * (s % 2)) for s in range(n_seq)]
    out_theirs = lax.ppermute(take(out_part, (1 - c) * tokens, tokens), "seq", swap)
    out_own = take(out_part, c * tokens, tokens) + out_theirs
    layer_out = (last_stream + (out_own + outbound_bias.astype(F32) + contract_bias.astype(F32))).astype(BF16)

    normed_part = jnp.stack(
        [
            against(dq_low, weight_q),
            against(dk_low, weight_k),
            against(dv_low, weight_v),
            normed_feed,
        ]
    )
    normed_theirs = lax.ppermute(take(normed_part, (1 - c) * tokens, tokens, 1).astype(BF16), "seq", swap)
    normed_own = take(normed_part, c * tokens, tokens, 1)

    chunks = [
        (0, half, "ab", 0, pick(0, half)),
        (1, half, "ba", 0, pick(width, half)),
        (2, half, "ab", 0, pick(2 * width, half)),
        (3, half, "ba", 1, pick(0, half)),
        (4, hidden_half, "", 2, pick(0, hidden_half)),
        (5, hidden_half, "", 3, pick(0, hidden_half)),
    ]
    history_grad, owned, small = mix_backward(
        grid,
        history,
        normed_own,
        normed_theirs,
        cotangent,
        mix_pre,
        coeffs,
        [gain, mixer_inner, mixer_outer, stream_gain_full],
        [head_bias_grads, expand_bias_part],
        [
            inner(lowered[0], dq_low).astype(BF16),
            inner(lowered[1], dk_low).astype(BF16),
            inner(lowered[2], dv_low).astype(BF16),
            inner(grad_low, attended_low).astype(BF16),
        ],
        folded,
        chunks,
        [[0, 1], [2, 3]],
        [3 * width, width, hidden_width, hidden_width],
        4,
    )
    gain_grad, inner_grad, outer_grad, bias_grad, stream_gain_grad, stream_bias_grad, in_bias_grad, out_bias_grad, expand_bias_grad = small
    return (
        layer_out[None],
        history_grad,
        gain_grad.reshape(width),
        inner_grad.T,
        outer_grad,
        bias_grad.reshape(-1),
        stream_gain_grad,
        stream_bias_grad,
        owned[0],
        in_bias_grad.reshape(3 * width),
        owned[1],
        out_bias_grad.reshape(width),
        owned[2],
        expand_bias_grad.reshape(hidden_width),
        owned[3],
        out_bias_grad.reshape(width),
    )


def solution(mesh):
    rows = P(("dp", "seq"), None)
    placed = (
        P(None, "dp", "seq", None),
        P("dp", None),
        P("dp", "seq", None),
        P(),
        P(),
        P(),
        P(),
        P(),
        P(),
        rows,
        P(),
        rows,
        P(),
        rows,
        P(),
        rows,
        P(),
    )
    grid = Grid(mesh.shape["dp"], mesh.shape["seq"])
    return jax.shard_map(
        functools.partial(on_device, grid),
        mesh=mesh,
        in_specs=placed,
        out_specs=(
            P("dp", "seq", None),
            P(None, "dp", "seq", None),
            P(),
            P(),
            P(),
            P(),
            P(),
            P(),
            rows,
            P(),
            rows,
            P(),
            rows,
            P(),
            rows,
            P(),
        ),
        check_vma=False,
    )
```

```python
import functools
import math

import jax
import jax.numpy as jnp
from jax import lax
from jax.experimental import pallas as pl
from jax.experimental.pallas import tpu as pltpu
from jax.sharding import PartitionSpec as P

HEADS = 16
HEAD_DIM = 64
ROT_DIMS = 16
EPS = 1e-05
HIGHEST = lax.Precision.HIGHEST
NEG = -1e30
MESH = pl.DeviceIdType.MESH
F32 = jnp.float32
BF16 = jnp.bfloat16
VMEM_LIMIT = 56 * 1024 * 1024


def inner(left, right):
    return lax.dot_general(left, right, (((0,), (0,)), ((), ())), preferred_element_type=F32)


def against(left, right):
    return lax.dot_general(left, right, (((1,), (1,)), ((), ())), preferred_element_type=F32)


def product(left, right):
    return jnp.dot(left, right, preferred_element_type=F32)


def exact_gelu(value):
    return jax.nn.gelu(value, approximate=False)


def phi(value):
    return 0.5 * (1.0 + lax.erf(value * (1.0 / math.sqrt(2.0))))


def gelu_slope(value):
    return phi(value) + value * jnp.exp(-0.5 * value * value) * (1.0 / math.sqrt(2.0 * math.pi))


def rotate(value, tables, sign):
    half = ROT_DIMS // 2
    cosine, above, below = tables
    width = value.shape[-1]
    up = pltpu.roll(value, width - half, 1)
    down = pltpu.roll(value, half, 1)
    return value * cosine + sign * (up * above + down * below)


class Grid:
    def __init__(self, n_dp, n_seq):
        self.n_dp, self.n_seq = n_dp, n_seq
        self.na, self.nb, self.nz = 2, n_dp // 2, n_seq // 2

    def here(self):
        dp, seq = lax.axis_index("dp"), lax.axis_index("seq")
        return dp // self.nb, lax.rem(dp, self.nb), seq // 2, lax.rem(seq, 2)

    def device(self, a, b, z, c):
        return (a * self.nb + b, z * 2 + c)

    def peers(self, a, b, z, c):
        found = [self.device(a, b, z, 1 - c), self.device(1 - a, b, z, c)]
        found += [self.device(a, lax.rem(b + k, self.nb), z, c) for k in range(1, self.nb)]
        found += [self.device(a, b, lax.rem(z + k, self.nz), c) for k in range(1, self.nz)]
        return found

    def greet(self, a, b, z, c):
        barrier = pltpu.get_barrier_semaphore()
        found = self.peers(a, b, z, c)
        for peer in found:
            pl.semaphore_signal(barrier, inc=1, device_id=peer, device_id_type=MESH)
        pl.semaphore_wait(barrier, len(found))


def remote(src, dst, send, recv, device):
    return pltpu.make_async_remote_copy(
        src_ref=src, dst_ref=dst, send_sem=send, recv_sem=recv, device_id=device, device_id_type=MESH
    )


def remote(src, dst, send, recv, device):
    return pltpu.make_async_remote_copy(
        src_ref=src, dst_ref=dst, send_sem=send, recv_sem=recv, device_id=device, device_id_type=MESH
    )


def start(copies):
    for copy in copies:
        copy.start()


def finish(copies):
    for copy in copies:
        copy.wait()


class Gathering:
    def __init__(self, grid, place, rows, chunks, ins, outs, local_sem, send_sem, recv_sem):
        self.grid, self.place, self.rows, self.chunks = grid, place, rows, chunks
        self.ins, self.outs = ins, outs
        self.local_sem, self.send_sem, self.recv_sem = local_sem, send_sem, recv_sem

    def copies(self, t, stage):
        a, b, z, c = self.place
        grid, rows = self.grid, self.rows
        nz, nb = grid.nz, grid.nb
        source, base, result, col, n, order = self.chunks[t]
        out, cols = self.outs[result], pl.ds(col, n)

        def send(src, dst, slot, device):
            return remote(src, dst, self.send_sem.at[t, slot], self.recv_sem.at[t, slot], device)

        if stage == 0:
            mine = self.ins[source].at[:, pl.ds(pl.multiple_of(base(c), 128), n)]
            theirs = self.ins[source].at[:, pl.ds(pl.multiple_of(base(1 - c), 128), n)]
            spot = out.at[a, b, z, pl.ds(pl.multiple_of(c * rows, rows), rows), cols]
            return [pltpu.make_async_copy(mine, spot, self.local_sem.at[t]), send(theirs, spot, 0, grid.device(a, b, z, 1 - c))]
        if stage == 1:
            block = out.at[a, b, z, :, cols]
            return [send(block, block, k, grid.device(a, b, lax.rem(z + k, nz), c)) for k in range(1, nz)]
        if order[stage - 2] == "b":
            block = out.at[a, b, :, :, cols] if stage == 2 else out.at[:, b, :, :, cols]
            return [send(block, block, nz + k - 1, grid.device(a, lax.rem(b + k, nb), z, c)) for k in range(1, nb)]
        block = out.at[a, b, :, :, cols] if stage == 2 else out.at[a, :, :, :, cols]
        return [send(block, block, nz + nb - 1, grid.device(1 - a, b, z, c))]

    def begin(self, group, stage):
        for t in group:
            start(self.copies(t, stage))

    def end(self, group, stage):
        for t in group:
            finish(self.copies(t, stage))

    def events(self, whole, partial):
        groups = whole + partial

        def first():
            for group in groups:
                self.begin(group, 0)

        def second():
            self.end(groups[0], 0)
            self.begin(groups[0], 1)

        def turn(u):
            if u < len(groups):
                self.end(groups[u], 1)
                if u + 1 < len(groups):
                    self.end(groups[u + 1], 0)
                    self.begin(groups[u + 1], 1)
                if u < len(whole):
                    self.begin(groups[u], 2)
            if 0 <= u - 1 < len(whole):
                self.end(groups[u - 1], 2)
                self.begin(groups[u - 1], 3)
            if 0 <= u - 2 < len(whole):
                self.end(groups[u - 2], 3)

        turns = max(len(whole) + 2, len(groups))
        return [first, second] + [functools.partial(turn, u) for u in range(turns)]

    def late_events(self, groups):
        def turn(u):
            if u < len(groups):
                self.begin(groups[u], 2)
            if 0 <= u - 1 < len(groups):
                self.end(groups[u - 1], 2)
                self.begin(groups[u - 1], 3)
            if 0 <= u - 2 < len(groups):
                self.end(groups[u - 2], 3)

        return [functools.partial(turn, u) for u in range(len(groups) + 2)]


def gather_kernel(grid, chunks, groups, n, *refs):
    outs = refs[n : 2 * n]
    place = grid.here()
    grid.greet(*place)
    for event in Gathering(grid, place, None, chunks, None, outs, *refs[2 * n :]).late_events(groups):
        event()


def gather_sems(grid, chunks):
    slots = grid.nz + grid.nb
    return [
        pltpu.SemaphoreType.DMA((len(chunks),)),
        pltpu.SemaphoreType.DMA((len(chunks), slots)),
        pltpu.SemaphoreType.DMA((len(chunks), slots)),
    ]


def gather(grid, arrays, chunks, groups, collective_id, name):
    n = len(arrays)
    moved = sum(x.size for x in arrays) * 2
    results = pl.pallas_call(
        functools.partial(gather_kernel, grid, chunks, groups, n),
        out_shape=[jax.ShapeDtypeStruct(x.shape, x.dtype) for x in arrays],
        in_specs=[pl.BlockSpec(memory_space=pl.ANY)] * n,
        out_specs=[pl.BlockSpec(memory_space=pl.ANY)] * n,
        input_output_aliases={k: k for k in range(n)},
        scratch_shapes=gather_sems(grid, chunks),
        compiler_params=pltpu.CompilerParams(collective_id=collective_id, has_side_effects=True),
        cost_estimate=pl.CostEstimate(flops=0, bytes_accessed=moved * 20, transcendentals=0),
        name=name,
    )(*arrays)
    return [r.reshape(-1, r.shape[-1]) for r in results]


def fold_copies(grid, place, order, stage, part, first, second, sems):
    a, b, z, c = place
    nz, nb = grid.nz, grid.nb

    def send(src, dst, slot, device):
        return remote(src, dst, sems[0].at[slot], sems[1].at[slot], device)

    if (order == "ab") == (stage == 0):
        src = part.at[1 - a] if stage == 0 else first.at[0, 1 - a]
        dst = first.at[0] if stage == 0 else second.at[0]
        return [send(src, dst, nz + nb - 1, grid.device(1 - a, b, z, c))]
    found = []
    for k in range(1, nb):
        to = lax.rem(b + k, nb)
        src = part.at[:, to] if stage == 0 else first.at[0, to]
        dst = first.at[k - 1] if stage == 0 else second.at[k - 1]
        found.append(send(src, dst, nz + k - 1, grid.device(a, to, z, c)))
    return found


def fold_add(grid, place, order, stage, own, first, second):
    a, b, z, c = place
    nz = grid.nz
    if stage == 0:

        def step(i, carry):
            o, j = i // nz, lax.rem(i, nz)
            total = own[o, j].astype(F32)
            for k in range(first.shape[0]):
                total = total + first[k, o, j].astype(F32)
            first[0, o, j] = total.astype(BF16)
            return carry

        lax.fori_loop(0, first.shape[1] * nz, step, 0)
        return
    mine = b if order == "ab" else a

    def step(j, carry):
        total = first[0, mine, j].astype(F32)
        for k in range(second.shape[0]):
            total = total + second[k, j].astype(F32)
        second[0, j] = total.astype(BF16)
        return carry

    lax.fori_loop(0, nz, step, 0)


def fold_scratch(grid, order, rows, n):
    na, nb, nz = grid.na, grid.nb, grid.nz
    own = pltpu.VMEM((nb if order == "ab" else na, nz, rows, n), BF16)
    first = pltpu.VMEM((1, nb, nz, rows, n) if order == "ab" else (nb - 1, na, nz, rows, n), BF16)
    second = pltpu.VMEM((nb - 1, nz, rows, n) if order == "ab" else (1, nz, rows, n), BF16)
    return own, first, second


class Summing:
    def __init__(self, grid, mine, held, total, done, send_sem, recv_sem):
        self.n_seq, self.count = grid.n_seq, grid.n_dp * grid.n_seq
        self.mine, self.held, self.total, self.done = mine, held, total, done
        self.send_sem, self.recv_sem = send_sem, recv_sem
        self.rows = total.shape[0]
        self.me = lax.axis_index("dp") * grid.n_seq + lax.axis_index("seq")

    def device(self, k):
        other = lax.rem(self.me + k, self.count)
        return other, (other // self.n_seq, lax.rem(other, self.n_seq))

    def part(self, ref, k):
        return ref.at[pl.ds(pl.multiple_of(k * self.rows, self.rows), self.rows)]

    def greet(self):
        barrier = pltpu.get_barrier_semaphore()

        def step(k, carry):
            pl.semaphore_signal(barrier, inc=1, device_id=self.device(k)[1], device_id_type=MESH)
            return carry

        lax.fori_loop(1, self.count, step, 0)

    def settle(self, dst, slot):
        most = pl.ds(0, (self.count - 1) * self.rows)
        remote(self.mine.at[most], dst.at[most], self.send_sem.at[slot], self.recv_sem.at[slot], self.device(1)[1]).wait()

    def deal(self):
        def step(k, carry):
            other, place = self.device(k)
            remote(self.part(self.mine, other), self.part(self.held, self.me), self.send_sem.at[0], self.recv_sem.at[0], place).start()
            return carry

        lax.fori_loop(1, self.count, step, 0)
        at = pl.ds(pl.multiple_of(self.me * self.rows, self.rows), self.rows)
        self.held[at, :] = self.mine[at, :]

    def tell(self):
        self.settle(self.held, 0)

        def add(k, carry):
            return carry + self.held[pl.ds(pl.multiple_of(k * self.rows, self.rows), self.rows), :]

        self.total[...] = lax.fori_loop(0, self.count, add, jnp.zeros(self.total.shape, F32))

        def step(k, carry):
            place = self.device(k)[1]
            remote(self.total, self.part(self.done, self.me), self.send_sem.at[1], self.recv_sem.at[1], place).start()
            return carry

        lax.fori_loop(1, self.count, step, 0)
        self.done[pl.ds(pl.multiple_of(self.me * self.rows, self.rows), self.rows), :] = self.total[...]

    def close(self):
        self.settle(self.done, 1)


def blend(h_ref, coeffs, streams_ref):
    hist, block, width = h_ref.shape[0], h_ref.shape[2], h_ref.shape[3]
    spread = [jnp.broadcast_to(coeffs[:, k : k + 1], (block, 128)) for k in range(4 * hist)]
    for at in range(0, width, 128):
        lanes = slice(at, at + 128)
        inputs = [h_ref[j, 0, :, lanes].astype(F32) for j in range(hist)]
        for c in range(4):
            total = spread[c * hist] * inputs[0]
            for j in range(1, hist):
                total = total + spread[c * hist + j] * inputs[j]
            streams_ref[c, :, lanes] = total
    return spread


def mix_kernel(grid, rows, chunks, whole, partial, h_ref, g_ref, gain_ref, inner_ref, outer_ref, bias_ref, sgain_ref, sbias_ref, *refs):
    ins, (lowered_ref, gpair_ref, last_ref, pre_ref, coeffs_ref, cos_ref, above_ref, below_ref) = refs[:4], refs[4:12]
    weights_ref, outs = refs[12], refs[13:15]
    streams_ref, held_ref, local_sem, send_sem, recv_sem, pair_local, pair_send, pair_recv = refs[15:]
    i, steps = pl.program_id(0), pl.num_programs(0)
    a, b, z, c = place = grid.here()
    block = h_ref.shape[2]
    outs = [weights_ref.at[k] for k in range(4)] + list(outs)
    events = Gathering(grid, place, rows, chunks, ins, outs, local_sem, send_sem, recv_sem).events(whole, partial)
    other = grid.device(a, b, z, 1 - c)

    def pair(k, src, dst):
        return [
            pltpu.make_async_copy(src, dst, pair_local.at[k]),
            remote(src, dst, pair_send.at[k], pair_recv.at[k], other),
        ]

    grads = lambda: pair(0, g_ref.at[0], gpair_ref.at[c])
    lowereds = lambda: pair(1, held_ref, lowered_ref.at[:, c])

    @pl.when(i == 0)
    def _():
        grid.greet(*place)
        events[0]()
        start(grads())

    @pl.when(i == 1)
    def _():
        events[1]()

    @pl.when(i == 2)
    def _():
        both, wide = cos_ref.shape
        half = ROT_DIMS // 2
        place_in = lax.rem(lax.broadcasted_iota(jnp.int32, (1, wide), 1), HEAD_DIM)
        step = lax.rem(place_in, half)
        freq = jnp.ones((1, wide), F32)
        for k in range(1, half):
            freq = jnp.where(step == k, 10000.0 ** (-2.0 * k / ROT_DIMS), freq)
        angles = (z * both + lax.broadcasted_iota(jnp.int32, (both, wide), 0)).astype(F32) * freq
        turned = place_in < ROT_DIMS
        sine = jnp.where(turned, jnp.sin(angles), 0.0)
        cos_ref[...] = jnp.where(turned, jnp.cos(angles), 1.0)
        above_ref[...] = jnp.where(place_in < half, -sine, 0.0)
        below_ref[...] = jnp.where(place_in < half, 0.0, sine)

    last = h_ref[h_ref.shape[0] - 1, 0].astype(F32)
    r = lax.rsqrt(jnp.mean(last * last, axis=1, keepdims=True) + EPS)
    scaled_low = (last * r * gain_ref[...].astype(F32)).astype(BF16)
    pre = against(scaled_low, inner_ref[...])
    pre_ref[...] = pre
    coeffs = product((pre * phi(pre)).astype(BF16), outer_ref[...]) + bias_ref[...].astype(F32)
    coeffs_ref[...] = coeffs
    blend(h_ref, coeffs, streams_ref)
    at = pl.ds(pl.multiple_of(i * block, block), block)
    for k in range(4):
        stream = streams_ref[k]
        centered = stream - jnp.mean(stream, axis=1, keepdims=True)
        rs = lax.rsqrt(jnp.mean(centered * centered, axis=1, keepdims=True) + EPS)
        gain, bias = sgain_ref[k : k + 1, :].astype(F32), sbias_ref[k : k + 1, :].astype(F32)
        held_ref[k, at, :] = (centered * rs * gain + bias).astype(BF16)
    last_ref[...] = streams_ref[3]

    @pl.when(i == steps - 1)
    def _():
        start(lowereds())
        for event in events[2:]:
            event()
        finish(grads())
        finish(lowereds())


def mix_forward(grid, history, cotangent, params, weights, chunks, groups, partial, widths, collective_id):
    hist, _, tokens, width = history.shape
    mix = params[1].shape[0]
    block = 32
    rows = weights[0].shape[0]
    whole = pl.BlockSpec(memory_space=pltpu.VMEM)
    anywhere = pl.BlockSpec(memory_space=pl.ANY)
    part = lambda n: pl.BlockSpec((block, n), lambda i: (i, 0))
    chips = (grid.na, grid.nb, grid.nz, 2 * rows)
    results = pl.pallas_call(
        functools.partial(mix_kernel, grid, rows, chunks, groups, partial),
        grid=(tokens // block,),
        out_shape=[
            jax.ShapeDtypeStruct((4, 2, tokens, width), BF16),
            jax.ShapeDtypeStruct((2, tokens, width), BF16),
            jax.ShapeDtypeStruct((tokens, width), F32),
            jax.ShapeDtypeStruct((tokens, mix), F32),
            jax.ShapeDtypeStruct((tokens, mix), F32),
        ]
        + [jax.ShapeDtypeStruct((2 * tokens, 128), F32)] * 3
        + [jax.ShapeDtypeStruct((4, *chips, width // 2), BF16)]
        + [jax.ShapeDtypeStruct((*chips, w), BF16) for w in widths],
        in_specs=[pl.BlockSpec((hist, 1, block, width), lambda i: (0, 0, i, 0))] + [whole] * 11,
        out_specs=[anywhere, anywhere, part(width), part(mix), part(mix)]
        + [pl.BlockSpec((2 * tokens, 128), lambda i: (0, 0))] * 3
        + [anywhere] * 3,
        scratch_shapes=[
            pltpu.VMEM((4, block, width), F32),
            pltpu.VMEM((4, tokens, width), BF16),
            *gather_sems(grid, chunks),
            pltpu.SemaphoreType.DMA((2,)),
            pltpu.SemaphoreType.DMA((2,)),
            pltpu.SemaphoreType.DMA((2,)),
        ],
        compiler_params=pltpu.CompilerParams(collective_id=collective_id, has_side_effects=True, vmem_limit_bytes=VMEM_LIMIT),
        cost_estimate=pl.CostEstimate(flops=tokens * width * 80, bytes_accessed=history.size * 40, transcendentals=0),
        name="mix_forward",
    )(history, cotangent, *params, *weights)
    lowered, gpair, last, pre, coeffs = results[:5]
    return (
        lowered.reshape(4, 2 * tokens, width),
        gpair.reshape(2 * tokens, width),
        last,
        pre,
        coeffs,
        results[5:8],
        results[8].reshape(4, width, width // 2),
        results[9:],
    )


def small_rows(width, mix, hidden_width):
    wl, padded = width // 128, -(-mix // 8) * 8
    sizes = [wl, wl * padded, padded, 8, 4 * wl, 4 * wl, 3 * wl, wl, hidden_width // 128]
    firsts = [sum(sizes[:k]) for k in range(len(sizes))]
    return firsts, sum(sizes)


def unmix_kernel(h_ref, own_ref, theirs_ref, g_ref, pre_ref, coeffs_ref, gain_ref, inner_ref, outer_ref, sgain_ref,
                 hist_ref, sgg_ref, sbg_ref, gg_ref, ig_ref, og_ref, bg_ref, ob_ref,
                 streams_ref, sg_ref, scaled_ref, mpg_ref, hidden_ref, cgl_ref):
    i, steps = pl.program_id(0), pl.num_programs(0)
    hist, block, width = h_ref.shape[0], h_ref.shape[2], h_ref.shape[3]
    mix = 4 * hist

    @pl.when(i == 0)
    def _():
        for ref in (sgg_ref, sbg_ref, gg_ref, bg_ref, ob_ref):
            ref[...] = jnp.zeros_like(ref)

    def down(x):
        return jnp.sum(x, axis=0, keepdims=True)

    coeffs = coeffs_ref[...]
    spread = blend(h_ref, coeffs, streams_ref)
    grad = g_ref[0].astype(F32)
    ob_ref[...] += down(grad)
    for k in range(4):
        stream = streams_ref[k]
        centered = stream - jnp.mean(stream, axis=1, keepdims=True)
        rs = lax.rsqrt(jnp.mean(centered * centered, axis=1, keepdims=True) + EPS)
        n = centered * rs
        ng = own_ref[k] + theirs_ref[k].astype(F32)
        sgg_ref[k : k + 1, :] += down(ng * n)
        sbg_ref[k : k + 1, :] += down(ng)
        w = ng * sgain_ref[k : k + 1, :].astype(F32)
        pulled = rs * (w - jnp.mean(w, axis=1, keepdims=True) - n * jnp.mean(w * n, axis=1, keepdims=True))
        sg_ref[k] = pulled + grad if k == 3 else pulled

    lane = lax.broadcasted_iota(jnp.int32, (block, mix), 1)
    cg = jnp.zeros((block, mix), F32)
    for j in range(hist):
        value = h_ref[j, 0].astype(F32)
        for k in range(4):
            cg = jnp.where(lane == k * hist + j, jnp.sum(value * sg_ref[k], axis=1, keepdims=True), cg)
    bg_ref[...] += down(cg)
    cg_low = cg.astype(BF16)
    pre = pre_ref[...]
    at = pl.ds(pl.multiple_of(i * block, block), block)
    mpg = (against(cg_low, outer_ref[...]) * gelu_slope(pre)).astype(BF16)
    last = h_ref[hist - 1, 0].astype(F32)
    r = lax.rsqrt(jnp.mean(last * last, axis=1, keepdims=True) + EPS)
    gain = gain_ref[...].astype(F32)
    scaled_ref[at, :] = (last * r * gain).astype(BF16)
    mpg_ref[at, :] = mpg
    hidden_ref[at, :] = (pre * phi(pre)).astype(BF16)
    cgl_ref[at, :] = cg_low
    scaled_grad = product(mpg, inner_ref[...])
    gg_ref[...] += down(scaled_grad * last * r)
    w = scaled_grad * gain
    last_grad = r * (w - last * (r * r) * jnp.mean(w * last, axis=1, keepdims=True))
    for from_ in range(0, width, 128):
        lanes = slice(from_, from_ + 128)
        pulls = [sg_ref[k, :, lanes] for k in range(4)]
        for j in range(hist):
            total = spread[j] * pulls[0]
            for k in range(1, 4):
                total = total + spread[k * hist + j] * pulls[k]
            hist_ref[j, 0, :, lanes] = total + last_grad[:, lanes] if j == hist - 1 else total

    @pl.when(i == steps - 1)
    def _():
        ig_ref[...] = inner(mpg_ref[...], scaled_ref[...])
        og_ref[...] = inner(hidden_ref[...], cgl_ref[...])


def mix_backward(history, own, theirs, cotangent, pre, coeffs, params):
    hist, _, tokens, width = history.shape
    mix = pre.shape[1]
    block = 32
    whole = pl.BlockSpec(memory_space=pltpu.VMEM)
    part = lambda n: pl.BlockSpec((block, n), lambda i: (i, 0))
    four = pl.BlockSpec((4, block, width), lambda i: (0, i, 0))
    story = pl.BlockSpec((hist, 1, block, width), lambda i: (0, 0, i, 0))
    small = [(4, width), (4, width), (1, width), (mix, width), (mix, mix), (1, mix), (1, width)]
    return pl.pallas_call(
        unmix_kernel,
        grid=(tokens // block,),
        out_shape=[jax.ShapeDtypeStruct(history.shape, F32)] + [jax.ShapeDtypeStruct(shape, F32) for shape in small],
        in_specs=[story, four, four, pl.BlockSpec((1, block, width), lambda i: (0, i, 0)), part(mix), part(mix)] + [whole] * 4,
        out_specs=[story] + [pl.BlockSpec(shape, lambda i: (0, 0)) for shape in small],
        scratch_shapes=[
            pltpu.VMEM((4, block, width), F32),
            pltpu.VMEM((4, block, width), F32),
            pltpu.VMEM((tokens, width), BF16),
            pltpu.VMEM((tokens, mix), BF16),
            pltpu.VMEM((tokens, mix), BF16),
            pltpu.VMEM((tokens, mix), BF16),
        ],
        compiler_params=pltpu.CompilerParams(vmem_limit_bytes=VMEM_LIMIT),
        cost_estimate=pl.CostEstimate(flops=tokens * width * 1000, bytes_accessed=history.size * 12, transcendentals=0),
        name="mix_backward",
    )(history, own, theirs, cotangent, pre, coeffs, *params)


def finish_kernel(grid, orders, n_kept, *refs):
    nz = grid.nz
    kept, refs = refs[:n_kept], refs[n_kept:]
    came_a, came_b, refs = refs[:1], refs[1 : grid.nb], refs[grid.nb :]
    folded, refs = refs[:nz], refs[nz:]
    sgg_ref, sbg_ref, gg_ref, ig_ref, og_ref, bg_ref, ob_ref, hb_ref, eb_ref = refs[:9]
    done_ref, outs, refs = refs[9], refs[10:14], refs[14:]
    first, second, third, final, refs = refs[:4], refs[4:8], refs[8:12], refs[12:18], refs[18:]
    sums = Summing(grid, *refs[:3], done_ref, *refs[3:5])
    local_sem, send_sem, recv_sem = refs[5:]
    a, b, z, c = place = grid.here()
    width, mix = gg_ref.shape[1], bg_ref.shape[1]
    wl, padded, hidden_rows = width // 128, -(-mix // 8) * 8, eb_ref.shape[1] // 128
    firsts, _ = small_rows(width, mix, 2 * eb_ref.shape[1])
    half = width // 2
    spots = [(0, lambda core: core * half), (0, lambda core: width + core * half), (0, lambda core: 2 * width + core * half),
             (1, lambda core: core * half), (2, lambda core: core * eb_ref.shape[1]), (3, lambda core: core * eb_ref.shape[1])]

    def copies(t, stage):
        if stage == 1:
            return fold_copies(grid, place, orders[t], 1, None, first[t], second[t], (send_sem.at[t], recv_sem.at[t]))
        if stage == 2:
            return [
                remote(second[t].at[0, lax.rem(z + k, nz)], third[t].at[k - 1], send_sem.at[t, k], recv_sem.at[t, k],
                       grid.device(a, b, lax.rem(z + k, nz), c))
                for k in range(1, nz)
            ]
        result, base = spots[t]
        n = final[t].shape[-1]
        spot = outs[result].at[:, pl.ds(pl.multiple_of(base(c), 128), n)]
        return [
            remote(final[t].at[1 - c], spot, send_sem.at[t, 0], recv_sem.at[t, 0], grid.device(a, b, z, 1 - c)),
            pltpu.make_async_copy(final[t].at[c], spot, local_sem.at[t]),
        ]

    sums.greet()
    for t in range(4):

        def step(i, carry, t=t):
            o, j = i // nz, lax.rem(i, nz)
            total = kept[t][o, j].astype(F32)
            for piece in came_a if orders[t] == "ab" else came_b:
                total = total + piece[t // 2, o, j].astype(F32)
            first[t][0, o, j] = total.astype(BF16)
            return carry

        lax.fori_loop(0, first[t].shape[1] * nz, step, 0)
    pl.semaphore_wait(pltpu.get_barrier_semaphore(), sums.count - 1)
    for t in range(4):
        start(copies(t, 1))

    mine = sums.mine
    mine[...] = jnp.zeros_like(mine)
    for l in range(wl):
        lanes = slice(l * 128, (l + 1) * 128)
        mine[firsts[0] + l : firsts[0] + l + 1, :] = gg_ref[:, lanes]
        mine[firsts[1] + l * padded : firsts[1] + l * padded + mix, :] = ig_ref[:, lanes]
        mine[firsts[4] + 4 * l : firsts[4] + 4 * l + 4, :] = sgg_ref[:, lanes]
        mine[firsts[5] + 4 * l : firsts[5] + 4 * l + 4, :] = sbg_ref[:, lanes]
        mine[firsts[7] + l : firsts[7] + l + 1, :] = ob_ref[:, lanes]
    mine[firsts[2] : firsts[2] + mix, 0:mix] = og_ref[...]
    mine[firsts[3] : firsts[3] + 1, 0:mix] = bg_ref[...]
    for k in range(3):
        for l in range(wl // 2):
            mine[pl.ds(firsts[6] + k * wl + c * (wl // 2) + l, 1), :] = hb_ref[k : k + 1, l * 128 : (l + 1) * 128]
    for l in range(hidden_rows):
        mine[pl.ds(firsts[8] + c * hidden_rows + l, 1), :] = eb_ref[:, l * 128 : (l + 1) * 128]
    sums.deal()

    for t in range(2):
        total = folded[0][t].astype(F32)
        for piece in folded[1:]:
            total = total + piece[t].astype(F32)
        final[4 + t][...] = total.reshape(final[4 + t].shape)
        start(copies(4 + t, 3))
    for t in range(4):
        finish(copies(t, 1))
        fold_add(grid, place, orders[t], 1, None, first[t], second[t])
        start(copies(t, 2))
    sums.tell()
    for t in range(4):
        finish(copies(t, 2))
        total = second[t][0, z].astype(F32)
        for k in range(nz - 1):
            total = total + third[t][k].astype(F32)
        final[t][...] = total.reshape(final[t].shape)
        start(copies(t, 3))
    sums.close()
    for t in range(6):
        finish(copies(t, 3))


def finish_sums(grid, orders, kept, came, folded, smalls, collective_id):
    sgg, _, _, ig, og, bg, _, hb, eb = smalls
    mix, width = ig.shape
    hidden_width = 2 * eb.shape[1]
    nz = grid.nz
    rows, n = kept[0].shape[-2:]
    devices = grid.n_dp * grid.n_seq
    each = -(-small_rows(width, mix, hidden_width)[1] // (devices * 8)) * 8
    vmem = pl.BlockSpec(memory_space=pltpu.VMEM)
    owned = [3 * width, width, hidden_width, hidden_width]
    folds = [fold_scratch(grid, order, rows, n) for order in orders]
    operands = list(kept) + list(came) + list(folded) + list(smalls)
    return pl.pallas_call(
        functools.partial(finish_kernel, grid, orders, len(kept)),
        out_shape=[jax.ShapeDtypeStruct((devices * each, 128), F32)] + [jax.ShapeDtypeStruct((rows // 2, w), F32) for w in owned],
        in_specs=[vmem] * len(operands),
        out_specs=[vmem] + [pl.BlockSpec(memory_space=pl.ANY)] * len(owned),
        scratch_shapes=[f for _, f, _ in folds]
        + [s for _, _, s in folds]
        + [pltpu.VMEM((nz - 1, rows, n), BF16)] * 4
        + [pltpu.VMEM((2, rows // 2, n), F32)] * 4
        + [pltpu.VMEM((2, rows // 2, hidden_width // 2), F32)] * 2
        + [
            pltpu.VMEM((devices * each, 128), F32),
            pltpu.VMEM((devices * each, 128), F32),
            pltpu.VMEM((each, 128), F32),
            pltpu.SemaphoreType.DMA((2,)),
            pltpu.SemaphoreType.DMA((2,)),
            pltpu.SemaphoreType.DMA((6,)),
            pltpu.SemaphoreType.DMA((6, nz + grid.nb)),
            pltpu.SemaphoreType.DMA((6, nz + grid.nb)),
        ],
        compiler_params=pltpu.CompilerParams(collective_id=collective_id, has_side_effects=True, vmem_limit_bytes=VMEM_LIMIT),
        cost_estimate=pl.CostEstimate(flops=0, bytes_accessed=100 * width * width, transcendentals=0),
        name="finish_sums",
    )(*operands)


def hand_kernel(mix, hidden_width, done, out_ref, *refs):
    owned, placed_ref, small, outs = refs[:4], refs[4], refs[5:14], refs[14:]
    width = out_ref.shape[1]
    wl, padded, hidden_rows = width // 128, -(-mix // 8) * 8, hidden_width // 256
    firsts, _ = small_rows(width, mix, hidden_width)
    placed_ref[...] = out_ref[...]
    for src, dst in zip(owned, outs):
        dst[...] = src[...]
    for l in range(wl):
        lanes = slice(l * 128, (l + 1) * 128)
        small[0][:, lanes] = done[firsts[0] + l : firsts[0] + l + 1, :]
        small[1][:, lanes] = done[firsts[1] + l * padded : firsts[1] + l * padded + mix, :]
        small[4][:, lanes] = done[firsts[4] + 4 * l : firsts[4] + 4 * l + 4, :]
        small[5][:, lanes] = done[firsts[5] + 4 * l : firsts[5] + 4 * l + 4, :]
        small[7][:, lanes] = done[firsts[7] + l : firsts[7] + l + 1, :]
    small[2][...] = done[firsts[2] : firsts[2] + mix, 0:mix]
    small[3][...] = done[firsts[3] : firsts[3] + 1, 0:mix]
    for l in range(3 * wl):
        small[6][:, l * 128 : (l + 1) * 128] = done[firsts[6] + l : firsts[6] + l + 1, :]
    for l in range(2 * hidden_rows):
        small[8][:, l * 128 : (l + 1) * 128] = done[firsts[8] + l : firsts[8] + l + 1, :]


def hand_over(summed, layer_out, owned, mix, hidden_width):
    width = layer_out.shape[1]
    small = [(1, width), (mix, width), (mix, mix), (1, mix), (4, width), (4, width), (1, 3 * width), (1, width), (1, hidden_width)]
    vmem = pl.BlockSpec(memory_space=pltpu.VMEM)
    return pl.pallas_call(
        functools.partial(hand_kernel, mix, hidden_width),
        out_shape=[jax.ShapeDtypeStruct(layer_out.shape, BF16)]
        + [jax.ShapeDtypeStruct(shape, F32) for shape in small]
        + [jax.ShapeDtypeStruct(x.shape, F32) for x in owned],
        in_specs=[vmem] * 6,
        out_specs=[vmem] * 14,
        name="hand_over",
    )(summed, layer_out, *owned)


def project_kernel(width, low_ref, g_ref, w_ref, bias_ref, cos_ref, above_ref, below_ref, sent_ref):
    wide = w_ref.shape[2]
    reps = max(wide // 128, 1)
    tables = [jnp.concatenate([t[...]] * reps, axis=1) for t in (cos_ref, above_ref, below_ref)]
    q = rotate(product(low_ref[0], w_ref[0]) + bias_ref[0:1, :], tables, 1.0)
    k = rotate(product(low_ref[1], w_ref[1]) + bias_ref[1:2, :], tables, 1.0)
    v = product(low_ref[2], w_ref[2]) + bias_ref[2:3, :]
    g = product(g_ref[...], w_ref[3])
    for n, x in enumerate((q, k, v, g)):
        x = x.astype(BF16)
        for m in range(wide // width):
            sent_ref[m, :, n * width : (n + 1) * width] = x[:, m * width : (m + 1) * width]


def project(grid, lowered, grad_low, weights, biases, tables, own_width):
    both = lowered.shape[1]
    nz = grid.nz
    wide = 2 * own_width
    whole = pl.BlockSpec(memory_space=pltpu.VMEM)
    return pl.pallas_call(
        functools.partial(project_kernel, own_width),
        grid=(nz // 2,),
        out_shape=jax.ShapeDtypeStruct((nz, both, 4 * own_width), BF16),
        in_specs=[whole, whole]
        + [pl.BlockSpec((4, weights.shape[1], wide), lambda i: (0, 0, i)), pl.BlockSpec((3, wide), lambda i: (0, i))]
        + [whole] * 3,
        out_specs=pl.BlockSpec((2, both, 4 * own_width), lambda i: (i, 0, 0)),
        compiler_params=pltpu.CompilerParams(vmem_limit_bytes=VMEM_LIMIT),
        cost_estimate=pl.CostEstimate(flops=2 * both * weights.size, bytes_accessed=lowered.size * 4, transcendentals=0),
        name="project",
    )(lowered, grad_low, weights, biases, *tables)


def unproject_kernel(grid, width, orders, col_ref, low_ref, g_ref, w_ref, feed_ref, normed_ref, last_ref, bias_ref, cos_ref, above_ref,
                     below_ref, own_ref, theirs_ref, hb_ref, out_ref, *refs):
    na, nb, nz = grid.na, grid.nb, grid.nz
    kept, over_a, over_b, refs = refs[:4], refs[4], refs[5 : 4 + nb], refs[4 + nb :]
    grad_ref, sending_ref, partial_ref, mine_ref, arrived_ref, split_sem, send_sem, recv_sem = refs
    i = pl.program_id(0)
    a, b, z, c = grid.here()
    tokens = out_ref.shape[0]
    other = grid.device(a, b, z, 1 - c)
    own_rows = pl.ds(pl.multiple_of(c * tokens, tokens), tokens)
    their_rows = pl.ds(pl.multiple_of((1 - c) * tokens, tokens), tokens)

    def swap(k):
        return [remote(sending_ref.at[k], theirs_ref.at[k], send_sem.at[k], recv_sem.at[k], other)]

    def swap_out():
        return [remote(partial_ref, arrived_ref, send_sem.at[4], recv_sem.at[4], other)]

    def split(k):
        grad = grad_ref.at[k]
        if orders[k] == "ab":
            found = [(grad.at[a], kept[k]), (grad.at[1 - a], over_a.at[k // 2])]
        else:
            found = [(grad.at[:, b], kept[k])]
            found += [(grad.at[:, lax.rem(b + m, nb)], over_b[m - 1].at[k // 2]) for m in range(1, nb)]
        return [pltpu.make_async_copy(src, dst, split_sem.at[k, n]) for n, (src, dst) in enumerate(found)]

    def piece(n):
        return jnp.concatenate([col_ref[m, :, n * width : (n + 1) * width] for m in range(nz)], axis=1)

    def keep(k, grad):
        grad_ref[k] = grad.astype(BF16).reshape(grad_ref.shape[1:])
        start(split(k))

    @pl.when(i == 0)
    def _():
        barrier = pltpu.get_barrier_semaphore()
        pl.semaphore_signal(barrier, inc=1, device_id=other, device_id_type=MESH)
        mine_ref[...] = piece(0)
        partial_ref[...] = against(mine_ref[their_rows, :], w_ref[0]) + feed_ref[their_rows, :]
        sending_ref[3] = normed_ref[their_rows, :].astype(BF16)
        pl.semaphore_wait(barrier, 1)
        start(swap_out())
        start(swap(3))
        own_ref[0] = normed_ref[own_rows, :]
        out = against(mine_ref[own_rows, :], w_ref[0]) + feed_ref[own_rows, :] + last_ref[...] + bias_ref[...]
        keep(3, inner(g_ref[...], mine_ref[...]))
        finish(swap_out())
        out_ref[...] = (out + arrived_ref[...]).astype(BF16)

    for k in range(3):

        @pl.when(i == k + 1)
        def _(k=k):
            grad = piece(k + 1).astype(F32)
            if k < 2:
                tables = [jnp.concatenate([t[...]] * (grad.shape[1] // 128), axis=1) for t in (cos_ref, above_ref, below_ref)]
                grad = rotate(grad, tables, -1.0)
            hb_ref[k : k + 1, :] = jnp.sum(grad, axis=0, keepdims=True)
            mine_ref[...] = grad.astype(BF16)
            sending_ref[k] = against(mine_ref[their_rows, :], w_ref[0]).astype(BF16)
            start(swap(k))
            own_ref[0] = against(mine_ref[own_rows, :], w_ref[0])
            keep(k, inner(low_ref[0], mine_ref[...]))
            if k == 2:
                for n in range(4):
                    finish(swap(n))
                    finish(split(n))


def unproject(grid, orders, collected, lowered, grad_low, weights, feed_part, normed_feed, last_stream, bias, tables, own_width, collective_id):
    tokens, width = last_stream.shape
    both, half = 2 * tokens, width // 2
    na, nb, nz = grid.na, grid.nb, grid.nz
    rows = width // (na * nb * nz)
    whole = pl.BlockSpec(memory_space=pltpu.VMEM)
    anywhere = pl.BlockSpec(memory_space=pl.ANY)
    turn = lambda i: lax.rem(i + 3, 4)
    split_shapes = [jax.ShapeDtypeStruct((nb if order == "ab" else na, nz, rows, half), BF16) for order in orders]
    sent_shapes = [jax.ShapeDtypeStruct((2, nb, nz, rows, half), BF16)] + [jax.ShapeDtypeStruct((2, na, nz, rows, half), BF16)] * (nb - 1)
    results = pl.pallas_call(
        functools.partial(unproject_kernel, grid, own_width, orders),
        grid=(4,),
        out_shape=[
            jax.ShapeDtypeStruct((4, tokens, width), F32),
            jax.ShapeDtypeStruct((4, tokens, width), BF16),
            jax.ShapeDtypeStruct((3, half), F32),
            jax.ShapeDtypeStruct((tokens, width), BF16),
        ]
        + split_shapes
        + sent_shapes,
        in_specs=[
            whole,
            pl.BlockSpec((1, both, width), lambda i: (jnp.maximum(i - 1, 0), 0, 0)),
            whole,
            pl.BlockSpec((1, width, half), lambda i: (turn(i), 0, 0)),
        ]
        + [whole] * 7,
        out_specs=[
            pl.BlockSpec((1, tokens, width), lambda i: (turn(i), 0, 0)),
            anywhere,
            pl.BlockSpec((3, half), lambda i: (0, 0)),
            pl.BlockSpec((tokens, width), lambda i: (0, 0)),
        ]
        + [anywhere] * (len(split_shapes) + len(sent_shapes)),
        scratch_shapes=[
            pltpu.VMEM((4, na, nb, nz, rows, half), BF16),
            pltpu.VMEM((4, tokens, width), BF16),
            pltpu.VMEM((tokens, width), F32),
            pltpu.VMEM((both, half), BF16),
            pltpu.VMEM((tokens, width), F32),
            pltpu.SemaphoreType.DMA((4, nb + 1)),
            pltpu.SemaphoreType.DMA((5,)),
            pltpu.SemaphoreType.DMA((5,)),
        ],
        compiler_params=pltpu.CompilerParams(collective_id=collective_id, has_side_effects=True, vmem_limit_bytes=VMEM_LIMIT),
        cost_estimate=pl.CostEstimate(flops=32 * both * width * half, bytes_accessed=40 * both * width, transcendentals=0),
        name="unproject",
    )(collected, lowered, grad_low, weights, feed_part, normed_feed, last_stream, bias, *tables)
    own, theirs, head_bias, layer_out = results[:4]
    return own, theirs, head_bias, layer_out, results[4:8], results[8:]


def feed_kernel(grid, steps, low_ref, g_ref, we_ref, wc_ref, bias_ref, feed_ref, normed_ref, eb_ref, *refs):
    nz = grid.nz
    outs, refs = refs[:nz], refs[nz:]
    parts, refs = refs[: 2 * steps], refs[2 * steps :]
    first, second, refs = refs[: 2 * steps], refs[2 * steps : 4 * steps], refs[4 * steps :]
    send_sem, recv_sem, out_sem = refs
    i = pl.program_id(0)
    a, b, z, c = place = grid.here()
    orders = ["ab", "ba"] * steps

    def copies(t, stage):
        if stage < 2:
            return fold_copies(grid, place, orders[t], stage, parts[t], first[t], second[t], (send_sem.at[t], recv_sem.at[t]))
        n = parts[t].shape[-1]
        cols = pl.ds((t // 2) * n, n)
        return [
            pltpu.make_async_copy(second[t].at[0, lax.rem(z + k, nz)], outs[k].at[t % 2, :, cols], out_sem.at[t, k]) for k in range(nz)
        ]

    def begin(u):
        for t in (2 * u, 2 * u + 1):
            start(copies(t, 0))

    def end(u, stage):
        for t in (2 * u, 2 * u + 1):
            finish(copies(t, stage))
            if stage < 2:
                own = parts[t].at[a] if orders[t] == "ab" else parts[t].at[:, b]
                fold_add(grid, place, orders[t], stage, own, first[t], second[t])
                start(copies(t, stage + 1))

    def turn(u):
        if u < steps:
            end(u, 0)
        if 0 <= u - 1 < steps:
            end(u - 1, 1)

    @pl.when(i == 0)
    def _():
        grid.greet(*place)
        feed_ref[...] = jnp.zeros_like(feed_ref)
        normed_ref[...] = jnp.zeros_like(normed_ref)

    low, grad, expand, contract = low_ref[0], g_ref[...], we_ref[...], wc_ref[...]
    expanded = product(low, expand) + bias_ref[...]
    share = phi(expanded)
    hidden = (expanded * share).astype(BF16)
    slope = share + expanded * jnp.exp(-0.5 * expanded * expanded) * (1.0 / math.sqrt(2.0 * math.pi))
    feed_ref[...] += against(hidden, contract)
    hidden_grad = inner(grad, hidden).astype(BF16)
    pulled = product(grad, contract) * slope
    eb_ref[...] = jnp.sum(pulled, axis=0, keepdims=True)
    pulled_low = pulled.astype(BF16)
    normed_ref[...] += against(pulled_low, expand)
    expand_grad = inner(low, pulled_low).astype(BF16)
    for u in range(steps):

        @pl.when(i == u)
        def _(u=u):
            parts[2 * u][...] = expand_grad.reshape(parts[2 * u].shape)
            parts[2 * u + 1][...] = hidden_grad.reshape(parts[2 * u + 1].shape)
            begin(u)
            if u >= 2:
                turn(u - 2)
            if u == steps - 1:
                for v in range(max(steps - 2, 0), steps + 1):
                    turn(v)
                for v in range(steps):
                    end(v, 2)


def feed_forward(grid, lowered, grad_low, weight_e, weight_c, bias, steps, collective_id):
    both, width = grad_low.shape
    n = weight_e.shape[1] // steps
    na, nb, nz = grid.na, grid.nb, grid.nz
    rows = width // (na * nb * nz)
    whole = lambda *shape: pl.BlockSpec(shape, lambda i: (0,) * len(shape))
    cols = lambda m: pl.BlockSpec((m, n), lambda i: (0, i))
    orders = ["ab", "ba"] * steps
    folds = [fold_scratch(grid, order, rows, n) for order in orders]
    sem = pltpu.SemaphoreType.DMA((2 * steps, nz + nb))
    return pl.pallas_call(
        functools.partial(feed_kernel, grid, steps),
        grid=(steps,),
        out_shape=[
            jax.ShapeDtypeStruct((both, width), F32),
            jax.ShapeDtypeStruct((both, width), F32),
            jax.ShapeDtypeStruct((1, n * steps), F32),
        ]
        + [jax.ShapeDtypeStruct((2, rows, n * steps), BF16)] * nz,
        in_specs=[
            pl.BlockSpec((1, both, width), lambda i: (3, 0, 0)),
            whole(both, width),
            cols(width),
            cols(width),
            cols(1),
        ],
        out_specs=[
            whole(both, width),
            whole(both, width),
            cols(1),
        ]
        + [pl.BlockSpec(memory_space=pl.ANY)] * nz,
        scratch_shapes=[pltpu.VMEM((na, nb, nz, rows, n), BF16)] * (2 * steps)
        + [f for _, f, _ in folds]
        + [s for _, _, s in folds]
        + [sem, sem, pltpu.SemaphoreType.DMA((2 * steps, nz))],
        compiler_params=pltpu.CompilerParams(collective_id=collective_id, has_side_effects=True, vmem_limit_bytes=VMEM_LIMIT),
        cost_estimate=pl.CostEstimate(flops=12 * both * width * n * steps * 2, bytes_accessed=width * n * steps * 20, transcendentals=0),
        name="feed_forward",
    )(lowered, grad_low, weight_e, weight_c, bias)


def attention_kernel(width, heads, tile, step, edge, length, x_ref, qdoc_ref, out_ref, kdoc_ref,
                     s_ref, kt_ref, vt_ref, ot_ref, dqt_ref, dka_ref, dva_ref, top_ref):
    i = pl.program_id(0)
    tiles = length // tile
    scale = 1.0 / math.sqrt(HEAD_DIM)
    @pl.when(i == 0)
    def _():
        dka_ref[...] = jnp.zeros_like(dka_ref)
        dva_ref[...] = jnp.zeros_like(dva_ref)
        def turn(j, carry):
            at = pl.ds(pl.multiple_of(j * tile, tile), tile)
            kt_ref[:, at] = x_ref[at, width : 2 * width].T
            kdoc_ref[at, :] = jnp.broadcast_to(qdoc_ref[:, at], (128, tile)).T
            vt_ref[:, at] = x_ref[at, 2 * width : 3 * width].T
            return carry
        lax.fori_loop(0, tiles, turn, 0)
    rows = pl.ds(pl.multiple_of(i * tile, tile), tile)
    query = x_ref[rows, 0:width] * jnp.asarray(scale, BF16)
    grad = x_ref[rows, 3 * width : 4 * width]
    query_t, grad_t = query.T, grad.T
    lanes = lax.broadcasted_iota(jnp.int32, (tile, width), 1) // HEAD_DIM
    subs = lax.broadcasted_iota(jnp.int32, (width, tile), 0) // HEAD_DIM
    zero = jnp.zeros((), BF16)
    queries_t = [jnp.where(subs == h, query_t, zero) for h in range(heads)]
    grads_t = [jnp.where(subs == h, grad_t, zero) for h in range(heads)]
    all_queries = jnp.concatenate([jnp.where(lanes == h, query, zero) for h in range(heads)], axis=0)
    all_grads = jnp.concatenate([jnp.where(lanes == h, grad, zero) for h in range(heads)], axis=0)
    qdoc = qdoc_ref[:, rows]
    qpos = i * tile + lax.broadcasted_iota(jnp.int32, (step, tile), 1)
    head_edge = -(-edge // step)
    tail_edge = (length - edge) // tile
    per = tile // step
    count = (i + 1) * per
    ot_ref[...] = jnp.zeros_like(ot_ref)
    dqt_ref[...] = jnp.zeros_like(dqt_ref)
    top_ref[...] = jnp.full_like(top_ref, NEG)

    def fold(x, f):
        return f(x.reshape(step // 8, 8, tile), axis=0)

    def scores(j, carry):
        at = pl.ds(pl.multiple_of(j * step, step), step)
        checked = (j >= i * per) | (j < head_edge) | (i >= tail_edge)
        def run(mask):
            keys = x_ref[at, width : 2 * width]
            if mask:
                kdoc = jnp.concatenate([kdoc_ref[at, :]] * (tile // 128), axis=1)
                kpos = j * step + lax.broadcasted_iota(jnp.int32, (step, tile), 0)
                allowed = (kdoc == qdoc) & (kpos <= qpos)
            for h in range(heads):
                s = product(keys, queries_t[h])
                if mask:
                    s = jnp.where(allowed, s, NEG)
                s_ref[h, at, :] = s
                top_ref[h] = jnp.maximum(top_ref[h], fold(s, jnp.max))
        pl.when(checked)(lambda: run(True))
        pl.when(jnp.logical_not(checked))(lambda: run(False))
        return carry
    lax.fori_loop(0, count, scores, 0)
    tops = [jnp.max(top_ref[h], axis=0, keepdims=True) for h in range(heads)]

    def weigh(j, totals):
        at = pl.ds(pl.multiple_of(j * step, step), step)
        new = []
        for h in range(heads):
            own = slice(h * HEAD_DIM, (h + 1) * HEAD_DIM)
            weights = jnp.exp(s_ref[h, at, :] - tops[h])
            s_ref[h, at, :] = weights
            new.append(totals[h] + fold(weights, jnp.sum))
            ot_ref[own, :] += product(vt_ref[own, at], weights.astype(BF16))
        return new
    totals = lax.fori_loop(0, count, weigh, [jnp.zeros((8, tile), F32)] * heads)
    inverse = [1.0 / jnp.sum(t, axis=0, keepdims=True) for t in totals]
    grad_f = grad_t.astype(F32)
    deltas = []
    for h in range(heads):
        own = slice(h * HEAD_DIM, (h + 1) * HEAD_DIM)
        value = ot_ref[own, :] * inverse[h]
        ot_ref[own, :] = value
        deltas.append(jnp.sum(value * grad_f[own], axis=0, keepdims=True))
    out_ref[rows, 0:width] = ot_ref[...].T.astype(BF16)

    def back(j, carry):
        at = pl.ds(pl.multiple_of(j * step, step), step)
        values = x_ref[at, 2 * width : 3 * width]
        probs_low, grads_low = [], []
        for h in range(heads):
            own = slice(h * HEAD_DIM, (h + 1) * HEAD_DIM)
            probs_grad = product(values, grads_t[h])
            probs = s_ref[h, at, :] * inverse[h]
            scores_grad = (probs * (probs_grad - deltas[h])).astype(BF16)
            probs_low.append(probs.astype(BF16))
            grads_low.append(scores_grad)
            dqt_ref[own, :] += product(kt_ref[own, at], scores_grad)
        dva_ref[at, :] += product(jnp.concatenate(probs_low, axis=1), all_grads)
        dka_ref[at, :] += product(jnp.concatenate(grads_low, axis=1), all_queries)
        return carry
    lax.fori_loop(0, count, back, 0)
    out_ref[rows, width : 2 * width] = (dqt_ref[...].T * scale).astype(BF16)

    @pl.when(i == tiles - 1)
    def _():
        out_ref[:, 2 * width : 3 * width] = dka_ref[...].astype(BF16)
        out_ref[:, 3 * width : 4 * width] = dva_ref[...].astype(BF16)


def attention(dealt, documents, heads, edge):
    length = dealt.shape[0]
    width = heads * HEAD_DIM
    tile = step = 2 * edge
    pairs = length * length // 2 * heads
    whole = lambda i: (0, 0)
    return pl.pallas_call(
        functools.partial(attention_kernel, width, heads, tile, step, edge, length),
        grid=(length // tile,),
        out_shape=jax.ShapeDtypeStruct((length, 4 * width), BF16),
        in_specs=[pl.BlockSpec((length, 4 * width), whole), pl.BlockSpec((1, length), whole)],
        out_specs=pl.BlockSpec((length, 4 * width), whole),
        scratch_shapes=[
            pltpu.VMEM((length, 128), F32), pltpu.VMEM((heads, length, tile), F32), pltpu.VMEM((width, length), BF16), pltpu.VMEM((width, length), BF16),
            pltpu.VMEM((width, tile), F32), pltpu.VMEM((width, tile), F32), pltpu.VMEM((length, width), F32), pltpu.VMEM((length, width), F32),
            pltpu.VMEM((heads, 8, tile), F32)],
        compiler_params=pltpu.CompilerParams(vmem_limit_bytes=VMEM_LIMIT),
        cost_estimate=pl.CostEstimate(flops=pairs * 64 * 2 * 6 * 4, bytes_accessed=length * width * 20, transcendentals=pairs),
        name="attention",
    )(dealt, documents)


def on_device(
    grid,
    history,
    documents,
    cotangent,
    mixer_gain,
    mixer_inner,
    mixer_outer,
    mixer_bias,
    stream_gain,
    stream_bias,
    inbound_weight,
    inbound_bias,
    outbound_weight,
    outbound_bias,
    expand,
    expand_bias,
    contract,
    contract_bias,
):
    n_dp, n_seq, nz = grid.n_dp, grid.n_seq, grid.nz
    tokens, width = history.shape[2], history.shape[3]
    hidden_width = expand.shape[1]
    half, hidden_half = width // 2, hidden_width // 2
    both = 2 * tokens
    length = documents.shape[1]
    mix = mixer_bias.shape[0]
    heads = HEADS // n_seq
    own_width = heads * HEAD_DIM
    seq = lax.axis_index("seq")
    z, c = seq // 2, lax.rem(seq, 2)

    def take(array, start, size, axis=0):
        return lax.dynamic_slice_in_dim(array, start, size, axis)

    pick = lambda base, n: (lambda core: base + core * n)
    parts = 4
    piece = hidden_half // parts
    feed = []
    for part in range(parts):
        base = lambda core, part=part: core * hidden_half + part * piece
        feed.append((2, base, 4, part * piece, piece, "ba"))
        feed.append((3, base, 5, part * piece, piece, "ab"))
    pairs = [[2 * part, 2 * part + 1] for part in range(parts)]
    inner_t = mixer_inner.T
    lowered, grad_low, last_stream, mix_pre, coeffs, tables, weights, started = mix_forward(
        grid,
        history,
        cotangent,
        [mixer_gain[None], inner_t, mixer_outer, mixer_bias[None], stream_gain, stream_bias],
        [inbound_weight, outbound_weight, expand, contract],
        [
            (0, pick(width, half), 1, 0, half, "ba"),
            (0, pick(2 * width, half), 2, 0, half, "ab"),
            (0, pick(0, half), 0, 0, half, "ba"),
            (1, pick(0, half), 3, 0, half, "ab"),
        ]
        + feed,
        [[0, 1], [2, 3]],
        [[4 + n for n in pair] for pair in pairs],
        [hidden_half] * 2,
        1,
    )

    bias_in = take(inbound_bias.astype(F32).reshape(3, width), c * half, half, 1)
    sent = project(grid, lowered, grad_low, weights, bias_in, tables, own_width)
    groups = [[2 * k + core for k in range(nz)] for core in range(2)]
    dealt = lax.all_to_all(sent, "seq", 0, 0, axis_index_groups=groups, tiled=True)

    started_e, started_c, _ = lax.optimization_barrier((*started, sent[0, 0]))
    chunks = [(0, None, n - 4, col, size, order) for _, _, n, col, size, order in feed]
    weight_e, weight_c = gather(grid, [started_e, started_c], chunks, pairs, 2, "gather_feed")
    dealt, weight_e, weight_c = lax.optimization_barrier((dealt, weight_e, weight_c))

    returned = attention(dealt.reshape(length, 4 * own_width), documents.astype(F32), heads, tokens)
    returned = returned.reshape(nz, both, 4 * own_width)
    collected = lax.all_to_all(returned, "seq", 0, 0, axis_index_groups=groups, tiled=True)

    bias_e = take(expand_bias.astype(F32), c * hidden_half, hidden_half)[None]
    lowered_seen, _ = lax.optimization_barrier((lowered, returned[0, 0]))
    feed_part, normed_feed, expand_bias_part, *folded = feed_forward(
        grid, lowered_seen, grad_low, weight_e, weight_c, bias_e, parts, 3
    )

    def along_z(k):
        return [(s, (s // 2 + k) % nz * 2 + s % 2) for s in range(n_seq)]

    folded = [folded[0]] + [lax.ppermute(folded[k], "seq", along_z(k)) for k in range(1, nz)]

    orders = ("ab", "ba", "ab", "ba")
    bias_out = (outbound_bias.astype(F32) + contract_bias.astype(F32))[None]
    normed_own, normed_theirs, head_bias_part, layer_out, kept, leaving = unproject(
        grid, orders, collected, lowered, grad_low, weights, feed_part, normed_feed, last_stream, bias_out, tables, own_width, 4
    )
    nb = grid.nb
    over_a = [(d, (d + nb) % n_dp) for d in range(n_dp)]
    over_b = [[(d, d // nb * nb + (d + k) % nb) for d in range(n_dp)] for k in range(1, nb)]
    came_a = lax.ppermute(leaving[0], "dp", over_a)
    came_b = [lax.ppermute(x, "dp", perm) for x, perm in zip(leaving[1:], over_b)]

    history_grad, *small = mix_backward(
        history, normed_own, normed_theirs, cotangent, mix_pre, coeffs, [mixer_gain[None], inner_t, mixer_outer, stream_gain]
    )
    smalls = [*small, head_bias_part, expand_bias_part]
    summed, *owned = finish_sums(grid, orders, kept, [came_a, *came_b], folded, smalls, 5)
    layer_out, *small, inbound_grad, outbound_grad, expand_grad, contract_grad = hand_over(summed, layer_out, owned, mix, hidden_width)
    gain_grad, inner_grad, outer_grad, bias_grad, stream_gain_grad, stream_bias_grad, in_bias_grad, out_bias_grad, expand_bias_grad = small
    return (
        layer_out[None],
        history_grad,
        gain_grad.reshape(width),
        inner_grad.T,
        outer_grad,
        bias_grad.reshape(-1),
        stream_gain_grad,
        stream_bias_grad,
        inbound_grad,
        in_bias_grad.reshape(3 * width),
        outbound_grad,
        out_bias_grad.reshape(width),
        expand_grad,
        expand_bias_grad.reshape(hidden_width),
        contract_grad,
        out_bias_grad.reshape(width),
    )


def solution(mesh):
    rows = P(("dp", "seq"), None)
    placed = (
        P(None, "dp", "seq", None),
        P("dp", None),
        P("dp", "seq", None),
        P(),
        P(),
        P(),
        P(),
        P(),
        P(),
        rows,
        P(),
        rows,
        P(),
        rows,
        P(),
        rows,
        P(),
    )
    grid = Grid(mesh.shape["dp"], mesh.shape["seq"])
    return jax.shard_map(
        functools.partial(on_device, grid),
        mesh=mesh,
        in_specs=placed,
        out_specs=(
            P("dp", "seq", None),
            P(None, "dp", "seq", None),
            P(),
            P(),
            P(),
            P(),
            P(),
            P(),
            rows,
            P(),
            rows,
            P(),
            rows,
            P(),
            rows,
            P(),
        ),
        check_vma=False,
    )
```

```python
import functools
import math

import jax
import jax.numpy as jnp
from jax import lax
from jax.experimental import pallas as pl
from jax.experimental.pallas import tpu as pltpu
from jax.sharding import PartitionSpec as P

HEADS = 16
HEAD_DIM = 64
ROT_DIMS = 16
EPS = 1e-05
HIGHEST = lax.Precision.HIGHEST
NEG = -1e30
MESH = pl.DeviceIdType.MESH
F32 = jnp.float32
BF16 = jnp.bfloat16
VMEM_LIMIT = 56 * 1024 * 1024


def inner(left, right):
    return lax.dot_general(left, right, (((0,), (0,)), ((), ())), preferred_element_type=F32)


def against(left, right):
    return lax.dot_general(left, right, (((1,), (1,)), ((), ())), preferred_element_type=F32)


def product(left, right):
    return jnp.dot(left, right, preferred_element_type=F32)


def exact_gelu(value):
    return jax.nn.gelu(value, approximate=False)


def phi(value):
    return 0.5 * (1.0 + lax.erf(value * (1.0 / math.sqrt(2.0))))


def gelu_slope(value):
    return phi(value) + value * jnp.exp(-0.5 * value * value) * (1.0 / math.sqrt(2.0 * math.pi))


def rotate(value, tables, sign):
    half = ROT_DIMS // 2
    cosine, above, below = tables
    width = value.shape[-1]
    up = pltpu.roll(value, width - half, 1)
    down = pltpu.roll(value, half, 1)
    return value * cosine + sign * (up * above + down * below)


class Grid:
    def __init__(self, n_dp, n_seq):
        self.n_dp, self.n_seq = n_dp, n_seq
        self.na, self.nb, self.nz = 2, n_dp // 2, n_seq // 2

    def here(self):
        dp, seq = lax.axis_index("dp"), lax.axis_index("seq")
        return dp // self.nb, lax.rem(dp, self.nb), seq // 2, lax.rem(seq, 2)

    def device(self, a, b, z, c):
        return (a * self.nb + b, z * 2 + c)

    def peers(self, a, b, z, c):
        found = [self.device(a, b, z, 1 - c), self.device(1 - a, b, z, c)]
        found += [self.device(a, lax.rem(b + k, self.nb), z, c) for k in range(1, self.nb)]
        found += [self.device(a, b, lax.rem(z + k, self.nz), c) for k in range(1, self.nz)]
        return found

    def greet(self, a, b, z, c):
        barrier = pltpu.get_barrier_semaphore()
        found = self.peers(a, b, z, c)
        for peer in found:
            pl.semaphore_signal(barrier, inc=1, device_id=peer, device_id_type=MESH)
        pl.semaphore_wait(barrier, len(found))


def remote(src, dst, send, recv, device):
    return pltpu.make_async_remote_copy(
        src_ref=src, dst_ref=dst, send_sem=send, recv_sem=recv, device_id=device, device_id_type=MESH
    )


def remote(src, dst, send, recv, device):
    return pltpu.make_async_remote_copy(
        src_ref=src, dst_ref=dst, send_sem=send, recv_sem=recv, device_id=device, device_id_type=MESH
    )


def start(copies):
    for copy in copies:
        copy.start()


def finish(copies):
    for copy in copies:
        copy.wait()


class Gathering:
    def __init__(self, grid, place, rows, chunks, ins, outs, local_sem, send_sem, recv_sem):
        self.grid, self.place, self.rows, self.chunks = grid, place, rows, chunks
        self.ins, self.outs = ins, outs
        self.local_sem, self.send_sem, self.recv_sem = local_sem, send_sem, recv_sem

    def copies(self, t, stage):
        a, b, z, c = self.place
        grid, rows = self.grid, self.rows
        nz, nb = grid.nz, grid.nb
        source, base, result, col, n, order = self.chunks[t]
        out, cols = self.outs[result], pl.ds(col, n)

        def send(src, dst, slot, device):
            return remote(src, dst, self.send_sem.at[t, slot], self.recv_sem.at[t, slot], device)

        if stage == 0:
            mine = self.ins[source].at[:, pl.ds(pl.multiple_of(base(c), 128), n)]
            theirs = self.ins[source].at[:, pl.ds(pl.multiple_of(base(1 - c), 128), n)]
            spot = out.at[a, b, z, pl.ds(pl.multiple_of(c * rows, rows), rows), cols]
            return [pltpu.make_async_copy(mine, spot, self.local_sem.at[t]), send(theirs, spot, 0, grid.device(a, b, z, 1 - c))]
        if order[stage - 2] == "b":
            block = out.at[a, b, :, :, cols] if stage == 2 else out.at[:, b, :, :, cols]
            return [send(block, block, k, grid.device(a, lax.rem(b + k, nb), z, c)) for k in range(1, nb)]
        block = out.at[a, b, :, :, cols] if stage == 2 else out.at[a, :, :, :, cols]
        return [send(block, block, nb, grid.device(1 - a, b, z, c))]

    def hop(self, t, step, begin):
        a, b, z, c = self.place
        nz, nb = self.grid.nz, self.grid.nb
        _, _, result, col, n, _ = self.chunks[t]
        out, cols = self.outs[result], pl.ds(col, n)
        for side, way in enumerate((1, -1)):
            slot = nb + 1 + side * (nz - 1) + step - 1
            there, arriving = z + way, z - way * step
            going = there - way * step
            inside = (there >= 0) & (there < nz) & (going >= 0) & (going < nz)
            coming = (arriving >= 0) & (arriving < nz)

            def link(which, slot=slot, there=there):
                block = out.at[a, b, which, :, cols]
                return remote(block, block, self.send_sem.at[t, slot], self.recv_sem.at[t, slot], self.grid.device(a, b, there, c))

            if begin:
                pl.when(inside)(lambda link=link, going=going: link(going).start())
            else:
                pl.when(inside)(lambda link=link, going=going: link(going).wait_send())
                pl.when(coming)(lambda link=link, arriving=arriving: link(arriving).wait_recv())

    def begin(self, group, stage):
        for t in group:
            start(self.copies(t, stage))

    def end(self, group, stage):
        for t in group:
            finish(self.copies(t, stage))

    def ticks(self, whole, partial):
        groups, nz = whole + partial, self.grid.nz

        def advance(u, at):
            group = groups[u]
            if at == 0:
                self.end(group, 0)
            elif at < nz:
                for t in group:
                    self.hop(t, at, False)
            else:
                self.end(group, 2)
            for t in group:
                if at < nz - 1:
                    self.hop(t, at + 1, True)
                elif u < len(whole):
                    start(self.copies(t, 2 if at == nz - 1 else 3))

        def first():
            for group in groups:
                self.begin(group, 0)

        def tick(now):
            for u in range(len(groups)):
                if 0 <= now - u <= (nz if u < len(whole) else nz - 1):
                    advance(u, now - u)

        def last():
            for group in whole:
                self.end(group, 3)

        return [first] + [functools.partial(tick, now) for now in range(len(groups) + nz)] + [last]


def gather_sems(grid, chunks):
    slots = 2 * grid.nz + grid.nb - 1
    return [
        pltpu.SemaphoreType.DMA((len(chunks),)),
        pltpu.SemaphoreType.DMA((len(chunks), slots)),
        pltpu.SemaphoreType.DMA((len(chunks), slots)),
    ]


def fold_copies(grid, place, order, stage, part, first, second, sems):
    a, b, z, c = place
    nz, nb = grid.nz, grid.nb

    def send(src, dst, slot, device):
        return remote(src, dst, sems[0].at[slot], sems[1].at[slot], device)

    if (order == "ab") == (stage == 0):
        src = part.at[1 - a] if stage == 0 else first.at[0, 1 - a]
        dst = first.at[0] if stage == 0 else second.at[0]
        return [send(src, dst, nz + nb - 1, grid.device(1 - a, b, z, c))]
    found = []
    for k in range(1, nb):
        to = lax.rem(b + k, nb)
        src = part.at[:, to] if stage == 0 else first.at[0, to]
        dst = first.at[k - 1] if stage == 0 else second.at[k - 1]
        found.append(send(src, dst, nz + k - 1, grid.device(a, to, z, c)))
    return found


def fold_add(grid, place, order, stage, own, first, second):
    a, b, z, c = place
    nz = grid.nz
    if stage == 0:

        def step(i, carry):
            o, j = i // nz, lax.rem(i, nz)
            total = own[o, j].astype(F32)
            for k in range(first.shape[0]):
                total = total + first[k, o, j].astype(F32)
            first[0, o, j] = total.astype(BF16)
            return carry

        lax.fori_loop(0, first.shape[1] * nz, step, 0)
        return
    mine = b if order == "ab" else a

    def step(j, carry):
        total = first[0, mine, j].astype(F32)
        for k in range(second.shape[0]):
            total = total + second[k, j].astype(F32)
        second[0, j] = total.astype(BF16)
        return carry

    lax.fori_loop(0, nz, step, 0)


def fold_scratch(grid, order, rows, n):
    na, nb, nz = grid.na, grid.nb, grid.nz
    own = pltpu.VMEM((nb if order == "ab" else na, nz, rows, n), BF16)
    first = pltpu.VMEM((1, nb, nz, rows, n) if order == "ab" else (nb - 1, na, nz, rows, n), BF16)
    second = pltpu.VMEM((nb - 1, nz, rows, n) if order == "ab" else (1, nz, rows, n), BF16)
    return own, first, second


class Summing:
    def __init__(self, grid, mine, held, total, done, send_sem, recv_sem):
        self.n_seq, self.count = grid.n_seq, grid.n_dp * grid.n_seq
        self.mine, self.held, self.total, self.done = mine, held, total, done
        self.send_sem, self.recv_sem = send_sem, recv_sem
        self.rows = total.shape[0]
        self.me = lax.axis_index("dp") * grid.n_seq + lax.axis_index("seq")

    def device(self, k):
        other = lax.rem(self.me + k, self.count)
        return other, (other // self.n_seq, lax.rem(other, self.n_seq))

    def part(self, ref, k):
        return ref.at[pl.ds(pl.multiple_of(k * self.rows, self.rows), self.rows)]

    def greet(self):
        barrier = pltpu.get_barrier_semaphore()

        def step(k, carry):
            pl.semaphore_signal(barrier, inc=1, device_id=self.device(k)[1], device_id_type=MESH)
            return carry

        lax.fori_loop(1, self.count, step, 0)

    def settle(self, dst, slot):
        most = pl.ds(0, (self.count - 1) * self.rows)
        remote(self.mine.at[most], dst.at[most], self.send_sem.at[slot], self.recv_sem.at[slot], self.device(1)[1]).wait()

    def deal(self):
        def step(k, carry):
            other, place = self.device(k)
            remote(self.part(self.mine, other), self.part(self.held, self.me), self.send_sem.at[0], self.recv_sem.at[0], place).start()
            return carry

        lax.fori_loop(1, self.count, step, 0)
        at = pl.ds(pl.multiple_of(self.me * self.rows, self.rows), self.rows)
        self.held[at, :] = self.mine[at, :]

    def tell(self):
        self.settle(self.held, 0)

        def add(k, carry):
            return carry + self.held[pl.ds(pl.multiple_of(k * self.rows, self.rows), self.rows), :]

        self.total[...] = lax.fori_loop(0, self.count, add, jnp.zeros(self.total.shape, F32))

        def step(k, carry):
            place = self.device(k)[1]
            remote(self.total, self.part(self.done, self.me), self.send_sem.at[1], self.recv_sem.at[1], place).start()
            return carry

        lax.fori_loop(1, self.count, step, 0)
        self.done[pl.ds(pl.multiple_of(self.me * self.rows, self.rows), self.rows), :] = self.total[...]

    def close(self):
        self.settle(self.done, 1)


def blend(h_ref, coeffs, streams_ref):
    hist, block, width = h_ref.shape[0], h_ref.shape[2], h_ref.shape[3]
    spread = [jnp.broadcast_to(coeffs[:, k : k + 1], (block, 128)) for k in range(4 * hist)]
    for at in range(0, width, 128):
        lanes = slice(at, at + 128)
        inputs = [h_ref[j, 0, :, lanes].astype(F32) for j in range(hist)]
        for c in range(4):
            total = spread[c * hist] * inputs[0]
            for j in range(1, hist):
                total = total + spread[c * hist + j] * inputs[j]
            streams_ref[c, :, lanes] = total
    return spread


def mix_kernel(grid, rows, chunks, whole, partial, h_ref, g_ref, gain_ref, inner_ref, outer_ref, bias_ref, sgain_ref, sbias_ref, *refs):
    ins, (lowered_ref, gpair_ref, last_ref, pre_ref, coeffs_ref, cos_ref, above_ref, below_ref) = refs[:4], refs[4:12]
    weights_ref, outs = refs[12], refs[13:15]
    streams_ref, held_ref, local_sem, send_sem, recv_sem, pair_local, pair_send, pair_recv = refs[15:]
    i, steps = pl.program_id(0), pl.num_programs(0)
    a, b, z, c = place = grid.here()
    block = h_ref.shape[2]
    outs = [weights_ref.at[k] for k in range(4)] + list(outs)
    events = Gathering(grid, place, rows, chunks, ins, outs, local_sem, send_sem, recv_sem).ticks(whole, partial)
    other = grid.device(a, b, z, 1 - c)

    def pair(k, src, dst):
        return [
            pltpu.make_async_copy(src, dst, pair_local.at[k]),
            remote(src, dst, pair_send.at[k], pair_recv.at[k], other),
        ]

    grads = lambda: pair(0, g_ref.at[0], gpair_ref.at[c])
    lowereds = lambda: pair(1, held_ref, lowered_ref.at[:, c])

    @pl.when(i == 0)
    def _():
        grid.greet(*place)
        events[0]()
        start(grads())

    for n, at in enumerate((0, 2, 3, 4)):

        @pl.when(i == at)
        def _(n=n):
            events[n + 1]()

    @pl.when(i == 2)
    def _():
        both, wide = cos_ref.shape
        half = ROT_DIMS // 2
        place_in = lax.rem(lax.broadcasted_iota(jnp.int32, (1, wide), 1), HEAD_DIM)
        step = lax.rem(place_in, half)
        freq = jnp.ones((1, wide), F32)
        for k in range(1, half):
            freq = jnp.where(step == k, 10000.0 ** (-2.0 * k / ROT_DIMS), freq)
        angles = (z * both + lax.broadcasted_iota(jnp.int32, (both, wide), 0)).astype(F32) * freq
        turned = place_in < ROT_DIMS
        sine = jnp.where(turned, jnp.sin(angles), 0.0)
        cos_ref[...] = jnp.where(turned, jnp.cos(angles), 1.0)
        above_ref[...] = jnp.where(place_in < half, -sine, 0.0)
        below_ref[...] = jnp.where(place_in < half, 0.0, sine)

    last = h_ref[h_ref.shape[0] - 1, 0].astype(F32)
    r = lax.rsqrt(jnp.mean(last * last, axis=1, keepdims=True) + EPS)
    scaled_low = (last * r * gain_ref[...].astype(F32)).astype(BF16)
    pre = against(scaled_low, inner_ref[...])
    pre_ref[...] = pre
    coeffs = product((pre * phi(pre)).astype(BF16), outer_ref[...]) + bias_ref[...].astype(F32)
    coeffs_ref[...] = coeffs
    blend(h_ref, coeffs, streams_ref)
    at = pl.ds(pl.multiple_of(i * block, block), block)
    for k in range(4):
        stream = streams_ref[k]
        centered = stream - jnp.mean(stream, axis=1, keepdims=True)
        rs = lax.rsqrt(jnp.mean(centered * centered, axis=1, keepdims=True) + EPS)
        gain, bias = sgain_ref[k : k + 1, :].astype(F32), sbias_ref[k : k + 1, :].astype(F32)
        held_ref[k, at, :] = (centered * rs * gain + bias).astype(BF16)
    last_ref[...] = streams_ref[3]

    @pl.when(i == steps - 1)
    def _():
        start(lowereds())
        for event in events[5:]:
            event()
        finish(grads())
        finish(lowereds())


def mix_forward(grid, history, cotangent, params, weights, chunks, groups, partial, widths, collective_id):
    hist, _, tokens, width = history.shape
    mix = params[1].shape[0]
    block = 64
    rows = weights[0].shape[0]
    whole = pl.BlockSpec(memory_space=pltpu.VMEM)
    anywhere = pl.BlockSpec(memory_space=pl.ANY)
    part = lambda n: pl.BlockSpec((block, n), lambda i: (i, 0))
    chips = (grid.na, grid.nb, grid.nz, 2 * rows)
    results = pl.pallas_call(
        functools.partial(mix_kernel, grid, rows, chunks, groups, partial),
        grid=(tokens // block,),
        out_shape=[
            jax.ShapeDtypeStruct((4, 2, tokens, width), BF16),
            jax.ShapeDtypeStruct((2, tokens, width), BF16),
            jax.ShapeDtypeStruct((tokens, width), F32),
            jax.ShapeDtypeStruct((tokens, mix), F32),
            jax.ShapeDtypeStruct((tokens, mix), F32),
        ]
        + [jax.ShapeDtypeStruct((2 * tokens, 128), F32)] * 3
        + [jax.ShapeDtypeStruct((4, *chips, width // 2), BF16)]
        + [jax.ShapeDtypeStruct((*chips, w), BF16) for w in widths],
        in_specs=[pl.BlockSpec((hist, 1, block, width), lambda i: (0, 0, i, 0))] + [whole] * 11,
        out_specs=[anywhere, anywhere, part(width), part(mix), part(mix)]
        + [pl.BlockSpec((2 * tokens, 128), lambda i: (0, 0))] * 3
        + [anywhere] * 3,
        scratch_shapes=[
            pltpu.VMEM((4, block, width), F32),
            pltpu.VMEM((4, tokens, width), BF16),
            *gather_sems(grid, chunks),
            pltpu.SemaphoreType.DMA((2,)),
            pltpu.SemaphoreType.DMA((2,)),
            pltpu.SemaphoreType.DMA((2,)),
        ],
        compiler_params=pltpu.CompilerParams(collective_id=collective_id, has_side_effects=True, vmem_limit_bytes=VMEM_LIMIT),
        cost_estimate=pl.CostEstimate(flops=tokens * width * 80, bytes_accessed=history.size * 40, transcendentals=0),
        name="mix_forward",
    )(history, cotangent, *params, *weights)
    lowered, gpair, last, pre, coeffs = results[:5]
    return (
        lowered.reshape(4, 2 * tokens, width),
        gpair.reshape(2 * tokens, width),
        last,
        pre,
        coeffs,
        results[5:8],
        results[8].reshape(4, width, width // 2),
        results[9:],
    )


def small_rows(width, mix, hidden_width):
    wl, padded = width // 128, -(-mix // 8) * 8
    sizes = [wl, wl * padded, padded, 8, 4 * wl, 4 * wl, 3 * wl, wl, hidden_width // 128]
    firsts = [sum(sizes[:k]) for k in range(len(sizes))]
    return firsts, sum(sizes)


def unmix_kernel(h_ref, own_ref, theirs_ref, g_ref, pre_ref, coeffs_ref, gain_ref, inner_ref, outer_ref, sgain_ref,
                 hist_ref, sgg_ref, sbg_ref, gg_ref, ig_ref, og_ref, bg_ref, ob_ref,
                 streams_ref, sg_ref, scaled_ref, mpg_ref, hidden_ref, cgl_ref):
    i, steps = pl.program_id(0), pl.num_programs(0)
    hist, block, width = h_ref.shape[0], h_ref.shape[2], h_ref.shape[3]
    mix = 4 * hist

    @pl.when(i == 0)
    def _():
        for ref in (sgg_ref, sbg_ref, gg_ref, bg_ref, ob_ref):
            ref[...] = jnp.zeros_like(ref)

    def down(x):
        return jnp.sum(x, axis=0, keepdims=True)

    coeffs = coeffs_ref[...]
    spread = blend(h_ref, coeffs, streams_ref)
    grad = g_ref[0].astype(F32)
    ob_ref[...] += down(grad)
    for k in range(4):
        stream = streams_ref[k]
        centered = stream - jnp.mean(stream, axis=1, keepdims=True)
        rs = lax.rsqrt(jnp.mean(centered * centered, axis=1, keepdims=True) + EPS)
        n = centered * rs
        ng = own_ref[k] + theirs_ref[k].astype(F32)
        sgg_ref[k : k + 1, :] += down(ng * n)
        sbg_ref[k : k + 1, :] += down(ng)
        w = ng * sgain_ref[k : k + 1, :].astype(F32)
        pulled = rs * (w - jnp.mean(w, axis=1, keepdims=True) - n * jnp.mean(w * n, axis=1, keepdims=True))
        sg_ref[k] = pulled + grad if k == 3 else pulled

    lane = lax.broadcasted_iota(jnp.int32, (block, mix), 1)
    cg = jnp.zeros((block, mix), F32)
    for j in range(hist):
        value = h_ref[j, 0].astype(F32)
        for k in range(4):
            cg = jnp.where(lane == k * hist + j, jnp.sum(value * sg_ref[k], axis=1, keepdims=True), cg)
    bg_ref[...] += down(cg)
    cg_low = cg.astype(BF16)
    pre = pre_ref[...]
    at = pl.ds(pl.multiple_of(i * block, block), block)
    mpg = (against(cg_low, outer_ref[...]) * gelu_slope(pre)).astype(BF16)
    last = h_ref[hist - 1, 0].astype(F32)
    r = lax.rsqrt(jnp.mean(last * last, axis=1, keepdims=True) + EPS)
    gain = gain_ref[...].astype(F32)
    scaled_ref[at, :] = (last * r * gain).astype(BF16)
    mpg_ref[at, :] = mpg
    hidden_ref[at, :] = (pre * phi(pre)).astype(BF16)
    cgl_ref[at, :] = cg_low
    scaled_grad = product(mpg, inner_ref[...])
    gg_ref[...] += down(scaled_grad * last * r)
    w = scaled_grad * gain
    last_grad = r * (w - last * (r * r) * jnp.mean(w * last, axis=1, keepdims=True))
    for from_ in range(0, width, 128):
        lanes = slice(from_, from_ + 128)
        pulls = [sg_ref[k, :, lanes] for k in range(4)]
        for j in range(hist):
            total = spread[j] * pulls[0]
            for k in range(1, 4):
                total = total + spread[k * hist + j] * pulls[k]
            hist_ref[j, 0, :, lanes] = total + last_grad[:, lanes] if j == hist - 1 else total

    @pl.when(i == steps - 1)
    def _():
        ig_ref[...] = inner(mpg_ref[...], scaled_ref[...])
        og_ref[...] = inner(hidden_ref[...], cgl_ref[...])


def mix_backward(history, own, theirs, cotangent, pre, coeffs, params):
    hist, _, tokens, width = history.shape
    mix = pre.shape[1]
    block = 64
    whole = pl.BlockSpec(memory_space=pltpu.VMEM)
    part = lambda n: pl.BlockSpec((block, n), lambda i: (i, 0))
    four = pl.BlockSpec((4, block, width), lambda i: (0, i, 0))
    story = pl.BlockSpec((hist, 1, block, width), lambda i: (0, 0, i, 0))
    small = [(4, width), (4, width), (1, width), (mix, width), (mix, mix), (1, mix), (1, width)]
    return pl.pallas_call(
        unmix_kernel,
        grid=(tokens // block,),
        out_shape=[jax.ShapeDtypeStruct(history.shape, F32)] + [jax.ShapeDtypeStruct(shape, F32) for shape in small],
        in_specs=[story, four, four, pl.BlockSpec((1, block, width), lambda i: (0, i, 0)), part(mix), part(mix)] + [whole] * 4,
        out_specs=[story] + [pl.BlockSpec(shape, lambda i: (0, 0)) for shape in small],
        scratch_shapes=[
            pltpu.VMEM((4, block, width), F32),
            pltpu.VMEM((4, block, width), F32),
            pltpu.VMEM((tokens, width), BF16),
            pltpu.VMEM((tokens, mix), BF16),
            pltpu.VMEM((tokens, mix), BF16),
            pltpu.VMEM((tokens, mix), BF16),
        ],
        compiler_params=pltpu.CompilerParams(vmem_limit_bytes=VMEM_LIMIT),
        cost_estimate=pl.CostEstimate(flops=tokens * width * 1000, bytes_accessed=history.size * 12, transcendentals=0),
        name="mix_backward",
    )(history, own, theirs, cotangent, pre, coeffs, *params)


def finish_kernel(grid, orders, n_kept, *refs):
    nz = grid.nz
    kept, refs = refs[:n_kept], refs[n_kept:]
    came_a, came_b, refs = refs[:1], refs[1 : grid.nb], refs[grid.nb :]
    sums_refs, folded, refs = refs[:2], refs[2 : 2 + nz], refs[2 + nz :]
    sgg_ref, sbg_ref, gg_ref, ig_ref, og_ref, bg_ref, ob_ref, hb_ref, eb_ref = refs[:9]
    done_ref, outs, refs = refs[9], refs[10:14], refs[14:]
    first, second, third, final, refs = refs[:4], refs[4:8], refs[8:12], refs[12:18], refs[18:]
    sums = Summing(grid, *refs[:3], done_ref, *refs[3:5])
    local_sem, send_sem, recv_sem = refs[5:]
    a, b, z, c = place = grid.here()
    width, mix = gg_ref.shape[1], bg_ref.shape[1]
    wl, padded, hidden_rows = width // 128, -(-mix // 8) * 8, eb_ref.shape[1] // 128
    firsts, _ = small_rows(width, mix, 2 * eb_ref.shape[1])
    half = width // 2
    spots = [(0, lambda core: core * half), (0, lambda core: width + core * half), (0, lambda core: 2 * width + core * half),
             (1, lambda core: core * half), (2, lambda core: core * eb_ref.shape[1]), (3, lambda core: core * eb_ref.shape[1])]

    def copies(t, stage):
        if stage == 1:
            return fold_copies(grid, place, orders[t], 1, None, first[t], second[t], (send_sem.at[t], recv_sem.at[t]))
        if stage == 2:
            return [
                remote(second[t].at[0, lax.rem(z + k, nz)], third[t].at[k - 1], send_sem.at[t, k], recv_sem.at[t, k],
                       grid.device(a, b, lax.rem(z + k, nz), c))
                for k in range(1, nz)
            ]
        result, base = spots[t]
        n = final[t].shape[-1]
        spot = outs[result].at[:, pl.ds(pl.multiple_of(base(c), 128), n)]
        return [
            remote(final[t].at[1 - c], spot, send_sem.at[t, 0], recv_sem.at[t, 0], grid.device(a, b, z, 1 - c)),
            pltpu.make_async_copy(final[t].at[c], spot, local_sem.at[t]),
        ]

    sums.greet()
    for t in range(4):

        def step(i, carry, t=t):
            o, j = i // nz, lax.rem(i, nz)
            total = kept[t][o, j].astype(F32)
            for piece in came_a if orders[t] == "ab" else came_b:
                total = total + piece[t // 2, o, j].astype(F32)
            first[t][0, o, j] = total.astype(BF16)
            return carry

        lax.fori_loop(0, first[t].shape[1] * nz, step, 0)
    pl.semaphore_wait(pltpu.get_barrier_semaphore(), sums.count - 1)
    for t in range(2):
        start(copies(t, 1))

    mine = sums.mine
    mine[...] = jnp.zeros_like(mine)
    for l in range(wl):
        lanes = slice(l * 128, (l + 1) * 128)
        mine[firsts[0] + l : firsts[0] + l + 1, :] = gg_ref[:, lanes]
        mine[firsts[1] + l * padded : firsts[1] + l * padded + mix, :] = ig_ref[:, lanes]
        mine[firsts[4] + 4 * l : firsts[4] + 4 * l + 4, :] = sgg_ref[:, lanes]
        mine[firsts[5] + 4 * l : firsts[5] + 4 * l + 4, :] = sbg_ref[:, lanes]
        mine[firsts[7] + l : firsts[7] + l + 1, :] = ob_ref[:, lanes]
    mine[firsts[2] : firsts[2] + mix, 0:mix] = og_ref[...]
    mine[firsts[3] : firsts[3] + 1, 0:mix] = bg_ref[...]
    for k in range(3):
        for l in range(wl // 2):
            mine[pl.ds(firsts[6] + k * wl + c * (wl // 2) + l, 1), :] = hb_ref[k : k + 1, l * 128 : (l + 1) * 128]
    for l in range(hidden_rows):
        mine[pl.ds(firsts[8] + c * hidden_rows + l, 1), :] = eb_ref[:, l * 128 : (l + 1) * 128]
    sums.deal()

    for t in range(2):
        total = folded[0][t].astype(F32)
        for piece in folded[1:]:
            total = total + piece[t].astype(F32)
        at = 0
        for piece in [ref[t] for ref in sums_refs] + [total]:
            n = piece.shape[1]
            final[4 + t][:, :, at : at + n] = piece.reshape(2, -1, n)
            at += n
        start(copies(4 + t, 3))
    for t in range(4):
        finish(copies(t, 1))
        if t < 2:
            start(copies(t + 2, 1))
        fold_add(grid, place, orders[t], 1, None, first[t], second[t])
        start(copies(t, 2))
    sums.tell()
    for t in range(4):
        finish(copies(t, 2))
        total = second[t][0, z].astype(F32)
        for k in range(nz - 1):
            total = total + third[t][k].astype(F32)
        final[t][...] = total.reshape(final[t].shape)
        start(copies(t, 3))
    sums.close()
    for t in range(6):
        finish(copies(t, 3))


def finish_sums(grid, orders, kept, came, folded, smalls, collective_id):
    sgg, _, _, ig, og, bg, _, hb, eb = smalls
    mix, width = ig.shape
    hidden_width = 2 * eb.shape[1]
    nz = grid.nz
    rows, n = kept[0].shape[-2:]
    devices = grid.n_dp * grid.n_seq
    each = -(-small_rows(width, mix, hidden_width)[1] // (devices * 8)) * 8
    vmem = pl.BlockSpec(memory_space=pltpu.VMEM)
    owned = [3 * width, width, hidden_width, hidden_width]
    folds = [fold_scratch(grid, order, rows, n) for order in orders]
    operands = list(kept) + list(came) + list(folded) + list(smalls)
    return pl.pallas_call(
        functools.partial(finish_kernel, grid, orders, len(kept)),
        out_shape=[jax.ShapeDtypeStruct((devices * each, 128), F32)] + [jax.ShapeDtypeStruct((rows // 2, w), F32) for w in owned],
        in_specs=[vmem] * len(operands),
        out_specs=[vmem] + [pl.BlockSpec(memory_space=pl.ANY)] * len(owned),
        scratch_shapes=[f for _, f, _ in folds]
        + [s for _, _, s in folds]
        + [pltpu.VMEM((nz - 1, rows, n), BF16)] * 4
        + [pltpu.VMEM((2, rows // 2, n), F32)] * 4
        + [pltpu.VMEM((2, rows // 2, hidden_width // 2), F32)] * 2
        + [
            pltpu.VMEM((devices * each, 128), F32),
            pltpu.VMEM((devices * each, 128), F32),
            pltpu.VMEM((each, 128), F32),
            pltpu.SemaphoreType.DMA((2,)),
            pltpu.SemaphoreType.DMA((2,)),
            pltpu.SemaphoreType.DMA((6,)),
            pltpu.SemaphoreType.DMA((6, nz + grid.nb)),
            pltpu.SemaphoreType.DMA((6, nz + grid.nb)),
        ],
        compiler_params=pltpu.CompilerParams(collective_id=collective_id, has_side_effects=True, vmem_limit_bytes=VMEM_LIMIT),
        cost_estimate=pl.CostEstimate(flops=0, bytes_accessed=100 * width * width, transcendentals=0),
        name="finish_sums",
    )(*operands)


def hand_kernel(mix, hidden_width, done, out_ref, *refs):
    owned, placed_ref, small, outs = refs[:4], refs[4], refs[5:14], refs[14:]
    width = out_ref.shape[1]
    wl, padded, hidden_rows = width // 128, -(-mix // 8) * 8, hidden_width // 256
    firsts, _ = small_rows(width, mix, hidden_width)
    placed_ref[...] = out_ref[...]
    for src, dst in zip(owned, outs):
        dst[...] = src[...]
    for l in range(wl):
        lanes = slice(l * 128, (l + 1) * 128)
        small[0][:, lanes] = done[firsts[0] + l : firsts[0] + l + 1, :]
        small[1][:, lanes] = done[firsts[1] + l * padded : firsts[1] + l * padded + mix, :]
        small[4][:, lanes] = done[firsts[4] + 4 * l : firsts[4] + 4 * l + 4, :]
        small[5][:, lanes] = done[firsts[5] + 4 * l : firsts[5] + 4 * l + 4, :]
        small[7][:, lanes] = done[firsts[7] + l : firsts[7] + l + 1, :]
    small[2][...] = done[firsts[2] : firsts[2] + mix, 0:mix]
    small[3][...] = done[firsts[3] : firsts[3] + 1, 0:mix]
    for l in range(3 * wl):
        small[6][:, l * 128 : (l + 1) * 128] = done[firsts[6] + l : firsts[6] + l + 1, :]
    for l in range(2 * hidden_rows):
        small[8][:, l * 128 : (l + 1) * 128] = done[firsts[8] + l : firsts[8] + l + 1, :]


def hand_over(summed, layer_out, owned, mix, hidden_width):
    width = layer_out.shape[1]
    small = [(1, width), (mix, width), (mix, mix), (1, mix), (4, width), (4, width), (1, 3 * width), (1, width), (1, hidden_width)]
    vmem = pl.BlockSpec(memory_space=pltpu.VMEM)
    return pl.pallas_call(
        functools.partial(hand_kernel, mix, hidden_width),
        out_shape=[jax.ShapeDtypeStruct(layer_out.shape, BF16)]
        + [jax.ShapeDtypeStruct(shape, F32) for shape in small]
        + [jax.ShapeDtypeStruct(x.shape, F32) for x in owned],
        in_specs=[vmem] * 6,
        out_specs=[vmem] * 14,
        name="hand_over",
    )(summed, layer_out, *owned)


def exchange_kernel(grid, width, chunks, groups, low_ref, g_ref, w_ref, bias_ref, cos_ref, above_ref, below_ref, _e, _c,
                    dealt_ref, e_ref, c_ref, sent_ref, deal_send, deal_recv, local_sem, send_sem, recv_sem):
    i, steps = pl.program_id(0), pl.num_programs(0)
    a, b, z, c = place = grid.here()
    nz = grid.nz
    work = Gathering(grid, place, None, chunks, None, [e_ref, c_ref], local_sem, send_sem, recv_sem)

    def link(to):
        k = lax.rem(to - z + nz, nz)
        return remote(sent_ref.at[to], dealt_ref.at[z], deal_send.at[k], deal_recv.at[k], grid.device(a, b, to, c))

    def stay():
        return pltpu.make_async_copy(sent_ref.at[z], dealt_ref.at[z], deal_send.at[0])

    @pl.when(i == 0)
    def _():
        grid.greet(*place)
        for group in groups:
            work.begin(group, 2)

    wide = w_ref.shape[2]
    each = wide // width
    tables = [jnp.concatenate([t[...]] * max(wide // 128, 1), axis=1) for t in (cos_ref, above_ref, below_ref)]
    q = rotate(product(low_ref[0], w_ref[0]) + bias_ref[0:1, :], tables, 1.0)
    k = rotate(product(low_ref[1], w_ref[1]) + bias_ref[1:2, :], tables, 1.0)
    v = product(low_ref[2], w_ref[2]) + bias_ref[2:3, :]
    g = product(g_ref[...], w_ref[3])
    for n, x in enumerate((q, k, v, g)):
        x = x.astype(BF16)
        for m in range(each):
            sent_ref[i * each + m, :, n * width : (n + 1) * width] = x[:, m * width : (m + 1) * width]
    for m in range(each):
        to = i * each + m
        pl.when(to != z)(lambda to=to: link(to).start())
        pl.when(to == z)(lambda: stay().start())

    @pl.when(i == steps - 1)
    def _():
        for group in groups:
            work.end(group, 2)
            work.begin(group, 3)
        for m in range(1, nz):
            link(lax.rem(z + m, nz)).wait()
        stay().wait()
        for group in groups:
            work.end(group, 3)


def exchange(grid, lowered, grad_low, weights, biases, tables, started, chunks, groups, own_width, collective_id):
    both, width = grad_low.shape
    nz = grid.nz
    wide = 2 * own_width
    whole = pl.BlockSpec(memory_space=pltpu.VMEM)
    anywhere = pl.BlockSpec(memory_space=pl.ANY)
    dealt, *full = pl.pallas_call(
        functools.partial(exchange_kernel, grid, own_width, chunks, groups),
        grid=(nz // 2,),
        out_shape=[jax.ShapeDtypeStruct((nz, both, 4 * own_width), BF16)] + [jax.ShapeDtypeStruct(x.shape, x.dtype) for x in started],
        in_specs=[
            pl.BlockSpec((3, both, width), lambda i: (0, 0, 0)),
            whole,
            pl.BlockSpec((4, width, wide), lambda i: (0, 0, i)),
            pl.BlockSpec((3, wide), lambda i: (0, i)),
        ]
        + [whole] * 3
        + [anywhere] * 2,
        out_specs=[anywhere] * 3,
        input_output_aliases={7: 1, 8: 2},
        scratch_shapes=[
            pltpu.VMEM((nz, both, 4 * own_width), BF16),
            pltpu.SemaphoreType.DMA((nz,)),
            pltpu.SemaphoreType.DMA((nz,)),
            *gather_sems(grid, chunks),
        ],
        compiler_params=pltpu.CompilerParams(collective_id=collective_id, has_side_effects=True, vmem_limit_bytes=VMEM_LIMIT),
        cost_estimate=pl.CostEstimate(flops=2 * both * weights.size, bytes_accessed=weights.size * 60, transcendentals=0),
        name="exchange",
    )(lowered, grad_low, weights, biases, *tables, *started)
    return dealt, [x.reshape(-1, x.shape[-1]) for x in full]


def unproject_kernel(grid, width, orders, *all_refs):
    mids, all_refs = all_refs[: grid.nz], all_refs[grid.nz :]
    (col_ref, low_ref, g_ref, w_ref, feed_ref, normed_ref, last_ref, bias_ref, cos_ref, above_ref,
     below_ref, own_ref, theirs_ref, hb_ref, out_ref, sum_ref, *refs) = all_refs
    na, nb, nz = grid.na, grid.nb, grid.nz
    kept, over_a, over_b, refs = refs[:4], refs[4], refs[5 : 4 + nb], refs[4 + nb :]
    grad_ref, sending_ref, partial_ref, mine_ref, arrived_ref, along_ref, split_sem, send_sem, recv_sem, along_send, along_recv = refs
    i = pl.program_id(0)
    a, b, z, c = grid.here()
    tokens = out_ref.shape[0]
    other = grid.device(a, b, z, 1 - c)
    own_rows = pl.ds(pl.multiple_of(c * tokens, tokens), tokens)
    their_rows = pl.ds(pl.multiple_of((1 - c) * tokens, tokens), tokens)

    def swap(k):
        return [remote(sending_ref.at[k], theirs_ref.at[k], send_sem.at[k], recv_sem.at[k], other)]

    def swap_out():
        return [remote(partial_ref, arrived_ref, send_sem.at[4], recv_sem.at[4], other)]

    def along():
        return [
            remote(mids[k], along_ref.at[k - 1], along_send.at[k - 1], along_recv.at[k - 1], grid.device(a, b, lax.rem(z + k, nz), c))
            for k in range(1, nz)
        ]

    def split(k):
        grad = grad_ref.at[k]
        if orders[k] == "ab":
            found = [(grad.at[a], kept[k]), (grad.at[1 - a], over_a.at[k // 2])]
        else:
            found = [(grad.at[:, b], kept[k])]
            found += [(grad.at[:, lax.rem(b + m, nb)], over_b[m - 1].at[k // 2]) for m in range(1, nb)]
        return [pltpu.make_async_copy(src, dst, split_sem.at[k, n]) for n, (src, dst) in enumerate(found)]

    def piece(n):
        return jnp.concatenate([col_ref[m, :, n * width : (n + 1) * width] for m in range(nz)], axis=1)

    def keep(k, grad):
        grad_ref[k] = grad.astype(BF16).reshape(grad_ref.shape[1:])
        start(split(k))

    @pl.when(i == 0)
    def _():
        grid.greet(a, b, z, c)
        start(along())
        mine_ref[...] = piece(0)
        partial_ref[...] = against(mine_ref[their_rows, :], w_ref[0]) + feed_ref[their_rows, :]
        sending_ref[3] = normed_ref[their_rows, :].astype(BF16)
        start(swap_out())
        start(swap(3))
        own_ref[0] = normed_ref[own_rows, :]
        out = against(mine_ref[own_rows, :], w_ref[0]) + feed_ref[own_rows, :] + last_ref[...] + bias_ref[...]
        keep(3, inner(g_ref[...], mine_ref[...]))
        finish(swap_out())
        out_ref[...] = (out + arrived_ref[...]).astype(BF16)

    for k in range(3):

        @pl.when(i == k + 1)
        def _(k=k):
            grad = piece(k + 1).astype(F32)
            if k < 2:
                tables = [jnp.concatenate([t[...]] * (grad.shape[1] // 128), axis=1) for t in (cos_ref, above_ref, below_ref)]
                grad = rotate(grad, tables, -1.0)
            hb_ref[k : k + 1, :] = jnp.sum(grad, axis=0, keepdims=True)
            mine_ref[...] = grad.astype(BF16)
            sending_ref[k] = against(mine_ref[their_rows, :], w_ref[0]).astype(BF16)
            start(swap(k))
            own_ref[0] = against(mine_ref[own_rows, :], w_ref[0])
            keep(k, inner(low_ref[0], mine_ref[...]))
            if k == 2:
                for n in range(4):
                    finish(swap(n))
                    finish(split(n))
                finish(along())
                total = mids[0][...].astype(F32)
                for n in range(nz - 1):
                    total = total + along_ref[n].astype(F32)
                sum_ref[...] = total


def unproject(grid, orders, mids, collected, lowered, grad_low, weights, feed_part, normed_feed, last_stream, bias, tables, own_width, collective_id):
    tokens, width = last_stream.shape
    both, half = 2 * tokens, width // 2
    na, nb, nz = grid.na, grid.nb, grid.nz
    rows = width // (na * nb * nz)
    whole = pl.BlockSpec(memory_space=pltpu.VMEM)
    anywhere = pl.BlockSpec(memory_space=pl.ANY)
    turn = lambda i: lax.rem(i + 3, 4)
    split_shapes = [jax.ShapeDtypeStruct((nb if order == "ab" else na, nz, rows, half), BF16) for order in orders]
    sent_shapes = [jax.ShapeDtypeStruct((2, nb, nz, rows, half), BF16)] + [jax.ShapeDtypeStruct((2, na, nz, rows, half), BF16)] * (nb - 1)
    results = pl.pallas_call(
        functools.partial(unproject_kernel, grid, own_width, orders),
        grid=(4,),
        out_shape=[
            jax.ShapeDtypeStruct((4, tokens, width), F32),
            jax.ShapeDtypeStruct((4, tokens, width), BF16),
            jax.ShapeDtypeStruct((3, half), F32),
            jax.ShapeDtypeStruct((tokens, width), BF16),
            jax.ShapeDtypeStruct(mids[0].shape, F32),
        ]
        + split_shapes
        + sent_shapes,
        in_specs=[whole]
        + [anywhere] * (nz - 1)
        + [
            whole,
            pl.BlockSpec((1, both, width), lambda i: (jnp.maximum(i - 1, 0), 0, 0)),
            whole,
            pl.BlockSpec((1, width, half), lambda i: (turn(i), 0, 0)),
        ]
        + [whole] * 7,
        out_specs=[
            pl.BlockSpec((1, tokens, width), lambda i: (turn(i), 0, 0)),
            anywhere,
            pl.BlockSpec((3, half), lambda i: (0, 0)),
            pl.BlockSpec((tokens, width), lambda i: (0, 0)),
            pl.BlockSpec(mids[0].shape, lambda i: (0, 0, 0)),
        ]
        + [anywhere] * (len(split_shapes) + len(sent_shapes)),
        scratch_shapes=[
            pltpu.VMEM((4, na, nb, nz, rows, half), BF16),
            pltpu.VMEM((4, tokens, width), BF16),
            pltpu.VMEM((tokens, width), F32),
            pltpu.VMEM((both, half), BF16),
            pltpu.VMEM((tokens, width), F32),
            pltpu.VMEM((nz - 1, *mids[0].shape), BF16),
            pltpu.SemaphoreType.DMA((4, nb + 1)),
            pltpu.SemaphoreType.DMA((5,)),
            pltpu.SemaphoreType.DMA((5,)),
            pltpu.SemaphoreType.DMA((nz - 1,)),
            pltpu.SemaphoreType.DMA((nz - 1,)),
        ],
        compiler_params=pltpu.CompilerParams(collective_id=collective_id, has_side_effects=True, vmem_limit_bytes=VMEM_LIMIT),
        cost_estimate=pl.CostEstimate(flops=32 * both * width * half, bytes_accessed=40 * both * width, transcendentals=0),
        name="unproject",
    )(*mids, collected, lowered, grad_low, weights, feed_part, normed_feed, last_stream, bias, *tables)
    own, theirs, head_bias, layer_out, mid_sums = results[:5]
    return own, theirs, head_bias, layer_out, mid_sums, results[5:9], results[9:]


def feed_kernel(grid, steps, back_ref, low_ref, g_ref, we_ref, wc_ref, bias_ref, collected_ref, feed_ref, normed_ref, eb_ref, sum_ref, *refs):
    nz = grid.nz
    mids, outs, refs = refs[:nz], refs[nz : 2 * nz], refs[2 * nz :]
    parts, refs = refs[: 2 * steps], refs[2 * steps :]
    first, second, refs = refs[: 2 * steps], refs[2 * steps : 4 * steps], refs[4 * steps :]
    third, (send_sem, recv_sem, out_sem, back_send, back_recv) = refs[:2], refs[2:]
    i = pl.program_id(0)
    a, b, z, c = place = grid.here()
    orders = ["ab", "ba"] * steps

    def copies(t, stage):
        if stage < 2:
            return fold_copies(grid, place, orders[t], stage, parts[t], first[t], second[t], (send_sem.at[t], recv_sem.at[t]))
        along = [lax.rem(z + k, nz) for k in range(nz)]
        if t >= 2:
            n = parts[t].shape[-1]
            spot = outs if t >= 2 * steps - 2 else [mid.at[:, :, pl.ds((t // 2 - 1) * n, n)] for mid in mids]
            return [pltpu.make_async_copy(second[t].at[0, along[k]], spot[k].at[t % 2], out_sem.at[t, k]) for k in range(nz)]
        return [
            remote(second[t].at[0, along[k]], third[t].at[k - 1], send_sem.at[t, k], recv_sem.at[t, k], grid.device(a, b, along[k], c))
            for k in range(1, nz)
        ]

    def begin(u):
        for t in (2 * u, 2 * u + 1):
            start(copies(t, 0))

    def end(u, stage):
        for t in (2 * u, 2 * u + 1):
            finish(copies(t, stage))
            if stage < 2:
                own = parts[t].at[a] if orders[t] == "ab" else parts[t].at[:, b]
                fold_add(grid, place, orders[t], stage, own, first[t], second[t])
                start(copies(t, stage + 1))
            elif u == 0:
                total = second[t][0, z].astype(F32)
                for k in range(nz - 1):
                    total = total + third[t][k].astype(F32)
                sum_ref[t % 2] = total

    def turn(u):
        for stage in range(3):
            if 0 <= u - stage < steps:
                end(u - stage, stage)

    def backs():
        found = [pltpu.make_async_copy(back_ref.at[z], collected_ref.at[z], back_send.at[0])]
        for k in range(1, nz):
            to = lax.rem(z + k, nz)
            found.append(remote(back_ref.at[to], collected_ref.at[z], back_send.at[k], back_recv.at[k], grid.device(a, b, to, c)))
        return found

    @pl.when(i == 0)
    def _():
        grid.greet(*place)
        start(backs())
        feed_ref[...] = jnp.zeros_like(feed_ref)
        normed_ref[...] = jnp.zeros_like(normed_ref)

    low, grad, expand, contract = low_ref[0], g_ref[...], we_ref[...], wc_ref[...]
    expanded = product(low, expand) + bias_ref[...]
    share = phi(expanded)
    hidden = (expanded * share).astype(BF16)
    slope = share + expanded * jnp.exp(-0.5 * expanded * expanded) * (1.0 / math.sqrt(2.0 * math.pi))
    feed_ref[...] += against(hidden, contract)
    hidden_grad = inner(grad, hidden).astype(BF16)
    pulled = product(grad, contract) * slope
    eb_ref[...] = jnp.sum(pulled, axis=0, keepdims=True)
    pulled_low = pulled.astype(BF16)
    normed_ref[...] += against(pulled_low, expand)
    expand_grad = inner(low, pulled_low).astype(BF16)
    for u in range(steps):

        @pl.when(i == u)
        def _(u=u):
            parts[2 * u][...] = expand_grad.reshape(parts[2 * u].shape)
            parts[2 * u + 1][...] = hidden_grad.reshape(parts[2 * u + 1].shape)
            begin(u)
            if u >= 2:
                turn(u - 2)
            if u == steps - 1:
                for v in range(max(steps - 2, 0), steps + 2):
                    turn(v)
                finish(backs())


def feed_forward(grid, returned, lowered, grad_low, weight_e, weight_c, bias, steps, collective_id):
    both, width = grad_low.shape
    n = weight_e.shape[1] // steps
    na, nb, nz = grid.na, grid.nb, grid.nz
    rows = width // (na * nb * nz)
    whole = lambda *shape: pl.BlockSpec(shape, lambda i: (0,) * len(shape))
    cols = lambda m: pl.BlockSpec((m, n), lambda i: (0, i))
    orders = ["ab", "ba"] * steps
    folds = [fold_scratch(grid, order, rows, n) for order in orders]
    sem = pltpu.SemaphoreType.DMA((2 * steps, nz + nb))
    return pl.pallas_call(
        functools.partial(feed_kernel, grid, steps),
        grid=(steps,),
        out_shape=[
            jax.ShapeDtypeStruct(returned.shape, BF16),
            jax.ShapeDtypeStruct((both, width), F32),
            jax.ShapeDtypeStruct((both, width), F32),
            jax.ShapeDtypeStruct((1, n * steps), F32),
            jax.ShapeDtypeStruct((2, rows, n), F32),
        ]
        + [jax.ShapeDtypeStruct((2, rows, n * (steps - 2)), BF16)] * nz
        + [jax.ShapeDtypeStruct((2, rows, n), BF16)] * nz,
        in_specs=[
            pl.BlockSpec(memory_space=pltpu.VMEM),
            pl.BlockSpec((1, both, width), lambda i: (3, 0, 0)),
            whole(both, width),
            cols(width),
            cols(width),
            cols(1),
        ],
        out_specs=[
            pl.BlockSpec(memory_space=pl.ANY),
            whole(both, width),
            whole(both, width),
            cols(1),
            whole(2, rows, n),
        ]
        + [pl.BlockSpec(memory_space=pl.ANY)] * (2 * nz),
        scratch_shapes=[pltpu.VMEM((na, nb, nz, rows, n), BF16)] * (2 * steps)
        + [f for _, f, _ in folds]
        + [s for _, _, s in folds]
        + [pltpu.VMEM((nz - 1, rows, n), BF16)] * 2
        + [sem, sem, pltpu.SemaphoreType.DMA((2 * steps, nz)), pltpu.SemaphoreType.DMA((nz,)), pltpu.SemaphoreType.DMA((nz,))],
        compiler_params=pltpu.CompilerParams(collective_id=collective_id, has_side_effects=True, vmem_limit_bytes=VMEM_LIMIT),
        cost_estimate=pl.CostEstimate(flops=12 * both * width * n * steps * 2, bytes_accessed=width * n * steps * 20, transcendentals=0),
        name="feed_forward",
    )(returned, lowered, grad_low, weight_e, weight_c, bias)


def attention_kernel(width, heads, tile, step, edge, length, x_ref, qdoc_ref, out_ref, kdoc_ref,
                     s_ref, kt_ref, vt_ref, ot_ref, dqt_ref, dka_ref, dva_ref, top_ref):
    i = pl.program_id(0)
    tiles = length // tile
    scale = 1.0 / math.sqrt(HEAD_DIM)
    @pl.when(i == 0)
    def _():
        dka_ref[...] = jnp.zeros_like(dka_ref)
        dva_ref[...] = jnp.zeros_like(dva_ref)
        def turn(j, carry):
            at = pl.ds(pl.multiple_of(j * tile, tile), tile)
            kt_ref[:, at] = x_ref[at, width : 2 * width].T
            kdoc_ref[at, :] = jnp.broadcast_to(qdoc_ref[:, at], (128, tile)).T
            vt_ref[:, at] = x_ref[at, 2 * width : 3 * width].T
            return carry
        lax.fori_loop(0, tiles, turn, 0)
    rows = pl.ds(pl.multiple_of(i * tile, tile), tile)
    query = x_ref[rows, 0:width] * jnp.asarray(scale, BF16)
    grad = x_ref[rows, 3 * width : 4 * width]
    query_t, grad_t = query.T, grad.T
    lanes = lax.broadcasted_iota(jnp.int32, (tile, width), 1) // HEAD_DIM
    subs = lax.broadcasted_iota(jnp.int32, (width, tile), 0) // HEAD_DIM
    zero = jnp.zeros((), BF16)
    queries_t = [jnp.where(subs == h, query_t, zero) for h in range(heads)]
    grads_t = [jnp.where(subs == h, grad_t, zero) for h in range(heads)]
    all_queries = jnp.concatenate([jnp.where(lanes == h, query, zero) for h in range(heads)], axis=0)
    all_grads = jnp.concatenate([jnp.where(lanes == h, grad, zero) for h in range(heads)], axis=0)
    qdoc = qdoc_ref[:, rows]
    qpos = i * tile + lax.broadcasted_iota(jnp.int32, (step, tile), 1)
    head_edge = -(-edge // step)
    tail_edge = (length - edge) // tile
    per = tile // step
    count = (i + 1) * per
    ot_ref[...] = jnp.zeros_like(ot_ref)
    dqt_ref[...] = jnp.zeros_like(dqt_ref)
    top_ref[...] = jnp.full_like(top_ref, NEG)

    def fold(x, f):
        return f(x.reshape(step // 8, 8, tile), axis=0)

    def scores(j, carry):
        at = pl.ds(pl.multiple_of(j * step, step), step)
        checked = (j >= i * per) | (j < head_edge) | (i >= tail_edge)
        def run(mask):
            keys = x_ref[at, width : 2 * width]
            if mask:
                kdoc = jnp.concatenate([kdoc_ref[at, :]] * (tile // 128), axis=1)
                kpos = j * step + lax.broadcasted_iota(jnp.int32, (step, tile), 0)
                allowed = (kdoc == qdoc) & (kpos <= qpos)
            for h in range(heads):
                s = product(keys, queries_t[h])
                if mask:
                    s = jnp.where(allowed, s, NEG)
                s_ref[h, at, :] = s
                top_ref[h] = jnp.maximum(top_ref[h], fold(s, jnp.max))
        pl.when(checked)(lambda: run(True))
        pl.when(jnp.logical_not(checked))(lambda: run(False))
        return carry
    lax.fori_loop(0, count, scores, 0)
    tops = [jnp.max(top_ref[h], axis=0, keepdims=True) for h in range(heads)]

    def weigh(j, totals):
        at = pl.ds(pl.multiple_of(j * step, step), step)
        new = []
        for h in range(heads):
            own = slice(h * HEAD_DIM, (h + 1) * HEAD_DIM)
            weights = jnp.exp(s_ref[h, at, :] - tops[h])
            s_ref[h, at, :] = weights
            new.append(totals[h] + fold(weights, jnp.sum))
            ot_ref[own, :] += product(vt_ref[own, at], weights.astype(BF16))
        return new
    totals = lax.fori_loop(0, count, weigh, [jnp.zeros((8, tile), F32)] * heads)
    inverse = [1.0 / jnp.sum(t, axis=0, keepdims=True) for t in totals]
    grad_f = grad_t.astype(F32)
    deltas = []
    for h in range(heads):
        own = slice(h * HEAD_DIM, (h + 1) * HEAD_DIM)
        value = ot_ref[own, :] * inverse[h]
        ot_ref[own, :] = value
        deltas.append(jnp.sum(value * grad_f[own], axis=0, keepdims=True))
    out_ref[rows, 0:width] = ot_ref[...].T.astype(BF16)

    def back(j, carry):
        at = pl.ds(pl.multiple_of(j * step, step), step)
        values = x_ref[at, 2 * width : 3 * width]
        probs_low, grads_low = [], []
        for h in range(heads):
            own = slice(h * HEAD_DIM, (h + 1) * HEAD_DIM)
            probs_grad = product(values, grads_t[h])
            probs = s_ref[h, at, :] * inverse[h]
            scores_grad = (probs * (probs_grad - deltas[h])).astype(BF16)
            probs_low.append(probs.astype(BF16))
            grads_low.append(scores_grad)
            dqt_ref[own, :] += product(kt_ref[own, at], scores_grad)
        dva_ref[at, :] += product(jnp.concatenate(probs_low, axis=1), all_grads)
        dka_ref[at, :] += product(jnp.concatenate(grads_low, axis=1), all_queries)
        return carry
    lax.fori_loop(0, count, back, 0)
    out_ref[rows, width : 2 * width] = (dqt_ref[...].T * scale).astype(BF16)

    @pl.when(i == tiles - 1)
    def _():
        out_ref[:, 2 * width : 3 * width] = dka_ref[...].astype(BF16)
        out_ref[:, 3 * width : 4 * width] = dva_ref[...].astype(BF16)


def attention(dealt, documents, heads, edge):
    length = dealt.shape[0]
    width = heads * HEAD_DIM
    tile = step = 2 * edge
    pairs = length * length // 2 * heads
    whole = lambda i: (0, 0)
    return pl.pallas_call(
        functools.partial(attention_kernel, width, heads, tile, step, edge, length),
        grid=(length // tile,),
        out_shape=jax.ShapeDtypeStruct((length, 4 * width), BF16),
        in_specs=[pl.BlockSpec((length, 4 * width), whole), pl.BlockSpec((1, length), whole)],
        out_specs=pl.BlockSpec((length, 4 * width), whole),
        scratch_shapes=[
            pltpu.VMEM((length, 128), F32), pltpu.VMEM((heads, length, tile), F32), pltpu.VMEM((width, length), BF16), pltpu.VMEM((width, length), BF16),
            pltpu.VMEM((width, tile), F32), pltpu.VMEM((width, tile), F32), pltpu.VMEM((length, width), F32), pltpu.VMEM((length, width), F32),
            pltpu.VMEM((heads, 8, tile), F32)],
        compiler_params=pltpu.CompilerParams(vmem_limit_bytes=VMEM_LIMIT),
        cost_estimate=pl.CostEstimate(flops=pairs * 64 * 2 * 6 * 4, bytes_accessed=length * width * 20, transcendentals=pairs),
        name="attention",
    )(dealt, documents)


def on_device(
    grid,
    history,
    documents,
    cotangent,
    mixer_gain,
    mixer_inner,
    mixer_outer,
    mixer_bias,
    stream_gain,
    stream_bias,
    inbound_weight,
    inbound_bias,
    outbound_weight,
    outbound_bias,
    expand,
    expand_bias,
    contract,
    contract_bias,
):
    n_dp, n_seq, nz = grid.n_dp, grid.n_seq, grid.nz
    tokens, width = history.shape[2], history.shape[3]
    hidden_width = expand.shape[1]
    half, hidden_half = width // 2, hidden_width // 2
    both = 2 * tokens
    length = documents.shape[1]
    mix = mixer_bias.shape[0]
    heads = HEADS // n_seq
    own_width = heads * HEAD_DIM
    seq = lax.axis_index("seq")
    z, c = seq // 2, lax.rem(seq, 2)

    def take(array, start, size, axis=0):
        return lax.dynamic_slice_in_dim(array, start, size, axis)

    pick = lambda base, n: (lambda core: base + core * n)
    parts = 4
    piece = hidden_half // parts
    feed = []
    for part in range(parts):
        base = lambda core, part=part: core * hidden_half + part * piece
        feed.append((2, base, 4, part * piece, piece, "ba"))
        feed.append((3, base, 5, part * piece, piece, "ab"))
    pairs = [[4 + 2 * part, 5 + 2 * part] for part in range(parts)]
    inner_t = mixer_inner.T
    lowered, grad_low, last_stream, mix_pre, coeffs, tables, weights, started = mix_forward(
        grid,
        history,
        cotangent,
        [mixer_gain[None], inner_t, mixer_outer, mixer_bias[None], stream_gain, stream_bias],
        [inbound_weight, outbound_weight, expand, contract],
        [
            (0, pick(width, half), 1, 0, half, "ba"),
            (0, pick(2 * width, half), 2, 0, half, "ab"),
            (0, pick(0, half), 0, 0, half, "ba"),
            (1, pick(0, half), 3, 0, half, "ab"),
        ]
        + feed,
        [[0, 1], [2, 3]],
        pairs,
        [hidden_half] * 2,
        1,
    )

    bias_in = take(inbound_bias.astype(F32).reshape(3, width), c * half, half, 1)
    chunks = [(0, None, n - 4, col, size, order) for _, _, n, col, size, order in feed]
    dealt, (weight_e, weight_c) = exchange(
        grid,
        lowered,
        grad_low,
        weights,
        bias_in,
        tables,
        started,
        chunks,
        [[2 * part, 2 * part + 1] for part in range(parts)],
        own_width,
        2,
    )
    returned = attention(dealt.reshape(length, 4 * own_width), documents.astype(F32), heads, tokens)
    returned = returned.reshape(nz, both, 4 * own_width)

    bias_e = take(expand_bias.astype(F32), c * hidden_half, hidden_half)[None]
    collected, feed_part, normed_feed, expand_bias_part, feed_sums, *rest = feed_forward(
        grid, returned, lowered, grad_low, weight_e, weight_c, bias_e, parts, 3
    )

    def along_z(k):
        return [(s, (s // 2 + k) % nz * 2 + s % 2) for s in range(n_seq)]

    mids, folded = rest[:nz], rest[nz:]
    folded = [folded[0]] + [lax.ppermute(folded[k], "seq", along_z(k)) for k in range(1, nz)]

    orders = ("ab", "ba", "ab", "ba")
    bias_out = (outbound_bias.astype(F32) + contract_bias.astype(F32))[None]
    normed_own, normed_theirs, head_bias_part, layer_out, mid_sums, kept, leaving = unproject(
        grid, orders, mids, collected, lowered, grad_low, weights, feed_part, normed_feed, last_stream, bias_out, tables, own_width, 4
    )
    nb = grid.nb
    over_a = [(d, (d + nb) % n_dp) for d in range(n_dp)]
    over_b = [[(d, d // nb * nb + (d + k) % nb) for d in range(n_dp)] for k in range(1, nb)]
    came_a = lax.ppermute(leaving[0], "dp", over_a)
    came_b = [lax.ppermute(x, "dp", perm) for x, perm in zip(leaving[1:], over_b)]

    history_grad, *small = mix_backward(
        history, normed_own, normed_theirs, cotangent, mix_pre, coeffs, [mixer_gain[None], inner_t, mixer_outer, stream_gain]
    )
    smalls = [*small, head_bias_part, expand_bias_part]
    summed, *owned = finish_sums(grid, orders, kept, [came_a, *came_b], [feed_sums, mid_sums, *folded], smalls, 5)
    layer_out, *small, inbound_grad, outbound_grad, expand_grad, contract_grad = hand_over(summed, layer_out, owned, mix, hidden_width)
    gain_grad, inner_grad, outer_grad, bias_grad, stream_gain_grad, stream_bias_grad, in_bias_grad, out_bias_grad, expand_bias_grad = small
    return (
        layer_out[None],
        history_grad,
        gain_grad.reshape(width),
        inner_grad.T,
        outer_grad,
        bias_grad.reshape(-1),
        stream_gain_grad,
        stream_bias_grad,
        inbound_grad,
        in_bias_grad.reshape(3 * width),
        outbound_grad,
        out_bias_grad.reshape(width),
        expand_grad,
        expand_bias_grad.reshape(hidden_width),
        contract_grad,
        out_bias_grad.reshape(width),
    )


def solution(mesh):
    rows = P(("dp", "seq"), None)
    placed = (
        P(None, "dp", "seq", None),
        P("dp", None),
        P("dp", "seq", None),
        P(),
        P(),
        P(),
        P(),
        P(),
        P(),
        rows,
        P(),
        rows,
        P(),
        rows,
        P(),
        rows,
        P(),
    )
    grid = Grid(mesh.shape["dp"], mesh.shape["seq"])
    return jax.shard_map(
        functools.partial(on_device, grid),
        mesh=mesh,
        in_specs=placed,
        out_specs=(
            P("dp", "seq", None),
            P(None, "dp", "seq", None),
            P(),
            P(),
            P(),
            P(),
            P(),
            P(),
            rows,
            P(),
            rows,
            P(),
            rows,
            P(),
            rows,
            P(),
        ),
        check_vma=False,
    )
```

```python
import functools
import math

import jax
import jax.numpy as jnp
from jax import lax
from jax.experimental import pallas as pl
from jax.experimental.pallas import tpu as pltpu
from jax.sharding import PartitionSpec as P

HEADS = 16
HEAD_DIM = 64
ROT_DIMS = 16
EPS = 1e-05
HIGHEST = lax.Precision.HIGHEST
NEG = -1e30
MESH = pl.DeviceIdType.MESH
F32 = jnp.float32
BF16 = jnp.bfloat16
VMEM_LIMIT = 56 * 1024 * 1024
STEPS = 4


def inner(left, right):
    return lax.dot_general(left, right, (((0,), (0,)), ((), ())), preferred_element_type=F32)


def against(left, right):
    return lax.dot_general(left, right, (((1,), (1,)), ((), ())), preferred_element_type=F32)


def product(left, right):
    return jnp.dot(left, right, preferred_element_type=F32)


def exact_gelu(value):
    return jax.nn.gelu(value, approximate=False)


def phi(value):
    return 0.5 * (1.0 + lax.erf(value * (1.0 / math.sqrt(2.0))))


def gelu_slope(value):
    return phi(value) + value * jnp.exp(-0.5 * value * value) * (1.0 / math.sqrt(2.0 * math.pi))


def rotate(value, tables, sign):
    half = ROT_DIMS // 2
    cosine, above, below = tables
    width = value.shape[-1]
    up = pltpu.roll(value, width - half, 1)
    down = pltpu.roll(value, half, 1)
    return value * cosine + sign * (up * above + down * below)


class Grid:
    def __init__(self, n_dp, n_seq):
        self.n_dp, self.n_seq = n_dp, n_seq
        self.na, self.nb, self.nz = 2, n_dp // 2, n_seq // 2

    def here(self):
        dp, seq = lax.axis_index("dp"), lax.axis_index("seq")
        return dp // self.nb, lax.rem(dp, self.nb), seq // 2, lax.rem(seq, 2)

    def device(self, a, b, z, c):
        return (a * self.nb + b, z * 2 + c)

    def peers(self, a, b, z, c):
        found = [self.device(a, b, z, 1 - c), self.device(1 - a, b, z, c)]
        found += [self.device(a, lax.rem(b + k, self.nb), z, c) for k in range(1, self.nb)]
        found += [self.device(a, b, lax.rem(z + k, self.nz), c) for k in range(1, self.nz)]
        return found

    def greet(self, a, b, z, c):
        barrier = pltpu.get_barrier_semaphore()
        found = self.peers(a, b, z, c)
        for peer in found:
            pl.semaphore_signal(barrier, inc=1, device_id=peer, device_id_type=MESH)
        pl.semaphore_wait(barrier, len(found))


def row(ref):
    value = ref[...].astype(F32)
    return jnp.concatenate([value[l : l + 1] for l in range(value.shape[0])], axis=1)


def remote(src, dst, send, recv, device):
    return pltpu.make_async_remote_copy(
        src_ref=src, dst_ref=dst, send_sem=send, recv_sem=recv, device_id=device, device_id_type=MESH
    )


def start(copies):
    for copy in copies:
        copy.start()


def finish(copies):
    for copy in copies:
        copy.wait()


class Gathering:
    def __init__(self, grid, place, rows, chunks, ins, outs, local_sem, send_sem, recv_sem):
        self.grid, self.place, self.rows, self.chunks = grid, place, rows, chunks
        self.ins, self.outs = ins, outs
        self.local_sem, self.send_sem, self.recv_sem = local_sem, send_sem, recv_sem

    def copies(self, t, stage):
        a, b, z, c = self.place
        grid, rows = self.grid, self.rows
        nz, nb = grid.nz, grid.nb
        source, base, result, col, n, order = self.chunks[t]
        out, cols = self.outs[result], pl.ds(col, n)

        def send(src, dst, slot, device):
            return remote(src, dst, self.send_sem.at[t, slot], self.recv_sem.at[t, slot], device)

        if stage == 0:
            mine = self.ins[source].at[:, pl.ds(pl.multiple_of(base(c), 128), n)]
            theirs = self.ins[source].at[:, pl.ds(pl.multiple_of(base(1 - c), 128), n)]
            spot = out.at[a, b, z, pl.ds(pl.multiple_of(c * rows, rows), rows), cols]
            return [pltpu.make_async_copy(mine, spot, self.local_sem.at[t]), send(theirs, spot, 0, grid.device(a, b, z, 1 - c))]
        if order[stage - 2] == "b":
            block = out.at[a, b, :, :, cols] if stage == 2 else out.at[:, b, :, :, cols]
            return [send(block, block, k, grid.device(a, lax.rem(b + k, nb), z, c)) for k in range(1, nb)]
        block = out.at[a, b, :, :, cols] if stage == 2 else out.at[a, :, :, :, cols]
        return [send(block, block, nb, grid.device(1 - a, b, z, c))]

    def hop(self, t, step, begin):
        a, b, z, c = self.place
        nz, nb = self.grid.nz, self.grid.nb
        _, _, result, col, n, _ = self.chunks[t]
        out, cols = self.outs[result], pl.ds(col, n)
        for side, way in enumerate((1, -1)):
            slot = nb + 1 + side * (nz - 1) + step - 1
            there, arriving = z + way, z - way * step
            going = there - way * step
            inside = (there >= 0) & (there < nz) & (going >= 0) & (going < nz)
            coming = (arriving >= 0) & (arriving < nz)

            def link(which, slot=slot, there=there):
                block = out.at[a, b, which, :, cols]
                return remote(block, block, self.send_sem.at[t, slot], self.recv_sem.at[t, slot], self.grid.device(a, b, there, c))

            if begin:
                pl.when(inside)(lambda link=link, going=going: link(going).start())
            else:
                pl.when(inside)(lambda link=link, going=going: link(going).wait_send())
                pl.when(coming)(lambda link=link, arriving=arriving: link(arriving).wait_recv())

    def begin(self, group, stage):
        for t in group:
            start(self.copies(t, stage))

    def end(self, group, stage):
        for t in group:
            finish(self.copies(t, stage))

    def ticks(self, whole, partial):
        groups, nz = whole + partial, self.grid.nz

        def advance(u, at):
            group = groups[u]
            if at == 0:
                self.end(group, 0)
            elif at < nz:
                for t in group:
                    self.hop(t, at, False)
            else:
                self.end(group, 2)
            for t in group:
                if at < nz - 1:
                    self.hop(t, at + 1, True)
                elif u < len(whole):
                    start(self.copies(t, 2 if at == nz - 1 else 3))

        def first():
            for group in groups:
                self.begin(group, 0)

        enter = [u if u < len(whole) else len(whole) + (u - len(whole)) // 2 for u in range(len(groups))]

        def tick(now):
            for u in range(len(groups)):
                if 0 <= now - enter[u] <= (nz if u < len(whole) else nz - 1):
                    advance(u, now - enter[u])

        def last():
            for group in whole:
                self.end(group, 3)

        return [first] + [functools.partial(tick, now) for now in range(max(enter) + nz + 1)] + [last]


def gather_sems(grid, chunks):
    slots = 2 * grid.nz + grid.nb - 1
    return [
        pltpu.SemaphoreType.DMA((len(chunks),)),
        pltpu.SemaphoreType.DMA((len(chunks), slots)),
        pltpu.SemaphoreType.DMA((len(chunks), slots)),
    ]


def fold_copies(grid, place, order, stage, part, first, second, sems):
    a, b, z, c = place
    nz, nb = grid.nz, grid.nb

    def send(src, dst, slot, device):
        return remote(src, dst, sems[0].at[slot], sems[1].at[slot], device)

    if (order == "ab") == (stage == 0):
        src = part.at[1 - a] if stage == 0 else first.at[0, 1 - a]
        dst = first.at[0] if stage == 0 else second.at[0]
        return [send(src, dst, nz + nb - 1, grid.device(1 - a, b, z, c))]
    found = []
    for k in range(1, nb):
        to = lax.rem(b + k, nb)
        src = part.at[:, to] if stage == 0 else first.at[0, to]
        dst = first.at[k - 1] if stage == 0 else second.at[k - 1]
        found.append(send(src, dst, nz + k - 1, grid.device(a, to, z, c)))
    return found


def fold_add(grid, place, order, stage, own, first, second):
    a, b, z, c = place
    nz = grid.nz
    if stage == 0:

        def step(i, carry):
            o, j = i // nz, lax.rem(i, nz)
            total = own[o, j].astype(F32)
            for k in range(first.shape[0]):
                total = total + first[k, o, j].astype(F32)
            first[0, o, j] = total.astype(BF16)
            return carry

        lax.fori_loop(0, first.shape[1] * nz, step, 0)
        return
    mine = b if order == "ab" else a

    def step(j, carry):
        total = first[0, mine, j].astype(F32)
        for k in range(second.shape[0]):
            total = total + second[k, j].astype(F32)
        second[0, j] = total.astype(BF16)
        return carry

    lax.fori_loop(0, nz, step, 0)


def fold_scratch(grid, order, rows, n):
    na, nb, nz = grid.na, grid.nb, grid.nz
    own = pltpu.VMEM((nb if order == "ab" else na, nz, rows, n), BF16)
    first = pltpu.VMEM((1, nb, nz, rows, n) if order == "ab" else (nb - 1, na, nz, rows, n), BF16)
    second = pltpu.VMEM((nb - 1, nz, rows, n) if order == "ab" else (1, nz, rows, n), BF16)
    return own, first, second


class Summing:
    def __init__(self, grid, mine, held, total, done, send_sem, recv_sem):
        self.n_seq, self.count = grid.n_seq, grid.n_dp * grid.n_seq
        self.mine, self.held, self.total, self.done = mine, held, total, done
        self.send_sem, self.recv_sem = send_sem, recv_sem
        self.rows = total.shape[0]
        self.me = lax.axis_index("dp") * grid.n_seq + lax.axis_index("seq")

    def device(self, k):
        other = lax.rem(self.me + k, self.count)
        return other, (other // self.n_seq, lax.rem(other, self.n_seq))

    def part(self, ref, k):
        return ref.at[pl.ds(pl.multiple_of(k * self.rows, self.rows), self.rows)]

    def greet(self):
        barrier = pltpu.get_barrier_semaphore()

        def step(k, carry):
            pl.semaphore_signal(barrier, inc=1, device_id=self.device(k)[1], device_id_type=MESH)
            return carry

        lax.fori_loop(1, self.count, step, 0)

    def settle(self, dst, slot):
        most = pl.ds(0, (self.count - 1) * self.rows)
        remote(self.mine.at[most], dst.at[most], self.send_sem.at[slot], self.recv_sem.at[slot], self.device(1)[1]).wait()

    def deal(self):
        def step(k, carry):
            other, place = self.device(k)
            remote(self.part(self.mine, other), self.part(self.held, self.me), self.send_sem.at[0], self.recv_sem.at[0], place).start()
            return carry

        lax.fori_loop(1, self.count, step, 0)
        at = pl.ds(pl.multiple_of(self.me * self.rows, self.rows), self.rows)
        self.held[at, :] = self.mine[at, :]

    def tell(self):
        self.settle(self.held, 0)

        def add(k, carry):
            return carry + self.held[pl.ds(pl.multiple_of(k * self.rows, self.rows), self.rows), :]

        self.total[...] = lax.fori_loop(0, self.count, add, jnp.zeros(self.total.shape, F32))

        def step(k, carry):
            place = self.device(k)[1]
            remote(self.total, self.part(self.done, self.me), self.send_sem.at[1], self.recv_sem.at[1], place).start()
            return carry

        lax.fori_loop(1, self.count, step, 0)
        self.done[pl.ds(pl.multiple_of(self.me * self.rows, self.rows), self.rows), :] = self.total[...]

    def close(self):
        self.settle(self.done, 1)


def blend(h_ref, coeffs, streams_ref):
    hist, block, width = h_ref.shape[0], h_ref.shape[2], h_ref.shape[3]
    spread = [jnp.broadcast_to(coeffs[:, k : k + 1], (block, 128)) for k in range(4 * hist)]
    for at in range(0, width, 128):
        lanes = slice(at, at + 128)
        inputs = [h_ref[j, 0, :, lanes].astype(F32) for j in range(hist)]
        for c in range(4):
            total = spread[c * hist] * inputs[0]
            for j in range(1, hist):
                total = total + spread[c * hist + j] * inputs[j]
            streams_ref[c, :, lanes] = total
    return spread


def mix_kernel(grid, rows, chunks, whole, partial, h_ref, g_ref, gain_ref, inner_ref, outer_ref, bias_ref, sgain_ref, sbias_ref, *refs):
    ins, (lowered_ref, gpair_ref, last_ref, pre_ref, coeffs_ref, cos_ref, above_ref, below_ref) = refs[:4], refs[4:12]
    weights_ref, outs = refs[12], refs[13:15]
    streams_ref, held_ref, local_sem, send_sem, recv_sem, pair_local, pair_send, pair_recv = refs[15:]
    i, steps = pl.program_id(0), pl.num_programs(0)
    a, b, z, c = place = grid.here()
    block = h_ref.shape[2]
    outs = [weights_ref.at[k] for k in range(4)] + list(outs)
    events = Gathering(grid, place, rows, chunks, ins, outs, local_sem, send_sem, recv_sem).ticks(whole, partial)
    other = grid.device(a, b, z, 1 - c)

    def pair(k, src, dst):
        return [
            pltpu.make_async_copy(src, dst, pair_local.at[k]),
            remote(src, dst, pair_send.at[k], pair_recv.at[k], other),
        ]

    grads = lambda: pair(0, g_ref.at[0], gpair_ref.at[c])
    lowereds = lambda: pair(1, held_ref, lowered_ref.at[:, c])

    @pl.when(i == 0)
    def _():
        grid.greet(*place)
        events[0]()
        start(grads())

    for n, at in enumerate((0, 2, 3, 4)):

        @pl.when(i == at)
        def _(n=n):
            events[n + 1]()

    @pl.when(i == 2)
    def _():
        both, wide = cos_ref.shape
        half = ROT_DIMS // 2
        place_in = lax.rem(lax.broadcasted_iota(jnp.int32, (1, wide), 1), HEAD_DIM)
        step = lax.rem(place_in, half)
        freq = jnp.ones((1, wide), F32)
        for k in range(1, half):
            freq = jnp.where(step == k, 10000.0 ** (-2.0 * k / ROT_DIMS), freq)
        angles = (z * both + lax.broadcasted_iota(jnp.int32, (both, wide), 0)).astype(F32) * freq
        turned = place_in < ROT_DIMS
        sine = jnp.where(turned, jnp.sin(angles), 0.0)
        cos_ref[...] = jnp.where(turned, jnp.cos(angles), 1.0)
        above_ref[...] = jnp.where(place_in < half, -sine, 0.0)
        below_ref[...] = jnp.where(place_in < half, 0.0, sine)

    last = h_ref[h_ref.shape[0] - 1, 0].astype(F32)
    r = lax.rsqrt(jnp.mean(last * last, axis=1, keepdims=True) + EPS)
    scaled_low = (last * r * row(gain_ref)).astype(BF16)
    pre = against(scaled_low, inner_ref[...])
    pre_ref[...] = pre
    coeffs = product((pre * phi(pre)).astype(BF16), outer_ref[...]) + bias_ref[...].astype(F32)
    coeffs_ref[...] = coeffs
    blend(h_ref, coeffs, streams_ref)
    at = pl.ds(pl.multiple_of(i * block, block), block)
    for k in range(4):
        stream = streams_ref[k]
        centered = stream - jnp.mean(stream, axis=1, keepdims=True)
        rs = lax.rsqrt(jnp.mean(centered * centered, axis=1, keepdims=True) + EPS)
        gain, bias = sgain_ref[k : k + 1, :].astype(F32), sbias_ref[k : k + 1, :].astype(F32)
        held_ref[k, at, :] = (centered * rs * gain + bias).astype(BF16)
    last_ref[...] = streams_ref[3]

    @pl.when(i == steps - 1)
    def _():
        start(lowereds())
        for event in events[5:]:
            event()
        finish(grads())
        finish(lowereds())


def mix_forward(grid, history, cotangent, params, weights, chunks, groups, partial, widths, collective_id):
    hist, _, tokens, width = history.shape
    mix = params[1].shape[0]
    block = 64
    rows = weights[0].shape[0]
    whole = pl.BlockSpec(memory_space=pltpu.VMEM)
    anywhere = pl.BlockSpec(memory_space=pl.ANY)
    part = lambda n: pl.BlockSpec((block, n), lambda i: (i, 0))
    chips = (grid.na, grid.nb, grid.nz, 2 * rows)
    results = pl.pallas_call(
        functools.partial(mix_kernel, grid, rows, chunks, groups, partial),
        grid=(tokens // block,),
        out_shape=[
            jax.ShapeDtypeStruct((4, 2, tokens, width), BF16),
            jax.ShapeDtypeStruct((2, tokens, width), BF16),
            jax.ShapeDtypeStruct((tokens, width), F32),
            jax.ShapeDtypeStruct((tokens, mix), F32),
            jax.ShapeDtypeStruct((tokens, mix), F32),
        ]
        + [jax.ShapeDtypeStruct((2 * tokens, 128), F32)] * 3
        + [jax.ShapeDtypeStruct((4, *chips, width // 2), BF16)]
        + [jax.ShapeDtypeStruct((*chips, w), BF16) for w in widths],
        in_specs=[pl.BlockSpec((hist, 1, block, width), lambda i: (0, 0, i, 0))] + [whole] * 11,
        out_specs=[anywhere, anywhere, part(width), part(mix), part(mix)]
        + [pl.BlockSpec((2 * tokens, 128), lambda i: (0, 0))] * 3
        + [anywhere] * 3,
        scratch_shapes=[
            pltpu.VMEM((4, block, width), F32),
            pltpu.VMEM((4, tokens, width), BF16),
            *gather_sems(grid, chunks),
            pltpu.SemaphoreType.DMA((2,)),
            pltpu.SemaphoreType.DMA((2,)),
            pltpu.SemaphoreType.DMA((2,)),
        ],
        compiler_params=pltpu.CompilerParams(collective_id=collective_id, has_side_effects=True, vmem_limit_bytes=VMEM_LIMIT),
        cost_estimate=pl.CostEstimate(flops=tokens * width * 80, bytes_accessed=history.size * 40, transcendentals=0),
        name="mix_forward",
    )(history, cotangent, *params, *weights)
    lowered, gpair, last, pre, coeffs = results[:5]
    return (
        lowered.reshape(4, 2 * tokens, width),
        gpair.reshape(2 * tokens, width),
        last,
        pre,
        coeffs,
        results[5:8],
        results[8].reshape(4, width, width // 2),
        results[9:],
    )


def small_rows(width, mix, hidden_width):
    wl, padded = width // 128, -(-mix // 8) * 8
    sizes = [wl, wl * padded, padded, 8, 4 * wl, 4 * wl, 3 * wl, wl, hidden_width // 128]
    firsts = [sum(sizes[:k]) for k in range(len(sizes))]
    return firsts, sum(sizes)


def unmix_kernel(h_ref, own_ref, theirs_ref, g_ref, pre_ref, coeffs_ref, gain_ref, inner_ref, outer_ref, sgain_ref,
                 hist_ref, sgg_ref, sbg_ref, gg_ref, ig_ref, og_ref, bg_ref, ob_ref,
                 streams_ref, sg_ref, scaled_ref, mpg_ref, hidden_ref, cgl_ref):
    i, steps = pl.program_id(0), pl.num_programs(0)
    hist, block, width = h_ref.shape[0], h_ref.shape[2], h_ref.shape[3]
    mix = 4 * hist

    @pl.when(i == 0)
    def _():
        for ref in (sgg_ref, sbg_ref, gg_ref, bg_ref, ob_ref):
            ref[...] = jnp.zeros_like(ref)

    def down(x):
        return jnp.sum(x, axis=0, keepdims=True)

    coeffs = coeffs_ref[...]
    spread = blend(h_ref, coeffs, streams_ref)
    grad = g_ref[0].astype(F32)
    ob_ref[...] += down(grad)
    for k in range(4):
        stream = streams_ref[k]
        centered = stream - jnp.mean(stream, axis=1, keepdims=True)
        rs = lax.rsqrt(jnp.mean(centered * centered, axis=1, keepdims=True) + EPS)
        n = centered * rs
        ng = own_ref[k] + theirs_ref[k].astype(F32)
        sgg_ref[k : k + 1, :] += down(ng * n)
        sbg_ref[k : k + 1, :] += down(ng)
        w = ng * sgain_ref[k : k + 1, :].astype(F32)
        pulled = rs * (w - jnp.mean(w, axis=1, keepdims=True) - n * jnp.mean(w * n, axis=1, keepdims=True))
        sg_ref[k] = pulled + grad if k == 3 else pulled

    lane = lax.broadcasted_iota(jnp.int32, (block, mix), 1)
    cg = jnp.zeros((block, mix), F32)
    for j in range(hist):
        value = h_ref[j, 0].astype(F32)
        for k in range(4):
            cg = jnp.where(lane == k * hist + j, jnp.sum(value * sg_ref[k], axis=1, keepdims=True), cg)
    bg_ref[...] += down(cg)
    cg_low = cg.astype(BF16)
    pre = pre_ref[...]
    at = pl.ds(pl.multiple_of(i * block, block), block)
    mpg = (against(cg_low, outer_ref[...]) * gelu_slope(pre)).astype(BF16)
    last = h_ref[hist - 1, 0].astype(F32)
    r = lax.rsqrt(jnp.mean(last * last, axis=1, keepdims=True) + EPS)
    gain = row(gain_ref)
    scaled_ref[at, :] = (last * r * gain).astype(BF16)
    mpg_ref[at, :] = mpg
    hidden_ref[at, :] = (pre * phi(pre)).astype(BF16)
    cgl_ref[at, :] = cg_low
    scaled_grad = product(mpg, inner_ref[...])
    gg_ref[...] += down(scaled_grad * last * r)
    w = scaled_grad * gain
    last_grad = r * (w - last * (r * r) * jnp.mean(w * last, axis=1, keepdims=True))
    for from_ in range(0, width, 128):
        lanes = slice(from_, from_ + 128)
        pulls = [sg_ref[k, :, lanes] for k in range(4)]
        for j in range(hist):
            total = spread[j] * pulls[0]
            for k in range(1, 4):
                total = total + spread[k * hist + j] * pulls[k]
            hist_ref[j, 0, :, lanes] = total + last_grad[:, lanes] if j == hist - 1 else total

    @pl.when(i == steps - 1)
    def _():
        ig_ref[...] = inner(mpg_ref[...], scaled_ref[...])
        og_ref[...] = inner(hidden_ref[...], cgl_ref[...])


def mix_backward(history, own, theirs, cotangent, pre, coeffs, params):
    hist, _, tokens, width = history.shape
    mix = pre.shape[1]
    block = 64
    whole = pl.BlockSpec(memory_space=pltpu.VMEM)
    part = lambda n: pl.BlockSpec((block, n), lambda i: (i, 0))
    four = pl.BlockSpec((4, block, width), lambda i: (0, i, 0))
    story = pl.BlockSpec((hist, 1, block, width), lambda i: (0, 0, i, 0))
    small = [(4, width), (4, width), (1, width), (mix, width), (mix, mix), (1, mix), (1, width)]
    return pl.pallas_call(
        unmix_kernel,
        grid=(tokens // block,),
        out_shape=[jax.ShapeDtypeStruct(history.shape, F32)] + [jax.ShapeDtypeStruct(shape, F32) for shape in small],
        in_specs=[story, four, four, pl.BlockSpec((1, block, width), lambda i: (0, i, 0)), part(mix), part(mix)] + [whole] * 4,
        out_specs=[story] + [pl.BlockSpec(shape, lambda i: (0, 0)) for shape in small],
        scratch_shapes=[
            pltpu.VMEM((4, block, width), F32),
            pltpu.VMEM((4, block, width), F32),
            pltpu.VMEM((tokens, width), BF16),
            pltpu.VMEM((tokens, mix), BF16),
            pltpu.VMEM((tokens, mix), BF16),
            pltpu.VMEM((tokens, mix), BF16),
        ],
        compiler_params=pltpu.CompilerParams(vmem_limit_bytes=VMEM_LIMIT),
        cost_estimate=pl.CostEstimate(flops=tokens * width * 1000, bytes_accessed=history.size * 12, transcendentals=0),
        name="mix_backward",
    )(history, own, theirs, cotangent, pre, coeffs, *params)


def finish_kernel(grid, orders, n_kept, *refs):
    nz = grid.nz
    kept, refs = refs[:n_kept], refs[n_kept:]
    came_a, came_b, refs = refs[:1], refs[1 : grid.nb], refs[grid.nb :]
    sum_ref, folded, refs = refs[0], refs[1 : 1 + nz], refs[1 + nz :]
    sgg_ref, sbg_ref, gg_ref, ig_ref, og_ref, bg_ref, ob_ref, hb_ref, eb_ref = refs[:9]
    done_ref, outs, refs = refs[9], refs[10:14], refs[14:]
    first, second, third, final, refs = refs[:4], refs[4:8], refs[8:12], refs[12:18], refs[18:]
    sums = Summing(grid, *refs[:3], done_ref, *refs[3:5])
    local_sem, send_sem, recv_sem = refs[5:]
    a, b, z, c = place = grid.here()
    width, mix = gg_ref.shape[1], bg_ref.shape[1]
    wl, padded, hidden_rows = width // 128, -(-mix // 8) * 8, eb_ref.shape[1] // 128
    firsts, _ = small_rows(width, mix, 2 * eb_ref.shape[1])
    half = width // 2
    spots = [(0, lambda core: core * half), (0, lambda core: width + core * half), (0, lambda core: 2 * width + core * half),
             (1, lambda core: core * half), (2, lambda core: core * eb_ref.shape[1]), (3, lambda core: core * eb_ref.shape[1])]

    def copies(t, stage):
        if stage == 1:
            return fold_copies(grid, place, orders[t], 1, None, first[t], second[t], (send_sem.at[t], recv_sem.at[t]))
        if stage == 2:
            return [
                remote(second[t].at[0, lax.rem(z + k, nz)], third[t].at[k - 1], send_sem.at[t, k], recv_sem.at[t, k],
                       grid.device(a, b, lax.rem(z + k, nz), c))
                for k in range(1, nz)
            ]
        result, base = spots[t]
        n = final[t].shape[-1]
        spot = outs[result].at[:, pl.ds(pl.multiple_of(base(c), 128), n)]
        return [
            remote(final[t].at[1 - c], spot, send_sem.at[t, 0], recv_sem.at[t, 0], grid.device(a, b, z, 1 - c)),
            pltpu.make_async_copy(final[t].at[c], spot, local_sem.at[t]),
        ]

    def add_first(t):
        def step(i, carry):
            o, j = i // nz, lax.rem(i, nz)
            total = kept[t][o, j].astype(F32)
            for piece in came_a if orders[t] == "ab" else came_b:
                total = total + piece[t // 2, o, j].astype(F32)
            first[t][0, o, j] = total.astype(BF16)
            return carry

        lax.fori_loop(0, first[t].shape[1] * nz, step, 0)

    sums.greet()
    add_first(0)
    add_first(1)
    pl.semaphore_wait(pltpu.get_barrier_semaphore(), sums.count - 1)
    for t in range(2):
        start(copies(t, 1))
    add_first(2)
    add_first(3)

    mine = sums.mine
    mine[...] = jnp.zeros_like(mine)
    for l in range(wl):
        lanes = slice(l * 128, (l + 1) * 128)
        mine[firsts[0] + l : firsts[0] + l + 1, :] = gg_ref[:, lanes]
        mine[firsts[1] + l * padded : firsts[1] + l * padded + mix, :] = ig_ref[:, lanes]
        mine[firsts[4] + 4 * l : firsts[4] + 4 * l + 4, :] = sgg_ref[:, lanes]
        mine[firsts[5] + 4 * l : firsts[5] + 4 * l + 4, :] = sbg_ref[:, lanes]
        mine[firsts[7] + l : firsts[7] + l + 1, :] = ob_ref[:, lanes]
    mine[firsts[2] : firsts[2] + mix, 0:mix] = og_ref[...]
    mine[firsts[3] : firsts[3] + 1, 0:mix] = bg_ref[...]
    for k in range(3):
        for l in range(wl // 2):
            mine[pl.ds(firsts[6] + k * wl + c * (wl // 2) + l, 1), :] = hb_ref[k : k + 1, l * 128 : (l + 1) * 128]
    for l in range(hidden_rows):
        mine[pl.ds(firsts[8] + c * hidden_rows + l, 1), :] = eb_ref[:, l * 128 : (l + 1) * 128]
    sums.deal()

    for t in range(2):
        total = folded[0][t].astype(F32)
        for piece in folded[1:]:
            total = total + piece[t].astype(F32)
        at = 0
        for piece in (sum_ref[t], total):
            n = piece.shape[1]
            final[4 + t][:, :, at : at + n] = piece.reshape(2, -1, n)
            at += n
        start(copies(4 + t, 3))
    for t in range(4):
        finish(copies(t, 1))
        if t < 2:
            start(copies(t + 2, 1))
        fold_add(grid, place, orders[t], 1, None, first[t], second[t])
        start(copies(t, 2))
    sums.tell()
    for t in range(4):
        finish(copies(t, 2))
        total = second[t][0, z].astype(F32)
        for k in range(nz - 1):
            total = total + third[t][k].astype(F32)
        final[t][...] = total.reshape(final[t].shape)
        start(copies(t, 3))
    sums.close()
    for t in range(6):
        finish(copies(t, 3))


def finish_sums(grid, orders, kept, came, folded, smalls, collective_id):
    sgg, _, _, ig, og, bg, _, hb, eb = smalls
    mix, width = ig.shape
    hidden_width = 2 * eb.shape[1]
    nz = grid.nz
    rows, n = kept[0].shape[-2:]
    devices = grid.n_dp * grid.n_seq
    each = -(-small_rows(width, mix, hidden_width)[1] // (devices * 8)) * 8
    vmem = pl.BlockSpec(memory_space=pltpu.VMEM)
    owned = [3 * width, width, hidden_width, hidden_width]
    folds = [fold_scratch(grid, order, rows, n) for order in orders]
    operands = list(kept) + list(came) + list(folded) + list(smalls)
    return pl.pallas_call(
        functools.partial(finish_kernel, grid, orders, len(kept)),
        out_shape=[jax.ShapeDtypeStruct((devices * each, 128), F32)] + [jax.ShapeDtypeStruct((rows // 2, w), F32) for w in owned],
        in_specs=[vmem] * len(operands),
        out_specs=[vmem] + [pl.BlockSpec(memory_space=pl.ANY)] * len(owned),
        scratch_shapes=[f for _, f, _ in folds]
        + [s for _, _, s in folds]
        + [pltpu.VMEM((nz - 1, rows, n), BF16)] * 4
        + [pltpu.VMEM((2, rows // 2, n), F32)] * 4
        + [pltpu.VMEM((2, rows // 2, hidden_width // 2), F32)] * 2
        + [
            pltpu.VMEM((devices * each, 128), F32),
            pltpu.VMEM((devices * each, 128), F32),
            pltpu.VMEM((each, 128), F32),
            pltpu.SemaphoreType.DMA((2,)),
            pltpu.SemaphoreType.DMA((2,)),
            pltpu.SemaphoreType.DMA((6,)),
            pltpu.SemaphoreType.DMA((6, nz + grid.nb)),
            pltpu.SemaphoreType.DMA((6, nz + grid.nb)),
        ],
        compiler_params=pltpu.CompilerParams(collective_id=collective_id, has_side_effects=True, vmem_limit_bytes=VMEM_LIMIT),
        cost_estimate=pl.CostEstimate(flops=0, bytes_accessed=100 * width * width, transcendentals=0),
        name="finish_sums",
    )(*operands)


def hand_kernel(mix, hidden_width, done, out_ref, *refs):
    owned, placed_ref, small, outs = refs[:4], refs[4], refs[5:14], refs[14:]
    width = out_ref.shape[1]
    wl, padded, hidden_rows = width // 128, -(-mix // 8) * 8, hidden_width // 256
    firsts, _ = small_rows(width, mix, hidden_width)
    placed_ref[...] = out_ref[...]
    outs, again = outs[:4], outs[4]
    for src, dst in zip(owned, outs):
        dst[...] = src[...]
    for l in range(wl):
        lanes = slice(l * 128, (l + 1) * 128)
        small[0][:, lanes] = done[firsts[0] + l : firsts[0] + l + 1, :]
        small[1][:, lanes] = done[firsts[1] + l * padded : firsts[1] + l * padded + mix, :]
        small[4][:, lanes] = done[firsts[4] + 4 * l : firsts[4] + 4 * l + 4, :]
        small[5][:, lanes] = done[firsts[5] + 4 * l : firsts[5] + 4 * l + 4, :]
        small[7][:, lanes] = again[:, lanes] = done[firsts[7] + l : firsts[7] + l + 1, :]
    small[2][...] = done[firsts[2] : firsts[2] + mix, 0:mix]
    small[3][...] = done[firsts[3] : firsts[3] + 1, 0:mix]
    for l in range(3 * wl):
        small[6][:, l * 128 : (l + 1) * 128] = done[firsts[6] + l : firsts[6] + l + 1, :]
    for l in range(2 * hidden_rows):
        small[8][:, l * 128 : (l + 1) * 128] = done[firsts[8] + l : firsts[8] + l + 1, :]


def hand_over(summed, layer_out, owned, mix, hidden_width):
    width = layer_out.shape[1]
    small = [(1, width), (mix, width), (mix, mix), (1, mix), (4, width), (4, width), (1, 3 * width), (1, width), (1, hidden_width)]
    vmem = pl.BlockSpec(memory_space=pltpu.VMEM)
    return pl.pallas_call(
        functools.partial(hand_kernel, mix, hidden_width),
        out_shape=[jax.ShapeDtypeStruct(layer_out.shape, BF16)]
        + [jax.ShapeDtypeStruct(shape, F32) for shape in small]
        + [jax.ShapeDtypeStruct(x.shape, F32) for x in owned]
        + [jax.ShapeDtypeStruct((1, width), F32)],
        in_specs=[vmem] * 6,
        out_specs=[vmem] * 15,
        name="hand_over",
    )(summed, layer_out, *owned)


def exchange_kernel(grid, width, chunks, groups, low_ref, g_ref, w_ref, bias_ref, cos_ref, above_ref, below_ref, _e, _c,
                    dealt_ref, e_ref, c_ref, sent_ref, bias_full, deal_send, deal_recv, local_sem, send_sem, recv_sem):
    i, steps = pl.program_id(0), pl.num_programs(0)
    a, b, z, c = place = grid.here()
    nz = grid.nz
    work = Gathering(grid, place, None, chunks, None, [e_ref, c_ref], local_sem, send_sem, recv_sem)

    def link(to):
        k = lax.rem(to - z + nz, nz)
        return remote(sent_ref.at[to], dealt_ref.at[z], deal_send.at[k], deal_recv.at[k], grid.device(a, b, to, c))

    def stay():
        return pltpu.make_async_copy(sent_ref.at[z], dealt_ref.at[z], deal_send.at[0])

    @pl.when(i == 0)
    def _():
        grid.greet(*place)
        for group in groups:
            work.begin(group, 2)
        bias_full[...] = bias_ref[...].astype(F32)

    wide = w_ref.shape[2]
    each = wide // width
    tables = [jnp.concatenate([t[...]] * max(wide // 128, 1), axis=1) for t in (cos_ref, above_ref, below_ref)]
    third = bias_full.shape[0] // 3

    def bias(n):
        first_row = n * third + c * (third // 2) + i * (wide // 128)
        return jnp.concatenate([bias_full[pl.ds(first_row + l, 1), :] for l in range(wide // 128)], axis=1)

    q = rotate(product(low_ref[0], w_ref[0]) + bias(0), tables, 1.0)
    k = rotate(product(low_ref[1], w_ref[1]) + bias(1), tables, 1.0)
    v = product(low_ref[2], w_ref[2]) + bias(2)
    g = product(g_ref[...], w_ref[3])
    for n, x in enumerate((q, k, v, g)):
        x = x.astype(BF16)
        for m in range(each):
            sent_ref[i * each + m, :, n * width : (n + 1) * width] = x[:, m * width : (m + 1) * width]
    for m in range(each):
        to = i * each + m
        pl.when(to != z)(lambda to=to: link(to).start())
        pl.when(to == z)(lambda: stay().start())

    @pl.when(i == steps - 1)
    def _():
        for group in groups:
            work.end(group, 2)
            work.begin(group, 3)
        for m in range(1, nz):
            link(lax.rem(z + m, nz)).wait()
        stay().wait()
        for group in groups:
            work.end(group, 3)


def exchange(grid, lowered, grad_low, weights, biases, tables, started, chunks, groups, own_width, collective_id):
    both, width = grad_low.shape
    nz = grid.nz
    wide = 2 * own_width
    whole = pl.BlockSpec(memory_space=pltpu.VMEM)
    anywhere = pl.BlockSpec(memory_space=pl.ANY)
    dealt, *full = pl.pallas_call(
        functools.partial(exchange_kernel, grid, own_width, chunks, groups),
        grid=(nz // 2,),
        out_shape=[jax.ShapeDtypeStruct((nz, both, 4 * own_width), BF16)] + [jax.ShapeDtypeStruct(x.shape, x.dtype) for x in started],
        in_specs=[
            pl.BlockSpec((3, both, width), lambda i: (0, 0, 0)),
            whole,
            pl.BlockSpec((4, width, wide), lambda i: (0, 0, i)),
            whole,
        ]
        + [whole] * 3
        + [anywhere] * 2,
        out_specs=[anywhere] * 3,
        input_output_aliases={7: 1, 8: 2},
        scratch_shapes=[
            pltpu.VMEM((nz, both, 4 * own_width), BF16),
            pltpu.VMEM(biases.shape, F32),
            pltpu.SemaphoreType.DMA((nz,)),
            pltpu.SemaphoreType.DMA((nz,)),
            *gather_sems(grid, chunks),
        ],
        compiler_params=pltpu.CompilerParams(collective_id=collective_id, has_side_effects=True, vmem_limit_bytes=VMEM_LIMIT),
        cost_estimate=pl.CostEstimate(flops=2 * both * weights.size, bytes_accessed=weights.size * 60, transcendentals=0),
        name="exchange",
    )(lowered, grad_low, weights, biases, *tables, *started)
    return dealt, [x.reshape(-1, x.shape[-1]) for x in full]


def unproject_kernel(grid, width, orders, *all_refs):
    nz = grid.nz
    mids, lates, last_parts, all_refs = all_refs[:nz], all_refs[nz : 2 * nz], all_refs[2 * nz : 2 * nz + 2], all_refs[2 * nz + 2 :]
    (col_ref, low_ref, g_ref, w_ref, feed_ref, normed_ref, last_ref, bias_ref, bias2_ref, cos_ref, above_ref,
     below_ref, own_ref, theirs_ref, hb_ref, out_ref, sum_ref, *refs) = all_refs
    nb = grid.nb
    lasts, refs = refs[:nz], refs[nz:]
    kept, over_a, over_b, refs = refs[:4], refs[4], refs[5 : 4 + nb], refs[4 + nb :]
    grad_ref, sending_ref, partial_ref, mine_ref, arrived_ref, along_ref, split_sem, send_sem, recv_sem, along_send, along_recv = refs[:11]
    keep_refs, firsts, seconds, (fold_send, fold_recv, late_sem) = refs[11:13], refs[13:15], refs[15:17], refs[17:]
    i = pl.program_id(0)
    a, b, z, c = grid.here()
    tokens = out_ref.shape[0]
    other = grid.device(a, b, z, 1 - c)
    own_rows = pl.ds(pl.multiple_of(c * tokens, tokens), tokens)
    their_rows = pl.ds(pl.multiple_of((1 - c) * tokens, tokens), tokens)

    def swap(k):
        return [remote(sending_ref.at[k], theirs_ref.at[k], send_sem.at[k], recv_sem.at[k], other)]

    def swap_out():
        return [remote(partial_ref, arrived_ref, send_sem.at[4], recv_sem.at[4], other)]

    def along():
        return [
            remote(mids[k], along_ref.at[k - 1], along_send.at[k - 1], along_recv.at[k - 1], grid.device(a, b, lax.rem(z + k, nz), c))
            for k in range(1, nz)
        ]

    def fold(t, stage):
        if stage < 2:
            order = ("ab", "ba")[t]
            found = fold_copies(grid, (a, b, z, c), order, stage, last_parts[t], firsts[t], seconds[t], (fold_send.at[t], fold_recv.at[t]))
            if stage == 0:
                kept_part = last_parts[t].at[a] if order == "ab" else last_parts[t].at[:, b]
                found.append(pltpu.make_async_copy(kept_part, keep_refs[t], late_sem.at[t]))
            return found
        n = seconds[t].shape[-1]
        return [
            pltpu.make_async_copy(seconds[t].at[0, lax.rem(z + k, nz)], lasts[k].at[t, :, pl.ds(n, n)], late_sem.at[2 + t * nz + k])
            for k in range(nz)
        ]

    def settle(stage):
        for t in range(2):
            finish(fold(t, stage))
            fold_add(grid, (a, b, z, c), ("ab", "ba")[t], stage, keep_refs[t], firsts[t], seconds[t])
            start(fold(t, stage + 1))

    def place_lates():
        n = lates[0].shape[-1]
        return [pltpu.make_async_copy(lates[k], lasts[k].at[:, :, pl.ds(0, n)], late_sem.at[2 + 2 * nz + k]) for k in range(nz)]

    def split(k):
        grad = grad_ref.at[k]
        if orders[k] == "ab":
            found = [(grad.at[a], kept[k]), (grad.at[1 - a], over_a.at[k // 2])]
        else:
            found = [(grad.at[:, b], kept[k])]
            found += [(grad.at[:, lax.rem(b + m, nb)], over_b[m - 1].at[k // 2]) for m in range(1, nb)]
        return [pltpu.make_async_copy(src, dst, split_sem.at[k, n]) for n, (src, dst) in enumerate(found)]

    def piece(n):
        return jnp.concatenate([col_ref[m, :, n * width : (n + 1) * width] for m in range(nz)], axis=1)

    def keep(k, grad):
        grad_ref[k] = grad.astype(BF16).reshape(grad_ref.shape[1:])
        start(split(k))

    @pl.when(i == 0)
    def _():
        grid.greet(a, b, z, c)
        for t in range(2):
            start(fold(t, 0))
        start(along())
        start(place_lates())
        mine_ref[...] = piece(0)
        partial_ref[...] = against(mine_ref[their_rows, :], w_ref[0]) + feed_ref[their_rows, :]
        sending_ref[3] = normed_ref[their_rows, :].astype(BF16)
        start(swap_out())
        start(swap(3))
        own_ref[0] = normed_ref[own_rows, :]
        out = against(mine_ref[own_rows, :], w_ref[0]) + feed_ref[own_rows, :] + last_ref[...] + (row(bias_ref) + row(bias2_ref))
        keep(3, inner(g_ref[...], mine_ref[...]))
        finish(swap_out())
        out_ref[...] = (out + arrived_ref[...]).astype(BF16)

    for k in range(3):

        @pl.when(i == k + 1)
        def _(k=k):
            if k == 2:
                settle(0)
            grad = piece(k + 1).astype(F32)
            if k < 2:
                tables = [jnp.concatenate([t[...]] * (grad.shape[1] // 128), axis=1) for t in (cos_ref, above_ref, below_ref)]
                grad = rotate(grad, tables, -1.0)
            hb_ref[k : k + 1, :] = jnp.sum(grad, axis=0, keepdims=True)
            mine_ref[...] = grad.astype(BF16)
            sending_ref[k] = against(mine_ref[their_rows, :], w_ref[0]).astype(BF16)
            start(swap(k))
            own_ref[0] = against(mine_ref[own_rows, :], w_ref[0])
            keep(k, inner(low_ref[0], mine_ref[...]))
            if k == 2:
                for n in range(4):
                    finish(swap(n))
                    finish(split(n))
                settle(1)
                finish(along())
                total = mids[0][...].astype(F32)
                for n in range(nz - 1):
                    total = total + along_ref[n].astype(F32)
                sum_ref[...] = total
                for t in range(2):
                    finish(fold(t, 2))
                finish(place_lates())


def unproject(grid, orders, mids, lates, last_parts, collected, lowered, grad_low, weights, feed_part, normed_feed, last_stream, biases, tables, own_width, collective_id):
    tokens, width = last_stream.shape
    both, half = 2 * tokens, width // 2
    na, nb, nz = grid.na, grid.nb, grid.nz
    rows = width // (na * nb * nz)
    n = lates[0].shape[-1]
    folds = [fold_scratch(grid, order, rows, n) for order in ("ab", "ba")]
    whole = pl.BlockSpec(memory_space=pltpu.VMEM)
    anywhere = pl.BlockSpec(memory_space=pl.ANY)
    turn = lambda i: lax.rem(i + 3, 4)
    split_shapes = [jax.ShapeDtypeStruct((nb if order == "ab" else na, nz, rows, half), BF16) for order in orders]
    sent_shapes = [jax.ShapeDtypeStruct((2, nb, nz, rows, half), BF16)] + [jax.ShapeDtypeStruct((2, na, nz, rows, half), BF16)] * (nb - 1)
    results = pl.pallas_call(
        functools.partial(unproject_kernel, grid, own_width, orders),
        grid=(4,),
        out_shape=[
            jax.ShapeDtypeStruct((4, tokens, width), F32),
            jax.ShapeDtypeStruct((4, tokens, width), BF16),
            jax.ShapeDtypeStruct((3, half), F32),
            jax.ShapeDtypeStruct((tokens, width), BF16),
            jax.ShapeDtypeStruct(mids[0].shape, F32),
        ]
        + [jax.ShapeDtypeStruct((2, rows, 2 * n), BF16)] * nz
        + split_shapes
        + sent_shapes,
        in_specs=[whole]
        + [anywhere] * (nz - 1)
        + [whole] * nz
        + [anywhere] * 2
        + [
            whole,
            pl.BlockSpec((1, both, width), lambda i: (jnp.maximum(i - 1, 0), 0, 0)),
            whole,
            pl.BlockSpec((1, width, half), lambda i: (turn(i), 0, 0)),
        ]
        + [whole] * 8,
        out_specs=[
            pl.BlockSpec((1, tokens, width), lambda i: (turn(i), 0, 0)),
            anywhere,
            pl.BlockSpec((3, half), lambda i: (0, 0)),
            pl.BlockSpec((tokens, width), lambda i: (0, 0)),
            pl.BlockSpec(mids[0].shape, lambda i: (0, 0, 0)),
        ]
        + [anywhere] * (nz + len(split_shapes) + len(sent_shapes)),
        scratch_shapes=[
            pltpu.VMEM((4, na, nb, nz, rows, half), BF16),
            pltpu.VMEM((4, tokens, width), BF16),
            pltpu.VMEM((tokens, width), F32),
            pltpu.VMEM((both, half), BF16),
            pltpu.VMEM((tokens, width), F32),
            pltpu.VMEM((nz - 1, *mids[0].shape), BF16),
            pltpu.SemaphoreType.DMA((4, nb + 1)),
            pltpu.SemaphoreType.DMA((5,)),
            pltpu.SemaphoreType.DMA((5,)),
            pltpu.SemaphoreType.DMA((nz - 1,)),
            pltpu.SemaphoreType.DMA((nz - 1,)),
            *[o for o, _, _ in folds],
            *[f for _, f, _ in folds],
            *[f for _, _, f in folds],
            pltpu.SemaphoreType.DMA((2, nz + nb)),
            pltpu.SemaphoreType.DMA((2, nz + nb)),
            pltpu.SemaphoreType.DMA((2 + 3 * nz,)),
        ],
        compiler_params=pltpu.CompilerParams(collective_id=collective_id, has_side_effects=True, vmem_limit_bytes=VMEM_LIMIT),
        cost_estimate=pl.CostEstimate(flops=32 * both * width * half, bytes_accessed=40 * both * width, transcendentals=0),
        name="unproject",
    )(*mids, *lates, *last_parts, collected, lowered, grad_low, weights, feed_part, normed_feed, last_stream, *biases, *tables)
    own, theirs, head_bias, layer_out, mid_sums = results[:5]
    lasts, results = results[5 : 5 + nz], results[5 + nz :]
    return own, theirs, head_bias, layer_out, mid_sums, lasts, results[:4], results[4:]


def feed_kernel(grid, steps, back_ref, low_ref, g_ref, we_ref, wc_ref, bias_ref, collected_ref, feed_ref, normed_ref, eb_ref, *refs):
    nz = grid.nz
    groups = steps - 1
    mids, outs, whole_outs, refs = refs[:nz], refs[nz : 2 * nz], refs[2 * nz : 2 * nz + 2], refs[2 * nz + 2 :]
    parts, refs = refs[: 2 * steps], refs[2 * steps :]
    first, second, refs = refs[: 2 * groups], refs[2 * groups : 4 * groups], refs[4 * groups :]
    bias_full, send_sem, recv_sem, out_sem, back_send, back_recv = refs
    i = pl.program_id(0)
    a, b, z, c = place = grid.here()
    orders = ["ab", "ba"] * steps

    def copies(t, stage):
        if stage < 2:
            return fold_copies(grid, place, orders[t], stage, parts[t], first[t], second[t], (send_sem.at[t], recv_sem.at[t]))
        along = [lax.rem(z + k, nz) for k in range(nz)]
        u, n = t // 2, parts[t].shape[-1]
        late = u == groups - 1
        cols = pl.ds(0 if late else u * n, n)
        spot = outs if late else mids
        return [pltpu.make_async_copy(second[t].at[0, along[k]], spot[k].at[t % 2, :, cols], out_sem.at[t, k]) for k in range(nz)]

    def last_parts():
        return [pltpu.make_async_copy(parts[2 * groups + k], whole_outs[k], out_sem.at[2 * groups + k, 0]) for k in range(2)]

    def begin(u):
        for t in (2 * u, 2 * u + 1):
            start(copies(t, 0))

    def end(u, stage):
        for t in (2 * u, 2 * u + 1):
            finish(copies(t, stage))
            if stage < 2:
                own = parts[t].at[a] if orders[t] == "ab" else parts[t].at[:, b]
                fold_add(grid, place, orders[t], stage, own, first[t], second[t])
                start(copies(t, stage + 1))

    def turn(u):
        for stage in range(3):
            if 0 <= u - stage < groups:
                end(u - stage, stage)

    def backs():
        found = [pltpu.make_async_copy(back_ref.at[z], collected_ref.at[z], back_send.at[0])]
        for k in range(1, nz):
            to = lax.rem(z + k, nz)
            found.append(remote(back_ref.at[to], collected_ref.at[z], back_send.at[k], back_recv.at[k], grid.device(a, b, to, c)))
        return found

    @pl.when(i == 0)
    def _():
        grid.greet(*place)
        start(backs())
        bias_full[...] = bias_ref[...].astype(F32)
        feed_ref[...] = jnp.zeros_like(feed_ref)
        normed_ref[...] = jnp.zeros_like(normed_ref)

    low, grad, expand, contract = low_ref[0], g_ref[...], we_ref[...], wc_ref[...]
    wide = expand.shape[1] // 128
    first_row = c * (bias_full.shape[0] // 2) + i * wide
    bias = jnp.concatenate([bias_full[pl.ds(first_row + l, 1), :] for l in range(wide)], axis=1)
    expanded = product(low, expand) + bias
    share = phi(expanded)
    hidden = (expanded * share).astype(BF16)
    slope = share + expanded * jnp.exp(-0.5 * expanded * expanded) * (1.0 / math.sqrt(2.0 * math.pi))
    feed_ref[...] += against(hidden, contract)
    hidden_grad = inner(grad, hidden).astype(BF16)
    pulled = product(grad, contract) * slope
    eb_ref[...] = jnp.sum(pulled, axis=0, keepdims=True)
    pulled_low = pulled.astype(BF16)
    normed_ref[...] += against(pulled_low, expand)
    expand_grad = inner(low, pulled_low).astype(BF16)
    for u in range(steps):

        @pl.when(i == u)
        def _(u=u):
            parts[2 * u][...] = expand_grad.reshape(parts[2 * u].shape)
            parts[2 * u + 1][...] = hidden_grad.reshape(parts[2 * u + 1].shape)
            if u < groups:
                begin(u)
            else:
                start(last_parts())
            if u >= 2:
                turn(u - 2)
            if u == steps - 1:
                for v in range(max(steps - 2, 0), groups + 2):
                    turn(v)
                finish(last_parts())
                finish(backs())


def feed_forward(grid, returned, lowered, grad_low, weight_e, weight_c, bias, steps, collective_id):
    both, width = grad_low.shape
    n = weight_e.shape[1] // steps
    na, nb, nz = grid.na, grid.nb, grid.nz
    rows = width // (na * nb * nz)
    whole = lambda *shape: pl.BlockSpec(shape, lambda i: (0,) * len(shape))
    cols = lambda m: pl.BlockSpec((m, n), lambda i: (0, i))
    orders = ["ab", "ba"] * steps
    folds = [fold_scratch(grid, order, rows, n) for order in orders]
    sem = pltpu.SemaphoreType.DMA((2 * steps, nz + nb))
    return pl.pallas_call(
        functools.partial(feed_kernel, grid, steps),
        grid=(steps,),
        out_shape=[
            jax.ShapeDtypeStruct(returned.shape, BF16),
            jax.ShapeDtypeStruct((both, width), F32),
            jax.ShapeDtypeStruct((both, width), F32),
            jax.ShapeDtypeStruct((1, n * steps), F32),
        ]
        + [jax.ShapeDtypeStruct((2, rows, n * (steps - 2)), BF16)] * nz
        + [jax.ShapeDtypeStruct((2, rows, n), BF16)] * nz
        + [jax.ShapeDtypeStruct((na, nb, nz, rows, n), BF16)] * 2,
        in_specs=[
            pl.BlockSpec(memory_space=pltpu.VMEM),
            pl.BlockSpec((1, both, width), lambda i: (3, 0, 0)),
            whole(both, width),
            cols(width),
            cols(width),
            whole(*bias.shape),
        ],
        out_specs=[
            pl.BlockSpec(memory_space=pl.ANY),
            whole(both, width),
            whole(both, width),
            cols(1),
        ]
        + [pl.BlockSpec(memory_space=pl.ANY)] * (2 * nz + 2),
        scratch_shapes=[pltpu.VMEM((na, nb, nz, rows, n), BF16)] * (2 * steps)
        + [f for _, f, _ in folds[:-2]]
        + [s for _, _, s in folds[:-2]]
        + [pltpu.VMEM(bias.shape, F32)]
        + [sem, sem, pltpu.SemaphoreType.DMA((2 * steps, nz)), pltpu.SemaphoreType.DMA((nz,)), pltpu.SemaphoreType.DMA((nz,))],
        compiler_params=pltpu.CompilerParams(collective_id=collective_id, has_side_effects=True, vmem_limit_bytes=VMEM_LIMIT),
        cost_estimate=pl.CostEstimate(flops=12 * both * width * n * steps * 2, bytes_accessed=width * n * steps * 20, transcendentals=0),
        name="feed_forward",
    )(returned, lowered, grad_low, weight_e, weight_c, bias)


def attention_kernel(width, heads, tile, edge, length, x_ref, qdoc_ref, out_ref, kdoc_ref,
                     s_ref, kt_ref, vt_ref, ot_ref, dqt_ref, dka_ref, dva_ref, top_ref):
    i = pl.program_id(0)
    tiles = length // tile
    scale = 1.0 / math.sqrt(HEAD_DIM)
    @pl.when(i == 0)
    def _():
        dka_ref[...] = jnp.zeros_like(dka_ref)
        dva_ref[...] = jnp.zeros_like(dva_ref)
        def turn(j, carry):
            at = pl.ds(pl.multiple_of(j * tile, tile), tile)
            kt_ref[:, at] = x_ref[at, width : 2 * width].T
            kdoc_ref[at, :] = jnp.broadcast_to(qdoc_ref[:, at].astype(F32), (128, tile)).T
            vt_ref[:, at] = x_ref[at, 2 * width : 3 * width].T
            return carry
        lax.fori_loop(0, tiles, turn, 0)
    rows = pl.ds(pl.multiple_of(i * tile, tile), tile)
    query = x_ref[rows, 0:width] * jnp.asarray(scale, BF16)
    grad = x_ref[rows, 3 * width : 4 * width]
    query_t, grad_t = query.T, grad.T
    lanes = lax.broadcasted_iota(jnp.int32, (tile, width), 1) // HEAD_DIM
    subs = lax.broadcasted_iota(jnp.int32, (width, tile), 0) // HEAD_DIM
    zero = jnp.zeros((), BF16)
    queries_t = [jnp.where(subs == h, query_t, zero) for h in range(heads)]
    grads_t = [jnp.where(subs == h, grad_t, zero) for h in range(heads)]
    spread_queries = [jnp.where(lanes == h, query, zero) for h in range(heads)]
    spread_grads = [jnp.where(lanes == h, grad, zero) for h in range(heads)]
    qdoc = qdoc_ref[:, rows].astype(F32)
    head_edge = -(-edge // tile)
    tail_edge = (length - edge) // tile
    half = tile // 2
    corners = [(0, half, 0), (half, half, half)]
    ot_ref[...] = jnp.zeros_like(ot_ref)
    dqt_ref[...] = jnp.zeros_like(dqt_ref)
    top_ref[...] = jnp.full_like(top_ref, NEG)

    def fold(x, f):
        return f(x.reshape(x.shape[0] // 8, 8, x.shape[1]), axis=0)

    def score(first, size, left, documents, causal):
        at = pl.ds(pl.multiple_of(first, size), size)
        keys = x_ref[at, width : 2 * width]
        wide = tile - left
        if documents:
            allowed = jnp.concatenate([kdoc_ref[at, :]] * (wide // 128), axis=1) == qdoc[:, left:]
        if causal:
            allowed &= lax.broadcasted_iota(jnp.int32, (size, wide), 0) <= lax.broadcasted_iota(jnp.int32, (size, wide), 1)
        for h in range(heads):
            s = product(keys, queries_t[h][:, left:])
            if documents:
                s = jnp.where(allowed, s, NEG)
            s_ref[h, at, left:] = s
            top_ref[h, :, left:] = jnp.maximum(top_ref[h, :, left:], fold(s, jnp.max))

    def scores(j, carry):
        checked = (j < head_edge) | (i >= tail_edge)
        pl.when(checked)(lambda: score(j * tile, tile, 0, True, False))
        pl.when(jnp.logical_not(checked))(lambda: score(j * tile, tile, 0, False, False))
        return carry

    lax.fori_loop(0, i, scores, 0)
    for first, size, left in corners:
        score(i * tile + first, size, left, True, True)
    tops = [jnp.max(top_ref[h], axis=0, keepdims=True) for h in range(heads)]
    top_ref[...] = jnp.zeros_like(top_ref)

    def weigh(first, size, left):
        at = pl.ds(pl.multiple_of(first, size), size)
        for h in range(heads):
            own = slice(h * HEAD_DIM, (h + 1) * HEAD_DIM)
            weights = jnp.exp(s_ref[h, at, left:] - tops[h][:, left:])
            s_ref[h, at, left:] = weights
            top_ref[h, :, left:] += fold(weights, jnp.sum)
            ot_ref[own, left:] += product(vt_ref[own, at], weights.astype(BF16))

    lax.fori_loop(0, i, lambda j, carry: (weigh(j * tile, tile, 0), carry)[1], 0)
    for first, size, left in corners:
        weigh(i * tile + first, size, left)
    inverse = [1.0 / jnp.sum(top_ref[h], axis=0, keepdims=True) for h in range(heads)]
    grad_f = grad_t.astype(F32)
    deltas = []
    for h in range(heads):
        own = slice(h * HEAD_DIM, (h + 1) * HEAD_DIM)
        value = ot_ref[own, :] * inverse[h]
        ot_ref[own, :] = value
        deltas.append(jnp.sum(value * grad_f[own], axis=0, keepdims=True))
    out_ref[rows, 0:width] = ot_ref[...].T.astype(BF16)

    def back(first, size, left):
        at = pl.ds(pl.multiple_of(first, size), size)
        values = x_ref[at, 2 * width : 3 * width]
        probs_low, grads_low = [], []
        for h in range(heads):
            own = slice(h * HEAD_DIM, (h + 1) * HEAD_DIM)
            probs_grad = product(values, grads_t[h][:, left:])
            probs = s_ref[h, at, left:] * inverse[h][:, left:]
            scores_grad = (probs * (probs_grad - deltas[h][:, left:])).astype(BF16)
            probs_low.append(probs.astype(BF16))
            grads_low.append(scores_grad)
            dqt_ref[own, left:] += product(kt_ref[own, at], scores_grad)
        dva_ref[at, :] += product(jnp.concatenate(probs_low, axis=1), jnp.concatenate([x[left:] for x in spread_grads], axis=0))
        dka_ref[at, :] += product(jnp.concatenate(grads_low, axis=1), jnp.concatenate([x[left:] for x in spread_queries], axis=0))

    lax.fori_loop(0, i, lambda j, carry: (back(j * tile, tile, 0), carry)[1], 0)
    for first, size, left in corners:
        back(i * tile + first, size, left)
    out_ref[rows, width : 2 * width] = (dqt_ref[...].T * scale).astype(BF16)

    @pl.when(i == tiles - 1)
    def _():
        out_ref[:, 2 * width : 3 * width] = dka_ref[...].astype(BF16)
        out_ref[:, 3 * width : 4 * width] = dva_ref[...].astype(BF16)


def attention(dealt, documents, heads, edge):
    length = dealt.shape[0]
    width = heads * HEAD_DIM
    tile = 2 * edge
    pairs = length * length // 2 * heads
    whole = lambda i: (0, 0)
    return pl.pallas_call(
        functools.partial(attention_kernel, width, heads, tile, edge, length),
        grid=(length // tile,),
        out_shape=jax.ShapeDtypeStruct((length, 4 * width), BF16),
        in_specs=[pl.BlockSpec((length, 4 * width), whole), pl.BlockSpec((1, length), whole)],
        out_specs=pl.BlockSpec((length, 4 * width), whole),
        scratch_shapes=[
            pltpu.VMEM((length, 128), F32), pltpu.VMEM((heads, length, tile), F32), pltpu.VMEM((width, length), BF16), pltpu.VMEM((width, length), BF16),
            pltpu.VMEM((width, tile), F32), pltpu.VMEM((width, tile), F32), pltpu.VMEM((length, width), F32), pltpu.VMEM((length, width), F32),
            pltpu.VMEM((heads, 8, tile), F32)],
        compiler_params=pltpu.CompilerParams(vmem_limit_bytes=VMEM_LIMIT),
        cost_estimate=pl.CostEstimate(flops=pairs * 64 * 2 * 6 * 4, bytes_accessed=length * width * 20, transcendentals=pairs),
        name="attention",
    )(dealt, documents)


def on_device(
    grid,
    history,
    documents,
    cotangent,
    mixer_gain,
    mixer_inner,
    mixer_outer,
    mixer_bias,
    stream_gain,
    stream_bias,
    inbound_weight,
    inbound_bias,
    outbound_weight,
    outbound_bias,
    expand,
    expand_bias,
    contract,
    contract_bias,
):
    n_dp, n_seq, nz = grid.n_dp, grid.n_seq, grid.nz
    tokens, width = history.shape[2], history.shape[3]
    hidden_width = expand.shape[1]
    half, hidden_half = width // 2, hidden_width // 2
    both = 2 * tokens
    length = documents.shape[1]
    mix = mixer_bias.shape[0]
    heads = HEADS // n_seq
    own_width = heads * HEAD_DIM
    pick = lambda base, n: (lambda core: base + core * n)
    parts = 4
    piece = hidden_half // parts
    feed = []
    for part in range(parts):
        base = lambda core, part=part: core * hidden_half + part * piece
        feed.append((2, base, 4, part * piece, piece, "ba"))
        feed.append((3, base, 5, part * piece, piece, "ab"))
    pairs = [[4 + 2 * part, 5 + 2 * part] for part in range(parts)]
    inner_t = mixer_inner.T
    lowered, grad_low, last_stream, mix_pre, coeffs, tables, weights, started = mix_forward(
        grid,
        history,
        cotangent,
        [mixer_gain.reshape(-1, 128), inner_t, mixer_outer, mixer_bias[None], stream_gain, stream_bias],
        [inbound_weight, outbound_weight, expand, contract],
        [
            (0, pick(width, half), 1, 0, half, "ba"),
            (0, pick(2 * width, half), 2, 0, half, "ab"),
            (0, pick(0, half), 0, 0, half, "ba"),
            (1, pick(0, half), 3, 0, half, "ab"),
        ]
        + feed,
        [[0, 1], [2, 3]],
        pairs,
        [hidden_half] * 2,
        1,
    )

    chunks = [(0, None, n - 4, col, size, order) for _, _, n, col, size, order in feed]
    dealt, (weight_e, weight_c) = exchange(
        grid,
        lowered,
        grad_low,
        weights,
        inbound_bias.reshape(-1, 128),
        tables,
        started,
        chunks,
        [[2 * part, 2 * part + 1] for part in range(parts)],
        own_width,
        2,
    )
    returned = attention(dealt.reshape(length, 4 * own_width), documents, heads, tokens)
    returned = returned.reshape(nz, both, 4 * own_width)

    collected, feed_part, normed_feed, expand_bias_part, *rest = feed_forward(
        grid, returned, lowered, grad_low, weight_e, weight_c, expand_bias.reshape(-1, 128), STEPS, 3
    )

    orders = ("ab", "ba", "ab", "ba")
    bias_out = [outbound_bias.reshape(-1, 128), contract_bias.reshape(-1, 128)]
    mids, lates, last_parts = rest[:nz], rest[nz : 2 * nz], rest[2 * nz :]
    normed_own, normed_theirs, head_bias_part, layer_out, mid_sums, lasts, kept, leaving = unproject(
        grid, orders, mids, lates, last_parts, collected, lowered, grad_low, weights, feed_part, normed_feed, last_stream, bias_out, tables, own_width, 4
    )

    along_z = [[(s, (s // 2 + k) % nz * 2 + s % 2) for s in range(n_seq)] for k in range(nz)]
    folded = [lasts[0]] + [lax.ppermute(lasts[k], "seq", along_z[k]) for k in range(1, nz)]
    nb = grid.nb
    over_a = [(d, (d + nb) % n_dp) for d in range(n_dp)]
    over_b = [[(d, d // nb * nb + (d + k) % nb) for d in range(n_dp)] for k in range(1, nb)]
    came_a = lax.ppermute(leaving[0], "dp", over_a)
    came_b = [lax.ppermute(x, "dp", perm) for x, perm in zip(leaving[1:], over_b)]

    history_grad, *small = mix_backward(
        history, normed_own, normed_theirs, cotangent, mix_pre, coeffs, [mixer_gain.reshape(-1, 128), inner_t, mixer_outer, stream_gain]
    )
    smalls = [*small, head_bias_part, expand_bias_part]
    summed, *owned = finish_sums(grid, orders, kept, [came_a, *came_b], [mid_sums, *folded], smalls, 5)
    layer_out, *small, inbound_grad, outbound_grad, expand_grad, contract_grad, again = hand_over(summed, layer_out, owned, mix, hidden_width)
    gain_grad, inner_grad, outer_grad, bias_grad, stream_gain_grad, stream_bias_grad, in_bias_grad, out_bias_grad, expand_bias_grad = small
    return (
        layer_out[None],
        history_grad,
        gain_grad.reshape(width),
        inner_grad.T,
        outer_grad,
        bias_grad.reshape(-1),
        stream_gain_grad,
        stream_bias_grad,
        inbound_grad,
        in_bias_grad.reshape(3 * width),
        outbound_grad,
        out_bias_grad.reshape(width),
        expand_grad,
        expand_bias_grad.reshape(hidden_width),
        contract_grad,
        again.reshape(width),
    )


def solution(mesh):
    rows = P(("dp", "seq"), None)
    placed = (
        P(None, "dp", "seq", None),
        P("dp", None),
        P("dp", "seq", None),
        P(),
        P(),
        P(),
        P(),
        P(),
        P(),
        rows,
        P(),
        rows,
        P(),
        rows,
        P(),
        rows,
        P(),
    )
    grid = Grid(mesh.shape["dp"], mesh.shape["seq"])
    return jax.shard_map(
        functools.partial(on_device, grid),
        mesh=mesh,
        in_specs=placed,
        out_specs=(
            P("dp", "seq", None),
            P(None, "dp", "seq", None),
            P(),
            P(),
            P(),
            P(),
            P(),
            P(),
            rows,
            P(),
            rows,
            P(),
            rows,
            P(),
            rows,
            P(),
        ),
        check_vma=False,
    )
```

```python
import functools
import math

import jax
import jax.numpy as jnp
from jax import lax
from jax.experimental import pallas as pl
from jax.experimental.pallas import tpu as pltpu
from jax.sharding import PartitionSpec as P

HEADS = 16
HEAD_DIM = 64
ROT_DIMS = 16
EPS = 1e-05
HIGHEST = lax.Precision.HIGHEST
NEG = -1e30
MESH = pl.DeviceIdType.MESH
F32 = jnp.float32
BF16 = jnp.bfloat16
VMEM_LIMIT = 56 * 1024 * 1024
STEPS = 4


def inner(left, right):
    return lax.dot_general(left, right, (((0,), (0,)), ((), ())), preferred_element_type=F32)


def against(left, right):
    return lax.dot_general(left, right, (((1,), (1,)), ((), ())), preferred_element_type=F32)


def product(left, right):
    return jnp.dot(left, right, preferred_element_type=F32)


def exact_gelu(value):
    return jax.nn.gelu(value, approximate=False)


def phi(value):
    return 0.5 * (1.0 + lax.erf(value * (1.0 / math.sqrt(2.0))))


def gelu_slope(value):
    return phi(value) + value * jnp.exp(-0.5 * value * value) * (1.0 / math.sqrt(2.0 * math.pi))


def rotate(value, tables, sign):
    half = ROT_DIMS // 2
    cosine, above, below = tables
    width = value.shape[-1]
    up = pltpu.roll(value, width - half, 1)
    down = pltpu.roll(value, half, 1)
    return value * cosine + sign * (up * above + down * below)


class Grid:
    def __init__(self, n_dp, n_seq):
        self.n_dp, self.n_seq = n_dp, n_seq
        self.na, self.nb, self.nz = 2, n_dp // 2, n_seq // 2

    def here(self):
        dp, seq = lax.axis_index("dp"), lax.axis_index("seq")
        return dp // self.nb, lax.rem(dp, self.nb), seq // 2, lax.rem(seq, 2)

    def device(self, a, b, z, c):
        return (a * self.nb + b, z * 2 + c)

    def peers(self, a, b, z, c):
        found = [self.device(a, b, z, 1 - c), self.device(1 - a, b, z, c)]
        found += [self.device(a, lax.rem(b + k, self.nb), z, c) for k in range(1, self.nb)]
        found += [self.device(a, b, lax.rem(z + k, self.nz), c) for k in range(1, self.nz)]
        return found

    def greet(self, a, b, z, c):
        barrier = pltpu.get_barrier_semaphore()
        found = self.peers(a, b, z, c)
        for peer in found:
            pl.semaphore_signal(barrier, inc=1, device_id=peer, device_id_type=MESH)
        pl.semaphore_wait(barrier, len(found))


def row(ref):
    value = ref[...].astype(F32)
    return jnp.concatenate([value[l : l + 1] for l in range(value.shape[0])], axis=1)


def remote(src, dst, send, recv, device):
    return pltpu.make_async_remote_copy(
        src_ref=src, dst_ref=dst, send_sem=send, recv_sem=recv, device_id=device, device_id_type=MESH
    )


def start(copies):
    for copy in copies:
        copy.start()


def finish(copies):
    for copy in copies:
        copy.wait()


class Gathering:
    def __init__(self, grid, place, rows, chunks, ins, outs, local_sem, send_sem, recv_sem):
        self.grid, self.place, self.rows, self.chunks = grid, place, rows, chunks
        self.ins, self.outs = ins, outs
        self.local_sem, self.send_sem, self.recv_sem = local_sem, send_sem, recv_sem

    def copies(self, t, stage):
        a, b, z, c = self.place
        grid, rows = self.grid, self.rows
        nz, nb = grid.nz, grid.nb
        source, base, result, col, n, order = self.chunks[t]
        out, cols = self.outs[result], pl.ds(col, n)

        def send(src, dst, slot, device):
            return remote(src, dst, self.send_sem.at[t, slot], self.recv_sem.at[t, slot], device)

        if stage == 0:
            mine = self.ins[source].at[:, pl.ds(pl.multiple_of(base(c), 128), n)]
            theirs = self.ins[source].at[:, pl.ds(pl.multiple_of(base(1 - c), 128), n)]
            spot = out.at[a, b, z, pl.ds(pl.multiple_of(c * rows, rows), rows), cols]
            return [pltpu.make_async_copy(mine, spot, self.local_sem.at[t]), send(theirs, spot, 0, grid.device(a, b, z, 1 - c))]
        if order[stage - 2] == "b":
            block = out.at[a, b, :, :, cols] if stage == 2 else out.at[:, b, :, :, cols]
            return [send(block, block, k, grid.device(a, lax.rem(b + k, nb), z, c)) for k in range(1, nb)]
        block = out.at[a, b, :, :, cols] if stage == 2 else out.at[a, :, :, :, cols]
        return [send(block, block, nb, grid.device(1 - a, b, z, c))]

    def hop(self, t, step, begin):
        a, b, z, c = self.place
        nz, nb = self.grid.nz, self.grid.nb
        _, _, result, col, n, _ = self.chunks[t]
        out, cols = self.outs[result], pl.ds(col, n)
        for side, way in enumerate((1, -1)):
            slot = nb + 1 + side * (nz - 1) + step - 1
            there, arriving = z + way, z - way * step
            going = there - way * step
            inside = (there >= 0) & (there < nz) & (going >= 0) & (going < nz)
            coming = (arriving >= 0) & (arriving < nz)

            def link(which, slot=slot, there=there):
                block = out.at[a, b, which, :, cols]
                return remote(block, block, self.send_sem.at[t, slot], self.recv_sem.at[t, slot], self.grid.device(a, b, there, c))

            if begin:
                pl.when(inside)(lambda link=link, going=going: link(going).start())
            else:
                pl.when(inside)(lambda link=link, going=going: link(going).wait_send())
                pl.when(coming)(lambda link=link, arriving=arriving: link(arriving).wait_recv())

    def begin(self, group, stage):
        for t in group:
            start(self.copies(t, stage))

    def end(self, group, stage):
        for t in group:
            finish(self.copies(t, stage))

    def ticks(self, whole, partial):
        groups, nz = whole + partial, self.grid.nz

        def advance(u, at):
            group = groups[u]
            if at == 0:
                self.end(group, 0)
            elif at < nz:
                for t in group:
                    self.hop(t, at, False)
            else:
                self.end(group, 2)
            for t in group:
                if at < nz - 1:
                    self.hop(t, at + 1, True)
                elif u < len(whole):
                    start(self.copies(t, 2 if at == nz - 1 else 3))

        def first():
            for group in groups:
                self.begin(group, 0)

        enter = [u if u < len(whole) else len(whole) + (u - len(whole)) // 2 for u in range(len(groups))]

        def tick(now):
            for u in range(len(groups)):
                if 0 <= now - enter[u] <= (nz if u < len(whole) else nz - 1):
                    advance(u, now - enter[u])

        def last():
            for group in whole:
                self.end(group, 3)

        return [first] + [functools.partial(tick, now) for now in range(max(enter) + nz + 1)] + [last]


def gather_sems(grid, chunks):
    slots = 2 * grid.nz + grid.nb - 1
    return [
        pltpu.SemaphoreType.DMA((len(chunks),)),
        pltpu.SemaphoreType.DMA((len(chunks), slots)),
        pltpu.SemaphoreType.DMA((len(chunks), slots)),
    ]


def fold_copies(grid, place, order, stage, part, first, second, sems):
    a, b, z, c = place
    nz, nb = grid.nz, grid.nb

    def send(src, dst, slot, device):
        return remote(src, dst, sems[0].at[slot], sems[1].at[slot], device)

    if (order == "ab") == (stage == 0):
        src = part.at[1 - a] if stage == 0 else first.at[0, 1 - a]
        dst = first.at[0] if stage == 0 else second.at[0]
        return [send(src, dst, nz + nb - 1, grid.device(1 - a, b, z, c))]
    found = []
    for k in range(1, nb):
        to = lax.rem(b + k, nb)
        src = part.at[:, to] if stage == 0 else first.at[0, to]
        dst = first.at[k - 1] if stage == 0 else second.at[k - 1]
        found.append(send(src, dst, nz + k - 1, grid.device(a, to, z, c)))
    return found


def fold_add(grid, place, order, stage, own, first, second):
    a, b, z, c = place
    nz = grid.nz
    if stage == 0:

        def step(i, carry):
            o, j = i // nz, lax.rem(i, nz)
            total = own[o, j].astype(F32)
            for k in range(first.shape[0]):
                total = total + first[k, o, j].astype(F32)
            first[0, o, j] = total.astype(BF16)
            return carry

        lax.fori_loop(0, first.shape[1] * nz, step, 0)
        return
    mine = b if order == "ab" else a

    def step(j, carry):
        total = first[0, mine, j].astype(F32)
        for k in range(second.shape[0]):
            total = total + second[k, j].astype(F32)
        second[0, j] = total.astype(BF16)
        return carry

    lax.fori_loop(0, nz, step, 0)


def fold_scratch(grid, order, rows, n):
    na, nb, nz = grid.na, grid.nb, grid.nz
    own = pltpu.VMEM((nb if order == "ab" else na, nz, rows, n), BF16)
    first = pltpu.VMEM((1, nb, nz, rows, n) if order == "ab" else (nb - 1, na, nz, rows, n), BF16)
    second = pltpu.VMEM((nb - 1, nz, rows, n) if order == "ab" else (1, nz, rows, n), BF16)
    return own, first, second


class Summing:
    def __init__(self, grid, mine, held, total, done, send_sem, recv_sem):
        self.n_seq, self.count = grid.n_seq, grid.n_dp * grid.n_seq
        self.mine, self.held, self.total, self.done = mine, held, total, done
        self.send_sem, self.recv_sem = send_sem, recv_sem
        self.rows = total.shape[0]
        self.me = lax.axis_index("dp") * grid.n_seq + lax.axis_index("seq")

    def device(self, k):
        other = lax.rem(self.me + k, self.count)
        return other, (other // self.n_seq, lax.rem(other, self.n_seq))

    def part(self, ref, k):
        return ref.at[pl.ds(pl.multiple_of(k * self.rows, self.rows), self.rows)]

    def greet(self):
        barrier = pltpu.get_barrier_semaphore()

        def step(k, carry):
            pl.semaphore_signal(barrier, inc=1, device_id=self.device(k)[1], device_id_type=MESH)
            return carry

        lax.fori_loop(1, self.count, step, 0)

    def settle(self, dst, slot):
        most = pl.ds(0, (self.count - 1) * self.rows)
        remote(self.mine.at[most], dst.at[most], self.send_sem.at[slot], self.recv_sem.at[slot], self.device(1)[1]).wait()

    def deal(self):
        def step(k, carry):
            other, place = self.device(k)
            remote(self.part(self.mine, other), self.part(self.held, self.me), self.send_sem.at[0], self.recv_sem.at[0], place).start()
            return carry

        lax.fori_loop(1, self.count, step, 0)
        at = pl.ds(pl.multiple_of(self.me * self.rows, self.rows), self.rows)
        self.held[at, :] = self.mine[at, :]

    def tell(self):
        self.settle(self.held, 0)

        def add(k, carry):
            return carry + self.held[pl.ds(pl.multiple_of(k * self.rows, self.rows), self.rows), :]

        self.total[...] = lax.fori_loop(0, self.count, add, jnp.zeros(self.total.shape, F32))

        def step(k, carry):
            place = self.device(k)[1]
            remote(self.total, self.part(self.done, self.me), self.send_sem.at[1], self.recv_sem.at[1], place).start()
            return carry

        lax.fori_loop(1, self.count, step, 0)
        self.done[pl.ds(pl.multiple_of(self.me * self.rows, self.rows), self.rows), :] = self.total[...]

    def close(self):
        self.settle(self.done, 1)


def spread_out(coeffs):
    return [jnp.broadcast_to(coeffs[:, k : k + 1], (coeffs.shape[0], 128)) for k in range(coeffs.shape[1])]


def blend(h_ref, coeffs, streams_ref):
    hist, width = h_ref.shape[0], h_ref.shape[3]
    spread = spread_out(coeffs)
    for at in range(0, width, 128):
        lanes = slice(at, at + 128)
        inputs = [h_ref[j, 0, :, lanes].astype(F32) for j in range(hist)]
        for c in range(4):
            total = spread[c * hist] * inputs[0]
            for j in range(1, hist):
                total = total + spread[c * hist + j] * inputs[j]
            streams_ref[c, :, lanes] = total


def mix_kernel(grid, rows, chunks, whole, partial, own_width, h_ref, g_ref, gain_ref, inner_ref, outer_ref, bias_ref, sgain_ref, sbias_ref,
               in_bias_ref, *refs):
    ins, (lowered_ref, gpair_ref, kept_ref, pre_ref, coeffs_ref, cos_ref, above_ref, below_ref) = refs[:4], refs[4:12]
    weights_ref, outs, dealt_ref, refs = refs[12], refs[13:15], refs[15], refs[16:]
    streams_ref, full_ref, gfull_ref, held_ref, sent_ref, bias_full, local_sem, send_sem, recv_sem = refs[:9]
    pair_local, pair_send, pair_recv, deal_send, deal_recv = refs[9:]
    i, steps = pl.program_id(0), pl.num_programs(0)
    a, b, z, c = place = grid.here()
    block = h_ref.shape[2]
    outs = [weights_ref.at[k] for k in range(4)] + list(outs)
    work = Gathering(grid, place, rows, chunks, ins, outs, local_sem, send_sem, recv_sem)
    events = work.ticks(whole, partial)
    other = grid.device(a, b, z, 1 - c)
    nz = grid.nz

    def swap_grads():
        return [remote(g_ref.at[0], gfull_ref.at[c], pair_send.at[0], pair_recv.at[0], other)]

    def swap_lowered():
        return [remote(full_ref.at[:, c], full_ref.at[:, c], pair_send.at[1], pair_recv.at[1], other)]

    def hand_out():
        return [
            pltpu.make_async_copy(full_ref, lowered_ref, pair_local.at[0]),
            pltpu.make_async_copy(gfull_ref, gpair_ref, pair_local.at[1]),
        ]

    def fetch():
        return [pltpu.make_async_copy(weights_ref, held_ref, pair_local.at[2])]

    def link(to):
        k = lax.rem(to - z + nz, nz)
        return remote(sent_ref.at[to], dealt_ref.at[z], deal_send.at[k], deal_recv.at[k], grid.device(a, b, to, c))

    def stay():
        return pltpu.make_async_copy(sent_ref.at[z], dealt_ref.at[z], deal_send.at[0])

    def project(n):
        wide = 2 * own_width
        turn = far_first(nz, z, n)
        cols = pl.ds(pl.multiple_of(turn * wide, wide), wide)
        both, width = 2 * full_ref.shape[2], full_ref.shape[3]
        third = bias_full.shape[0] // 3
        tables = [jnp.concatenate([t[...]] * (wide // 128), axis=1) for t in (cos_ref, above_ref, below_ref)]

        def one(k):
            inputs = gfull_ref[...] if k == 3 else full_ref[k]
            found = product(inputs.reshape(both, width), held_ref[k, :, :, :, :, cols].reshape(width, wide))
            if k == 3:
                return found
            first_row = k * third + c * (third // 2) + turn * (wide // 128)
            found = found + jnp.concatenate([bias_full[pl.ds(first_row + l, 1), :] for l in range(wide // 128)], axis=1)
            return rotate(found, tables, 1.0) if k < 2 else found

        for k in range(4):
            x = one(k).astype(BF16)
            for m in range(2):
                sent_ref[turn * 2 + m, :, k * own_width : (k + 1) * own_width] = x[:, m * own_width : (m + 1) * own_width]
        for m in range(2):
            to = turn * 2 + m
            pl.when(to != z)(lambda to=to: link(to).start())
            pl.when(to == z)(lambda: stay().start())

    @pl.when(i == 0)
    def _():
        grid.greet(*place)
        events[0]()
        start(swap_grads())
        gfull_ref[c] = g_ref[0]
        bias_full[...] = in_bias_ref[...].astype(F32)

    for n, at in enumerate((0, 2, 3, 4)):

        @pl.when(i == at)
        def _(n=n):
            events[n + 1]()

    @pl.when(i == 2)
    def _():
        both, wide = cos_ref.shape
        half = ROT_DIMS // 2
        place_in = lax.rem(lax.broadcasted_iota(jnp.int32, (1, wide), 1), HEAD_DIM)
        step = lax.rem(place_in, half)
        freq = jnp.ones((1, wide), F32)
        for k in range(1, half):
            freq = jnp.where(step == k, 10000.0 ** (-2.0 * k / ROT_DIMS), freq)
        angles = (z * both + lax.broadcasted_iota(jnp.int32, (both, wide), 0)).astype(F32) * freq
        turned = place_in < ROT_DIMS
        sine = jnp.where(turned, jnp.sin(angles), 0.0)
        cos_ref[...] = jnp.where(turned, jnp.cos(angles), 1.0)
        above_ref[...] = jnp.where(place_in < half, -sine, 0.0)
        below_ref[...] = jnp.where(place_in < half, 0.0, sine)

    last = h_ref[h_ref.shape[0] - 1, 0].astype(F32)
    r = lax.rsqrt(jnp.mean(last * last, axis=1, keepdims=True) + EPS)
    scaled_low = (last * r * row(gain_ref)).astype(BF16)
    pre = against(scaled_low, inner_ref[...])
    pre_ref[...] = pre
    coeffs = product((pre * phi(pre)).astype(BF16), outer_ref[...]) + bias_ref[...].astype(F32)
    coeffs_ref[...] = coeffs
    blend(h_ref, coeffs, streams_ref)
    at = pl.ds(pl.multiple_of(i * block, block), block)
    for k in range(4):
        stream = streams_ref[k]
        centered = stream - jnp.mean(stream, axis=1, keepdims=True)
        rs = lax.rsqrt(jnp.mean(centered * centered, axis=1, keepdims=True) + EPS)
        gain, bias = sgain_ref[k : k + 1, :].astype(F32), sbias_ref[k : k + 1, :].astype(F32)
        full_ref[k, c, at, :] = (centered * rs * gain + bias).astype(BF16)
    kept_ref[...] = streams_ref[...]

    @pl.when(i == steps - 1)
    def _():
        start(swap_lowered())
        ready = len(whole) + nz - 1
        for event in events[5 : 1 + ready + 1]:
            event()
        events[-1]()
        start(fetch())
        finish(swap_grads())
        finish(swap_lowered())
        start(hand_out())
        hopped = [u for u in range(len(partial)) if u // 2 + len(whole) + nz - 1 <= ready]
        for u in hopped:
            work.begin(partial[u], 2)
        finish(fetch())
        for n in range(nz // 2):
            project(n)
        for event in events[1 + ready + 1 : -1]:
            event()
        for u in range(len(partial)):
            if u not in hopped:
                work.begin(partial[u], 2)
        for group in partial:
            work.end(group, 2)
            work.begin(group, 3)
        for m in range(1, nz):
            link(lax.rem(z + m, nz)).wait()
        stay().wait()
        finish(hand_out())
        for group in partial:
            work.end(group, 3)


def mix_forward(grid, history, cotangent, params, weights, chunks, groups, partial, widths, own_width, collective_id):
    hist, _, tokens, width = history.shape
    mix = params[1].shape[0]
    block = 64
    rows = weights[0].shape[0]
    whole = pl.BlockSpec(memory_space=pltpu.VMEM)
    anywhere = pl.BlockSpec(memory_space=pl.ANY)
    part = lambda n: pl.BlockSpec((block, n), lambda i: (i, 0))
    chips = (grid.na, grid.nb, grid.nz, 2 * rows)
    results = pl.pallas_call(
        functools.partial(mix_kernel, grid, rows, chunks, groups, partial, own_width),
        grid=(tokens // block,),
        out_shape=[
            jax.ShapeDtypeStruct((4, 2, tokens, width), BF16),
            jax.ShapeDtypeStruct((2, tokens, width), BF16),
            jax.ShapeDtypeStruct((4, tokens, width), F32),
            jax.ShapeDtypeStruct((tokens, mix), F32),
            jax.ShapeDtypeStruct((tokens, mix), F32),
        ]
        + [jax.ShapeDtypeStruct((2 * tokens, 128), F32)] * 3
        + [jax.ShapeDtypeStruct((4, *chips, width // 2), BF16)]
        + [jax.ShapeDtypeStruct((*chips, w), BF16) for w in widths]
        + [jax.ShapeDtypeStruct((grid.nz, 2 * tokens, 4 * own_width), BF16)],
        in_specs=[pl.BlockSpec((hist, 1, block, width), lambda i: (0, 0, i, 0))] + [whole] * 12,
        out_specs=[anywhere, anywhere, pl.BlockSpec((4, block, width), lambda i: (0, i, 0)), part(mix), part(mix)]
        + [pl.BlockSpec((2 * tokens, 128), lambda i: (0, 0))] * 3
        + [anywhere] * 4,
        scratch_shapes=[
            pltpu.VMEM((4, block, width), F32),
            pltpu.VMEM((4, 2, tokens, width), BF16),
            pltpu.VMEM((2, tokens, width), BF16),
            pltpu.VMEM((4, *chips, width // 2), BF16),
            pltpu.VMEM((grid.nz, 2 * tokens, 4 * own_width), BF16),
            pltpu.VMEM(params[-1].shape, F32),
            *gather_sems(grid, chunks),
            pltpu.SemaphoreType.DMA((3,)),
            pltpu.SemaphoreType.DMA((2,)),
            pltpu.SemaphoreType.DMA((2,)),
            pltpu.SemaphoreType.DMA((grid.nz,)),
            pltpu.SemaphoreType.DMA((grid.nz,)),
        ],
        compiler_params=pltpu.CompilerParams(collective_id=collective_id, has_side_effects=True, vmem_limit_bytes=VMEM_LIMIT),
        cost_estimate=pl.CostEstimate(flops=tokens * width * 80, bytes_accessed=history.size * 40, transcendentals=0),
        name="mix_forward",
    )(history, cotangent, *params, *weights)
    lowered, gpair, streams, pre, coeffs = results[:5]
    return (
        lowered.reshape(4, 2 * tokens, width),
        gpair.reshape(2 * tokens, width),
        streams,
        pre,
        coeffs,
        results[5:8],
        results[8].reshape(4, width, width // 2),
        [x.reshape(-1, x.shape[-1]) for x in results[9:-1]],
        results[-1],
    )


def small_rows(width, mix, hidden_width):
    wl, padded = width // 128, -(-mix // 8) * 8
    sizes = [wl, wl * padded, padded, 8, 4 * wl, 4 * wl, 3 * wl, wl, hidden_width // 128]
    firsts = [sum(sizes[:k]) for k in range(len(sizes))]
    return firsts, sum(sizes)


def unmix_kernel(h_ref, streams_ref, own_ref, theirs_ref, g_ref, pre_ref, coeffs_ref, gain_ref, inner_ref, outer_ref, sgain_ref,
                 hist_ref, sgg_ref, sbg_ref, gg_ref, ig_ref, og_ref, bg_ref, ob_ref,
                 sg_ref, scaled_ref, mpg_ref, hidden_ref, cgl_ref):
    i, steps = pl.program_id(0), pl.num_programs(0)
    hist, block, width = h_ref.shape[0], h_ref.shape[2], h_ref.shape[3]
    mix = 4 * hist

    @pl.when(i == 0)
    def _():
        for ref in (sgg_ref, sbg_ref, gg_ref, bg_ref, ob_ref):
            ref[...] = jnp.zeros_like(ref)

    def down(x):
        return jnp.sum(x, axis=0, keepdims=True)

    spread = spread_out(coeffs_ref[...])
    grad = g_ref[0].astype(F32)
    ob_ref[...] += down(grad)
    for k in range(4):
        stream = streams_ref[k]
        centered = stream - jnp.mean(stream, axis=1, keepdims=True)
        rs = lax.rsqrt(jnp.mean(centered * centered, axis=1, keepdims=True) + EPS)
        n = centered * rs
        ng = own_ref[k] + theirs_ref[k].astype(F32)
        sgg_ref[k : k + 1, :] += down(ng * n)
        sbg_ref[k : k + 1, :] += down(ng)
        w = ng * sgain_ref[k : k + 1, :].astype(F32)
        pulled = rs * (w - jnp.mean(w, axis=1, keepdims=True) - n * jnp.mean(w * n, axis=1, keepdims=True))
        sg_ref[k] = pulled + grad if k == 3 else pulled

    lane = lax.broadcasted_iota(jnp.int32, (block, mix), 1)
    cg = jnp.zeros((block, mix), F32)
    for j in range(hist):
        value = h_ref[j, 0].astype(F32)
        for k in range(4):
            cg = jnp.where(lane == k * hist + j, jnp.sum(value * sg_ref[k], axis=1, keepdims=True), cg)
    bg_ref[...] += down(cg)
    cg_low = cg.astype(BF16)
    pre = pre_ref[...]
    at = pl.ds(pl.multiple_of(i * block, block), block)
    mpg = (against(cg_low, outer_ref[...]) * gelu_slope(pre)).astype(BF16)
    last = h_ref[hist - 1, 0].astype(F32)
    r = lax.rsqrt(jnp.mean(last * last, axis=1, keepdims=True) + EPS)
    gain = row(gain_ref)
    scaled_ref[at, :] = (last * r * gain).astype(BF16)
    mpg_ref[at, :] = mpg
    hidden_ref[at, :] = (pre * phi(pre)).astype(BF16)
    cgl_ref[at, :] = cg_low
    scaled_grad = product(mpg, inner_ref[...])
    gg_ref[...] += down(scaled_grad * last * r)
    w = scaled_grad * gain
    last_grad = r * (w - last * (r * r) * jnp.mean(w * last, axis=1, keepdims=True))
    for from_ in range(0, width, 128):
        lanes = slice(from_, from_ + 128)
        pulls = [sg_ref[k, :, lanes] for k in range(4)]
        for j in range(hist):
            total = spread[j] * pulls[0]
            for k in range(1, 4):
                total = total + spread[k * hist + j] * pulls[k]
            hist_ref[j, 0, :, lanes] = total + last_grad[:, lanes] if j == hist - 1 else total

    @pl.when(i == steps - 1)
    def _():
        ig_ref[...] = inner(mpg_ref[...], scaled_ref[...])
        og_ref[...] = inner(hidden_ref[...], cgl_ref[...])


def mix_backward(history, streams, own, theirs, cotangent, pre, coeffs, params):
    hist, _, tokens, width = history.shape
    mix = pre.shape[1]
    block = 64
    whole = pl.BlockSpec(memory_space=pltpu.VMEM)
    part = lambda n: pl.BlockSpec((block, n), lambda i: (i, 0))
    four = pl.BlockSpec((4, block, width), lambda i: (0, i, 0))
    story = pl.BlockSpec((hist, 1, block, width), lambda i: (0, 0, i, 0))
    small = [(4, width), (4, width), (1, width), (mix, width), (mix, mix), (1, mix), (1, width)]
    return pl.pallas_call(
        unmix_kernel,
        grid=(tokens // block,),
        out_shape=[jax.ShapeDtypeStruct(history.shape, F32)] + [jax.ShapeDtypeStruct(shape, F32) for shape in small],
        in_specs=[story, four, four, four, pl.BlockSpec((1, block, width), lambda i: (0, i, 0)), part(mix), part(mix)] + [whole] * 4,
        out_specs=[story] + [pl.BlockSpec(shape, lambda i: (0, 0)) for shape in small],
        scratch_shapes=[
            pltpu.VMEM((4, block, width), F32),
            pltpu.VMEM((tokens, width), BF16),
            pltpu.VMEM((tokens, mix), BF16),
            pltpu.VMEM((tokens, mix), BF16),
            pltpu.VMEM((tokens, mix), BF16),
        ],
        compiler_params=pltpu.CompilerParams(vmem_limit_bytes=VMEM_LIMIT),
        cost_estimate=pl.CostEstimate(flops=tokens * width * 1000, bytes_accessed=history.size * 12, transcendentals=0),
        name="mix_backward",
    )(history, streams, own, theirs, cotangent, pre, coeffs, *params)


def finish_kernel(grid, orders, n_kept, *refs):
    nz = grid.nz
    kept, refs = refs[:n_kept], refs[n_kept:]
    came_a, came_b, refs = refs[:1], refs[1 : grid.nb], refs[grid.nb :]
    sum_ref, folded, refs = refs[0], refs[1 : 1 + nz], refs[1 + nz :]
    sgg_ref, sbg_ref, gg_ref, ig_ref, og_ref, bg_ref, ob_ref, hb_ref, eb_ref = refs[:9]
    done_ref, outs, refs = refs[9], refs[10:14], refs[14:]
    first, second, third, final, refs = refs[:4], refs[4:8], refs[8:12], refs[12:18], refs[18:]
    sums = Summing(grid, *refs[:3], done_ref, *refs[3:5])
    local_sem, send_sem, recv_sem = refs[5:]
    a, b, z, c = place = grid.here()
    width, mix = gg_ref.shape[1], bg_ref.shape[1]
    wl, padded, hidden_rows = width // 128, -(-mix // 8) * 8, eb_ref.shape[1] // 128
    firsts, _ = small_rows(width, mix, 2 * eb_ref.shape[1])
    half = width // 2
    spots = [(0, lambda core: core * half), (0, lambda core: width + core * half), (0, lambda core: 2 * width + core * half),
             (1, lambda core: core * half), (2, lambda core: core * eb_ref.shape[1]), (3, lambda core: core * eb_ref.shape[1])]

    def copies(t, stage):
        if stage == 1:
            return fold_copies(grid, place, orders[t], 1, None, first[t], second[t], (send_sem.at[t], recv_sem.at[t]))
        if stage == 2:
            return [
                remote(second[t].at[0, lax.rem(z + k, nz)], third[t].at[k - 1], send_sem.at[t, k], recv_sem.at[t, k],
                       grid.device(a, b, lax.rem(z + k, nz), c))
                for k in range(1, nz)
            ]
        result, base = spots[t]
        n = final[t].shape[-1]
        spot = outs[result].at[:, pl.ds(pl.multiple_of(base(c), 128), n)]
        return [
            remote(final[t].at[1 - c], spot, send_sem.at[t, 0], recv_sem.at[t, 0], grid.device(a, b, z, 1 - c)),
            pltpu.make_async_copy(final[t].at[c], spot, local_sem.at[t]),
        ]

    def add_first(t):
        def step(i, carry):
            o, j = i // nz, lax.rem(i, nz)
            total = kept[t][o, j].astype(F32)
            for piece in came_a if orders[t] == "ab" else came_b:
                total = total + piece[t // 2, o, j].astype(F32)
            first[t][0, o, j] = total.astype(BF16)
            return carry

        lax.fori_loop(0, first[t].shape[1] * nz, step, 0)

    sums.greet()
    add_first(0)
    add_first(1)
    pl.semaphore_wait(pltpu.get_barrier_semaphore(), sums.count - 1)
    for t in range(2):
        start(copies(t, 1))
    add_first(2)
    add_first(3)

    for t in range(2):
        total = folded[0][t].astype(F32)
        for piece in folded[1:]:
            total = total + piece[t].astype(F32)
        at = 0
        for piece in (sum_ref[t], total):
            n = piece.shape[1]
            final[4 + t][:, :, at : at + n] = piece.reshape(2, -1, n)
            at += n
        start(copies(4 + t, 3))
    def second_step(t):
        finish(copies(t, 1))
        if t < 2:
            start(copies(t + 2, 1))
        fold_add(grid, place, orders[t], 1, None, first[t], second[t])
        start(copies(t, 2))

    second_step(0)
    second_step(1)
    mine = sums.mine
    mine[...] = jnp.zeros_like(mine)
    for l in range(wl):
        lanes = slice(l * 128, (l + 1) * 128)
        mine[firsts[0] + l : firsts[0] + l + 1, :] = gg_ref[:, lanes]
        mine[firsts[1] + l * padded : firsts[1] + l * padded + mix, :] = ig_ref[:, lanes]
        mine[firsts[4] + 4 * l : firsts[4] + 4 * l + 4, :] = sgg_ref[:, lanes]
        mine[firsts[5] + 4 * l : firsts[5] + 4 * l + 4, :] = sbg_ref[:, lanes]
        mine[firsts[7] + l : firsts[7] + l + 1, :] = ob_ref[:, lanes]
    mine[firsts[2] : firsts[2] + mix, 0:mix] = og_ref[...]
    mine[firsts[3] : firsts[3] + 1, 0:mix] = bg_ref[...]
    for k in range(3):
        for l in range(wl // 2):
            mine[pl.ds(firsts[6] + k * wl + c * (wl // 2) + l, 1), :] = hb_ref[k : k + 1, l * 128 : (l + 1) * 128]
    for l in range(hidden_rows):
        mine[pl.ds(firsts[8] + c * hidden_rows + l, 1), :] = eb_ref[:, l * 128 : (l + 1) * 128]
    sums.deal()
    second_step(2)
    second_step(3)
    sums.tell()
    for t in range(4):
        finish(copies(t, 2))
        total = second[t][0, z].astype(F32)
        for k in range(nz - 1):
            total = total + third[t][k].astype(F32)
        final[t][...] = total.reshape(final[t].shape)
        start(copies(t, 3))
    sums.close()
    for t in range(6):
        finish(copies(t, 3))


def finish_sums(grid, orders, kept, came, folded, smalls, collective_id):
    sgg, _, _, ig, og, bg, _, hb, eb = smalls
    mix, width = ig.shape
    hidden_width = 2 * eb.shape[1]
    nz = grid.nz
    rows, n = kept[0].shape[-2:]
    devices = grid.n_dp * grid.n_seq
    each = -(-small_rows(width, mix, hidden_width)[1] // (devices * 8)) * 8
    vmem = pl.BlockSpec(memory_space=pltpu.VMEM)
    owned = [3 * width, width, hidden_width, hidden_width]
    folds = [fold_scratch(grid, order, rows, n) for order in orders]
    operands = list(kept) + list(came) + list(folded) + list(smalls)
    return pl.pallas_call(
        functools.partial(finish_kernel, grid, orders, len(kept)),
        out_shape=[jax.ShapeDtypeStruct((devices * each, 128), F32)] + [jax.ShapeDtypeStruct((rows // 2, w), F32) for w in owned],
        in_specs=[vmem] * len(operands),
        out_specs=[vmem] + [pl.BlockSpec(memory_space=pl.ANY)] * len(owned),
        scratch_shapes=[f for _, f, _ in folds]
        + [s for _, _, s in folds]
        + [pltpu.VMEM((nz - 1, rows, n), BF16)] * 4
        + [pltpu.VMEM((2, rows // 2, n), F32)] * 4
        + [pltpu.VMEM((2, rows // 2, hidden_width // 2), F32)] * 2
        + [
            pltpu.VMEM((devices * each, 128), F32),
            pltpu.VMEM((devices * each, 128), F32),
            pltpu.VMEM((each, 128), F32),
            pltpu.SemaphoreType.DMA((2,)),
            pltpu.SemaphoreType.DMA((2,)),
            pltpu.SemaphoreType.DMA((6,)),
            pltpu.SemaphoreType.DMA((6, nz + grid.nb)),
            pltpu.SemaphoreType.DMA((6, nz + grid.nb)),
        ],
        compiler_params=pltpu.CompilerParams(collective_id=collective_id, has_side_effects=True, vmem_limit_bytes=VMEM_LIMIT),
        cost_estimate=pl.CostEstimate(flops=0, bytes_accessed=100 * width * width, transcendentals=0),
        name="finish_sums",
    )(*operands)


def hand_kernel(mix, hidden_width, done, out_ref, *refs):
    owned, placed_ref, small, outs = refs[:4], refs[4], refs[5:14], refs[14:]
    width = out_ref.shape[1]
    wl, padded, hidden_rows = width // 128, -(-mix // 8) * 8, hidden_width // 256
    firsts, _ = small_rows(width, mix, hidden_width)
    placed_ref[...] = out_ref[...]
    outs, again = outs[:4], outs[4]
    for src, dst in zip(owned, outs):
        dst[...] = src[...]
    for l in range(wl):
        lanes = slice(l * 128, (l + 1) * 128)
        small[0][:, lanes] = done[firsts[0] + l : firsts[0] + l + 1, :]
        small[1][:, lanes] = done[firsts[1] + l * padded : firsts[1] + l * padded + mix, :]
        small[4][:, lanes] = done[firsts[4] + 4 * l : firsts[4] + 4 * l + 4, :]
        small[5][:, lanes] = done[firsts[5] + 4 * l : firsts[5] + 4 * l + 4, :]
        small[7][:, lanes] = again[:, lanes] = done[firsts[7] + l : firsts[7] + l + 1, :]
    small[2][...] = done[firsts[2] : firsts[2] + mix, 0:mix]
    small[3][...] = done[firsts[3] : firsts[3] + 1, 0:mix]
    for l in range(3 * wl):
        small[6][:, l * 128 : (l + 1) * 128] = done[firsts[6] + l : firsts[6] + l + 1, :]
    for l in range(2 * hidden_rows):
        small[8][:, l * 128 : (l + 1) * 128] = done[firsts[8] + l : firsts[8] + l + 1, :]


def hand_over(summed, layer_out, owned, mix, hidden_width):
    width = layer_out.shape[1]
    small = [(1, width), (mix, width), (mix, mix), (1, mix), (4, width), (4, width), (1, 3 * width), (1, width), (1, hidden_width)]
    vmem = pl.BlockSpec(memory_space=pltpu.VMEM)
    return pl.pallas_call(
        functools.partial(hand_kernel, mix, hidden_width),
        out_shape=[jax.ShapeDtypeStruct(layer_out.shape, BF16)]
        + [jax.ShapeDtypeStruct(shape, F32) for shape in small]
        + [jax.ShapeDtypeStruct(x.shape, F32) for x in owned]
        + [jax.ShapeDtypeStruct((1, width), F32)],
        in_specs=[vmem] * 6,
        out_specs=[vmem] * 15,
        name="hand_over",
    )(summed, layer_out, *owned)


def far_first(nz, z, i):
    pairs = nz // 2
    return lax.rem(i + pairs // 2 * (1 - z // pairs), pairs)


def unproject_kernel(grid, width, orders, *all_refs):
    nz = grid.nz
    mids, lates, last_parts, all_refs = all_refs[:nz], all_refs[nz : 2 * nz], all_refs[2 * nz : 2 * nz + 2], all_refs[2 * nz + 2 :]
    (col_ref, low_ref, g_ref, w_ref, feed_ref, normed_ref, last_ref, bias_ref, bias2_ref, cos_ref, above_ref,
     below_ref, own_ref, theirs_ref, hb_ref, out_ref, sum_ref, *refs) = all_refs
    nb = grid.nb
    lasts, refs = refs[:nz], refs[nz:]
    kept, over_a, over_b, refs = refs[:4], refs[4], refs[5 : 4 + nb], refs[4 + nb :]
    grad_ref, sending_ref, partial_ref, mine_ref, arrived_ref, along_ref, split_sem, send_sem, recv_sem, along_send, along_recv = refs[:11]
    keep_refs, firsts, seconds, (fold_send, fold_recv, late_sem) = refs[11:13], refs[13:15], refs[15:17], refs[17:]
    i = pl.program_id(0)
    a, b, z, c = grid.here()
    tokens = out_ref.shape[0]
    other = grid.device(a, b, z, 1 - c)
    own_rows = pl.ds(pl.multiple_of(c * tokens, tokens), tokens)
    their_rows = pl.ds(pl.multiple_of((1 - c) * tokens, tokens), tokens)

    def swap(k):
        return [remote(sending_ref.at[k], theirs_ref.at[k], send_sem.at[k], recv_sem.at[k], other)]

    def swap_out():
        return [remote(partial_ref, arrived_ref, send_sem.at[4], recv_sem.at[4], other)]

    def along():
        return [
            remote(mids[k], along_ref.at[k - 1], along_send.at[k - 1], along_recv.at[k - 1], grid.device(a, b, lax.rem(z + k, nz), c))
            for k in range(1, nz)
        ]

    def fold(t, stage):
        if stage < 2:
            order = ("ab", "ba")[t]
            found = fold_copies(grid, (a, b, z, c), order, stage, last_parts[t], firsts[t], seconds[t], (fold_send.at[t], fold_recv.at[t]))
            if stage == 0:
                kept_part = last_parts[t].at[a] if order == "ab" else last_parts[t].at[:, b]
                found.append(pltpu.make_async_copy(kept_part, keep_refs[t], late_sem.at[t]))
            return found
        n = seconds[t].shape[-1]
        return [
            pltpu.make_async_copy(seconds[t].at[0, lax.rem(z + k, nz)], lasts[k].at[t, :, pl.ds(n, n)], late_sem.at[2 + t * nz + k])
            for k in range(nz)
        ]

    def settle(stage):
        for t in range(2):
            finish(fold(t, stage))
            fold_add(grid, (a, b, z, c), ("ab", "ba")[t], stage, keep_refs[t], firsts[t], seconds[t])
            start(fold(t, stage + 1))

    def place_lates():
        n = lates[0].shape[-1]
        return [pltpu.make_async_copy(lates[k], lasts[k].at[:, :, pl.ds(0, n)], late_sem.at[2 + 2 * nz + k]) for k in range(nz)]

    def split(k):
        grad = grad_ref.at[k]
        if orders[k] == "ab":
            found = [(grad.at[a], kept[k]), (grad.at[1 - a], over_a.at[k // 2])]
        else:
            found = [(grad.at[:, b], kept[k])]
            found += [(grad.at[:, lax.rem(b + m, nb)], over_b[m - 1].at[k // 2]) for m in range(1, nb)]
        return [pltpu.make_async_copy(src, dst, split_sem.at[k, n]) for n, (src, dst) in enumerate(found)]

    def piece(n):
        return jnp.concatenate([col_ref[m, :, n * width : (n + 1) * width] for m in range(nz)], axis=1)

    def keep(k, grad):
        grad_ref[k] = grad.astype(BF16).reshape(grad_ref.shape[1:])
        start(split(k))

    @pl.when(i == 0)
    def _():
        grid.greet(a, b, z, c)
        for t in range(2):
            start(fold(t, 0))
        start(along())
        start(place_lates())
        mine_ref[...] = piece(0)
        partial_ref[...] = against(mine_ref[their_rows, :], w_ref[0]) + feed_ref[their_rows, :]
        sending_ref[3] = normed_ref[their_rows, :].astype(BF16)
        start(swap_out())
        start(swap(3))
        own_ref[0] = normed_ref[own_rows, :]
        out = against(mine_ref[own_rows, :], w_ref[0]) + feed_ref[own_rows, :] + last_ref[0] + (row(bias_ref) + row(bias2_ref))
        keep(3, inner(g_ref[...], mine_ref[...]))
        finish(swap_out())
        out_ref[...] = (out + arrived_ref[...]).astype(BF16)

    for k in range(3):

        @pl.when(i == k + 1)
        def _(k=k):
            if k == 2:
                settle(0)
            grad = piece(k + 1).astype(F32)
            if k < 2:
                tables = [jnp.concatenate([t[...]] * (grad.shape[1] // 128), axis=1) for t in (cos_ref, above_ref, below_ref)]
                grad = rotate(grad, tables, -1.0)
            hb_ref[k : k + 1, :] = jnp.sum(grad, axis=0, keepdims=True)
            mine_ref[...] = grad.astype(BF16)
            sending_ref[k] = against(mine_ref[their_rows, :], w_ref[0]).astype(BF16)
            start(swap(k))
            own_ref[0] = against(mine_ref[own_rows, :], w_ref[0])
            keep(k, inner(low_ref[0], mine_ref[...]))
            if k == 2:
                for n in range(4):
                    finish(swap(n))
                    finish(split(n))
                settle(1)
                finish(along())
                total = mids[0][...].astype(F32)
                for n in range(nz - 1):
                    total = total + along_ref[n].astype(F32)
                sum_ref[...] = total
                for t in range(2):
                    finish(fold(t, 2))
                finish(place_lates())


def unproject(grid, orders, mids, lates, last_parts, collected, lowered, grad_low, weights, feed_part, normed_feed, streams, biases, tables, own_width, collective_id):
    _, tokens, width = streams.shape
    both, half = 2 * tokens, width // 2
    na, nb, nz = grid.na, grid.nb, grid.nz
    rows = width // (na * nb * nz)
    n = lates[0].shape[-1]
    folds = [fold_scratch(grid, order, rows, n) for order in ("ab", "ba")]
    whole = pl.BlockSpec(memory_space=pltpu.VMEM)
    anywhere = pl.BlockSpec(memory_space=pl.ANY)
    turn = lambda i: lax.rem(i + 3, 4)
    split_shapes = [jax.ShapeDtypeStruct((nb if order == "ab" else na, nz, rows, half), BF16) for order in orders]
    sent_shapes = [jax.ShapeDtypeStruct((2, nb, nz, rows, half), BF16)] + [jax.ShapeDtypeStruct((2, na, nz, rows, half), BF16)] * (nb - 1)
    results = pl.pallas_call(
        functools.partial(unproject_kernel, grid, own_width, orders),
        grid=(4,),
        out_shape=[
            jax.ShapeDtypeStruct((4, tokens, width), F32),
            jax.ShapeDtypeStruct((4, tokens, width), BF16),
            jax.ShapeDtypeStruct((3, half), F32),
            jax.ShapeDtypeStruct((tokens, width), BF16),
            jax.ShapeDtypeStruct(mids[0].shape, F32),
        ]
        + [jax.ShapeDtypeStruct((2, rows, 2 * n), BF16)] * nz
        + split_shapes
        + sent_shapes,
        in_specs=[whole]
        + [anywhere] * (nz - 1)
        + [whole] * nz
        + [anywhere] * 2
        + [
            whole,
            pl.BlockSpec((1, both, width), lambda i: (jnp.maximum(i - 1, 0), 0, 0)),
            whole,
            pl.BlockSpec((1, width, half), lambda i: (turn(i), 0, 0)),
        ]
        + [whole] * 2
        + [pl.BlockSpec((1, tokens, width), lambda i: (3, 0, 0))]
        + [whole] * 5,
        out_specs=[
            pl.BlockSpec((1, tokens, width), lambda i: (turn(i), 0, 0)),
            anywhere,
            pl.BlockSpec((3, half), lambda i: (0, 0)),
            pl.BlockSpec((tokens, width), lambda i: (0, 0)),
            pl.BlockSpec(mids[0].shape, lambda i: (0, 0, 0)),
        ]
        + [anywhere] * (nz + len(split_shapes) + len(sent_shapes)),
        scratch_shapes=[
            pltpu.VMEM((4, na, nb, nz, rows, half), BF16),
            pltpu.VMEM((4, tokens, width), BF16),
            pltpu.VMEM((tokens, width), F32),
            pltpu.VMEM((both, half), BF16),
            pltpu.VMEM((tokens, width), F32),
            pltpu.VMEM((nz - 1, *mids[0].shape), BF16),
            pltpu.SemaphoreType.DMA((4, nb + 1)),
            pltpu.SemaphoreType.DMA((5,)),
            pltpu.SemaphoreType.DMA((5,)),
            pltpu.SemaphoreType.DMA((nz - 1,)),
            pltpu.SemaphoreType.DMA((nz - 1,)),
            *[o for o, _, _ in folds],
            *[f for _, f, _ in folds],
            *[f for _, _, f in folds],
            pltpu.SemaphoreType.DMA((2, nz + nb)),
            pltpu.SemaphoreType.DMA((2, nz + nb)),
            pltpu.SemaphoreType.DMA((2 + 3 * nz,)),
        ],
        compiler_params=pltpu.CompilerParams(collective_id=collective_id, has_side_effects=True, vmem_limit_bytes=VMEM_LIMIT),
        cost_estimate=pl.CostEstimate(flops=32 * both * width * half, bytes_accessed=40 * both * width, transcendentals=0),
        name="unproject",
    )(*mids, *lates, *last_parts, collected, lowered, grad_low, weights, feed_part, normed_feed, streams, *biases, *tables)
    own, theirs, head_bias, layer_out, mid_sums = results[:5]
    lasts, results = results[5 : 5 + nz], results[5 + nz :]
    return own, theirs, head_bias, layer_out, mid_sums, lasts, results[:4], results[4:]


def feed_kernel(grid, steps, back_ref, low_ref, g_ref, we_ref, wc_ref, bias_ref, collected_ref, feed_ref, normed_ref, eb_ref, *refs):
    nz = grid.nz
    groups = steps - 1
    mids, outs, whole_outs, refs = refs[:nz], refs[nz : 2 * nz], refs[2 * nz : 2 * nz + 2], refs[2 * nz + 2 :]
    parts, refs = refs[: 2 * steps], refs[2 * steps :]
    first, second, refs = refs[: 2 * groups], refs[2 * groups : 4 * groups], refs[4 * groups :]
    bias_full, send_sem, recv_sem, out_sem, back_send, back_recv = refs
    i = pl.program_id(0)
    a, b, z, c = place = grid.here()
    orders = ["ab", "ba"] * steps

    def copies(t, stage):
        if stage < 2:
            return fold_copies(grid, place, orders[t], stage, parts[t], first[t], second[t], (send_sem.at[t], recv_sem.at[t]))
        along = [lax.rem(z + k, nz) for k in range(nz)]
        u, n = t // 2, parts[t].shape[-1]
        late = u == groups - 1
        cols = pl.ds(0 if late else u * n, n)
        spot = outs if late else mids
        return [pltpu.make_async_copy(second[t].at[0, along[k]], spot[k].at[t % 2, :, cols], out_sem.at[t, k]) for k in range(nz)]

    def last_parts():
        return [pltpu.make_async_copy(parts[2 * groups + k], whole_outs[k], out_sem.at[2 * groups + k, 0]) for k in range(2)]

    def begin(u):
        for t in (2 * u, 2 * u + 1):
            start(copies(t, 0))

    def end(u, stage):
        for t in (2 * u, 2 * u + 1):
            finish(copies(t, stage))
            if stage < 2:
                own = parts[t].at[a] if orders[t] == "ab" else parts[t].at[:, b]
                fold_add(grid, place, orders[t], stage, own, first[t], second[t])
                start(copies(t, stage + 1))

    def turn(u):
        for stage in range(3):
            if 0 <= u - stage < groups:
                end(u - stage, stage)

    def backs():
        found = [pltpu.make_async_copy(back_ref.at[z], collected_ref.at[z], back_send.at[0])]
        for k in range(1, nz):
            to = lax.rem(z + k, nz)
            found.append(remote(back_ref.at[to], collected_ref.at[z], back_send.at[k], back_recv.at[k], grid.device(a, b, to, c)))
        return found

    @pl.when(i == 0)
    def _():
        grid.greet(*place)
        start(backs())
        bias_full[...] = bias_ref[...].astype(F32)
        feed_ref[...] = jnp.zeros_like(feed_ref)
        normed_ref[...] = jnp.zeros_like(normed_ref)

    low, grad, expand, contract = low_ref[0], g_ref[...], we_ref[...], wc_ref[...]
    wide = expand.shape[1] // 128
    first_row = c * (bias_full.shape[0] // 2) + i * wide
    bias = jnp.concatenate([bias_full[pl.ds(first_row + l, 1), :] for l in range(wide)], axis=1)
    expanded = product(low, expand) + bias
    share = phi(expanded)
    hidden = (expanded * share).astype(BF16)
    slope = share + expanded * jnp.exp(-0.5 * expanded * expanded) * (1.0 / math.sqrt(2.0 * math.pi))
    feed_ref[...] += against(hidden, contract)
    hidden_grad = inner(grad, hidden).astype(BF16)
    pulled = product(grad, contract) * slope
    eb_ref[...] = jnp.sum(pulled, axis=0, keepdims=True)
    pulled_low = pulled.astype(BF16)
    normed_ref[...] += against(pulled_low, expand)
    expand_grad = inner(low, pulled_low).astype(BF16)
    for u in range(steps):

        @pl.when(i == u)
        def _(u=u):
            parts[2 * u][...] = expand_grad.reshape(parts[2 * u].shape)
            parts[2 * u + 1][...] = hidden_grad.reshape(parts[2 * u + 1].shape)
            if u < groups:
                begin(u)
            else:
                start(last_parts())
            if u >= 2:
                turn(u - 2)
            if u == steps - 1:
                for v in range(max(steps - 2, 0), groups + 2):
                    turn(v)
                finish(last_parts())
                finish(backs())


def feed_forward(grid, returned, lowered, grad_low, weight_e, weight_c, bias, steps, collective_id):
    both, width = grad_low.shape
    n = weight_e.shape[1] // steps
    na, nb, nz = grid.na, grid.nb, grid.nz
    rows = width // (na * nb * nz)
    whole = lambda *shape: pl.BlockSpec(shape, lambda i: (0,) * len(shape))
    cols = lambda m: pl.BlockSpec((m, n), lambda i: (0, i))
    orders = ["ab", "ba"] * steps
    folds = [fold_scratch(grid, order, rows, n) for order in orders]
    sem = pltpu.SemaphoreType.DMA((2 * steps, nz + nb))
    return pl.pallas_call(
        functools.partial(feed_kernel, grid, steps),
        grid=(steps,),
        out_shape=[
            jax.ShapeDtypeStruct(returned.shape, BF16),
            jax.ShapeDtypeStruct((both, width), F32),
            jax.ShapeDtypeStruct((both, width), F32),
            jax.ShapeDtypeStruct((1, n * steps), F32),
        ]
        + [jax.ShapeDtypeStruct((2, rows, n * (steps - 2)), BF16)] * nz
        + [jax.ShapeDtypeStruct((2, rows, n), BF16)] * nz
        + [jax.ShapeDtypeStruct((na, nb, nz, rows, n), BF16)] * 2,
        in_specs=[
            pl.BlockSpec(memory_space=pltpu.VMEM),
            pl.BlockSpec((1, both, width), lambda i: (3, 0, 0)),
            whole(both, width),
            cols(width),
            cols(width),
            whole(*bias.shape),
        ],
        out_specs=[
            pl.BlockSpec(memory_space=pl.ANY),
            whole(both, width),
            whole(both, width),
            cols(1),
        ]
        + [pl.BlockSpec(memory_space=pl.ANY)] * (2 * nz + 2),
        scratch_shapes=[pltpu.VMEM((na, nb, nz, rows, n), BF16)] * (2 * steps)
        + [f for _, f, _ in folds[:-2]]
        + [s for _, _, s in folds[:-2]]
        + [pltpu.VMEM(bias.shape, F32)]
        + [sem, sem, pltpu.SemaphoreType.DMA((2 * steps, nz)), pltpu.SemaphoreType.DMA((nz,)), pltpu.SemaphoreType.DMA((nz,))],
        compiler_params=pltpu.CompilerParams(collective_id=collective_id, has_side_effects=True, vmem_limit_bytes=VMEM_LIMIT),
        cost_estimate=pl.CostEstimate(flops=12 * both * width * n * steps * 2, bytes_accessed=width * n * steps * 20, transcendentals=0),
        name="feed_forward",
    )(returned, lowered, grad_low, weight_e, weight_c, bias)


def attention_kernel(width, heads, tile, edge, length, x_ref, qdoc_ref, out_ref, kdoc_ref,
                     s_ref, kt_ref, vt_ref, ot_ref, dqt_ref, dka_ref, dva_ref, top_ref):
    i = pl.program_id(0)
    tiles = length // tile
    scale = 1.0 / math.sqrt(HEAD_DIM)
    @pl.when(i == 0)
    def _():
        dka_ref[...] = jnp.zeros_like(dka_ref)
        dva_ref[...] = jnp.zeros_like(dva_ref)
        def turn(j, carry):
            at = pl.ds(pl.multiple_of(j * tile, tile), tile)
            kt_ref[:, at] = x_ref[at, width : 2 * width].T
            kdoc_ref[at, :] = jnp.broadcast_to(qdoc_ref[:, at].astype(F32), (128, tile)).T
            vt_ref[:, at] = x_ref[at, 2 * width : 3 * width].T
            return carry
        lax.fori_loop(0, tiles, turn, 0)
    rows = pl.ds(pl.multiple_of(i * tile, tile), tile)
    query = x_ref[rows, 0:width] * jnp.asarray(scale, BF16)
    grad = x_ref[rows, 3 * width : 4 * width]
    query_t, grad_t = query.T, grad.T
    lanes = lax.broadcasted_iota(jnp.int32, (tile, width), 1) // HEAD_DIM
    subs = lax.broadcasted_iota(jnp.int32, (width, tile), 0) // HEAD_DIM
    zero = jnp.zeros((), BF16)
    queries_t = [jnp.where(subs == h, query_t, zero) for h in range(heads)]
    grads_t = [jnp.where(subs == h, grad_t, zero) for h in range(heads)]
    spread_queries = [jnp.where(lanes == h, query, zero) for h in range(heads)]
    spread_grads = [jnp.where(lanes == h, grad, zero) for h in range(heads)]
    qdoc = qdoc_ref[:, rows].astype(F32)
    head_edge = -(-edge // tile)
    tail_edge = (length - edge) // tile
    half = tile // 2
    corners = [(0, half, 0), (half, half, half)]
    ot_ref[...] = jnp.zeros_like(ot_ref)
    dqt_ref[...] = jnp.zeros_like(dqt_ref)
    top_ref[...] = jnp.full_like(top_ref, NEG)

    def fold(x, f):
        return f(x.reshape(x.shape[0] // 8, 8, x.shape[1]), axis=0)

    def score(first, size, left, documents, causal):
        at = pl.ds(pl.multiple_of(first, size), size)
        keys = x_ref[at, width : 2 * width]
        wide = tile - left
        if documents:
            allowed = jnp.concatenate([kdoc_ref[at, :]] * (wide // 128), axis=1) == qdoc[:, left:]
        if causal:
            allowed &= lax.broadcasted_iota(jnp.int32, (size, wide), 0) <= lax.broadcasted_iota(jnp.int32, (size, wide), 1)
        for h in range(heads):
            s = product(keys, queries_t[h][:, left:])
            if documents:
                s = jnp.where(allowed, s, NEG)
            s_ref[h, at, left:] = s
            top_ref[h, :, left:] = jnp.maximum(top_ref[h, :, left:], fold(s, jnp.max))

    def scores(j, carry):
        checked = (j < head_edge) | (i >= tail_edge)
        pl.when(checked)(lambda: score(j * tile, tile, 0, True, False))
        pl.when(jnp.logical_not(checked))(lambda: score(j * tile, tile, 0, False, False))
        return carry

    lax.fori_loop(0, i, scores, 0)
    for first, size, left in corners:
        score(i * tile + first, size, left, True, True)
    tops = [jnp.max(top_ref[h], axis=0, keepdims=True) for h in range(heads)]
    top_ref[...] = jnp.zeros_like(top_ref)

    def weigh(first, size, left):
        at = pl.ds(pl.multiple_of(first, size), size)
        for h in range(heads):
            own = slice(h * HEAD_DIM, (h + 1) * HEAD_DIM)
            weights = jnp.exp(s_ref[h, at, left:] - tops[h][:, left:])
            s_ref[h, at, left:] = weights
            top_ref[h, :, left:] += fold(weights, jnp.sum)
            ot_ref[own, left:] += product(vt_ref[own, at], weights.astype(BF16))

    lax.fori_loop(0, i, lambda j, carry: (weigh(j * tile, tile, 0), carry)[1], 0)
    for first, size, left in corners:
        weigh(i * tile + first, size, left)
    inverse = [1.0 / jnp.sum(top_ref[h], axis=0, keepdims=True) for h in range(heads)]
    grad_f = grad_t.astype(F32)
    deltas = []
    for h in range(heads):
        own = slice(h * HEAD_DIM, (h + 1) * HEAD_DIM)
        value = ot_ref[own, :] * inverse[h]
        ot_ref[own, :] = value
        deltas.append(jnp.sum(value * grad_f[own], axis=0, keepdims=True))
    out_ref[rows, 0:width] = ot_ref[...].T.astype(BF16)

    def back(first, size, left):
        at = pl.ds(pl.multiple_of(first, size), size)
        values = x_ref[at, 2 * width : 3 * width]
        probs_low, grads_low = [], []
        for h in range(heads):
            own = slice(h * HEAD_DIM, (h + 1) * HEAD_DIM)
            probs_grad = product(values, grads_t[h][:, left:])
            probs = s_ref[h, at, left:] * inverse[h][:, left:]
            scores_grad = (probs * (probs_grad - deltas[h][:, left:])).astype(BF16)
            probs_low.append(probs.astype(BF16))
            grads_low.append(scores_grad)
            dqt_ref[own, left:] += product(kt_ref[own, at], scores_grad)
        dva_ref[at, :] += product(jnp.concatenate(probs_low, axis=1), jnp.concatenate([x[left:] for x in spread_grads], axis=0))
        dka_ref[at, :] += product(jnp.concatenate(grads_low, axis=1), jnp.concatenate([x[left:] for x in spread_queries], axis=0))

    lax.fori_loop(0, i, lambda j, carry: (back(j * tile, tile, 0), carry)[1], 0)
    for first, size, left in corners:
        back(i * tile + first, size, left)
    out_ref[rows, width : 2 * width] = (dqt_ref[...].T * scale).astype(BF16)

    @pl.when(i == tiles - 1)
    def _():
        out_ref[:, 2 * width : 3 * width] = dka_ref[...].astype(BF16)
        out_ref[:, 3 * width : 4 * width] = dva_ref[...].astype(BF16)


def attention(dealt, documents, heads, edge):
    length = dealt.shape[0]
    width = heads * HEAD_DIM
    tile = 2 * edge
    pairs = length * length // 2 * heads
    whole = lambda i: (0, 0)
    return pl.pallas_call(
        functools.partial(attention_kernel, width, heads, tile, edge, length),
        grid=(length // tile,),
        out_shape=jax.ShapeDtypeStruct((length, 4 * width), BF16),
        in_specs=[pl.BlockSpec((length, 4 * width), whole), pl.BlockSpec((1, length), whole)],
        out_specs=pl.BlockSpec((length, 4 * width), whole),
        scratch_shapes=[
            pltpu.VMEM((length, 128), F32), pltpu.VMEM((heads, length, tile), F32), pltpu.VMEM((width, length), BF16), pltpu.VMEM((width, length), BF16),
            pltpu.VMEM((width, tile), F32), pltpu.VMEM((width, tile), F32), pltpu.VMEM((length, width), F32), pltpu.VMEM((length, width), F32),
            pltpu.VMEM((heads, 8, tile), F32)],
        compiler_params=pltpu.CompilerParams(vmem_limit_bytes=VMEM_LIMIT),
        cost_estimate=pl.CostEstimate(flops=pairs * 64 * 2 * 6 * 4, bytes_accessed=length * width * 20, transcendentals=pairs),
        name="attention",
    )(dealt, documents)


def on_device(
    grid,
    history,
    documents,
    cotangent,
    mixer_gain,
    mixer_inner,
    mixer_outer,
    mixer_bias,
    stream_gain,
    stream_bias,
    inbound_weight,
    inbound_bias,
    outbound_weight,
    outbound_bias,
    expand,
    expand_bias,
    contract,
    contract_bias,
):
    n_dp, n_seq, nz = grid.n_dp, grid.n_seq, grid.nz
    tokens, width = history.shape[2], history.shape[3]
    hidden_width = expand.shape[1]
    half, hidden_half = width // 2, hidden_width // 2
    both = 2 * tokens
    length = documents.shape[1]
    mix = mixer_bias.shape[0]
    heads = HEADS // n_seq
    own_width = heads * HEAD_DIM
    pick = lambda base, n: (lambda core: base + core * n)
    parts = 4
    piece = hidden_half // parts
    feed = []
    for part in range(parts):
        base = lambda core, part=part: core * hidden_half + part * piece
        feed.append((2, base, 4, part * piece, piece, "ba"))
        feed.append((3, base, 5, part * piece, piece, "ab"))
    pairs = [[4 + 2 * part, 5 + 2 * part] for part in range(parts)]
    inner_t = mixer_inner.T
    lowered, grad_low, streams, mix_pre, coeffs, tables, weights, (weight_e, weight_c), dealt = mix_forward(
        grid,
        history,
        cotangent,
        [mixer_gain.reshape(-1, 128), inner_t, mixer_outer, mixer_bias[None], stream_gain, stream_bias, inbound_bias.reshape(-1, 128)],
        [inbound_weight, outbound_weight, expand, contract],
        [
            (0, pick(width, half), 1, 0, half, "ba"),
            (0, pick(2 * width, half), 2, 0, half, "ab"),
            (0, pick(0, half), 0, 0, half, "ba"),
            (1, pick(0, half), 3, 0, half, "ab"),
        ]
        + feed,
        [[0, 1], [2, 3]],
        pairs,
        [hidden_half] * 2,
        own_width,
        1,
    )

    returned = attention(dealt.reshape(length, 4 * own_width), documents, heads, tokens)
    returned = returned.reshape(nz, both, 4 * own_width)

    collected, feed_part, normed_feed, expand_bias_part, *rest = feed_forward(
        grid, returned, lowered, grad_low, weight_e, weight_c, expand_bias.reshape(-1, 128), STEPS, 3
    )

    orders = ("ab", "ba", "ab", "ba")
    bias_out = [outbound_bias.reshape(-1, 128), contract_bias.reshape(-1, 128)]
    mids, lates, last_parts = rest[:nz], rest[nz : 2 * nz], rest[2 * nz :]
    normed_own, normed_theirs, head_bias_part, layer_out, mid_sums, lasts, kept, leaving = unproject(
        grid, orders, mids, lates, last_parts, collected, lowered, grad_low, weights, feed_part, normed_feed, streams, bias_out, tables, own_width, 4
    )

    along_z = [[(s, (s // 2 + k) % nz * 2 + s % 2) for s in range(n_seq)] for k in range(nz)]
    folded = [lasts[0]] + [lax.ppermute(lasts[k], "seq", along_z[k]) for k in range(1, nz)]
    nb = grid.nb
    over_a = [(d, (d + nb) % n_dp) for d in range(n_dp)]
    over_b = [[(d, d // nb * nb + (d + k) % nb) for d in range(n_dp)] for k in range(1, nb)]
    came_a = lax.ppermute(leaving[0], "dp", over_a)
    came_b = [lax.ppermute(x, "dp", perm) for x, perm in zip(leaving[1:], over_b)]

    history_grad, *small = mix_backward(
        history, streams, normed_own, normed_theirs, cotangent, mix_pre, coeffs, [mixer_gain.reshape(-1, 128), inner_t, mixer_outer, stream_gain]
    )
    smalls = [*small, head_bias_part, expand_bias_part]
    summed, *owned = finish_sums(grid, orders, kept, [came_a, *came_b], [mid_sums, *folded], smalls, 5)
    layer_out, *small, inbound_grad, outbound_grad, expand_grad, contract_grad, again = hand_over(summed, layer_out, owned, mix, hidden_width)
    gain_grad, inner_grad, outer_grad, bias_grad, stream_gain_grad, stream_bias_grad, in_bias_grad, out_bias_grad, expand_bias_grad = small
    return (
        layer_out[None],
        history_grad,
        gain_grad.reshape(width),
        inner_grad.T,
        outer_grad,
        bias_grad.reshape(-1),
        stream_gain_grad,
        stream_bias_grad,
        inbound_grad,
        in_bias_grad.reshape(3 * width),
        outbound_grad,
        out_bias_grad.reshape(width),
        expand_grad,
        expand_bias_grad.reshape(hidden_width),
        contract_grad,
        again.reshape(width),
    )


def solution(mesh):
    rows = P(("dp", "seq"), None)
    placed = (
        P(None, "dp", "seq", None),
        P("dp", None),
        P("dp", "seq", None),
        P(),
        P(),
        P(),
        P(),
        P(),
        P(),
        rows,
        P(),
        rows,
        P(),
        rows,
        P(),
        rows,
        P(),
    )
    grid = Grid(mesh.shape["dp"], mesh.shape["seq"])
    return jax.shard_map(
        functools.partial(on_device, grid),
        mesh=mesh,
        in_specs=placed,
        out_specs=(
            P("dp", "seq", None),
            P(None, "dp", "seq", None),
            P(),
            P(),
            P(),
            P(),
            P(),
            P(),
            rows,
            P(),
            rows,
            P(),
            rows,
            P(),
            rows,
            P(),
        ),
        check_vma=False,
    )
```

```python
import functools
import math

import jax
import jax.numpy as jnp
from jax import lax
from jax.experimental import pallas as pl
from jax.experimental.pallas import tpu as pltpu
from jax.sharding import PartitionSpec as P

HEADS = 16
HEAD_DIM = 64
ROT_DIMS = 16
EPS = 1e-05
HIGHEST = lax.Precision.HIGHEST
NEG = -1e30
MESH = pl.DeviceIdType.MESH
F32 = jnp.float32
BF16 = jnp.bfloat16
VMEM_LIMIT = 56 * 1024 * 1024
STEPS = 4


def inner(left, right):
    return lax.dot_general(left, right, (((0,), (0,)), ((), ())), preferred_element_type=F32)


def against(left, right):
    return lax.dot_general(left, right, (((1,), (1,)), ((), ())), preferred_element_type=F32)


def product(left, right):
    return jnp.dot(left, right, preferred_element_type=F32)


def exact_gelu(value):
    return jax.nn.gelu(value, approximate=False)


def phi(value):
    return 0.5 * (1.0 + lax.erf(value * (1.0 / math.sqrt(2.0))))


def gelu_slope(value):
    return phi(value) + value * jnp.exp(-0.5 * value * value) * (1.0 / math.sqrt(2.0 * math.pi))


def rotate(value, tables, sign):
    half = ROT_DIMS // 2
    cosine, above, below = tables
    width = value.shape[-1]
    up = pltpu.roll(value, width - half, 1)
    down = pltpu.roll(value, half, 1)
    return value * cosine + sign * (up * above + down * below)


class Grid:
    def __init__(self, n_dp, n_seq):
        self.n_dp, self.n_seq = n_dp, n_seq
        self.na, self.nb, self.nz = 2, n_dp // 2, n_seq // 2

    def here(self):
        dp, seq = lax.axis_index("dp"), lax.axis_index("seq")
        return dp // self.nb, lax.rem(dp, self.nb), seq // 2, lax.rem(seq, 2)

    def device(self, a, b, z, c):
        return (a * self.nb + b, z * 2 + c)

    def peers(self, a, b, z, c):
        found = [self.device(a, b, z, 1 - c), self.device(1 - a, b, z, c)]
        found += [self.device(a, lax.rem(b + k, self.nb), z, c) for k in range(1, self.nb)]
        found += [self.device(a, b, lax.rem(z + k, self.nz), c) for k in range(1, self.nz)]
        return found

    def greet(self, a, b, z, c):
        barrier = pltpu.get_barrier_semaphore()
        found = self.peers(a, b, z, c)
        for peer in found:
            pl.semaphore_signal(barrier, inc=1, device_id=peer, device_id_type=MESH)
        pl.semaphore_wait(barrier, len(found))


def row(ref):
    value = ref[...].astype(F32)
    return jnp.concatenate([value[l : l + 1] for l in range(value.shape[0])], axis=1)


def remote(src, dst, send, recv, device):
    return pltpu.make_async_remote_copy(
        src_ref=src, dst_ref=dst, send_sem=send, recv_sem=recv, device_id=device, device_id_type=MESH
    )


def start(copies):
    for copy in copies:
        copy.start()


def finish(copies):
    for copy in copies:
        copy.wait()


class Gathering:
    def __init__(self, grid, place, rows, chunks, ins, outs, local_sem, send_sem, recv_sem):
        self.grid, self.place, self.rows, self.chunks = grid, place, rows, chunks
        self.ins, self.outs = ins, outs
        self.local_sem, self.send_sem, self.recv_sem = local_sem, send_sem, recv_sem

    def copies(self, t, stage):
        a, b, z, c = self.place
        grid, rows = self.grid, self.rows
        nz, nb = grid.nz, grid.nb
        source, base, result, col, n, order = self.chunks[t]
        out, cols = self.outs[result], pl.ds(col, n)

        def send(src, dst, slot, device):
            return remote(src, dst, self.send_sem.at[t, slot], self.recv_sem.at[t, slot], device)

        if stage == 0:
            mine = self.ins[source].at[:, pl.ds(pl.multiple_of(base(c), 128), n)]
            theirs = self.ins[source].at[:, pl.ds(pl.multiple_of(base(1 - c), 128), n)]
            spot = out.at[a, b, z, pl.ds(pl.multiple_of(c * rows, rows), rows), cols]
            return [pltpu.make_async_copy(mine, spot, self.local_sem.at[t]), send(theirs, spot, 0, grid.device(a, b, z, 1 - c))]
        if order[stage - 2] == "b":
            block = out.at[a, b, :, :, cols] if stage == 2 else out.at[:, b, :, :, cols]
            return [send(block, block, k, grid.device(a, lax.rem(b + k, nb), z, c)) for k in range(1, nb)]
        block = out.at[a, b, :, :, cols] if stage == 2 else out.at[a, :, :, :, cols]
        return [send(block, block, nb, grid.device(1 - a, b, z, c))]

    def hop(self, t, step, begin):
        a, b, z, c = self.place
        nz, nb = self.grid.nz, self.grid.nb
        _, _, result, col, n, _ = self.chunks[t]
        out, cols = self.outs[result], pl.ds(col, n)
        for side, way in enumerate((1, -1)):
            slot = nb + 1 + side * (nz - 1) + step - 1
            there, arriving = z + way, z - way * step
            going = there - way * step
            inside = (there >= 0) & (there < nz) & (going >= 0) & (going < nz)
            coming = (arriving >= 0) & (arriving < nz)

            def link(which, slot=slot, there=there):
                block = out.at[a, b, which, :, cols]
                return remote(block, block, self.send_sem.at[t, slot], self.recv_sem.at[t, slot], self.grid.device(a, b, there, c))

            if begin:
                pl.when(inside)(lambda link=link, going=going: link(going).start())
            else:
                pl.when(inside)(lambda link=link, going=going: link(going).wait_send())
                pl.when(coming)(lambda link=link, arriving=arriving: link(arriving).wait_recv())

    def begin(self, group, stage):
        for t in group:
            start(self.copies(t, stage))

    def end(self, group, stage):
        for t in group:
            finish(self.copies(t, stage))

    def ticks(self, whole, partial):
        groups, nz = whole + partial, self.grid.nz

        def advance(u, at):
            group = groups[u]
            if at == 0:
                self.end(group, 0)
            elif at < nz:
                for t in group:
                    self.hop(t, at, False)
            else:
                self.end(group, 2)
            for t in group:
                if at < nz - 1:
                    self.hop(t, at + 1, True)
                elif u < len(whole):
                    start(self.copies(t, 2 if at == nz - 1 else 3))

        def first():
            for group in groups:
                self.begin(group, 0)

        enter = [u if u < len(whole) else len(whole) + (u - len(whole)) // 2 for u in range(len(groups))]

        def tick(now):
            for u in range(len(groups)):
                if 0 <= now - enter[u] <= (nz if u < len(whole) else nz - 1):
                    advance(u, now - enter[u])

        def last():
            for group in whole:
                self.end(group, 3)

        return [first] + [functools.partial(tick, now) for now in range(max(enter) + nz + 1)] + [last]


def gather_sems(grid, chunks):
    slots = 2 * grid.nz + grid.nb - 1
    return [
        pltpu.SemaphoreType.DMA((len(chunks),)),
        pltpu.SemaphoreType.DMA((len(chunks), slots)),
        pltpu.SemaphoreType.DMA((len(chunks), slots)),
    ]


def fold_copies(grid, place, order, stage, part, first, second, sems):
    a, b, z, c = place
    nz, nb = grid.nz, grid.nb

    def send(src, dst, slot, device):
        return remote(src, dst, sems[0].at[slot], sems[1].at[slot], device)

    if (order == "ab") == (stage == 0):
        src = part.at[1 - a] if stage == 0 else first.at[0, 1 - a]
        dst = first.at[0] if stage == 0 else second.at[0]
        return [send(src, dst, nz + nb - 1, grid.device(1 - a, b, z, c))]
    found = []
    for k in range(1, nb):
        to = lax.rem(b + k, nb)
        src = part.at[:, to] if stage == 0 else first.at[0, to]
        dst = first.at[k - 1] if stage == 0 else second.at[k - 1]
        found.append(send(src, dst, nz + k - 1, grid.device(a, to, z, c)))
    return found


def fold_add(grid, place, order, stage, own, first, second):
    a, b, z, c = place
    nz = grid.nz
    if stage == 0:

        def step(i, carry):
            o, j = i // nz, lax.rem(i, nz)
            total = own[o, j].astype(F32)
            for k in range(first.shape[0]):
                total = total + first[k, o, j].astype(F32)
            first[0, o, j] = total.astype(BF16)
            return carry

        lax.fori_loop(0, first.shape[1] * nz, step, 0)
        return
    mine = b if order == "ab" else a

    def step(j, carry):
        total = first[0, mine, j].astype(F32)
        for k in range(second.shape[0]):
            total = total + second[k, j].astype(F32)
        second[0, j] = total.astype(BF16)
        return carry

    lax.fori_loop(0, nz, step, 0)


def fold_scratch(grid, order, rows, n):
    na, nb, nz = grid.na, grid.nb, grid.nz
    own = pltpu.VMEM((nb if order == "ab" else na, nz, rows, n), BF16)
    first = pltpu.VMEM((1, nb, nz, rows, n) if order == "ab" else (nb - 1, na, nz, rows, n), BF16)
    second = pltpu.VMEM((nb - 1, nz, rows, n) if order == "ab" else (1, nz, rows, n), BF16)
    return own, first, second


class Summing:
    def __init__(self, grid, mine, held, total, done, send_sem, recv_sem):
        self.n_seq, self.count = grid.n_seq, grid.n_dp * grid.n_seq
        self.mine, self.held, self.total, self.done = mine, held, total, done
        self.send_sem, self.recv_sem = send_sem, recv_sem
        self.rows = total.shape[0]
        self.me = lax.axis_index("dp") * grid.n_seq + lax.axis_index("seq")

    def device(self, k):
        other = lax.rem(self.me + k, self.count)
        return other, (other // self.n_seq, lax.rem(other, self.n_seq))

    def part(self, ref, k):
        return ref.at[pl.ds(pl.multiple_of(k * self.rows, self.rows), self.rows)]

    def greet(self):
        barrier = pltpu.get_barrier_semaphore()

        def step(k, carry):
            pl.semaphore_signal(barrier, inc=1, device_id=self.device(k)[1], device_id_type=MESH)
            return carry

        lax.fori_loop(1, self.count, step, 0)

    def settle(self, dst, slot):
        most = pl.ds(0, (self.count - 1) * self.rows)
        remote(self.mine.at[most], dst.at[most], self.send_sem.at[slot], self.recv_sem.at[slot], self.device(1)[1]).wait()

    def deal(self):
        def step(k, carry):
            other, place = self.device(k)
            remote(self.part(self.mine, other), self.part(self.held, self.me), self.send_sem.at[0], self.recv_sem.at[0], place).start()
            return carry

        lax.fori_loop(1, self.count, step, 0)
        at = pl.ds(pl.multiple_of(self.me * self.rows, self.rows), self.rows)
        self.held[at, :] = self.mine[at, :]

    def tell(self):
        self.settle(self.held, 0)

        def add(k, carry):
            return carry + self.held[pl.ds(pl.multiple_of(k * self.rows, self.rows), self.rows), :]

        self.total[...] = lax.fori_loop(0, self.count, add, jnp.zeros(self.total.shape, F32))

        def step(k, carry):
            place = self.device(k)[1]
            remote(self.total, self.part(self.done, self.me), self.send_sem.at[1], self.recv_sem.at[1], place).start()
            return carry

        lax.fori_loop(1, self.count, step, 0)
        self.done[pl.ds(pl.multiple_of(self.me * self.rows, self.rows), self.rows), :] = self.total[...]

    def close(self):
        self.settle(self.done, 1)


def spread_out(coeffs):
    return [jnp.broadcast_to(coeffs[:, k : k + 1], (coeffs.shape[0], 128)) for k in range(coeffs.shape[1])]


def blend(h_ref, coeffs, streams_ref):
    hist, width = h_ref.shape[0], h_ref.shape[3]
    spread = spread_out(coeffs)
    for at in range(0, width, 128):
        lanes = slice(at, at + 128)
        inputs = [h_ref[j, 0, :, lanes].astype(F32) for j in range(hist)]
        for c in range(4):
            total = spread[c * hist] * inputs[0]
            for j in range(1, hist):
                total = total + spread[c * hist + j] * inputs[j]
            streams_ref[c, :, lanes] = total


def mix_kernel(grid, rows, chunks, whole, partial, own_width, h_ref, g_ref, gain_ref, inner_ref, outer_ref, bias_ref, sgain_ref, sbias_ref,
               in_bias_ref, *refs):
    ins, (lowered_ref, gpair_ref, kept_ref, pre_ref, coeffs_ref, cos_ref, above_ref, below_ref) = refs[:4], refs[4:12]
    weights_ref, outs, dealt_ref, refs = refs[12], refs[13:15], refs[15], refs[16:]
    streams_ref, full_ref, gfull_ref, held_ref, sent_ref, bias_full, local_sem, send_sem, recv_sem = refs[:9]
    pair_local, pair_send, pair_recv, deal_send, deal_recv = refs[9:]
    i, steps = pl.program_id(0), pl.num_programs(0)
    a, b, z, c = place = grid.here()
    block = h_ref.shape[2]
    outs = [held_ref.at[k] for k in range(4)] + list(outs)
    work = Gathering(grid, place, rows, chunks, ins, outs, local_sem, send_sem, recv_sem)
    events = work.ticks(whole, partial)
    other = grid.device(a, b, z, 1 - c)
    nz = grid.nz

    def swap_grads():
        return [remote(g_ref.at[0], gfull_ref.at[c], pair_send.at[0], pair_recv.at[0], other)]

    def swap_lowered():
        return [remote(full_ref.at[:, c], full_ref.at[:, c], pair_send.at[1], pair_recv.at[1], other)]

    def hand_out():
        return [
            pltpu.make_async_copy(full_ref, lowered_ref, pair_local.at[0]),
            pltpu.make_async_copy(gfull_ref, gpair_ref, pair_local.at[1]),
            pltpu.make_async_copy(held_ref, weights_ref, pair_local.at[2]),
        ]

    def link(to):
        k = lax.rem(to - z + nz, nz)
        return remote(sent_ref.at[to], dealt_ref.at[z], deal_send.at[k], deal_recv.at[k], grid.device(a, b, to, c))

    def stay():
        return pltpu.make_async_copy(sent_ref.at[z], dealt_ref.at[z], deal_send.at[0])

    def project(n):
        wide = 2 * own_width
        turn = far_first(nz, z, n)
        cols = pl.ds(pl.multiple_of(turn * wide, wide), wide)
        both, width = 2 * full_ref.shape[2], full_ref.shape[3]
        third = bias_full.shape[0] // 3
        tables = [jnp.concatenate([t[...]] * (wide // 128), axis=1) for t in (cos_ref, above_ref, below_ref)]

        def one(k):
            inputs = gfull_ref[...] if k == 3 else full_ref[k]
            found = product(inputs.reshape(both, width), held_ref[k, :, :, :, :, cols].reshape(width, wide))
            if k == 3:
                return found
            first_row = k * third + c * (third // 2) + turn * (wide // 128)
            found = found + jnp.concatenate([bias_full[pl.ds(first_row + l, 1), :] for l in range(wide // 128)], axis=1)
            return rotate(found, tables, 1.0) if k < 2 else found

        for k in range(4):
            x = one(k).astype(BF16)
            for m in range(2):
                sent_ref[turn * 2 + m, :, k * own_width : (k + 1) * own_width] = x[:, m * own_width : (m + 1) * own_width]
        for m in range(2):
            to = turn * 2 + m
            pl.when(to != z)(lambda to=to: link(to).start())
            pl.when(to == z)(lambda: stay().start())

    @pl.when(i == 0)
    def _():
        grid.greet(*place)
        events[0]()
        start(swap_grads())
        gfull_ref[c] = g_ref[0]
        bias_full[...] = in_bias_ref[...].astype(F32)

    for n, at in enumerate((0, 1, 2, 3, 5)):

        @pl.when(i == at)
        def _(n=n):
            events[n + 1]()

    @pl.when(i == 2)
    def _():
        both, wide = cos_ref.shape
        half = ROT_DIMS // 2
        place_in = lax.rem(lax.broadcasted_iota(jnp.int32, (1, wide), 1), HEAD_DIM)
        step = lax.rem(place_in, half)
        freq = jnp.ones((1, wide), F32)
        for k in range(1, half):
            freq = jnp.where(step == k, 10000.0 ** (-2.0 * k / ROT_DIMS), freq)
        angles = (z * both + lax.broadcasted_iota(jnp.int32, (both, wide), 0)).astype(F32) * freq
        turned = place_in < ROT_DIMS
        sine = jnp.where(turned, jnp.sin(angles), 0.0)
        cos_ref[...] = jnp.where(turned, jnp.cos(angles), 1.0)
        above_ref[...] = jnp.where(place_in < half, -sine, 0.0)
        below_ref[...] = jnp.where(place_in < half, 0.0, sine)

    last = h_ref[h_ref.shape[0] - 1, 0].astype(F32)
    r = lax.rsqrt(jnp.mean(last * last, axis=1, keepdims=True) + EPS)
    scaled_low = (last * r * row(gain_ref)).astype(BF16)
    pre = against(scaled_low, inner_ref[...])
    pre_ref[...] = pre
    coeffs = product((pre * phi(pre)).astype(BF16), outer_ref[...]) + bias_ref[...].astype(F32)
    coeffs_ref[...] = coeffs
    blend(h_ref, coeffs, streams_ref)
    at = pl.ds(pl.multiple_of(i * block, block), block)
    for k in range(4):
        stream = streams_ref[k]
        centered = stream - jnp.mean(stream, axis=1, keepdims=True)
        rs = lax.rsqrt(jnp.mean(centered * centered, axis=1, keepdims=True) + EPS)
        gain, bias = sgain_ref[k : k + 1, :].astype(F32), sbias_ref[k : k + 1, :].astype(F32)
        full_ref[k, c, at, :] = (centered * rs * gain + bias).astype(BF16)
    kept_ref[...] = streams_ref[...]

    @pl.when(i == steps - 1)
    def _():
        start(swap_lowered())
        ready = len(whole) + nz - 1
        for event in events[6 : 1 + ready + 1]:
            event()
        events[-1]()
        finish(swap_grads())
        finish(swap_lowered())
        start(hand_out())
        hopped = [u for u in range(len(partial)) if u // 2 + len(whole) + nz - 1 <= ready]
        for u in hopped:
            work.begin(partial[u], 2)
        for n in range(nz // 2):
            project(n)
        for event in events[1 + ready + 1 : -1]:
            event()
        for u in range(len(partial)):
            if u not in hopped:
                work.begin(partial[u], 2)
        for group in partial:
            work.end(group, 2)
            work.begin(group, 3)
        for m in range(1, nz):
            link(lax.rem(z + m, nz)).wait()
        stay().wait()
        finish(hand_out())
        for group in partial:
            work.end(group, 3)


def mix_forward(grid, history, cotangent, params, weights, chunks, groups, partial, widths, own_width, collective_id):
    hist, _, tokens, width = history.shape
    mix = params[1].shape[0]
    block = 64
    rows = weights[0].shape[0]
    whole = pl.BlockSpec(memory_space=pltpu.VMEM)
    anywhere = pl.BlockSpec(memory_space=pl.ANY)
    part = lambda n: pl.BlockSpec((block, n), lambda i: (i, 0))
    chips = (grid.na, grid.nb, grid.nz, 2 * rows)
    results = pl.pallas_call(
        functools.partial(mix_kernel, grid, rows, chunks, groups, partial, own_width),
        grid=(tokens // block,),
        out_shape=[
            jax.ShapeDtypeStruct((4, 2, tokens, width), BF16),
            jax.ShapeDtypeStruct((2, tokens, width), BF16),
            jax.ShapeDtypeStruct((4, tokens, width), F32),
            jax.ShapeDtypeStruct((tokens, mix), F32),
            jax.ShapeDtypeStruct((tokens, mix), F32),
        ]
        + [jax.ShapeDtypeStruct((2 * tokens, 128), F32)] * 3
        + [jax.ShapeDtypeStruct((4, *chips, width // 2), BF16)]
        + [jax.ShapeDtypeStruct((*chips, w), BF16) for w in widths]
        + [jax.ShapeDtypeStruct((grid.nz, 2 * tokens, 4 * own_width), BF16)],
        in_specs=[pl.BlockSpec((hist, 1, block, width), lambda i: (0, 0, i, 0))] + [whole] * 12,
        out_specs=[anywhere, anywhere, pl.BlockSpec((4, block, width), lambda i: (0, i, 0)), part(mix), part(mix)]
        + [pl.BlockSpec((2 * tokens, 128), lambda i: (0, 0))] * 3
        + [anywhere] * 4,
        scratch_shapes=[
            pltpu.VMEM((4, block, width), F32),
            pltpu.VMEM((4, 2, tokens, width), BF16),
            pltpu.VMEM((2, tokens, width), BF16),
            pltpu.VMEM((4, *chips, width // 2), BF16),
            pltpu.VMEM((grid.nz, 2 * tokens, 4 * own_width), BF16),
            pltpu.VMEM(params[-1].shape, F32),
            *gather_sems(grid, chunks),
            pltpu.SemaphoreType.DMA((3,)),
            pltpu.SemaphoreType.DMA((2,)),
            pltpu.SemaphoreType.DMA((2,)),
            pltpu.SemaphoreType.DMA((grid.nz,)),
            pltpu.SemaphoreType.DMA((grid.nz,)),
        ],
        compiler_params=pltpu.CompilerParams(collective_id=collective_id, has_side_effects=True, vmem_limit_bytes=VMEM_LIMIT),
        cost_estimate=pl.CostEstimate(flops=tokens * width * 80, bytes_accessed=history.size * 40, transcendentals=0),
        name="mix_forward",
    )(history, cotangent, *params, *weights)
    lowered, gpair, streams, pre, coeffs = results[:5]
    return (
        lowered.reshape(4, 2 * tokens, width),
        gpair.reshape(2 * tokens, width),
        streams,
        pre,
        coeffs,
        results[5:8],
        results[8].reshape(4, width, width // 2),
        [x.reshape(-1, x.shape[-1]) for x in results[9:-1]],
        results[-1],
    )


def small_rows(width, mix, hidden_width):
    wl, padded = width // 128, -(-mix // 8) * 8
    sizes = [wl, wl * padded, padded, 8, 4 * wl, 4 * wl, 3 * wl, wl, hidden_width // 128]
    firsts = [sum(sizes[:k]) for k in range(len(sizes))]
    return firsts, sum(sizes)


def unmix_kernel(h_ref, streams_ref, own_ref, theirs_ref, g_ref, pre_ref, coeffs_ref, gain_ref, inner_ref, outer_ref, sgain_ref,
                 hist_ref, sgg_ref, sbg_ref, gg_ref, ig_ref, og_ref, bg_ref, ob_ref,
                 sg_ref, scaled_ref, mpg_ref, hidden_ref, cgl_ref):
    i, steps = pl.program_id(0), pl.num_programs(0)
    hist, block, width = h_ref.shape[0], h_ref.shape[2], h_ref.shape[3]
    mix = 4 * hist

    @pl.when(i == 0)
    def _():
        for ref in (sgg_ref, sbg_ref, gg_ref, bg_ref, ob_ref):
            ref[...] = jnp.zeros_like(ref)

    def down(x):
        return jnp.sum(x, axis=0, keepdims=True)

    spread = spread_out(coeffs_ref[...])
    grad = g_ref[0].astype(F32)
    ob_ref[...] += down(grad)
    for k in range(4):
        stream = streams_ref[k]
        centered = stream - jnp.mean(stream, axis=1, keepdims=True)
        rs = lax.rsqrt(jnp.mean(centered * centered, axis=1, keepdims=True) + EPS)
        n = centered * rs
        ng = own_ref[k] + theirs_ref[k].astype(F32)
        sgg_ref[k : k + 1, :] += down(ng * n)
        sbg_ref[k : k + 1, :] += down(ng)
        w = ng * sgain_ref[k : k + 1, :].astype(F32)
        pulled = rs * (w - jnp.mean(w, axis=1, keepdims=True) - n * jnp.mean(w * n, axis=1, keepdims=True))
        sg_ref[k] = pulled + grad if k == 3 else pulled

    lane = lax.broadcasted_iota(jnp.int32, (block, mix), 1)
    cg = jnp.zeros((block, mix), F32)
    for j in range(hist):
        value = h_ref[j, 0].astype(F32)
        for k in range(4):
            cg = jnp.where(lane == k * hist + j, jnp.sum(value * sg_ref[k], axis=1, keepdims=True), cg)
    bg_ref[...] += down(cg)
    cg_low = cg.astype(BF16)
    pre = pre_ref[...]
    at = pl.ds(pl.multiple_of(i * block, block), block)
    mpg = (against(cg_low, outer_ref[...]) * gelu_slope(pre)).astype(BF16)
    last = h_ref[hist - 1, 0].astype(F32)
    r = lax.rsqrt(jnp.mean(last * last, axis=1, keepdims=True) + EPS)
    gain = row(gain_ref)
    scaled_ref[at, :] = (last * r * gain).astype(BF16)
    mpg_ref[at, :] = mpg
    hidden_ref[at, :] = (pre * phi(pre)).astype(BF16)
    cgl_ref[at, :] = cg_low
    scaled_grad = product(mpg, inner_ref[...])
    gg_ref[...] += down(scaled_grad * last * r)
    w = scaled_grad * gain
    last_grad = r * (w - last * (r * r) * jnp.mean(w * last, axis=1, keepdims=True))
    for from_ in range(0, width, 128):
        lanes = slice(from_, from_ + 128)
        pulls = [sg_ref[k, :, lanes] for k in range(4)]
        for j in range(hist):
            total = spread[j] * pulls[0]
            for k in range(1, 4):
                total = total + spread[k * hist + j] * pulls[k]
            hist_ref[j, 0, :, lanes] = total + last_grad[:, lanes] if j == hist - 1 else total

    @pl.when(i == steps - 1)
    def _():
        ig_ref[...] = inner(mpg_ref[...], scaled_ref[...])
        og_ref[...] = inner(hidden_ref[...], cgl_ref[...])


def mix_backward(history, streams, own, theirs, cotangent, pre, coeffs, params):
    hist, _, tokens, width = history.shape
    mix = pre.shape[1]
    block = 64
    whole = pl.BlockSpec(memory_space=pltpu.VMEM)
    part = lambda n: pl.BlockSpec((block, n), lambda i: (i, 0))
    four = pl.BlockSpec((4, block, width), lambda i: (0, i, 0))
    story = pl.BlockSpec((hist, 1, block, width), lambda i: (0, 0, i, 0))
    small = [(4, width), (4, width), (1, width), (mix, width), (mix, mix), (1, mix), (1, width)]
    return pl.pallas_call(
        unmix_kernel,
        grid=(tokens // block,),
        out_shape=[jax.ShapeDtypeStruct(history.shape, F32)] + [jax.ShapeDtypeStruct(shape, F32) for shape in small],
        in_specs=[story, four, four, four, pl.BlockSpec((1, block, width), lambda i: (0, i, 0)), part(mix), part(mix)] + [whole] * 4,
        out_specs=[story] + [pl.BlockSpec(shape, lambda i: (0, 0)) for shape in small],
        scratch_shapes=[
            pltpu.VMEM((4, block, width), F32),
            pltpu.VMEM((tokens, width), BF16),
            pltpu.VMEM((tokens, mix), BF16),
            pltpu.VMEM((tokens, mix), BF16),
            pltpu.VMEM((tokens, mix), BF16),
        ],
        compiler_params=pltpu.CompilerParams(vmem_limit_bytes=VMEM_LIMIT),
        cost_estimate=pl.CostEstimate(flops=tokens * width * 1000, bytes_accessed=history.size * 12, transcendentals=0),
        name="mix_backward",
    )(history, streams, own, theirs, cotangent, pre, coeffs, *params)


def finish_kernel(grid, orders, n_kept, *refs):
    nz = grid.nz
    kept, refs = refs[:n_kept], refs[n_kept:]
    came_a, came_b, refs = refs[:1], refs[1 : grid.nb], refs[grid.nb :]
    sum_ref, folded, refs = refs[0], refs[1 : 1 + nz], refs[1 + nz :]
    sgg_ref, sbg_ref, gg_ref, ig_ref, og_ref, bg_ref, ob_ref, hb_ref, eb_ref = refs[:9]
    done_ref, outs, refs = refs[9], refs[10:14], refs[14:]
    first, second, third, final, refs = refs[:4], refs[4:8], refs[8:12], refs[12:18], refs[18:]
    sums = Summing(grid, *refs[:3], done_ref, *refs[3:5])
    local_sem, send_sem, recv_sem = refs[5:]
    a, b, z, c = place = grid.here()
    width, mix = gg_ref.shape[1], bg_ref.shape[1]
    wl, padded, hidden_rows = width // 128, -(-mix // 8) * 8, eb_ref.shape[1] // 128
    firsts, _ = small_rows(width, mix, 2 * eb_ref.shape[1])
    half = width // 2
    spots = [(0, lambda core: core * half), (0, lambda core: width + core * half), (0, lambda core: 2 * width + core * half),
             (1, lambda core: core * half), (2, lambda core: core * eb_ref.shape[1]), (3, lambda core: core * eb_ref.shape[1])]

    def copies(t, stage):
        if stage == 1:
            return fold_copies(grid, place, orders[t], 1, None, first[t], second[t], (send_sem.at[t], recv_sem.at[t]))
        if stage == 2:
            return [
                remote(second[t].at[0, lax.rem(z + k, nz)], third[t].at[k - 1], send_sem.at[t, k], recv_sem.at[t, k],
                       grid.device(a, b, lax.rem(z + k, nz), c))
                for k in range(1, nz)
            ]
        result, base = spots[t]
        n = final[t].shape[-1]
        spot = outs[result].at[:, pl.ds(pl.multiple_of(base(c), 128), n)]
        return [
            remote(final[t].at[1 - c], spot, send_sem.at[t, 0], recv_sem.at[t, 0], grid.device(a, b, z, 1 - c)),
            pltpu.make_async_copy(final[t].at[c], spot, local_sem.at[t]),
        ]

    def add_first(t):
        def step(i, carry):
            o, j = i // nz, lax.rem(i, nz)
            total = kept[t][o, j].astype(F32)
            for piece in came_a if orders[t] == "ab" else came_b:
                total = total + piece[t // 2, o, j].astype(F32)
            first[t][0, o, j] = total.astype(BF16)
            return carry

        lax.fori_loop(0, first[t].shape[1] * nz, step, 0)

    sums.greet()
    add_first(0)
    add_first(1)
    mine = sums.mine
    mine[...] = jnp.zeros_like(mine)
    for l in range(wl):
        lanes = slice(l * 128, (l + 1) * 128)
        mine[firsts[0] + l : firsts[0] + l + 1, :] = gg_ref[:, lanes]
        mine[firsts[1] + l * padded : firsts[1] + l * padded + mix, :] = ig_ref[:, lanes]
        mine[firsts[4] + 4 * l : firsts[4] + 4 * l + 4, :] = sgg_ref[:, lanes]
        mine[firsts[5] + 4 * l : firsts[5] + 4 * l + 4, :] = sbg_ref[:, lanes]
        mine[firsts[7] + l : firsts[7] + l + 1, :] = ob_ref[:, lanes]
    mine[firsts[2] : firsts[2] + mix, 0:mix] = og_ref[...]
    mine[firsts[3] : firsts[3] + 1, 0:mix] = bg_ref[...]
    for k in range(3):
        for l in range(wl // 2):
            mine[pl.ds(firsts[6] + k * wl + c * (wl // 2) + l, 1), :] = hb_ref[k : k + 1, l * 128 : (l + 1) * 128]
    for l in range(hidden_rows):
        mine[pl.ds(firsts[8] + c * hidden_rows + l, 1), :] = eb_ref[:, l * 128 : (l + 1) * 128]
    pl.semaphore_wait(pltpu.get_barrier_semaphore(), sums.count - 1)
    for t in range(2):
        start(copies(t, 1))
    sums.deal()
    add_first(2)
    add_first(3)
    for t in range(2):
        total = folded[0][t].astype(F32)
        for piece in folded[1:]:
            total = total + piece[t].astype(F32)
        at = 0
        for piece in (sum_ref[t], total):
            n = piece.shape[1]
            final[4 + t][:, :, at : at + n] = piece.reshape(2, -1, n)
            at += n
        start(copies(4 + t, 3))
    def second_step(t):
        finish(copies(t, 1))
        if t < 2:
            start(copies(t + 2, 1))
        fold_add(grid, place, orders[t], 1, None, first[t], second[t])
        start(copies(t, 2))

    for t in range(4):
        second_step(t)
    sums.tell()
    for t in range(4):
        finish(copies(t, 2))
        total = second[t][0, z].astype(F32)
        for k in range(nz - 1):
            total = total + third[t][k].astype(F32)
        final[t][...] = total.reshape(final[t].shape)
        start(copies(t, 3))
    sums.close()
    for t in range(6):
        finish(copies(t, 3))


def finish_sums(grid, orders, kept, came, folded, smalls, collective_id):
    sgg, _, _, ig, og, bg, _, hb, eb = smalls
    mix, width = ig.shape
    hidden_width = 2 * eb.shape[1]
    nz = grid.nz
    rows, n = kept[0].shape[-2:]
    devices = grid.n_dp * grid.n_seq
    each = -(-small_rows(width, mix, hidden_width)[1] // (devices * 8)) * 8
    vmem = pl.BlockSpec(memory_space=pltpu.VMEM)
    owned = [3 * width, width, hidden_width, hidden_width]
    folds = [fold_scratch(grid, order, rows, n) for order in orders]
    operands = list(kept) + list(came) + list(folded) + list(smalls)
    return pl.pallas_call(
        functools.partial(finish_kernel, grid, orders, len(kept)),
        out_shape=[jax.ShapeDtypeStruct((devices * each, 128), F32)] + [jax.ShapeDtypeStruct((rows // 2, w), F32) for w in owned],
        in_specs=[vmem] * len(operands),
        out_specs=[vmem] + [pl.BlockSpec(memory_space=pl.ANY)] * len(owned),
        scratch_shapes=[f for _, f, _ in folds]
        + [s for _, _, s in folds]
        + [pltpu.VMEM((nz - 1, rows, n), BF16)] * 4
        + [pltpu.VMEM((2, rows // 2, n), F32)] * 4
        + [pltpu.VMEM((2, rows // 2, hidden_width // 2), F32)] * 2
        + [
            pltpu.VMEM((devices * each, 128), F32),
            pltpu.VMEM((devices * each, 128), F32),
            pltpu.VMEM((each, 128), F32),
            pltpu.SemaphoreType.DMA((2,)),
            pltpu.SemaphoreType.DMA((2,)),
            pltpu.SemaphoreType.DMA((6,)),
            pltpu.SemaphoreType.DMA((6, nz + grid.nb)),
            pltpu.SemaphoreType.DMA((6, nz + grid.nb)),
        ],
        compiler_params=pltpu.CompilerParams(collective_id=collective_id, has_side_effects=True, vmem_limit_bytes=VMEM_LIMIT),
        cost_estimate=pl.CostEstimate(flops=0, bytes_accessed=100 * width * width, transcendentals=0),
        name="finish_sums",
    )(*operands)


def hand_kernel(mix, hidden_width, done, out_ref, *refs):
    owned, placed_ref, small, outs = refs[:4], refs[4], refs[5:14], refs[14:]
    width = out_ref.shape[1]
    wl, padded, hidden_rows = width // 128, -(-mix // 8) * 8, hidden_width // 256
    firsts, _ = small_rows(width, mix, hidden_width)
    placed_ref[...] = out_ref[...]
    outs, again = outs[:4], outs[4]
    for src, dst in zip(owned, outs):
        dst[...] = src[...]
    for l in range(wl):
        lanes = slice(l * 128, (l + 1) * 128)
        small[0][:, lanes] = done[firsts[0] + l : firsts[0] + l + 1, :]
        small[1][:, lanes] = done[firsts[1] + l * padded : firsts[1] + l * padded + mix, :]
        small[4][:, lanes] = done[firsts[4] + 4 * l : firsts[4] + 4 * l + 4, :]
        small[5][:, lanes] = done[firsts[5] + 4 * l : firsts[5] + 4 * l + 4, :]
        small[7][:, lanes] = again[:, lanes] = done[firsts[7] + l : firsts[7] + l + 1, :]
    small[2][...] = done[firsts[2] : firsts[2] + mix, 0:mix]
    small[3][...] = done[firsts[3] : firsts[3] + 1, 0:mix]
    for l in range(3 * wl):
        small[6][:, l * 128 : (l + 1) * 128] = done[firsts[6] + l : firsts[6] + l + 1, :]
    for l in range(2 * hidden_rows):
        small[8][:, l * 128 : (l + 1) * 128] = done[firsts[8] + l : firsts[8] + l + 1, :]


def hand_over(summed, layer_out, owned, mix, hidden_width):
    width = layer_out.shape[1]
    small = [(1, width), (mix, width), (mix, mix), (1, mix), (4, width), (4, width), (1, 3 * width), (1, width), (1, hidden_width)]
    vmem = pl.BlockSpec(memory_space=pltpu.VMEM)
    return pl.pallas_call(
        functools.partial(hand_kernel, mix, hidden_width),
        out_shape=[jax.ShapeDtypeStruct(layer_out.shape, BF16)]
        + [jax.ShapeDtypeStruct(shape, F32) for shape in small]
        + [jax.ShapeDtypeStruct(x.shape, F32) for x in owned]
        + [jax.ShapeDtypeStruct((1, width), F32)],
        in_specs=[vmem] * 6,
        out_specs=[vmem] * 15,
        name="hand_over",
    )(summed, layer_out, *owned)


def far_first(nz, z, i):
    pairs = nz // 2
    return lax.rem(i + pairs // 2 * (1 - z // pairs), pairs)


def unproject_kernel(grid, width, orders, *all_refs):
    nz = grid.nz
    mids, lates, last_parts, all_refs = all_refs[:nz], all_refs[nz : 2 * nz], all_refs[2 * nz : 2 * nz + 2], all_refs[2 * nz + 2 :]
    (col_ref, low_ref, g_ref, w_ref, feed_ref, normed_ref, last_ref, bias_ref, bias2_ref, cos_ref, above_ref,
     below_ref, own_ref, theirs_ref, hb_ref, out_ref, sum_ref, *refs) = all_refs
    nb = grid.nb
    lasts, refs = refs[:nz], refs[nz:]
    kept, over_a, over_b, refs = refs[:4], refs[4], refs[5 : 4 + nb], refs[4 + nb :]
    grad_ref, sending_ref, partial_ref, mine_ref, arrived_ref, along_ref, split_sem, send_sem, recv_sem, along_send, along_recv = refs[:11]
    keep_refs, firsts, seconds, (fold_send, fold_recv, late_sem) = refs[11:13], refs[13:15], refs[15:17], refs[17:]
    i = pl.program_id(0)
    a, b, z, c = grid.here()
    tokens = out_ref.shape[0]
    other = grid.device(a, b, z, 1 - c)
    own_rows = pl.ds(pl.multiple_of(c * tokens, tokens), tokens)
    their_rows = pl.ds(pl.multiple_of((1 - c) * tokens, tokens), tokens)

    def swap(k):
        return [remote(sending_ref.at[k], theirs_ref.at[k], send_sem.at[k], recv_sem.at[k], other)]

    def swap_out():
        return [remote(partial_ref, arrived_ref, send_sem.at[4], recv_sem.at[4], other)]

    def along():
        return [
            remote(mids[k], along_ref.at[k - 1], along_send.at[k - 1], along_recv.at[k - 1], grid.device(a, b, lax.rem(z + k, nz), c))
            for k in range(1, nz)
        ]

    def fold(t, stage):
        if stage < 2:
            order = ("ab", "ba")[t]
            found = fold_copies(grid, (a, b, z, c), order, stage, last_parts[t], firsts[t], seconds[t], (fold_send.at[t], fold_recv.at[t]))
            if stage == 0:
                kept_part = last_parts[t].at[a] if order == "ab" else last_parts[t].at[:, b]
                found.append(pltpu.make_async_copy(kept_part, keep_refs[t], late_sem.at[t]))
            return found
        n = seconds[t].shape[-1]
        return [
            pltpu.make_async_copy(seconds[t].at[0, lax.rem(z + k, nz)], lasts[k].at[t, :, pl.ds(n, n)], late_sem.at[2 + t * nz + k])
            for k in range(nz)
        ]

    def settle(stage):
        for t in range(2):
            finish(fold(t, stage))
            fold_add(grid, (a, b, z, c), ("ab", "ba")[t], stage, keep_refs[t], firsts[t], seconds[t])
            start(fold(t, stage + 1))

    def place_lates():
        n = lates[0].shape[-1]
        return [pltpu.make_async_copy(lates[k], lasts[k].at[:, :, pl.ds(0, n)], late_sem.at[2 + 2 * nz + k]) for k in range(nz)]

    def split(k):
        grad = grad_ref.at[k]
        if orders[k] == "ab":
            found = [(grad.at[a], kept[k]), (grad.at[1 - a], over_a.at[k // 2])]
        else:
            found = [(grad.at[:, b], kept[k])]
            found += [(grad.at[:, lax.rem(b + m, nb)], over_b[m - 1].at[k // 2]) for m in range(1, nb)]
        return [pltpu.make_async_copy(src, dst, split_sem.at[k, n]) for n, (src, dst) in enumerate(found)]

    def piece(n):
        return jnp.concatenate([col_ref[m, :, n * width : (n + 1) * width] for m in range(nz)], axis=1)

    def keep(k, grad):
        grad_ref[k] = grad.astype(BF16).reshape(grad_ref.shape[1:])
        start(split(k))

    @pl.when(i == 0)
    def _():
        grid.greet(a, b, z, c)
        for t in range(2):
            start(fold(t, 0))
        start(along())
        start(place_lates())
        mine_ref[...] = piece(0)
        partial_ref[...] = against(mine_ref[their_rows, :], w_ref[0]) + feed_ref[their_rows, :]
        sending_ref[3] = normed_ref[their_rows, :].astype(BF16)
        start(swap_out())
        start(swap(3))
        own_ref[0] = normed_ref[own_rows, :]
        out = against(mine_ref[own_rows, :], w_ref[0]) + feed_ref[own_rows, :] + last_ref[0] + (row(bias_ref) + row(bias2_ref))
        keep(3, inner(g_ref[...], mine_ref[...]))
        finish(swap_out())
        out_ref[...] = (out + arrived_ref[...]).astype(BF16)

    for k in range(3):

        @pl.when(i == k + 1)
        def _(k=k):
            if k == 2:
                settle(0)
            grad = piece(k + 1).astype(F32)
            if k < 2:
                tables = [jnp.concatenate([t[...]] * (grad.shape[1] // 128), axis=1) for t in (cos_ref, above_ref, below_ref)]
                grad = rotate(grad, tables, -1.0)
            hb_ref[k : k + 1, :] = jnp.sum(grad, axis=0, keepdims=True)
            mine_ref[...] = grad.astype(BF16)
            sending_ref[k] = against(mine_ref[their_rows, :], w_ref[0]).astype(BF16)
            start(swap(k))
            own_ref[0] = against(mine_ref[own_rows, :], w_ref[0])
            keep(k, inner(low_ref[0], mine_ref[...]))
            if k == 2:
                for n in range(4):
                    finish(swap(n))
                    finish(split(n))
                settle(1)
                finish(along())
                total = mids[0][...].astype(F32)
                for n in range(nz - 1):
                    total = total + along_ref[n].astype(F32)
                sum_ref[...] = total
                for t in range(2):
                    finish(fold(t, 2))
                finish(place_lates())


def unproject(grid, orders, mids, lates, last_parts, collected, lowered, grad_low, weights, feed_part, normed_feed, streams, biases, tables, own_width, collective_id):
    _, tokens, width = streams.shape
    both, half = 2 * tokens, width // 2
    na, nb, nz = grid.na, grid.nb, grid.nz
    rows = width // (na * nb * nz)
    n = lates[0].shape[-1]
    folds = [fold_scratch(grid, order, rows, n) for order in ("ab", "ba")]
    whole = pl.BlockSpec(memory_space=pltpu.VMEM)
    anywhere = pl.BlockSpec(memory_space=pl.ANY)
    turn = lambda i: lax.rem(i + 3, 4)
    split_shapes = [jax.ShapeDtypeStruct((nb if order == "ab" else na, nz, rows, half), BF16) for order in orders]
    sent_shapes = [jax.ShapeDtypeStruct((2, nb, nz, rows, half), BF16)] + [jax.ShapeDtypeStruct((2, na, nz, rows, half), BF16)] * (nb - 1)
    results = pl.pallas_call(
        functools.partial(unproject_kernel, grid, own_width, orders),
        grid=(4,),
        out_shape=[
            jax.ShapeDtypeStruct((4, tokens, width), F32),
            jax.ShapeDtypeStruct((4, tokens, width), BF16),
            jax.ShapeDtypeStruct((3, half), F32),
            jax.ShapeDtypeStruct((tokens, width), BF16),
            jax.ShapeDtypeStruct(mids[0].shape, F32),
        ]
        + [jax.ShapeDtypeStruct((2, rows, 2 * n), BF16)] * nz
        + split_shapes
        + sent_shapes,
        in_specs=[whole]
        + [anywhere] * (nz - 1)
        + [whole] * nz
        + [anywhere] * 2
        + [
            whole,
            pl.BlockSpec((1, both, width), lambda i: (jnp.maximum(i - 1, 0), 0, 0)),
            whole,
            pl.BlockSpec((1, width, half), lambda i: (turn(i), 0, 0)),
        ]
        + [whole] * 2
        + [pl.BlockSpec((1, tokens, width), lambda i: (3, 0, 0))]
        + [whole] * 5,
        out_specs=[
            pl.BlockSpec((1, tokens, width), lambda i: (turn(i), 0, 0)),
            anywhere,
            pl.BlockSpec((3, half), lambda i: (0, 0)),
            pl.BlockSpec((tokens, width), lambda i: (0, 0)),
            pl.BlockSpec(mids[0].shape, lambda i: (0, 0, 0)),
        ]
        + [anywhere] * (nz + len(split_shapes) + len(sent_shapes)),
        scratch_shapes=[
            pltpu.VMEM((4, na, nb, nz, rows, half), BF16),
            pltpu.VMEM((4, tokens, width), BF16),
            pltpu.VMEM((tokens, width), F32),
            pltpu.VMEM((both, half), BF16),
            pltpu.VMEM((tokens, width), F32),
            pltpu.VMEM((nz - 1, *mids[0].shape), BF16),
            pltpu.SemaphoreType.DMA((4, nb + 1)),
            pltpu.SemaphoreType.DMA((5,)),
            pltpu.SemaphoreType.DMA((5,)),
            pltpu.SemaphoreType.DMA((nz - 1,)),
            pltpu.SemaphoreType.DMA((nz - 1,)),
            *[o for o, _, _ in folds],
            *[f for _, f, _ in folds],
            *[f for _, _, f in folds],
            pltpu.SemaphoreType.DMA((2, nz + nb)),
            pltpu.SemaphoreType.DMA((2, nz + nb)),
            pltpu.SemaphoreType.DMA((2 + 3 * nz,)),
        ],
        compiler_params=pltpu.CompilerParams(collective_id=collective_id, has_side_effects=True, vmem_limit_bytes=VMEM_LIMIT),
        cost_estimate=pl.CostEstimate(flops=32 * both * width * half, bytes_accessed=40 * both * width, transcendentals=0),
        name="unproject",
    )(*mids, *lates, *last_parts, collected, lowered, grad_low, weights, feed_part, normed_feed, streams, *biases, *tables)
    own, theirs, head_bias, layer_out, mid_sums = results[:5]
    lasts, results = results[5 : 5 + nz], results[5 + nz :]
    return own, theirs, head_bias, layer_out, mid_sums, lasts, results[:4], results[4:]


def feed_kernel(grid, steps, back_ref, low_ref, g_ref, we_ref, wc_ref, bias_ref, collected_ref, feed_ref, normed_ref, eb_ref, *refs):
    nz = grid.nz
    groups = steps - 1
    mids, outs, whole_outs, refs = refs[:nz], refs[nz : 2 * nz], refs[2 * nz : 2 * nz + 2], refs[2 * nz + 2 :]
    parts, refs = refs[: 2 * steps], refs[2 * steps :]
    first, second, refs = refs[: 2 * groups], refs[2 * groups : 4 * groups], refs[4 * groups :]
    bias_full, send_sem, recv_sem, out_sem, back_send, back_recv = refs
    i = pl.program_id(0)
    a, b, z, c = place = grid.here()
    orders = ["ab", "ba"] * steps

    def copies(t, stage):
        if stage < 2:
            return fold_copies(grid, place, orders[t], stage, parts[t], first[t], second[t], (send_sem.at[t], recv_sem.at[t]))
        along = [lax.rem(z + k, nz) for k in range(nz)]
        u, n = t // 2, parts[t].shape[-1]
        late = u == groups - 1
        cols = pl.ds(0 if late else u * n, n)
        spot = outs if late else mids
        return [pltpu.make_async_copy(second[t].at[0, along[k]], spot[k].at[t % 2, :, cols], out_sem.at[t, k]) for k in range(nz)]

    def last_parts():
        return [pltpu.make_async_copy(parts[2 * groups + k], whole_outs[k], out_sem.at[2 * groups + k, 0]) for k in range(2)]

    def begin(u):
        for t in (2 * u, 2 * u + 1):
            start(copies(t, 0))

    def end(u, stage):
        for t in (2 * u, 2 * u + 1):
            finish(copies(t, stage))
            if stage < 2:
                own = parts[t].at[a] if orders[t] == "ab" else parts[t].at[:, b]
                fold_add(grid, place, orders[t], stage, own, first[t], second[t])
                start(copies(t, stage + 1))

    def turn(u):
        for stage in range(3):
            if 0 <= u - stage < groups:
                end(u - stage, stage)

    def backs():
        found = [pltpu.make_async_copy(back_ref.at[z], collected_ref.at[z], back_send.at[0])]
        for k in range(1, nz):
            to = lax.rem(z + k, nz)
            found.append(remote(back_ref.at[to], collected_ref.at[z], back_send.at[k], back_recv.at[k], grid.device(a, b, to, c)))
        return found

    @pl.when(i == 0)
    def _():
        grid.greet(*place)
        start(backs())
        bias_full[...] = bias_ref[...].astype(F32)
        feed_ref[...] = jnp.zeros_like(feed_ref)
        normed_ref[...] = jnp.zeros_like(normed_ref)

    low, grad, expand, contract = low_ref[0], g_ref[...], we_ref[...], wc_ref[...]
    wide = expand.shape[1] // 128
    first_row = c * (bias_full.shape[0] // 2) + i * wide
    bias = jnp.concatenate([bias_full[pl.ds(first_row + l, 1), :] for l in range(wide)], axis=1)
    expanded = product(low, expand) + bias
    share = phi(expanded)
    hidden = (expanded * share).astype(BF16)
    slope = share + expanded * jnp.exp(-0.5 * expanded * expanded) * (1.0 / math.sqrt(2.0 * math.pi))
    feed_ref[...] += against(hidden, contract)
    hidden_grad = inner(grad, hidden).astype(BF16)
    pulled = product(grad, contract) * slope
    eb_ref[...] = jnp.sum(pulled, axis=0, keepdims=True)
    pulled_low = pulled.astype(BF16)
    normed_ref[...] += against(pulled_low, expand)
    expand_grad = inner(low, pulled_low).astype(BF16)
    for u in range(steps):

        @pl.when(i == u)
        def _(u=u):
            parts[2 * u][...] = expand_grad.reshape(parts[2 * u].shape)
            parts[2 * u + 1][...] = hidden_grad.reshape(parts[2 * u + 1].shape)
            if u < groups:
                begin(u)
            else:
                start(last_parts())
            if u >= 2:
                turn(u - 2)
            if u == steps - 1:
                for v in range(max(steps - 2, 0), groups + 2):
                    turn(v)
                finish(last_parts())
                finish(backs())


def feed_forward(grid, returned, lowered, grad_low, weight_e, weight_c, bias, steps, collective_id):
    both, width = grad_low.shape
    n = weight_e.shape[1] // steps
    na, nb, nz = grid.na, grid.nb, grid.nz
    rows = width // (na * nb * nz)
    whole = lambda *shape: pl.BlockSpec(shape, lambda i: (0,) * len(shape))
    cols = lambda m: pl.BlockSpec((m, n), lambda i: (0, i))
    orders = ["ab", "ba"] * steps
    folds = [fold_scratch(grid, order, rows, n) for order in orders]
    sem = pltpu.SemaphoreType.DMA((2 * steps, nz + nb))
    return pl.pallas_call(
        functools.partial(feed_kernel, grid, steps),
        grid=(steps,),
        out_shape=[
            jax.ShapeDtypeStruct(returned.shape, BF16),
            jax.ShapeDtypeStruct((both, width), F32),
            jax.ShapeDtypeStruct((both, width), F32),
            jax.ShapeDtypeStruct((1, n * steps), F32),
        ]
        + [jax.ShapeDtypeStruct((2, rows, n * (steps - 2)), BF16)] * nz
        + [jax.ShapeDtypeStruct((2, rows, n), BF16)] * nz
        + [jax.ShapeDtypeStruct((na, nb, nz, rows, n), BF16)] * 2,
        in_specs=[
            pl.BlockSpec(memory_space=pltpu.VMEM),
            pl.BlockSpec((1, both, width), lambda i: (3, 0, 0)),
            whole(both, width),
            cols(width),
            cols(width),
            whole(*bias.shape),
        ],
        out_specs=[
            pl.BlockSpec(memory_space=pl.ANY),
            whole(both, width),
            whole(both, width),
            cols(1),
        ]
        + [pl.BlockSpec(memory_space=pl.ANY)] * (2 * nz + 2),
        scratch_shapes=[pltpu.VMEM((na, nb, nz, rows, n), BF16)] * (2 * steps)
        + [f for _, f, _ in folds[:-2]]
        + [s for _, _, s in folds[:-2]]
        + [pltpu.VMEM(bias.shape, F32)]
        + [sem, sem, pltpu.SemaphoreType.DMA((2 * steps, nz)), pltpu.SemaphoreType.DMA((nz,)), pltpu.SemaphoreType.DMA((nz,))],
        compiler_params=pltpu.CompilerParams(collective_id=collective_id, has_side_effects=True, vmem_limit_bytes=VMEM_LIMIT),
        cost_estimate=pl.CostEstimate(flops=12 * both * width * n * steps * 2, bytes_accessed=width * n * steps * 20, transcendentals=0),
        name="feed_forward",
    )(returned, lowered, grad_low, weight_e, weight_c, bias)


def attention_kernel(width, heads, tile, edge, length, x_ref, qdoc_ref, out_ref, kdoc_ref,
                     s_ref, kt_ref, vt_ref, ot_ref, dqt_ref, dka_ref, dva_ref, top_ref):
    i = pl.program_id(0)
    tiles = length // tile
    scale = 1.0 / math.sqrt(HEAD_DIM)
    @pl.when(i == 0)
    def _():
        dka_ref[...] = jnp.zeros_like(dka_ref)
        dva_ref[...] = jnp.zeros_like(dva_ref)
        def turn(j, carry):
            at = pl.ds(pl.multiple_of(j * tile, tile), tile)
            kt_ref[:, at] = x_ref[at, width : 2 * width].T
            kdoc_ref[at, :] = jnp.broadcast_to(qdoc_ref[:, at].astype(F32), (128, tile)).T
            vt_ref[:, at] = x_ref[at, 2 * width : 3 * width].T
            return carry
        lax.fori_loop(0, tiles, turn, 0)
    rows = pl.ds(pl.multiple_of(i * tile, tile), tile)
    query = x_ref[rows, 0:width] * jnp.asarray(scale, BF16)
    grad = x_ref[rows, 3 * width : 4 * width]
    query_t, grad_t = query.T, grad.T
    lanes = lax.broadcasted_iota(jnp.int32, (tile, width), 1) // HEAD_DIM
    subs = lax.broadcasted_iota(jnp.int32, (width, tile), 0) // HEAD_DIM
    zero = jnp.zeros((), BF16)
    queries_t = [jnp.where(subs == h, query_t, zero) for h in range(heads)]
    grads_t = [jnp.where(subs == h, grad_t, zero) for h in range(heads)]
    spread_queries = [jnp.where(lanes == h, query, zero) for h in range(heads)]
    spread_grads = [jnp.where(lanes == h, grad, zero) for h in range(heads)]
    qdoc = qdoc_ref[:, rows].astype(F32)
    head_edge = -(-edge // tile)
    tail_edge = (length - edge) // tile
    half = tile // 2
    corners = [(0, half, 0), (half, half, half)]
    ot_ref[...] = jnp.zeros_like(ot_ref)
    dqt_ref[...] = jnp.zeros_like(dqt_ref)
    top_ref[...] = jnp.full_like(top_ref, NEG)

    def fold(x, f):
        return f(x.reshape(x.shape[0] // 8, 8, x.shape[1]), axis=0)

    def score(first, size, left, documents, causal):
        at = pl.ds(pl.multiple_of(first, size), size)
        keys = x_ref[at, width : 2 * width]
        wide = tile - left
        if documents:
            allowed = jnp.concatenate([kdoc_ref[at, :]] * (wide // 128), axis=1) == qdoc[:, left:]
        if causal:
            allowed &= lax.broadcasted_iota(jnp.int32, (size, wide), 0) <= lax.broadcasted_iota(jnp.int32, (size, wide), 1)
        for h in range(heads):
            s = product(keys, queries_t[h][:, left:])
            if documents:
                s = jnp.where(allowed, s, NEG)
            s_ref[h, at, left:] = s
            top_ref[h, :, left:] = jnp.maximum(top_ref[h, :, left:], fold(s, jnp.max))

    def scores(j, carry):
        checked = (j < head_edge) | (i >= tail_edge)
        pl.when(checked)(lambda: score(j * tile, tile, 0, True, False))
        pl.when(jnp.logical_not(checked))(lambda: score(j * tile, tile, 0, False, False))
        return carry

    lax.fori_loop(0, i, scores, 0)
    for first, size, left in corners:
        score(i * tile + first, size, left, True, True)
    tops = [jnp.max(top_ref[h], axis=0, keepdims=True) for h in range(heads)]
    top_ref[...] = jnp.zeros_like(top_ref)

    def weigh(first, size, left):
        at = pl.ds(pl.multiple_of(first, size), size)
        for h in range(heads):
            own = slice(h * HEAD_DIM, (h + 1) * HEAD_DIM)
            weights = jnp.exp(s_ref[h, at, left:] - tops[h][:, left:])
            s_ref[h, at, left:] = weights
            top_ref[h, :, left:] += fold(weights, jnp.sum)
            ot_ref[own, left:] += product(vt_ref[own, at], weights.astype(BF16))

    lax.fori_loop(0, i, lambda j, carry: (weigh(j * tile, tile, 0), carry)[1], 0)
    for first, size, left in corners:
        weigh(i * tile + first, size, left)
    inverse = [1.0 / jnp.sum(top_ref[h], axis=0, keepdims=True) for h in range(heads)]
    grad_f = grad_t.astype(F32)
    deltas = []
    for h in range(heads):
        own = slice(h * HEAD_DIM, (h + 1) * HEAD_DIM)
        value = ot_ref[own, :] * inverse[h]
        ot_ref[own, :] = value
        deltas.append(jnp.sum(value * grad_f[own], axis=0, keepdims=True))
    out_ref[rows, 0:width] = ot_ref[...].T.astype(BF16)

    def back(first, size, left):
        at = pl.ds(pl.multiple_of(first, size), size)
        values = x_ref[at, 2 * width : 3 * width]
        probs_low, grads_low = [], []
        for h in range(heads):
            own = slice(h * HEAD_DIM, (h + 1) * HEAD_DIM)
            probs_grad = product(values, grads_t[h][:, left:])
            probs = s_ref[h, at, left:] * inverse[h][:, left:]
            scores_grad = (probs * (probs_grad - deltas[h][:, left:])).astype(BF16)
            probs_low.append(probs.astype(BF16))
            grads_low.append(scores_grad)
            dqt_ref[own, left:] += product(kt_ref[own, at], scores_grad)
        dva_ref[at, :] += product(jnp.concatenate(probs_low, axis=1), jnp.concatenate([x[left:] for x in spread_grads], axis=0))
        dka_ref[at, :] += product(jnp.concatenate(grads_low, axis=1), jnp.concatenate([x[left:] for x in spread_queries], axis=0))

    lax.fori_loop(0, i, lambda j, carry: (back(j * tile, tile, 0), carry)[1], 0)
    for first, size, left in corners:
        back(i * tile + first, size, left)
    out_ref[rows, width : 2 * width] = (dqt_ref[...].T * scale).astype(BF16)

    @pl.when(i == tiles - 1)
    def _():
        out_ref[:, 2 * width : 3 * width] = dka_ref[...].astype(BF16)
        out_ref[:, 3 * width : 4 * width] = dva_ref[...].astype(BF16)


def attention(dealt, documents, heads, edge):
    length = dealt.shape[0]
    width = heads * HEAD_DIM
    tile = 2 * edge
    pairs = length * length // 2 * heads
    whole = lambda i: (0, 0)
    return pl.pallas_call(
        functools.partial(attention_kernel, width, heads, tile, edge, length),
        grid=(length // tile,),
        out_shape=jax.ShapeDtypeStruct((length, 4 * width), BF16),
        in_specs=[pl.BlockSpec((length, 4 * width), whole), pl.BlockSpec((1, length), whole)],
        out_specs=pl.BlockSpec((length, 4 * width), whole),
        scratch_shapes=[
            pltpu.VMEM((length, 128), F32), pltpu.VMEM((heads, length, tile), F32), pltpu.VMEM((width, length), BF16), pltpu.VMEM((width, length), BF16),
            pltpu.VMEM((width, tile), F32), pltpu.VMEM((width, tile), F32), pltpu.VMEM((length, width), F32), pltpu.VMEM((length, width), F32),
            pltpu.VMEM((heads, 8, tile), F32)],
        compiler_params=pltpu.CompilerParams(vmem_limit_bytes=VMEM_LIMIT),
        cost_estimate=pl.CostEstimate(flops=pairs * 64 * 2 * 6 * 4, bytes_accessed=length * width * 20, transcendentals=pairs),
        name="attention",
    )(dealt, documents)


def on_device(
    grid,
    history,
    documents,
    cotangent,
    mixer_gain,
    mixer_inner,
    mixer_outer,
    mixer_bias,
    stream_gain,
    stream_bias,
    inbound_weight,
    inbound_bias,
    outbound_weight,
    outbound_bias,
    expand,
    expand_bias,
    contract,
    contract_bias,
):
    n_dp, n_seq, nz = grid.n_dp, grid.n_seq, grid.nz
    tokens, width = history.shape[2], history.shape[3]
    hidden_width = expand.shape[1]
    half, hidden_half = width // 2, hidden_width // 2
    both = 2 * tokens
    length = documents.shape[1]
    mix = mixer_bias.shape[0]
    heads = HEADS // n_seq
    own_width = heads * HEAD_DIM
    pick = lambda base, n: (lambda core: base + core * n)
    parts = 4
    piece = hidden_half // parts
    feed = []
    for part in range(parts):
        base = lambda core, part=part: core * hidden_half + part * piece
        feed.append((2, base, 4, part * piece, piece, "ba"))
        feed.append((3, base, 5, part * piece, piece, "ab"))
    pairs = [[4 + 2 * part, 5 + 2 * part] for part in range(parts)]
    inner_t = mixer_inner.T
    lowered, grad_low, streams, mix_pre, coeffs, tables, weights, (weight_e, weight_c), dealt = mix_forward(
        grid,
        history,
        cotangent,
        [mixer_gain.reshape(-1, 128), inner_t, mixer_outer, mixer_bias[None], stream_gain, stream_bias, inbound_bias.reshape(-1, 128)],
        [inbound_weight, outbound_weight, expand, contract],
        [
            (0, pick(width, half), 1, 0, half, "ba"),
            (0, pick(2 * width, half), 2, 0, half, "ab"),
            (0, pick(0, half), 0, 0, half, "ba"),
            (1, pick(0, half), 3, 0, half, "ab"),
        ]
        + feed,
        [[0, 1], [2, 3]],
        pairs,
        [hidden_half] * 2,
        own_width,
        1,
    )

    returned = attention(dealt.reshape(length, 4 * own_width), documents, heads, tokens)
    returned = returned.reshape(nz, both, 4 * own_width)

    collected, feed_part, normed_feed, expand_bias_part, *rest = feed_forward(
        grid, returned, lowered, grad_low, weight_e, weight_c, expand_bias.reshape(-1, 128), STEPS, 3
    )

    orders = ("ab", "ba", "ab", "ba")
    bias_out = [outbound_bias.reshape(-1, 128), contract_bias.reshape(-1, 128)]
    mids, lates, last_parts = rest[:nz], rest[nz : 2 * nz], rest[2 * nz :]
    normed_own, normed_theirs, head_bias_part, layer_out, mid_sums, lasts, kept, leaving = unproject(
        grid, orders, mids, lates, last_parts, collected, lowered, grad_low, weights, feed_part, normed_feed, streams, bias_out, tables, own_width, 4
    )

    along_z = [[(s, (s // 2 + k) % nz * 2 + s % 2) for s in range(n_seq)] for k in range(nz)]
    folded = [lasts[0]] + [lax.ppermute(lasts[k], "seq", along_z[k]) for k in range(1, nz)]
    nb = grid.nb
    over_a = [(d, (d + nb) % n_dp) for d in range(n_dp)]
    over_b = [[(d, d // nb * nb + (d + k) % nb) for d in range(n_dp)] for k in range(1, nb)]
    came_a = lax.ppermute(leaving[0], "dp", over_a)
    came_b = [lax.ppermute(x, "dp", perm) for x, perm in zip(leaving[1:], over_b)]

    history_grad, *small = mix_backward(
        history, streams, normed_own, normed_theirs, cotangent, mix_pre, coeffs, [mixer_gain.reshape(-1, 128), inner_t, mixer_outer, stream_gain]
    )
    smalls = [*small, head_bias_part, expand_bias_part]
    summed, *owned = finish_sums(grid, orders, kept, [came_a, *came_b], [mid_sums, *folded], smalls, 5)
    layer_out, *small, inbound_grad, outbound_grad, expand_grad, contract_grad, again = hand_over(summed, layer_out, owned, mix, hidden_width)
    gain_grad, inner_grad, outer_grad, bias_grad, stream_gain_grad, stream_bias_grad, in_bias_grad, out_bias_grad, expand_bias_grad = small
    return (
        layer_out[None],
        history_grad,
        gain_grad.reshape(width),
        inner_grad.T,
        outer_grad,
        bias_grad.reshape(-1),
        stream_gain_grad,
        stream_bias_grad,
        inbound_grad,
        in_bias_grad.reshape(3 * width),
        outbound_grad,
        out_bias_grad.reshape(width),
        expand_grad,
        expand_bias_grad.reshape(hidden_width),
        contract_grad,
        again.reshape(width),
    )


def solution(mesh):
    rows = P(("dp", "seq"), None)
    placed = (
        P(None, "dp", "seq", None),
        P("dp", None),
        P("dp", "seq", None),
        P(),
        P(),
        P(),
        P(),
        P(),
        P(),
        rows,
        P(),
        rows,
        P(),
        rows,
        P(),
        rows,
        P(),
    )
    grid = Grid(mesh.shape["dp"], mesh.shape["seq"])
    return jax.shard_map(
        functools.partial(on_device, grid),
        mesh=mesh,
        in_specs=placed,
        out_specs=(
            P("dp", "seq", None),
            P(None, "dp", "seq", None),
            P(),
            P(),
            P(),
            P(),
            P(),
            P(),
            rows,
            P(),
            rows,
            P(),
            rows,
            P(),
            rows,
            P(),
        ),
        check_vma=False,
    )
```

```python
import functools
import math

import jax
import jax.numpy as jnp
from jax import lax
from jax.experimental import pallas as pl
from jax.experimental.pallas import tpu as pltpu
from jax.sharding import PartitionSpec as P

HEADS = 16
HEAD_DIM = 64
ROT_DIMS = 16
EPS = 1e-05
HIGHEST = lax.Precision.HIGHEST
NEG = -1e30
MESH = pl.DeviceIdType.MESH
F32 = jnp.float32
BF16 = jnp.bfloat16
VMEM_LIMIT = 56 * 1024 * 1024
STEPS = 4


def inner(left, right):
    return lax.dot_general(left, right, (((0,), (0,)), ((), ())), preferred_element_type=F32)


def against(left, right):
    return lax.dot_general(left, right, (((1,), (1,)), ((), ())), preferred_element_type=F32)


def product(left, right):
    return jnp.dot(left, right, preferred_element_type=F32)


def exact_gelu(value):
    return jax.nn.gelu(value, approximate=False)


def phi(value):
    return 0.5 * (1.0 + lax.erf(value * (1.0 / math.sqrt(2.0))))


def gelu_slope(value):
    return phi(value) + value * jnp.exp(-0.5 * value * value) * (1.0 / math.sqrt(2.0 * math.pi))


def rotate(value, tables, sign):
    half = ROT_DIMS // 2
    cosine, above, below = tables
    width = value.shape[-1]
    up = pltpu.roll(value, width - half, 1)
    down = pltpu.roll(value, half, 1)
    return value * cosine + sign * (up * above + down * below)


class Grid:
    def __init__(self, n_dp, n_seq):
        self.n_dp, self.n_seq = n_dp, n_seq
        self.na, self.nb, self.nz = 2, n_dp // 2, n_seq // 2

    def here(self):
        dp, seq = lax.axis_index("dp"), lax.axis_index("seq")
        return dp // self.nb, lax.rem(dp, self.nb), seq // 2, lax.rem(seq, 2)

    def device(self, a, b, z, c):
        return (a * self.nb + b, z * 2 + c)

    def peers(self, a, b, z, c):
        found = [self.device(a, b, z, 1 - c), self.device(1 - a, b, z, c)]
        found += [self.device(a, lax.rem(b + k, self.nb), z, c) for k in range(1, self.nb)]
        found += [self.device(a, b, lax.rem(z + k, self.nz), c) for k in range(1, self.nz)]
        return found

    def greet(self, a, b, z, c):
        barrier = pltpu.get_barrier_semaphore()
        found = self.peers(a, b, z, c)
        for peer in found:
            pl.semaphore_signal(barrier, inc=1, device_id=peer, device_id_type=MESH)
        pl.semaphore_wait(barrier, len(found))


def row(ref):
    value = ref[...].astype(F32)
    return jnp.concatenate([value[l : l + 1] for l in range(value.shape[0])], axis=1)


def remote(src, dst, send, recv, device):
    return pltpu.make_async_remote_copy(
        src_ref=src, dst_ref=dst, send_sem=send, recv_sem=recv, device_id=device, device_id_type=MESH
    )


def start(copies):
    for copy in copies:
        copy.start()


def finish(copies):
    for copy in copies:
        copy.wait()


class Gathering:
    def __init__(self, grid, place, rows, chunks, ins, outs, local_sem, send_sem, recv_sem):
        self.grid, self.place, self.rows, self.chunks = grid, place, rows, chunks
        self.ins, self.outs = ins, outs
        self.local_sem, self.send_sem, self.recv_sem = local_sem, send_sem, recv_sem

    def copies(self, t, stage):
        a, b, z, c = self.place
        grid, rows = self.grid, self.rows
        nz, nb = grid.nz, grid.nb
        source, base, result, col, n, order = self.chunks[t]
        out, cols = self.outs[result], pl.ds(col, n)

        def send(src, dst, slot, device):
            return remote(src, dst, self.send_sem.at[t, slot], self.recv_sem.at[t, slot], device)

        if stage == 0:
            mine = self.ins[source].at[:, pl.ds(pl.multiple_of(base(c), 128), n)]
            theirs = self.ins[source].at[:, pl.ds(pl.multiple_of(base(1 - c), 128), n)]
            spot = out.at[a, b, z, pl.ds(pl.multiple_of(c * rows, rows), rows), cols]
            return [pltpu.make_async_copy(mine, spot, self.local_sem.at[t]), send(theirs, spot, 0, grid.device(a, b, z, 1 - c))]
        if order[stage - 2] == "b":
            block = out.at[a, b, :, :, cols] if stage == 2 else out.at[:, b, :, :, cols]
            return [send(block, block, k, grid.device(a, lax.rem(b + k, nb), z, c)) for k in range(1, nb)]
        block = out.at[a, b, :, :, cols] if stage == 2 else out.at[a, :, :, :, cols]
        return [send(block, block, nb, grid.device(1 - a, b, z, c))]

    def hop(self, t, step, begin):
        a, b, z, c = self.place
        nz, nb = self.grid.nz, self.grid.nb
        _, _, result, col, n, _ = self.chunks[t]
        out, cols = self.outs[result], pl.ds(col, n)
        for side, way in enumerate((1, -1)):
            slot = nb + 1 + side * (nz - 1) + step - 1
            there, arriving = z + way, z - way * step
            going = there - way * step
            inside = (there >= 0) & (there < nz) & (going >= 0) & (going < nz)
            coming = (arriving >= 0) & (arriving < nz)

            def link(which, slot=slot, there=there):
                block = out.at[a, b, which, :, cols]
                return remote(block, block, self.send_sem.at[t, slot], self.recv_sem.at[t, slot], self.grid.device(a, b, there, c))

            if begin:
                pl.when(inside)(lambda link=link, going=going: link(going).start())
            else:
                pl.when(inside)(lambda link=link, going=going: link(going).wait_send())
                pl.when(coming)(lambda link=link, arriving=arriving: link(arriving).wait_recv())

    def begin(self, group, stage):
        for t in group:
            start(self.copies(t, stage))

    def end(self, group, stage):
        for t in group:
            finish(self.copies(t, stage))

    def ticks(self, whole, partial):
        groups, nz = whole + partial, self.grid.nz

        def advance(u, at):
            group = groups[u]
            if at == 0:
                self.end(group, 0)
            elif at < nz:
                for t in group:
                    self.hop(t, at, False)
            else:
                self.end(group, 2)
            for t in group:
                if at < nz - 1:
                    self.hop(t, at + 1, True)
                elif u < len(whole):
                    start(self.copies(t, 2 if at == nz - 1 else 3))

        def first():
            for group in groups:
                self.begin(group, 0)

        enter = [u if u < len(whole) else len(whole) + (u - len(whole)) // 2 for u in range(len(groups))]

        def tick(now):
            for u in range(len(groups)):
                if 0 <= now - enter[u] <= (nz if u < len(whole) else nz - 1):
                    advance(u, now - enter[u])

        def last():
            for group in whole:
                self.end(group, 3)

        return [first] + [functools.partial(tick, now) for now in range(max(enter) + nz + 1)] + [last]


def gather_sems(grid, chunks):
    slots = 2 * grid.nz + grid.nb - 1
    return [
        pltpu.SemaphoreType.DMA((len(chunks),)),
        pltpu.SemaphoreType.DMA((len(chunks), slots)),
        pltpu.SemaphoreType.DMA((len(chunks), slots)),
    ]


def fold_copies(grid, place, order, stage, part, first, second, sems):
    a, b, z, c = place
    nz, nb = grid.nz, grid.nb

    def send(src, dst, slot, device):
        return remote(src, dst, sems[0].at[slot], sems[1].at[slot], device)

    if (order == "ab") == (stage == 0):
        src = part.at[1 - a] if stage == 0 else first.at[0, 1 - a]
        dst = first.at[0] if stage == 0 else second.at[0]
        return [send(src, dst, nz + nb - 1, grid.device(1 - a, b, z, c))]
    found = []
    for k in range(1, nb):
        to = lax.rem(b + k, nb)
        src = part.at[:, to] if stage == 0 else first.at[0, to]
        dst = first.at[k - 1] if stage == 0 else second.at[k - 1]
        found.append(send(src, dst, nz + k - 1, grid.device(a, to, z, c)))
    return found


def fold_add(grid, place, order, stage, own, first, second):
    a, b, z, c = place
    nz = grid.nz
    if stage == 0:

        def step(i, carry):
            o, j = i // nz, lax.rem(i, nz)
            total = own[o, j].astype(F32)
            for k in range(first.shape[0]):
                total = total + first[k, o, j].astype(F32)
            first[0, o, j] = total.astype(BF16)
            return carry

        lax.fori_loop(0, first.shape[1] * nz, step, 0)
        return
    mine = b if order == "ab" else a

    def step(j, carry):
        total = first[0, mine, j].astype(F32)
        for k in range(second.shape[0]):
            total = total + second[k, j].astype(F32)
        second[0, j] = total.astype(BF16)
        return carry

    lax.fori_loop(0, nz, step, 0)


def fold_scratch(grid, order, rows, n):
    na, nb, nz = grid.na, grid.nb, grid.nz
    own = pltpu.VMEM((nb if order == "ab" else na, nz, rows, n), BF16)
    first = pltpu.VMEM((1, nb, nz, rows, n) if order == "ab" else (nb - 1, na, nz, rows, n), BF16)
    second = pltpu.VMEM((nb - 1, nz, rows, n) if order == "ab" else (1, nz, rows, n), BF16)
    return own, first, second


class Summing:
    def __init__(self, grid, mine, held, total, done, send_sem, recv_sem):
        self.n_seq, self.count = grid.n_seq, grid.n_dp * grid.n_seq
        self.mine, self.held, self.total, self.done = mine, held, total, done
        self.send_sem, self.recv_sem = send_sem, recv_sem
        self.rows = total.shape[0]
        self.me = lax.axis_index("dp") * grid.n_seq + lax.axis_index("seq")

    def device(self, k):
        other = lax.rem(self.me + k, self.count)
        return other, (other // self.n_seq, lax.rem(other, self.n_seq))

    def part(self, ref, k):
        return ref.at[pl.ds(pl.multiple_of(k * self.rows, self.rows), self.rows)]

    def greet(self):
        barrier = pltpu.get_barrier_semaphore()

        def step(k, carry):
            pl.semaphore_signal(barrier, inc=1, device_id=self.device(k)[1], device_id_type=MESH)
            return carry

        lax.fori_loop(1, self.count, step, 0)

    def settle(self, dst, slot):
        most = pl.ds(0, (self.count - 1) * self.rows)
        remote(self.mine.at[most], dst.at[most], self.send_sem.at[slot], self.recv_sem.at[slot], self.device(1)[1]).wait()

    def deal(self):
        def step(k, carry):
            other, place = self.device(k)
            remote(self.part(self.mine, other), self.part(self.held, self.me), self.send_sem.at[0], self.recv_sem.at[0], place).start()
            return carry

        lax.fori_loop(1, self.count, step, 0)
        at = pl.ds(pl.multiple_of(self.me * self.rows, self.rows), self.rows)
        self.held[at, :] = self.mine[at, :]

    def tell(self):
        self.settle(self.held, 0)

        def add(k, carry):
            return carry + self.held[pl.ds(pl.multiple_of(k * self.rows, self.rows), self.rows), :]

        self.total[...] = lax.fori_loop(0, self.count, add, jnp.zeros(self.total.shape, F32))

        def step(k, carry):
            place = self.device(k)[1]
            remote(self.total, self.part(self.done, self.me), self.send_sem.at[1], self.recv_sem.at[1], place).start()
            return carry

        lax.fori_loop(1, self.count, step, 0)
        self.done[pl.ds(pl.multiple_of(self.me * self.rows, self.rows), self.rows), :] = self.total[...]

    def close(self):
        self.settle(self.done, 1)


def spread_out(coeffs):
    return [jnp.broadcast_to(coeffs[:, k : k + 1], (coeffs.shape[0], 128)) for k in range(coeffs.shape[1])]


def blend(h_ref, coeffs, streams_ref):
    hist, width = h_ref.shape[0], h_ref.shape[3]
    spread = spread_out(coeffs)
    for at in range(0, width, 128):
        lanes = slice(at, at + 128)
        inputs = [h_ref[j, 0, :, lanes].astype(F32) for j in range(hist)]
        for c in range(4):
            total = spread[c * hist] * inputs[0]
            for j in range(1, hist):
                total = total + spread[c * hist + j] * inputs[j]
            streams_ref[c, :, lanes] = total


def mix_kernel(grid, rows, chunks, whole, partial, own_width, h_ref, g_ref, gain_ref, inner_ref, outer_ref, bias_ref, sgain_ref, sbias_ref,
               in_bias_ref, *refs):
    ins, (lowered_ref, gpair_ref, kept_ref, pre_ref, coeffs_ref, cos_ref, above_ref, below_ref) = refs[:4], refs[4:12]
    weights_ref, outs, dealt_ref, refs = refs[12], refs[13:15], refs[15], refs[16:]
    streams_ref, full_ref, gfull_ref, held_ref, sent_ref, bias_full, local_sem, send_sem, recv_sem = refs[:9]
    pair_local, pair_send, pair_recv, deal_send, deal_recv = refs[9:]
    i, steps = pl.program_id(0), pl.num_programs(0)
    a, b, z, c = place = grid.here()
    block = h_ref.shape[2]
    outs = [held_ref.at[k] for k in range(4)] + list(outs)
    work = Gathering(grid, place, rows, chunks, ins, outs, local_sem, send_sem, recv_sem)
    events = work.ticks(whole, partial)
    other = grid.device(a, b, z, 1 - c)
    nz = grid.nz

    def swap_grads():
        return [remote(g_ref.at[0], gfull_ref.at[c], pair_send.at[0], pair_recv.at[0], other)]

    def swap_lowered():
        return [remote(full_ref.at[:, c], full_ref.at[:, c], pair_send.at[1], pair_recv.at[1], other)]

    def hand_out():
        return [
            pltpu.make_async_copy(full_ref, lowered_ref, pair_local.at[0]),
            pltpu.make_async_copy(gfull_ref, gpair_ref, pair_local.at[1]),
            pltpu.make_async_copy(held_ref, weights_ref, pair_local.at[2]),
        ]

    def link(to):
        k = lax.rem(to - z + nz, nz)
        return remote(sent_ref.at[to], dealt_ref.at[z], deal_send.at[k], deal_recv.at[k], grid.device(a, b, to, c))

    def stay():
        return pltpu.make_async_copy(sent_ref.at[z], dealt_ref.at[z], deal_send.at[0])

    def project(n):
        wide = 2 * own_width
        turn = far_first(nz, z, n)
        cols = pl.ds(pl.multiple_of(turn * wide, wide), wide)
        both, width = 2 * full_ref.shape[2], full_ref.shape[3]
        third = bias_full.shape[0] // 3
        tables = [jnp.concatenate([t[...]] * (wide // 128), axis=1) for t in (cos_ref, above_ref, below_ref)]

        def one(k):
            inputs = gfull_ref[...] if k == 3 else full_ref[k]
            found = product(inputs.reshape(both, width), held_ref[k, :, :, :, :, cols].reshape(width, wide))
            if k == 3:
                return found
            first_row = k * third + c * (third // 2) + turn * (wide // 128)
            found = found + jnp.concatenate([bias_full[pl.ds(first_row + l, 1), :] for l in range(wide // 128)], axis=1)
            return rotate(found, tables, 1.0) if k < 2 else found

        for k in range(4):
            x = one(k).astype(BF16)
            for m in range(2):
                sent_ref[turn * 2 + m, :, k * own_width : (k + 1) * own_width] = x[:, m * own_width : (m + 1) * own_width]
        for m in range(2):
            to = turn * 2 + m
            pl.when(to != z)(lambda to=to: link(to).start())
            pl.when(to == z)(lambda: stay().start())

    @pl.when(i == 0)
    def _():
        grid.greet(*place)
        events[0]()
        start(swap_grads())
        gfull_ref[c] = g_ref[0]
        bias_full[...] = in_bias_ref[...].astype(F32)

    for n, at in enumerate((0, 1, 2, 3, 5)):

        @pl.when(i == at)
        def _(n=n):
            events[n + 1]()

    @pl.when(i == 2)
    def _():
        both, wide = cos_ref.shape
        half = ROT_DIMS // 2
        place_in = lax.rem(lax.broadcasted_iota(jnp.int32, (1, wide), 1), HEAD_DIM)
        step = lax.rem(place_in, half)
        freq = jnp.ones((1, wide), F32)
        for k in range(1, half):
            freq = jnp.where(step == k, 10000.0 ** (-2.0 * k / ROT_DIMS), freq)
        angles = (z * both + lax.broadcasted_iota(jnp.int32, (both, wide), 0)).astype(F32) * freq
        turned = place_in < ROT_DIMS
        sine = jnp.where(turned, jnp.sin(angles), 0.0)
        cos_ref[...] = jnp.where(turned, jnp.cos(angles), 1.0)
        above_ref[...] = jnp.where(place_in < half, -sine, 0.0)
        below_ref[...] = jnp.where(place_in < half, 0.0, sine)

    last = h_ref[h_ref.shape[0] - 1, 0].astype(F32)
    r = lax.rsqrt(jnp.mean(last * last, axis=1, keepdims=True) + EPS)
    scaled_low = (last * r * row(gain_ref)).astype(BF16)
    pre = against(scaled_low, inner_ref[...])
    pre_ref[...] = pre
    coeffs = product((pre * phi(pre)).astype(BF16), outer_ref[...]) + bias_ref[...].astype(F32)
    coeffs_ref[...] = coeffs
    blend(h_ref, coeffs, streams_ref)
    at = pl.ds(pl.multiple_of(i * block, block), block)
    for k in range(4):
        stream = streams_ref[k]
        centered = stream - jnp.mean(stream, axis=1, keepdims=True)
        rs = lax.rsqrt(jnp.mean(centered * centered, axis=1, keepdims=True) + EPS)
        gain, bias = sgain_ref[k : k + 1, :].astype(F32), sbias_ref[k : k + 1, :].astype(F32)
        full_ref[k, c, at, :] = (centered * rs * gain + bias).astype(BF16)
    kept_ref[...] = streams_ref[...]

    @pl.when(i == steps - 1)
    def _():
        start(swap_lowered())
        ready = len(whole) + nz - 1
        for event in events[6 : 1 + ready + 1]:
            event()
        events[-1]()
        finish(swap_grads())
        finish(swap_lowered())
        start(hand_out())
        hopped = [u for u in range(len(partial)) if u // 2 + len(whole) + nz - 1 <= ready]
        for u in hopped:
            work.begin(partial[u], 2)
        for n in range(nz // 2):
            project(n)
        for event in events[1 + ready + 1 : -1]:
            event()
        for u in range(len(partial)):
            if u not in hopped:
                work.begin(partial[u], 2)
        for group in partial:
            work.end(group, 2)
            work.begin(group, 3)
        for m in range(1, nz):
            link(lax.rem(z + m, nz)).wait()
        stay().wait()
        finish(hand_out())
        for group in partial:
            work.end(group, 3)


def mix_forward(grid, history, cotangent, params, weights, chunks, groups, partial, widths, own_width, collective_id):
    hist, _, tokens, width = history.shape
    mix = params[1].shape[0]
    block = 64
    rows = weights[0].shape[0]
    whole = pl.BlockSpec(memory_space=pltpu.VMEM)
    anywhere = pl.BlockSpec(memory_space=pl.ANY)
    part = lambda n: pl.BlockSpec((block, n), lambda i: (i, 0))
    chips = (grid.na, grid.nb, grid.nz, 2 * rows)
    results = pl.pallas_call(
        functools.partial(mix_kernel, grid, rows, chunks, groups, partial, own_width),
        grid=(tokens // block,),
        out_shape=[
            jax.ShapeDtypeStruct((4, 2, tokens, width), BF16),
            jax.ShapeDtypeStruct((2, tokens, width), BF16),
            jax.ShapeDtypeStruct((4, tokens, width), F32),
            jax.ShapeDtypeStruct((tokens, mix), F32),
            jax.ShapeDtypeStruct((tokens, mix), F32),
        ]
        + [jax.ShapeDtypeStruct((2 * tokens, 128), F32)] * 3
        + [jax.ShapeDtypeStruct((4, *chips, width // 2), BF16)]
        + [jax.ShapeDtypeStruct((*chips, w), BF16) for w in widths]
        + [jax.ShapeDtypeStruct((grid.nz, 2 * tokens, 4 * own_width), BF16)],
        in_specs=[pl.BlockSpec((hist, 1, block, width), lambda i: (0, 0, i, 0))] + [whole] * 12,
        out_specs=[anywhere, anywhere, pl.BlockSpec((4, block, width), lambda i: (0, i, 0)), part(mix), part(mix)]
        + [pl.BlockSpec((2 * tokens, 128), lambda i: (0, 0))] * 3
        + [anywhere] * 4,
        scratch_shapes=[
            pltpu.VMEM((4, block, width), F32),
            pltpu.VMEM((4, 2, tokens, width), BF16),
            pltpu.VMEM((2, tokens, width), BF16),
            pltpu.VMEM((4, *chips, width // 2), BF16),
            pltpu.VMEM((grid.nz, 2 * tokens, 4 * own_width), BF16),
            pltpu.VMEM(params[-1].shape, F32),
            *gather_sems(grid, chunks),
            pltpu.SemaphoreType.DMA((3,)),
            pltpu.SemaphoreType.DMA((2,)),
            pltpu.SemaphoreType.DMA((2,)),
            pltpu.SemaphoreType.DMA((grid.nz,)),
            pltpu.SemaphoreType.DMA((grid.nz,)),
        ],
        compiler_params=pltpu.CompilerParams(collective_id=collective_id, has_side_effects=True, vmem_limit_bytes=VMEM_LIMIT),
        cost_estimate=pl.CostEstimate(flops=tokens * width * 80, bytes_accessed=history.size * 40, transcendentals=0),
        name="mix_forward",
    )(history, cotangent, *params, *weights)
    lowered, gpair, streams, pre, coeffs = results[:5]
    return (
        lowered.reshape(4, 2 * tokens, width),
        gpair.reshape(2 * tokens, width),
        streams,
        pre,
        coeffs,
        results[5:8],
        results[8].reshape(4, width, width // 2),
        [x.reshape(-1, x.shape[-1]) for x in results[9:-1]],
        results[-1],
    )


def small_rows(width, mix, hidden_width):
    wl, padded = width // 128, -(-mix // 8) * 8
    sizes = [wl, wl * padded, padded, 8, 4 * wl, 4 * wl, 3 * wl, wl, hidden_width // 128]
    firsts = [sum(sizes[:k]) for k in range(len(sizes))]
    return firsts, sum(sizes)


def unmix_kernel(h_ref, streams_ref, own_ref, theirs_ref, g_ref, pre_ref, coeffs_ref, gain_ref, inner_ref, outer_ref, sgain_ref,
                 hist_ref, sgg_ref, sbg_ref, gg_ref, ig_ref, og_ref, bg_ref, ob_ref,
                 sg_ref, scaled_ref, mpg_ref, hidden_ref, cgl_ref):
    i, steps = pl.program_id(0), pl.num_programs(0)
    hist, block, width = h_ref.shape[0], h_ref.shape[2], h_ref.shape[3]
    mix = 4 * hist

    @pl.when(i == 0)
    def _():
        for ref in (sgg_ref, sbg_ref, gg_ref, bg_ref, ob_ref):
            ref[...] = jnp.zeros_like(ref)

    def down(x):
        return jnp.sum(x, axis=0, keepdims=True)

    spread = spread_out(coeffs_ref[...])
    grad = g_ref[0].astype(F32)
    ob_ref[...] += down(grad)
    for k in range(4):
        stream = streams_ref[k]
        centered = stream - jnp.mean(stream, axis=1, keepdims=True)
        rs = lax.rsqrt(jnp.mean(centered * centered, axis=1, keepdims=True) + EPS)
        n = centered * rs
        ng = own_ref[k] + theirs_ref[k].astype(F32)
        sgg_ref[k : k + 1, :] += down(ng * n)
        sbg_ref[k : k + 1, :] += down(ng)
        w = ng * sgain_ref[k : k + 1, :].astype(F32)
        pulled = rs * (w - jnp.mean(w, axis=1, keepdims=True) - n * jnp.mean(w * n, axis=1, keepdims=True))
        sg_ref[k] = pulled + grad if k == 3 else pulled

    lane = lax.broadcasted_iota(jnp.int32, (block, mix), 1)
    cg = jnp.zeros((block, mix), F32)
    for j in range(hist):
        value = h_ref[j, 0].astype(F32)
        for k in range(4):
            cg = jnp.where(lane == k * hist + j, jnp.sum(value * sg_ref[k], axis=1, keepdims=True), cg)
    bg_ref[...] += down(cg)
    cg_low = cg.astype(BF16)
    pre = pre_ref[...]
    at = pl.ds(pl.multiple_of(i * block, block), block)
    mpg = (against(cg_low, outer_ref[...]) * gelu_slope(pre)).astype(BF16)
    last = h_ref[hist - 1, 0].astype(F32)
    r = lax.rsqrt(jnp.mean(last * last, axis=1, keepdims=True) + EPS)
    gain = row(gain_ref)
    scaled_ref[at, :] = (last * r * gain).astype(BF16)
    mpg_ref[at, :] = mpg
    hidden_ref[at, :] = (pre * phi(pre)).astype(BF16)
    cgl_ref[at, :] = cg_low
    scaled_grad = product(mpg, inner_ref[...])
    gg_ref[...] += down(scaled_grad * last * r)
    w = scaled_grad * gain
    last_grad = r * (w - last * (r * r) * jnp.mean(w * last, axis=1, keepdims=True))
    for from_ in range(0, width, 128):
        lanes = slice(from_, from_ + 128)
        pulls = [sg_ref[k, :, lanes] for k in range(4)]
        for j in range(hist):
            total = spread[j] * pulls[0]
            for k in range(1, 4):
                total = total + spread[k * hist + j] * pulls[k]
            hist_ref[j, 0, :, lanes] = total + last_grad[:, lanes] if j == hist - 1 else total

    @pl.when(i == steps - 1)
    def _():
        ig_ref[...] = inner(mpg_ref[...], scaled_ref[...])
        og_ref[...] = inner(hidden_ref[...], cgl_ref[...])


def mix_backward(history, streams, own, theirs, cotangent, pre, coeffs, params):
    hist, _, tokens, width = history.shape
    mix = pre.shape[1]
    block = 64
    whole = pl.BlockSpec(memory_space=pltpu.VMEM)
    part = lambda n: pl.BlockSpec((block, n), lambda i: (i, 0))
    four = pl.BlockSpec((4, block, width), lambda i: (0, i, 0))
    story = pl.BlockSpec((hist, 1, block, width), lambda i: (0, 0, i, 0))
    small = [(4, width), (4, width), (1, width), (mix, width), (mix, mix), (1, mix), (1, width)]
    return pl.pallas_call(
        unmix_kernel,
        grid=(tokens // block,),
        out_shape=[jax.ShapeDtypeStruct(history.shape, F32)] + [jax.ShapeDtypeStruct(shape, F32) for shape in small],
        in_specs=[story, four, four, four, pl.BlockSpec((1, block, width), lambda i: (0, i, 0)), part(mix), part(mix)] + [whole] * 4,
        out_specs=[story] + [pl.BlockSpec(shape, lambda i: (0, 0)) for shape in small],
        scratch_shapes=[
            pltpu.VMEM((4, block, width), F32),
            pltpu.VMEM((tokens, width), BF16),
            pltpu.VMEM((tokens, mix), BF16),
            pltpu.VMEM((tokens, mix), BF16),
            pltpu.VMEM((tokens, mix), BF16),
        ],
        compiler_params=pltpu.CompilerParams(vmem_limit_bytes=VMEM_LIMIT),
        cost_estimate=pl.CostEstimate(flops=tokens * width * 1000, bytes_accessed=history.size * 12, transcendentals=0),
        name="mix_backward",
    )(history, streams, own, theirs, cotangent, pre, coeffs, *params)


def finish_kernel(grid, orders, n_kept, *refs):
    nz = grid.nz
    kept, refs = refs[:n_kept], refs[n_kept:]
    came_a, came_b, refs = refs[:1], refs[1 : grid.nb], refs[grid.nb :]
    sum_ref, folded, refs = refs[0], refs[1 : 1 + nz], refs[1 + nz :]
    sgg_ref, sbg_ref, gg_ref, ig_ref, og_ref, bg_ref, ob_ref, hb_ref, eb_ref = refs[:9]
    done_ref, outs, refs = refs[9], refs[10:14], refs[14:]
    first, second, third, final, refs = refs[:4], refs[4:8], refs[8:12], refs[12:18], refs[18:]
    sums = Summing(grid, *refs[:3], done_ref, *refs[3:5])
    local_sem, send_sem, recv_sem = refs[5:]
    a, b, z, c = place = grid.here()
    width, mix = gg_ref.shape[1], bg_ref.shape[1]
    wl, padded, hidden_rows = width // 128, -(-mix // 8) * 8, eb_ref.shape[1] // 128
    firsts, _ = small_rows(width, mix, 2 * eb_ref.shape[1])
    half = width // 2
    spots = [(0, lambda core: core * half), (0, lambda core: width + core * half), (0, lambda core: 2 * width + core * half),
             (1, lambda core: core * half), (2, lambda core: core * eb_ref.shape[1]), (3, lambda core: core * eb_ref.shape[1])]

    def copies(t, stage):
        if stage == 1:
            return fold_copies(grid, place, orders[t], 1, None, first[t], second[t], (send_sem.at[t], recv_sem.at[t]))
        if stage == 2:
            return [
                remote(second[t].at[0, lax.rem(z + k, nz)], third[t].at[k - 1], send_sem.at[t, k], recv_sem.at[t, k],
                       grid.device(a, b, lax.rem(z + k, nz), c))
                for k in range(1, nz)
            ]
        result, base = spots[t]
        n = final[t].shape[-1]
        spot = outs[result].at[:, pl.ds(pl.multiple_of(base(c), 128), n)]
        return [
            remote(final[t].at[1 - c], spot, send_sem.at[t, 0], recv_sem.at[t, 0], grid.device(a, b, z, 1 - c)),
            pltpu.make_async_copy(final[t].at[c], spot, local_sem.at[t]),
        ]

    def add_first(t):
        def step(i, carry):
            o, j = i // nz, lax.rem(i, nz)
            total = kept[t][o, j].astype(F32)
            for piece in came_a if orders[t] == "ab" else came_b:
                total = total + piece[t // 2, o, j].astype(F32)
            first[t][0, o, j] = total.astype(BF16)
            return carry

        lax.fori_loop(0, first[t].shape[1] * nz, step, 0)

    sums.greet()
    add_first(0)
    add_first(1)
    mine = sums.mine
    mine[...] = jnp.zeros_like(mine)
    for l in range(wl):
        lanes = slice(l * 128, (l + 1) * 128)
        mine[firsts[0] + l : firsts[0] + l + 1, :] = gg_ref[:, lanes]
        mine[firsts[1] + l * padded : firsts[1] + l * padded + mix, :] = ig_ref[:, lanes]
        mine[firsts[4] + 4 * l : firsts[4] + 4 * l + 4, :] = sgg_ref[:, lanes]
        mine[firsts[5] + 4 * l : firsts[5] + 4 * l + 4, :] = sbg_ref[:, lanes]
        mine[firsts[7] + l : firsts[7] + l + 1, :] = ob_ref[:, lanes]
    mine[firsts[2] : firsts[2] + mix, 0:mix] = og_ref[...]
    mine[firsts[3] : firsts[3] + 1, 0:mix] = bg_ref[...]
    for k in range(3):
        for l in range(wl // 2):
            mine[pl.ds(firsts[6] + k * wl + c * (wl // 2) + l, 1), :] = hb_ref[k : k + 1, l * 128 : (l + 1) * 128]
    for l in range(hidden_rows):
        mine[pl.ds(firsts[8] + c * hidden_rows + l, 1), :] = eb_ref[:, l * 128 : (l + 1) * 128]
    pl.semaphore_wait(pltpu.get_barrier_semaphore(), sums.count - 1)
    for t in range(2):
        start(copies(t, 1))
    sums.deal()
    add_first(2)
    add_first(3)
    for t in range(2):
        total = folded[0][t].astype(F32)
        for piece in folded[1:]:
            total = total + piece[t].astype(F32)
        at = 0
        for piece in (sum_ref[t], total):
            n = piece.shape[1]
            final[4 + t][:, :, at : at + n] = piece.reshape(2, -1, n)
            at += n
        start(copies(4 + t, 3))
    def second_step(t):
        finish(copies(t, 1))
        if t < 2:
            start(copies(t + 2, 1))
        fold_add(grid, place, orders[t], 1, None, first[t], second[t])
        start(copies(t, 2))

    for t in range(4):
        second_step(t)
    sums.tell()
    for t in range(4):
        finish(copies(t, 2))
        total = second[t][0, z].astype(F32)
        for k in range(nz - 1):
            total = total + third[t][k].astype(F32)
        final[t][...] = total.reshape(final[t].shape)
        start(copies(t, 3))
    sums.close()
    for t in range(6):
        finish(copies(t, 3))


def finish_sums(grid, orders, kept, came, folded, smalls, collective_id):
    sgg, _, _, ig, og, bg, _, hb, eb = smalls
    mix, width = ig.shape
    hidden_width = 2 * eb.shape[1]
    nz = grid.nz
    rows, n = kept[0].shape[-2:]
    devices = grid.n_dp * grid.n_seq
    each = -(-small_rows(width, mix, hidden_width)[1] // (devices * 8)) * 8
    vmem = pl.BlockSpec(memory_space=pltpu.VMEM)
    owned = [3 * width, width, hidden_width, hidden_width]
    folds = [fold_scratch(grid, order, rows, n) for order in orders]
    operands = list(kept) + list(came) + list(folded) + list(smalls)
    return pl.pallas_call(
        functools.partial(finish_kernel, grid, orders, len(kept)),
        out_shape=[jax.ShapeDtypeStruct((devices * each, 128), F32)] + [jax.ShapeDtypeStruct((rows // 2, w), F32) for w in owned],
        in_specs=[vmem] * len(operands),
        out_specs=[vmem] + [pl.BlockSpec(memory_space=pl.ANY)] * len(owned),
        scratch_shapes=[f for _, f, _ in folds]
        + [s for _, _, s in folds]
        + [pltpu.VMEM((nz - 1, rows, n), BF16)] * 4
        + [pltpu.VMEM((2, rows // 2, n), F32)] * 4
        + [pltpu.VMEM((2, rows // 2, hidden_width // 2), F32)] * 2
        + [
            pltpu.VMEM((devices * each, 128), F32),
            pltpu.VMEM((devices * each, 128), F32),
            pltpu.VMEM((each, 128), F32),
            pltpu.SemaphoreType.DMA((2,)),
            pltpu.SemaphoreType.DMA((2,)),
            pltpu.SemaphoreType.DMA((6,)),
            pltpu.SemaphoreType.DMA((6, nz + grid.nb)),
            pltpu.SemaphoreType.DMA((6, nz + grid.nb)),
        ],
        compiler_params=pltpu.CompilerParams(collective_id=collective_id, has_side_effects=True, vmem_limit_bytes=VMEM_LIMIT),
        cost_estimate=pl.CostEstimate(flops=0, bytes_accessed=100 * width * width, transcendentals=0),
        name="finish_sums",
    )(*operands)


def hand_kernel(mix, hidden_width, done, out_ref, *refs):
    owned, placed_ref, small, outs = refs[:4], refs[4], refs[5:14], refs[14:]
    width = out_ref.shape[1]
    wl, padded, hidden_rows = width // 128, -(-mix // 8) * 8, hidden_width // 256
    firsts, _ = small_rows(width, mix, hidden_width)
    placed_ref[...] = out_ref[...]
    outs, again = outs[:4], outs[4]
    for src, dst in zip(owned, outs):
        dst[...] = src[...]
    for l in range(wl):
        lanes = slice(l * 128, (l + 1) * 128)
        small[0][:, lanes] = done[firsts[0] + l : firsts[0] + l + 1, :]
        small[1][:, lanes] = done[firsts[1] + l * padded : firsts[1] + l * padded + mix, :]
        small[4][:, lanes] = done[firsts[4] + 4 * l : firsts[4] + 4 * l + 4, :]
        small[5][:, lanes] = done[firsts[5] + 4 * l : firsts[5] + 4 * l + 4, :]
        small[7][:, lanes] = again[:, lanes] = done[firsts[7] + l : firsts[7] + l + 1, :]
    small[2][...] = done[firsts[2] : firsts[2] + mix, 0:mix]
    small[3][...] = done[firsts[3] : firsts[3] + 1, 0:mix]
    for l in range(3 * wl):
        small[6][:, l * 128 : (l + 1) * 128] = done[firsts[6] + l : firsts[6] + l + 1, :]
    for l in range(2 * hidden_rows):
        small[8][:, l * 128 : (l + 1) * 128] = done[firsts[8] + l : firsts[8] + l + 1, :]


def hand_over(summed, layer_out, owned, mix, hidden_width):
    width = layer_out.shape[1]
    small = [(1, width), (mix, width), (mix, mix), (1, mix), (4, width), (4, width), (1, 3 * width), (1, width), (1, hidden_width)]
    vmem = pl.BlockSpec(memory_space=pltpu.VMEM)
    return pl.pallas_call(
        functools.partial(hand_kernel, mix, hidden_width),
        out_shape=[jax.ShapeDtypeStruct(layer_out.shape, BF16)]
        + [jax.ShapeDtypeStruct(shape, F32) for shape in small]
        + [jax.ShapeDtypeStruct(x.shape, F32) for x in owned]
        + [jax.ShapeDtypeStruct((1, width), F32)],
        in_specs=[vmem] * 6,
        out_specs=[vmem] * 15,
        name="hand_over",
    )(summed, layer_out, *owned)


def far_first(nz, z, i):
    pairs = nz // 2
    return lax.rem(i + pairs // 2 * (1 - z // pairs), pairs)


def unproject_kernel(grid, width, orders, *all_refs):
    nz = grid.nz
    mids, lates, last_parts, all_refs = all_refs[:nz], all_refs[nz : 2 * nz], all_refs[2 * nz : 2 * nz + 2], all_refs[2 * nz + 2 :]
    (col_ref, low_ref, g_ref, w_ref, feed_ref, normed_ref, last_ref, bias_ref, bias2_ref, cos_ref, above_ref,
     below_ref, own_ref, theirs_ref, hb_ref, out_ref, sum_ref, *refs) = all_refs
    nb = grid.nb
    lasts, refs = refs[:nz], refs[nz:]
    kept, over_a, over_b, refs = refs[:4], refs[4], refs[5 : 4 + nb], refs[4 + nb :]
    grad_ref, sending_ref, partial_ref, mine_ref, arrived_ref, along_ref, split_sem, send_sem, recv_sem, along_send, along_recv = refs[:11]
    keep_refs, firsts, seconds, (fold_send, fold_recv, late_sem) = refs[11:13], refs[13:15], refs[15:17], refs[17:]
    i = pl.program_id(0)
    a, b, z, c = grid.here()
    tokens = out_ref.shape[0]
    other = grid.device(a, b, z, 1 - c)
    own_rows = pl.ds(pl.multiple_of(c * tokens, tokens), tokens)
    their_rows = pl.ds(pl.multiple_of((1 - c) * tokens, tokens), tokens)

    def swap(k):
        return [remote(sending_ref.at[k], theirs_ref.at[k], send_sem.at[k], recv_sem.at[k], other)]

    def swap_out():
        return [remote(partial_ref, arrived_ref, send_sem.at[4], recv_sem.at[4], other)]

    def along():
        return [
            remote(mids[k], along_ref.at[k - 1], along_send.at[k - 1], along_recv.at[k - 1], grid.device(a, b, lax.rem(z + k, nz), c))
            for k in range(1, nz)
        ]

    def fold(t, stage):
        if stage < 2:
            order = ("ab", "ba")[t]
            found = fold_copies(grid, (a, b, z, c), order, stage, last_parts[t], firsts[t], seconds[t], (fold_send.at[t], fold_recv.at[t]))
            if stage == 0:
                kept_part = last_parts[t].at[a] if order == "ab" else last_parts[t].at[:, b]
                found.append(pltpu.make_async_copy(kept_part, keep_refs[t], late_sem.at[t]))
            return found
        n = seconds[t].shape[-1]
        return [
            pltpu.make_async_copy(seconds[t].at[0, lax.rem(z + k, nz)], lasts[k].at[t, :, pl.ds(n, n)], late_sem.at[2 + t * nz + k])
            for k in range(nz)
        ]

    def settle(stage):
        for t in range(2):
            finish(fold(t, stage))
            fold_add(grid, (a, b, z, c), ("ab", "ba")[t], stage, keep_refs[t], firsts[t], seconds[t])
            start(fold(t, stage + 1))

    def place_lates():
        n = lates[0].shape[-1]
        return [pltpu.make_async_copy(lates[k], lasts[k].at[:, :, pl.ds(0, n)], late_sem.at[2 + 2 * nz + k]) for k in range(nz)]

    def split(k):
        grad = grad_ref.at[k]
        if orders[k] == "ab":
            found = [(grad.at[a], kept[k]), (grad.at[1 - a], over_a.at[k // 2])]
        else:
            found = [(grad.at[:, b], kept[k])]
            found += [(grad.at[:, lax.rem(b + m, nb)], over_b[m - 1].at[k // 2]) for m in range(1, nb)]
        return [pltpu.make_async_copy(src, dst, split_sem.at[k, n]) for n, (src, dst) in enumerate(found)]

    def piece(n):
        return jnp.concatenate([col_ref[m, :, n * width : (n + 1) * width] for m in range(nz)], axis=1)

    def keep(k, grad):
        grad_ref[k] = grad.astype(BF16).reshape(grad_ref.shape[1:])
        start(split(k))

    @pl.when(i == 0)
    def _():
        grid.greet(a, b, z, c)
        start(along())
        for t in range(2):
            start(fold(t, 0))
        start(place_lates())
        mine_ref[...] = piece(0)
        partial_ref[...] = against(mine_ref[their_rows, :], w_ref[0]) + feed_ref[their_rows, :]
        sending_ref[3] = normed_ref[their_rows, :].astype(BF16)
        start(swap_out())
        start(swap(3))
        own_ref[0] = normed_ref[own_rows, :]
        out = against(mine_ref[own_rows, :], w_ref[0]) + feed_ref[own_rows, :] + last_ref[0] + (row(bias_ref) + row(bias2_ref))
        keep(3, inner(g_ref[...], mine_ref[...]))
        finish(swap_out())
        out_ref[...] = (out + arrived_ref[...]).astype(BF16)

    for k in range(3):

        @pl.when(i == k + 1)
        def _(k=k):
            if k == 2:
                settle(0)
            grad = piece(k + 1).astype(F32)
            if k < 2:
                tables = [jnp.concatenate([t[...]] * (grad.shape[1] // 128), axis=1) for t in (cos_ref, above_ref, below_ref)]
                grad = rotate(grad, tables, -1.0)
            hb_ref[k : k + 1, :] = jnp.sum(grad, axis=0, keepdims=True)
            mine_ref[...] = grad.astype(BF16)
            sending_ref[k] = against(mine_ref[their_rows, :], w_ref[0]).astype(BF16)
            start(swap(k))
            own_ref[0] = against(mine_ref[own_rows, :], w_ref[0])
            keep(k, inner(low_ref[0], mine_ref[...]))
            if k == 2:
                for n in range(4):
                    finish(swap(n))
                    finish(split(n))
                settle(1)
                finish(along())
                total = mids[0][...].astype(F32)
                for n in range(nz - 1):
                    total = total + along_ref[n].astype(F32)
                sum_ref[...] = total
                for t in range(2):
                    finish(fold(t, 2))
                finish(place_lates())


def unproject(grid, orders, mids, lates, last_parts, collected, lowered, grad_low, weights, feed_part, normed_feed, streams, biases, tables, own_width, collective_id):
    _, tokens, width = streams.shape
    both, half = 2 * tokens, width // 2
    na, nb, nz = grid.na, grid.nb, grid.nz
    rows = width // (na * nb * nz)
    n = lates[0].shape[-1]
    folds = [fold_scratch(grid, order, rows, n) for order in ("ab", "ba")]
    whole = pl.BlockSpec(memory_space=pltpu.VMEM)
    anywhere = pl.BlockSpec(memory_space=pl.ANY)
    turn = lambda i: lax.rem(i + 3, 4)
    split_shapes = [jax.ShapeDtypeStruct((nb if order == "ab" else na, nz, rows, half), BF16) for order in orders]
    sent_shapes = [jax.ShapeDtypeStruct((2, nb, nz, rows, half), BF16)] + [jax.ShapeDtypeStruct((2, na, nz, rows, half), BF16)] * (nb - 1)
    results = pl.pallas_call(
        functools.partial(unproject_kernel, grid, own_width, orders),
        grid=(4,),
        out_shape=[
            jax.ShapeDtypeStruct((4, tokens, width), F32),
            jax.ShapeDtypeStruct((4, tokens, width), BF16),
            jax.ShapeDtypeStruct((3, half), F32),
            jax.ShapeDtypeStruct((tokens, width), BF16),
            jax.ShapeDtypeStruct(mids[0].shape, F32),
        ]
        + [jax.ShapeDtypeStruct((2, rows, 2 * n), BF16)] * nz
        + split_shapes
        + sent_shapes,
        in_specs=[whole]
        + [anywhere] * (nz - 1)
        + [whole] * nz
        + [anywhere] * 2
        + [
            whole,
            pl.BlockSpec((1, both, width), lambda i: (jnp.maximum(i - 1, 0), 0, 0)),
            whole,
            pl.BlockSpec((1, width, half), lambda i: (turn(i), 0, 0)),
        ]
        + [whole] * 2
        + [pl.BlockSpec((1, tokens, width), lambda i: (3, 0, 0))]
        + [whole] * 5,
        out_specs=[
            pl.BlockSpec((1, tokens, width), lambda i: (turn(i), 0, 0)),
            anywhere,
            pl.BlockSpec((3, half), lambda i: (0, 0)),
            pl.BlockSpec((tokens, width), lambda i: (0, 0)),
            pl.BlockSpec(mids[0].shape, lambda i: (0, 0, 0)),
        ]
        + [anywhere] * (nz + len(split_shapes) + len(sent_shapes)),
        scratch_shapes=[
            pltpu.VMEM((4, na, nb, nz, rows, half), BF16),
            pltpu.VMEM((4, tokens, width), BF16),
            pltpu.VMEM((tokens, width), F32),
            pltpu.VMEM((both, half), BF16),
            pltpu.VMEM((tokens, width), F32),
            pltpu.VMEM((nz - 1, *mids[0].shape), BF16),
            pltpu.SemaphoreType.DMA((4, nb + 1)),
            pltpu.SemaphoreType.DMA((5,)),
            pltpu.SemaphoreType.DMA((5,)),
            pltpu.SemaphoreType.DMA((nz - 1,)),
            pltpu.SemaphoreType.DMA((nz - 1,)),
            *[o for o, _, _ in folds],
            *[f for _, f, _ in folds],
            *[f for _, _, f in folds],
            pltpu.SemaphoreType.DMA((2, nz + nb)),
            pltpu.SemaphoreType.DMA((2, nz + nb)),
            pltpu.SemaphoreType.DMA((2 + 3 * nz,)),
        ],
        compiler_params=pltpu.CompilerParams(collective_id=collective_id, has_side_effects=True, vmem_limit_bytes=VMEM_LIMIT),
        cost_estimate=pl.CostEstimate(flops=32 * both * width * half, bytes_accessed=40 * both * width, transcendentals=0),
        name="unproject",
    )(*mids, *lates, *last_parts, collected, lowered, grad_low, weights, feed_part, normed_feed, streams, *biases, *tables)
    own, theirs, head_bias, layer_out, mid_sums = results[:5]
    lasts, results = results[5 : 5 + nz], results[5 + nz :]
    return own, theirs, head_bias, layer_out, mid_sums, lasts, results[:4], results[4:]


def feed_kernel(grid, steps, back_ref, low_ref, g_ref, we_ref, wc_ref, bias_ref, collected_ref, feed_ref, normed_ref, eb_ref, *refs):
    nz = grid.nz
    groups = steps - 1
    mids, outs, whole_outs, refs = refs[:nz], refs[nz : 2 * nz], refs[2 * nz : 2 * nz + 2], refs[2 * nz + 2 :]
    parts, refs = refs[: 2 * steps], refs[2 * steps :]
    first, second, refs = refs[: 2 * groups], refs[2 * groups : 4 * groups], refs[4 * groups :]
    bias_full, send_sem, recv_sem, out_sem, back_send, back_recv = refs
    i = pl.program_id(0)
    a, b, z, c = place = grid.here()
    orders = ["ab", "ba"] * steps

    def copies(t, stage):
        if stage < 2:
            return fold_copies(grid, place, orders[t], stage, parts[t], first[t], second[t], (send_sem.at[t], recv_sem.at[t]))
        along = [lax.rem(z + k, nz) for k in range(nz)]
        u, n = t // 2, parts[t].shape[-1]
        late = u == groups - 1
        cols = pl.ds(0 if late else u * n, n)
        spot = outs if late else mids
        return [pltpu.make_async_copy(second[t].at[0, along[k]], spot[k].at[t % 2, :, cols], out_sem.at[t, k]) for k in range(nz)]

    def last_parts():
        return [pltpu.make_async_copy(parts[2 * groups + k], whole_outs[k], out_sem.at[2 * groups + k, 0]) for k in range(2)]

    def begin(u):
        for t in (2 * u, 2 * u + 1):
            start(copies(t, 0))

    def end(u, stage):
        for t in (2 * u, 2 * u + 1):
            finish(copies(t, stage))
            if stage < 2:
                own = parts[t].at[a] if orders[t] == "ab" else parts[t].at[:, b]
                fold_add(grid, place, orders[t], stage, own, first[t], second[t])
                start(copies(t, stage + 1))

    def turn(u):
        for stage in range(3):
            if 0 <= u - stage < groups:
                end(u - stage, stage)

    def backs():
        found = [pltpu.make_async_copy(back_ref.at[z], collected_ref.at[z], back_send.at[0])]
        for k in range(1, nz):
            to = lax.rem(z + k, nz)
            found.append(remote(back_ref.at[to], collected_ref.at[z], back_send.at[k], back_recv.at[k], grid.device(a, b, to, c)))
        return found

    @pl.when(i == 0)
    def _():
        grid.greet(*place)
        start(backs())
        bias_full[...] = bias_ref[...].astype(F32)
        feed_ref[...] = jnp.zeros_like(feed_ref)
        normed_ref[...] = jnp.zeros_like(normed_ref)

    low, grad, expand, contract = low_ref[0], g_ref[...], we_ref[...], wc_ref[...]
    wide = expand.shape[1] // 128
    first_row = c * (bias_full.shape[0] // 2) + i * wide
    bias = jnp.concatenate([bias_full[pl.ds(first_row + l, 1), :] for l in range(wide)], axis=1)
    expanded = product(low, expand) + bias
    share = phi(expanded)
    hidden = (expanded * share).astype(BF16)
    slope = share + expanded * jnp.exp(-0.5 * expanded * expanded) * (1.0 / math.sqrt(2.0 * math.pi))
    feed_ref[...] += against(hidden, contract)
    hidden_grad = inner(grad, hidden).astype(BF16)
    pulled = product(grad, contract) * slope
    eb_ref[...] = jnp.sum(pulled, axis=0, keepdims=True)
    pulled_low = pulled.astype(BF16)
    normed_ref[...] += against(pulled_low, expand)
    expand_grad = inner(low, pulled_low).astype(BF16)
    for u in range(steps):

        @pl.when(i == u)
        def _(u=u):
            parts[2 * u][...] = expand_grad.reshape(parts[2 * u].shape)
            parts[2 * u + 1][...] = hidden_grad.reshape(parts[2 * u + 1].shape)
            if u < groups:
                begin(u)
            else:
                start(last_parts())
            if u >= 2:
                turn(u - 2)
            if u == steps - 1:
                for v in range(max(steps - 2, 0), groups + 2):
                    turn(v)
                finish(last_parts())
                finish(backs())


def feed_forward(grid, returned, lowered, grad_low, weight_e, weight_c, bias, steps, collective_id):
    both, width = grad_low.shape
    n = weight_e.shape[1] // steps
    na, nb, nz = grid.na, grid.nb, grid.nz
    rows = width // (na * nb * nz)
    whole = lambda *shape: pl.BlockSpec(shape, lambda i: (0,) * len(shape))
    cols = lambda m: pl.BlockSpec((m, n), lambda i: (0, i))
    orders = ["ab", "ba"] * steps
    folds = [fold_scratch(grid, order, rows, n) for order in orders]
    sem = pltpu.SemaphoreType.DMA((2 * steps, nz + nb))
    return pl.pallas_call(
        functools.partial(feed_kernel, grid, steps),
        grid=(steps,),
        out_shape=[
            jax.ShapeDtypeStruct(returned.shape, BF16),
            jax.ShapeDtypeStruct((both, width), F32),
            jax.ShapeDtypeStruct((both, width), F32),
            jax.ShapeDtypeStruct((1, n * steps), F32),
        ]
        + [jax.ShapeDtypeStruct((2, rows, n * (steps - 2)), BF16)] * nz
        + [jax.ShapeDtypeStruct((2, rows, n), BF16)] * nz
        + [jax.ShapeDtypeStruct((na, nb, nz, rows, n), BF16)] * 2,
        in_specs=[
            pl.BlockSpec(memory_space=pl.ANY),
            pl.BlockSpec((1, both, width), lambda i: (3, 0, 0)),
            whole(both, width),
            cols(width),
            cols(width),
            whole(*bias.shape),
        ],
        out_specs=[
            pl.BlockSpec(memory_space=pl.ANY),
            whole(both, width),
            whole(both, width),
            cols(1),
        ]
        + [pl.BlockSpec(memory_space=pl.ANY)] * (2 * nz + 2),
        scratch_shapes=[pltpu.VMEM((na, nb, nz, rows, n), BF16)] * (2 * steps)
        + [f for _, f, _ in folds[:-2]]
        + [s for _, _, s in folds[:-2]]
        + [pltpu.VMEM(bias.shape, F32)]
        + [sem, sem, pltpu.SemaphoreType.DMA((2 * steps, nz)), pltpu.SemaphoreType.DMA((nz,)), pltpu.SemaphoreType.DMA((nz,))],
        compiler_params=pltpu.CompilerParams(collective_id=collective_id, has_side_effects=True, vmem_limit_bytes=VMEM_LIMIT),
        cost_estimate=pl.CostEstimate(flops=12 * both * width * n * steps * 2, bytes_accessed=width * n * steps * 20, transcendentals=0),
        name="feed_forward",
    )(returned, lowered, grad_low, weight_e, weight_c, bias)


def attention_kernel(width, heads, tile, edge, length, x_ref, qdoc_ref, out_ref, kdoc_ref,
                     s_ref, kt_ref, vt_ref, ot_ref, dqt_ref, dka_ref, dva_ref, top_ref):
    i = pl.program_id(0)
    tiles = length // tile
    scale = 1.0 / math.sqrt(HEAD_DIM)
    @pl.when(i == 0)
    def _():
        dka_ref[...] = jnp.zeros_like(dka_ref)
        dva_ref[...] = jnp.zeros_like(dva_ref)
        def turn(j, carry):
            at = pl.ds(pl.multiple_of(j * tile, tile), tile)
            kt_ref[:, at] = x_ref[at, width : 2 * width].T
            kdoc_ref[at, :] = jnp.broadcast_to(qdoc_ref[:, at].astype(F32), (128, tile)).T
            vt_ref[:, at] = x_ref[at, 2 * width : 3 * width].T
            return carry
        lax.fori_loop(0, tiles, turn, 0)
    rows = pl.ds(pl.multiple_of(i * tile, tile), tile)
    query = x_ref[rows, 0:width] * jnp.asarray(scale, BF16)
    grad = x_ref[rows, 3 * width : 4 * width]
    query_t, grad_t = query.T, grad.T
    lanes = lax.broadcasted_iota(jnp.int32, (tile, width), 1) // HEAD_DIM
    subs = lax.broadcasted_iota(jnp.int32, (width, tile), 0) // HEAD_DIM
    zero = jnp.zeros((), BF16)
    queries_t = [jnp.where(subs == h, query_t, zero) for h in range(heads)]
    grads_t = [jnp.where(subs == h, grad_t, zero) for h in range(heads)]
    spread_queries = [jnp.where(lanes == h, query, zero) for h in range(heads)]
    spread_grads = [jnp.where(lanes == h, grad, zero) for h in range(heads)]
    qdoc = qdoc_ref[:, rows].astype(F32)
    head_edge = -(-edge // tile)
    tail_edge = (length - edge) // tile
    half = tile // 2
    corners = [(0, half, 0), (half, half, half)]
    ot_ref[...] = jnp.zeros_like(ot_ref)
    dqt_ref[...] = jnp.zeros_like(dqt_ref)
    top_ref[...] = jnp.full_like(top_ref, NEG)

    def fold(x, f):
        return f(x.reshape(x.shape[0] // 8, 8, x.shape[1]), axis=0)

    def score(first, size, left, documents, causal):
        at = pl.ds(pl.multiple_of(first, size), size)
        keys = x_ref[at, width : 2 * width]
        wide = tile - left
        if documents:
            allowed = jnp.concatenate([kdoc_ref[at, :]] * (wide // 128), axis=1) == qdoc[:, left:]
        if causal:
            allowed &= lax.broadcasted_iota(jnp.int32, (size, wide), 0) <= lax.broadcasted_iota(jnp.int32, (size, wide), 1)
        for h in range(heads):
            s = product(keys, queries_t[h][:, left:])
            if documents:
                s = jnp.where(allowed, s, NEG)
            s_ref[h, at, left:] = s
            top_ref[h, :, left:] = jnp.maximum(top_ref[h, :, left:], fold(s, jnp.max))

    def scores(j, carry):
        checked = (j < head_edge) | (i >= tail_edge)
        pl.when(checked)(lambda: score(j * tile, tile, 0, True, False))
        pl.when(jnp.logical_not(checked))(lambda: score(j * tile, tile, 0, False, False))
        return carry

    lax.fori_loop(0, i, scores, 0)
    for first, size, left in corners:
        score(i * tile + first, size, left, True, True)
    tops = [jnp.max(top_ref[h], axis=0, keepdims=True) for h in range(heads)]
    top_ref[...] = jnp.zeros_like(top_ref)

    def weigh(first, size, left):
        at = pl.ds(pl.multiple_of(first, size), size)
        for h in range(heads):
            own = slice(h * HEAD_DIM, (h + 1) * HEAD_DIM)
            weights = jnp.exp(s_ref[h, at, left:] - tops[h][:, left:])
            s_ref[h, at, left:] = weights
            top_ref[h, :, left:] += fold(weights, jnp.sum)
            ot_ref[own, left:] += product(vt_ref[own, at], weights.astype(BF16))

    lax.fori_loop(0, i, lambda j, carry: (weigh(j * tile, tile, 0), carry)[1], 0)
    for first, size, left in corners:
        weigh(i * tile + first, size, left)
    inverse = [1.0 / jnp.sum(top_ref[h], axis=0, keepdims=True) for h in range(heads)]
    grad_f = grad_t.astype(F32)
    deltas = []
    for h in range(heads):
        own = slice(h * HEAD_DIM, (h + 1) * HEAD_DIM)
        value = ot_ref[own, :] * inverse[h]
        ot_ref[own, :] = value
        deltas.append(jnp.sum(value * grad_f[own], axis=0, keepdims=True))
    out_ref[rows, 0:width] = ot_ref[...].T.astype(BF16)

    def back(first, size, left):
        at = pl.ds(pl.multiple_of(first, size), size)
        values = x_ref[at, 2 * width : 3 * width]
        probs_low, grads_low = [], []
        for h in range(heads):
            own = slice(h * HEAD_DIM, (h + 1) * HEAD_DIM)
            probs_grad = product(values, grads_t[h][:, left:])
            probs = s_ref[h, at, left:] * inverse[h][:, left:]
            scores_grad = (probs * (probs_grad - deltas[h][:, left:])).astype(BF16)
            probs_low.append(probs.astype(BF16))
            grads_low.append(scores_grad)
            dqt_ref[own, left:] += product(kt_ref[own, at], scores_grad)
        dva_ref[at, :] += product(jnp.concatenate(probs_low, axis=1), jnp.concatenate([x[left:] for x in spread_grads], axis=0))
        dka_ref[at, :] += product(jnp.concatenate(grads_low, axis=1), jnp.concatenate([x[left:] for x in spread_queries], axis=0))

    lax.fori_loop(0, i, lambda j, carry: (back(j * tile, tile, 0), carry)[1], 0)
    for first, size, left in corners:
        back(i * tile + first, size, left)
    out_ref[rows, width : 2 * width] = (dqt_ref[...].T * scale).astype(BF16)

    @pl.when(i == tiles - 1)
    def _():
        out_ref[:, 2 * width : 3 * width] = dka_ref[...].astype(BF16)
        out_ref[:, 3 * width : 4 * width] = dva_ref[...].astype(BF16)


def attention(dealt, documents, heads, edge):
    length = dealt.shape[0]
    width = heads * HEAD_DIM
    tile = 2 * edge
    pairs = length * length // 2 * heads
    whole = lambda i: (0, 0)
    return pl.pallas_call(
        functools.partial(attention_kernel, width, heads, tile, edge, length),
        grid=(length // tile,),
        out_shape=jax.ShapeDtypeStruct((length, 4 * width), BF16),
        in_specs=[pl.BlockSpec((length, 4 * width), whole), pl.BlockSpec((1, length), whole)],
        out_specs=pl.BlockSpec((length, 4 * width), whole),
        scratch_shapes=[
            pltpu.VMEM((length, 128), F32), pltpu.VMEM((heads, length, tile), F32), pltpu.VMEM((width, length), BF16), pltpu.VMEM((width, length), BF16),
            pltpu.VMEM((width, tile), F32), pltpu.VMEM((width, tile), F32), pltpu.VMEM((length, width), F32), pltpu.VMEM((length, width), F32),
            pltpu.VMEM((heads, 8, tile), F32)],
        compiler_params=pltpu.CompilerParams(vmem_limit_bytes=VMEM_LIMIT),
        cost_estimate=pl.CostEstimate(flops=pairs * 64 * 2 * 6 * 4, bytes_accessed=length * width * 20, transcendentals=pairs),
        name="attention",
    )(dealt, documents)


def on_device(
    grid,
    history,
    documents,
    cotangent,
    mixer_gain,
    mixer_inner,
    mixer_outer,
    mixer_bias,
    stream_gain,
    stream_bias,
    inbound_weight,
    inbound_bias,
    outbound_weight,
    outbound_bias,
    expand,
    expand_bias,
    contract,
    contract_bias,
):
    n_dp, n_seq, nz = grid.n_dp, grid.n_seq, grid.nz
    tokens, width = history.shape[2], history.shape[3]
    hidden_width = expand.shape[1]
    half, hidden_half = width // 2, hidden_width // 2
    both = 2 * tokens
    length = documents.shape[1]
    mix = mixer_bias.shape[0]
    heads = HEADS // n_seq
    own_width = heads * HEAD_DIM
    pick = lambda base, n: (lambda core: base + core * n)
    parts = 4
    piece = hidden_half // parts
    feed = []
    for part in range(parts):
        base = lambda core, part=part: core * hidden_half + part * piece
        feed.append((2, base, 4, part * piece, piece, "ba"))
        feed.append((3, base, 5, part * piece, piece, "ab"))
    pairs = [[4 + 2 * part, 5 + 2 * part] for part in range(parts)]
    inner_t = mixer_inner.T
    lowered, grad_low, streams, mix_pre, coeffs, tables, weights, (weight_e, weight_c), dealt = mix_forward(
        grid,
        history,
        cotangent,
        [mixer_gain.reshape(-1, 128), inner_t, mixer_outer, mixer_bias[None], stream_gain, stream_bias, inbound_bias.reshape(-1, 128)],
        [inbound_weight, outbound_weight, expand, contract],
        [
            (0, pick(width, half), 1, 0, half, "ba"),
            (0, pick(2 * width, half), 2, 0, half, "ab"),
            (0, pick(0, half), 0, 0, half, "ba"),
            (1, pick(0, half), 3, 0, half, "ab"),
        ]
        + feed,
        [[0, 1], [2, 3]],
        pairs,
        [hidden_half] * 2,
        own_width,
        1,
    )

    returned = attention(dealt.reshape(length, 4 * own_width), documents, heads, tokens)
    returned = returned.reshape(nz, both, 4 * own_width)

    collected, feed_part, normed_feed, expand_bias_part, *rest = feed_forward(
        grid, returned, lowered, grad_low, weight_e, weight_c, expand_bias.reshape(-1, 128), STEPS, 3
    )

    orders = ("ab", "ba", "ab", "ba")
    bias_out = [outbound_bias.reshape(-1, 128), contract_bias.reshape(-1, 128)]
    mids, lates, last_parts = rest[:nz], rest[nz : 2 * nz], rest[2 * nz :]
    normed_own, normed_theirs, head_bias_part, layer_out, mid_sums, lasts, kept, leaving = unproject(
        grid, orders, mids, lates, last_parts, collected, lowered, grad_low, weights, feed_part, normed_feed, streams, bias_out, tables, own_width, 4
    )

    along_z = [[(s, (s // 2 + k) % nz * 2 + s % 2) for s in range(n_seq)] for k in range(nz)]
    folded = [lasts[0]] + [lax.ppermute(lasts[k], "seq", along_z[k]) for k in range(1, nz)]
    nb = grid.nb
    over_a = [(d, (d + nb) % n_dp) for d in range(n_dp)]
    over_b = [[(d, d // nb * nb + (d + k) % nb) for d in range(n_dp)] for k in range(1, nb)]
    came_a = lax.ppermute(leaving[0], "dp", over_a)
    came_b = [lax.ppermute(x, "dp", perm) for x, perm in zip(leaving[1:], over_b)]

    history_grad, *small = mix_backward(
        history, streams, normed_own, normed_theirs, cotangent, mix_pre, coeffs, [mixer_gain.reshape(-1, 128), inner_t, mixer_outer, stream_gain]
    )
    smalls = [*small, head_bias_part, expand_bias_part]
    summed, *owned = finish_sums(grid, orders, kept, [came_a, *came_b], [mid_sums, *folded], smalls, 5)
    layer_out, *small, inbound_grad, outbound_grad, expand_grad, contract_grad, again = hand_over(summed, layer_out, owned, mix, hidden_width)
    gain_grad, inner_grad, outer_grad, bias_grad, stream_gain_grad, stream_bias_grad, in_bias_grad, out_bias_grad, expand_bias_grad = small
    return (
        layer_out[None],
        history_grad,
        gain_grad.reshape(width),
        inner_grad.T,
        outer_grad,
        bias_grad.reshape(-1),
        stream_gain_grad,
        stream_bias_grad,
        inbound_grad,
        in_bias_grad.reshape(3 * width),
        outbound_grad,
        out_bias_grad.reshape(width),
        expand_grad,
        expand_bias_grad.reshape(hidden_width),
        contract_grad,
        again.reshape(width),
    )


def solution(mesh):
    rows = P(("dp", "seq"), None)
    placed = (
        P(None, "dp", "seq", None),
        P("dp", None),
        P("dp", "seq", None),
        P(),
        P(),
        P(),
        P(),
        P(),
        P(),
        rows,
        P(),
        rows,
        P(),
        rows,
        P(),
        rows,
        P(),
    )
    grid = Grid(mesh.shape["dp"], mesh.shape["seq"])
    return jax.shard_map(
        functools.partial(on_device, grid),
        mesh=mesh,
        in_specs=placed,
        out_specs=(
            P("dp", "seq", None),
            P(None, "dp", "seq", None),
            P(),
            P(),
            P(),
            P(),
            P(),
            P(),
            rows,
            P(),
            rows,
            P(),
            rows,
            P(),
            rows,
            P(),
        ),
        check_vma=False,
    )
```
